32 devices in a mesh: groups: 1, ctx: 16 (over z, y, core), uly: 2 (over x), rep: 1.
Axes of the slice: x: 2, y: 2, z: 4, core: 2. Of those that a mesh axis runs over, the one named last changes fastest.
Arguments:
- q_proj: bfloat16 [4096, 5120], P(('groups', 'ctx', 'rep', 'uly')), may hold values from -8 to 8
- k_proj: bfloat16 [4096, 5120], P(('groups', 'ctx', 'rep', 'uly')), may hold values from -8 to 8
- v_proj: bfloat16 [4096, 5120], P(('groups', 'ctx', 'rep', 'uly')), may hold values from -4 to 4
- kv_list: int32 [32, 16], P('groups'), may hold values from -1 to 31, as said below
Outputs:
- attended: bfloat16 [4096, 5120], P(('groups', 'ctx', 'rep', 'uly'))
The draws below stay inside these ranges and needn't reach their ends.
Inputs may be any that keep to these rules, and one draw needn't show every extreme that they name: `kv_list`: frame f holds blocks f * 2 to (f + 1) * 2 - 1. Row i lists, in ascending order and padded with -1 at the end, the key blocks that query block i attends: all 2 blocks of its own frame and some blocks of frames at distance 1 to 7. For a query frame f and a distance d whose frame f + d exists, the blocks of frame f + d listed by the query blocks of f are exactly 1 distinct blocks if |d| = 1 and exactly one block if 2 <= |d| <= 7; up to |d| = 3 every query block of f lists all of them.
All inputs are finite; a program needn't handle non-finite values.
Results may differ from the reference program's by a relative error of at most 0.014.
Values may be sent and summed in bfloat16 or wider, within the bound.
No kernel may reach another device: no remote copies, remote signals or barrier semaphores. Data moves between devices by JAX's collectives and lax.ppermute only.
A program may use at most 128 MiB of HBM per device.

```python
import jax
import jax.numpy as jnp
from jax import lax

HEADS = 40
HD = 128
BLK = 128
BPF = 2
REACH = 7
FULL_REACH = 3
WIDTH = 5120
NEAR = 1
FRAMES = 16
BLOCKS = 32
SEQ = 4096


def draw_q_proj(key, part):
    base_draw = jnp.clip(jax.random.normal(jax.random.fold_in(key, 21), (SEQ, WIDTH), jnp.float32), -4.0, 4.0)
    return base_draw.astype(jnp.bfloat16)


def draw_k_proj(key, part):
    base_draw = jnp.clip(jax.random.normal(jax.random.fold_in(key, 31), (SEQ, WIDTH), jnp.float32), -4.0, 4.0)
    return base_draw.astype(jnp.bfloat16)


def draw_kv_list(key, part):
    offsets = [offset for offset in range(-REACH, REACH + 1) if offset != 0]
    frame_of = jnp.arange(BLOCKS, dtype=jnp.int32) // BPF
    place_in = jnp.arange(BLOCKS, dtype=jnp.int32) % BPF
    heavy_block = jax.random.randint(jax.random.fold_in(key, 1), (FRAMES,), 0, BPF)
    coin_flip = jax.random.randint(jax.random.fold_in(key, 2), (BLOCKS, len(offsets)), 0, 2)
    rank_draw = jax.random.randint(jax.random.fold_in(key, 3), (FRAMES, len(offsets), BPF), 0, 1 << 20)
    block_order = jnp.argsort(rank_draw * BPF + jnp.arange(BPF, dtype=jnp.int32), axis=-1).astype(jnp.int32)
    pieces = [frame_of[:, None] * BPF + jnp.arange(BPF, dtype=jnp.int32)[None, :]]
    for column, offset in enumerate(offsets):
        keep_count = NEAR if abs(offset) == 1 else 1
        source = frame_of + offset
        inside = (source >= 0) & (source < FRAMES)
        if abs(offset) <= FULL_REACH:
            listed = inside
        else:
            listed = inside & ((coin_flip[:, column] == 1) | (place_in == heavy_block[frame_of]))
        chosen = block_order[frame_of, column, :keep_count] + source[:, None] * BPF
        pieces.append(jnp.where(listed[:, None], chosen, -1))
    entries = jnp.concatenate(pieces, axis=1)
    beyond = BLOCKS + 1
    ordered = jnp.sort(jnp.where(entries >= 0, entries, beyond), axis=-1)
    return jnp.where(ordered == beyond, -1, ordered).astype(jnp.int32)


def level_of(stream_key, dims, cuts, least, high):
    loudness = 1.0
    for position, shards_of in cuts:
        steps = jax.random.uniform(jax.random.fold_in(jax.random.fold_in(stream_key, 6), position), (shards_of,), jnp.float32, least / len(cuts), high / len(cuts))
        loudness = loudness * jnp.repeat(jnp.exp(steps), dims[position] // shards_of).reshape((-1,) + (1,) * (len(dims) - 1 - position))
    return loudness


def scatter_about(rng, dims, scale, reach, cuts=(), kind=jnp.bfloat16):
    values = jax.random.normal(rng, dims, jnp.float32) * scale
    if len(cuts) > 0:
        values = level_of(rng, dims, cuts, -0.22, 0.18) * values
    return jnp.clip(values, min=-reach, max=reach).astype(kind)


def setup_inputs(seed: int = 0, part: int = 0) -> dict:
    seeds = jax.random.split(jax.random.key(seed), 5)
    part_splits = jax.random.split(jax.random.fold_in(seeds[4], part), 5)
    return {
        "q_proj": draw_q_proj(jax.random.fold_in(jax.random.fold_in(seeds[4], part), 71), part),
        "k_proj": draw_k_proj(jax.random.fold_in(jax.random.fold_in(seeds[4], part), 71), part),
        "v_proj": scatter_about(part_splits[2], (SEQ, WIDTH), 1.0, 4.0, ((0, 32),)),
        "kv_list": draw_kv_list(jax.random.fold_in(jax.random.fold_in(seeds[4], part), 71), part),
    }


def reference(q_proj, k_proj, v_proj, kv_list):
    seq_len, width = q_proj.shape
    block_count = seq_len // BLK
    q_tiles = q_proj.reshape(block_count, BLK, HEADS, HD)
    k_tiles = k_proj.reshape(block_count, BLK, HEADS, HD)
    v_tiles = v_proj.reshape(block_count, BLK, HEADS, HD)
    score_scale = HD ** -0.5

    def one_block(inputs):
        query, listed = inputs
        usable = listed >= 0
        safe_ids = jnp.where(usable, listed, 0).astype(jnp.int32)
        key_rows = jnp.take(k_tiles, safe_ids, axis=0).astype(jnp.float32)
        value_rows = jnp.take(v_tiles, safe_ids, axis=0).astype(jnp.float32)
        scores = jnp.einsum("qhd,lkhd->hqlk", query.astype(jnp.float32), key_rows) * score_scale
        scores = jnp.where(usable[None, None, :, None], scores, -jnp.inf)
        row_max = jnp.max(scores, axis=(2, 3), keepdims=True)
        exp_scores = jnp.exp(scores - row_max)
        row_total = jnp.sum(exp_scores, axis=(2, 3))
        weights = lax.optimization_barrier(exp_scores.astype(jnp.bfloat16)).astype(jnp.float32)
        mixed = jnp.einsum("hqlk,lkhd->qhd", weights, value_rows)
        return (mixed / jnp.transpose(row_total)[:, :, None]).astype(jnp.bfloat16)

    attended = lax.map(one_block, (q_tiles, kv_list))
    return attended.reshape(seq_len, width)
```

```python
import functools
import math

import jax
import jax.numpy as jnp
from jax import lax
from jax.experimental import pallas as pl
from jax.experimental.pallas import tpu as pltpu
from jax.sharding import Mesh, PartitionSpec as P

HD = 128
BLK = 128
BPF = 2
REACH = 7
CHUNKS = (1, 2, 2)

very_low = -1e30
to_log2 = math.log2(math.e) * HD ** -0.5
distances = [d for d in range(-REACH, REACH + 1) if d != 0]


def attend_kernel(frames, pieces_of, code_ref, q_ref, *refs):
    *piece_refs, out_ref, store, sems = refs
    heads = q_ref.shape[2] // HD
    copies = []
    start = 0
    for number, piece in enumerate(piece_refs):
        size = piece.shape[0]
        copies.append(pltpu.make_async_copy(piece, store.at[pl.ds(start, size)], sems.at[number]))
        copies[-1].start()
        start += size
    for copy in copies:
        copy.wait()

    per_frame = BPF * pieces_of
    width = len(distances)

    def item(index, carry):
        frame = index // heads
        head = index - frame * heads
        columns = pl.ds(pl.multiple_of(head * HD, HD), HD)

        def block(kind, position, count):
            rows = store[pl.ds(position, count), kind, :, columns]
            return rows.reshape(rows.shape[0] * rows.shape[1], HD)

        places = []
        biases = []
        for place, distance in enumerate(distances):
            codes = [code_ref[(frame * BPF + b) * width + place] for b in range(BPF)]
            pick = jnp.maximum(codes[0], codes[1]) // 2
            relative = frame + (distance + REACH)
            position = relative * BPF - 1 + pick
            if distance == -REACH:
                position = jnp.where(relative == 0, 0, position)
            if distance == REACH:
                position = jnp.where(frame == frames - 1, relative * BPF - 1, position)
            places.append(position * pieces_of)
            biases.append([jnp.where(code > 0, 0.0, very_low).astype(jnp.float32) for code in codes])

        own = ((frame + REACH) * BPF - 1) * pieces_of
        queries = q_ref[pl.ds(frame * per_frame, per_frame), :, columns].reshape(BPF * BLK, HD)

        def keys_or_values(kind):
            found = [block(kind, own, per_frame)]
            for a in range(0, width, 2):
                found.append(
                    jnp.concatenate([block(kind, places[a], pieces_of), block(kind, places[a + 1], pieces_of)], axis=0)
                )
            return found

        keys = keys_or_values(0)
        tiles = [[] for _ in range(BPF)]
        for pair, key in enumerate(keys):
            scores = lax.dot_general(queries, key, (((1,), (1,)), ((), ())), preferred_element_type=jnp.float32)
            for b in range(BPF):
                for side in range(2):
                    tile = scores[b * BLK : (b + 1) * BLK, side * BLK : (side + 1) * BLK]
                    if pair > 0:
                        tile = tile + biases[2 * (pair - 1) + side][b]
                    tiles[b].append(tile)
        weights = []
        totals = []
        for b in range(BPF):
            row_max = jnp.max(functools.reduce(jnp.maximum, tiles[b]), axis=1, keepdims=True)
            exps = [jnp.exp2((tile - row_max) * to_log2) for tile in tiles[b]]
            totals.append(jnp.sum(functools.reduce(jnp.add, exps), axis=1, keepdims=True))
            weights.append(jnp.concatenate([e.astype(jnp.bfloat16) for e in exps], axis=1))
        values = jnp.concatenate(keys_or_values(1), axis=0)
        mixed = jnp.dot(jnp.concatenate(weights, axis=0), values, preferred_element_type=jnp.float32)
        result = (mixed / jnp.concatenate(totals, axis=0)).astype(jnp.bfloat16)
        out_ref[pl.ds(frame * per_frame, per_frame), :, columns] = result.reshape(per_frame, BLK // pieces_of, HD)
        return carry

    lax.fori_loop(0, frames * heads, item, 0)


def attend(codes, queries, pieces, frames):
    pieces_of = BLK // queries.shape[1]
    rows, width = queries.shape[1:]
    heads = width // HD
    stored = sum(piece.shape[0] for piece in pieces)
    whole = pl.BlockSpec(memory_space=pltpu.VMEM)
    pairs = frames * BPF * heads * (2 * REACH + BPF)
    return pl.pallas_call(
        functools.partial(attend_kernel, frames, pieces_of),
        out_shape=jax.ShapeDtypeStruct(queries.shape, jnp.bfloat16),
        in_specs=[pl.BlockSpec(memory_space=pltpu.SMEM), whole] + [pl.BlockSpec(memory_space=pl.ANY)] * len(pieces),
        out_specs=whole,
        scratch_shapes=[
            pltpu.VMEM((stored, 2, rows, width), jnp.bfloat16),
            pltpu.SemaphoreType.DMA((len(pieces),)),
        ],
        compiler_params=pltpu.CompilerParams(vmem_limit_bytes=32 * 1024 * 1024),
        cost_estimate=pl.CostEstimate(
            flops=pairs * 4 * BLK * BLK * HD,
            bytes_accessed=2 * (stored * 2 + 2 * queries.shape[0]) * rows * width,
            transcendentals=pairs * BLK * BLK,
        ),
    )(codes, queries, *pieces)


def on_device(outer, inner, q_proj, k_proj, v_proj, kv_list):
    frames = inner
    rows, model_width = q_proj.shape
    team = ("inner", "rep", "uly")
    team_size = frames * BPF * BLK // rows
    heads_here = model_width // HD // team_size
    pieces_of = BLK // rows
    per_frame = BPF * pieces_of
    my_group = lax.axis_index("outer")

    def rows_of(reader_frame, count):
        start = jnp.clip(reader_frame * BPF, 0, kv_list.shape[0] - count * BPF)
        return lax.dynamic_slice_in_dim(kv_list, start, count * BPF, 0)

    lists = rows_of(my_group * frames, frames).reshape(frames, BPF, 1, -1)
    first_ids = BPF * (
        my_group * frames + jnp.arange(frames, dtype=jnp.int32)[:, None] + jnp.array(distances, jnp.int32)[None, :]
    )[:, None, :, None]
    hits = jnp.where(lists == first_ids, 1, 0) + jnp.where(lists == first_ids + 1, 2, 0)
    codes = jnp.sum(jnp.where(lists >= 0, hits, 0), axis=-1).reshape(-1)

    def picked(reader_frame, holder_frame):
        return jnp.any(rows_of(reader_frame, 1) == holder_frame * BPF + 1).astype(jnp.int32)

    bounds = []
    low = 0
    assert sum(CHUNKS) == heads_here
    for heads in CHUNKS:
        bounds.append((low * team_size * HD, (low + heads) * team_size * HD))
        low += heads

    def packed(array, bound):
        part = array[:, bound[0] : bound[1]]
        return jnp.transpose(part.reshape(rows, team_size, -1), (1, 0, 2))

    def exchange(array):
        return lax.all_to_all(array, team, split_axis=0, concat_axis=0, tiled=True)

    owned = [exchange(jnp.stack([packed(k_proj, b), packed(v_proj, b)], axis=1)) for b in bounds]
    queries = [exchange(packed(q_proj, b)) for b in bounds]

    def shifted(array, heading):
        route = [(i, i + heading) for i in range(outer) if 0 <= i + heading < outer]
        return lax.ppermute(array, "outer", route)

    hops = -(-REACH // frames)

    def halo(own):
        found = {}
        for heading in (1, -1):
            held = own
            held_frames = frames
            for hop in range(1, hops + 1):
                spare = hop * frames - REACH
                keep = frames - max(0, spare)
                single = spare >= 0
                if keep < held_frames or single:
                    whole = (keep - 1 if single else keep) * per_frame
                    if heading == 1:
                        kept = held[held.shape[0] - whole :]
                        edge = held.shape[0] - whole - per_frame
                        reader = (my_group + 1) * frames
                        holder = reader - REACH
                    else:
                        kept = held[:whole]
                        edge = whole
                        reader = my_group * frames - 1
                        holder = reader + REACH
                    if single:
                        place = edge + pieces_of * picked(reader, holder)
                        one = lax.dynamic_slice_in_dim(held, place, pieces_of, 0)
                        kept = jnp.concatenate([one, kept] if heading == 1 else [kept, one], axis=0)
                    held = kept
                held = shifted(held, heading)
                held_frames = keep
                found[heading, hop] = held
        lefts = [found[1, hop] for hop in range(hops, 0, -1)]
        rights = [found[-1, hop] for hop in range(1, hops + 1)]
        return lefts + [own] + rights

    outs = []
    for own, query in zip(owned, queries):
        result = exchange(attend(codes, query, halo(own), frames))
        outs.append(jnp.transpose(result, (1, 0, 2)).reshape(rows, -1))
    return jnp.concatenate(outs, axis=1)


def solution(mesh):
    sizes = dict(mesh.shape)
    members = sizes["uly"] * sizes["rep"]
    heads = 40
    inner = max(
        i for i in range(1, sizes["ctx"] + 1) if sizes["ctx"] % i == 0 and heads % (i * members) == 0
    )
    outer = sizes["ctx"] // inner
    finer = Mesh(
        mesh.devices.reshape(sizes["groups"], outer, inner, sizes["uly"], sizes["rep"]),
        ("groups", "outer", "inner", "uly", "rep"),
    )
    split = P(("groups", "outer", "inner", "rep", "uly"), None)
    return jax.shard_map(
        functools.partial(on_device, outer, inner),
        mesh=finer,
        in_specs=(split, split, split, P("groups", None)),
        out_specs=split,
        check_vma=False,
    )
```

```python
import functools
import math

import jax
import jax.numpy as jnp
from jax import lax
from jax.experimental import pallas as pl
from jax.experimental.pallas import tpu as pltpu
from jax.sharding import Mesh, PartitionSpec as P

HD = 128
BLK = 128
BPF = 2
REACH = 7
CHUNKS = (1, 2, 2)

very_low = -1e30
to_log2 = math.log2(math.e) * HD ** -0.5
distances = [d for d in range(-REACH, REACH + 1) if d != 0]


def run_copies(pairs, sems):
    copies = [pltpu.make_async_copy(source, target, sems.at[i]) for i, (source, target) in enumerate(pairs)]
    for copy in copies:
        copy.start()
    for copy in copies:
        copy.wait()


def copy_call(kernel, out_shape, copies, operands, scalars=(), after=()):
    anywhere = pl.BlockSpec(memory_space=pl.ANY)

    def body(*refs):
        used = refs[: len(scalars) + len(operands)]
        run_copies(kernel(*used, refs[-2]), refs[-1])

    return pl.pallas_call(
        body,
        out_shape=out_shape,
        in_specs=[pl.BlockSpec(memory_space=pltpu.SMEM)] * len(scalars) + [anywhere] * (len(operands) + len(after)),
        out_specs=anywhere,
        scratch_shapes=[pltpu.SemaphoreType.DMA((copies,))],
        cost_estimate=pl.CostEstimate(flops=0, bytes_accessed=4 * math.prod(out_shape.shape), transcendentals=0),
    )(*scalars, *operands, *after)


def pack(arrays, starts, widths, team_size, after=()):
    rows = arrays[0].shape[0]

    def kernel(*refs):
        *sources, out = refs
        pairs = []
        for member in range(team_size):
            for kind, source in enumerate(sources):
                low = 0
                for start, width in zip(starts, widths):
                    pairs.append(
                        (
                            source.at[:, pl.ds(start + member * width, width)],
                            out.at[member, kind, :, pl.ds(low, width)],
                        )
                    )
                    low += width
        return pairs

    shape = jax.ShapeDtypeStruct((team_size, len(arrays), rows, sum(widths)), jnp.bfloat16)
    return copy_call(kernel, shape, team_size * len(arrays) * len(starts), arrays, after=after)


def unpack(parts, starts, model_width):
    def kernel(*refs):
        *sources, out = refs
        return [
            (source.at[member], out.at[:, pl.ds(start + member * source.shape[2], source.shape[2])])
            for start, source in zip(starts, sources)
            for member in range(source.shape[0])
        ]

    shape = jax.ShapeDtypeStruct((parts[0].shape[1], model_width), jnp.bfloat16)
    return copy_call(kernel, shape, sum(part.shape[0] for part in parts), parts)


def select(held, place, count, whole_start, whole, heading):
    def kernel(place_ref, source, out):
        one, rest = (0, count) if heading == 1 else (whole, 0)
        pairs = [(source.at[pl.ds(place_ref[0], count)], out.at[pl.ds(one, count)])]
        if whole > 0:
            pairs.append((source.at[pl.ds(whole_start, whole)], out.at[pl.ds(rest, whole)]))
        return pairs

    shape = jax.ShapeDtypeStruct((count + whole,) + held.shape[1:], held.dtype)
    return copy_call(kernel, shape, 2, [held], scalars=[place])


def attend_kernel(frames, pieces_of, heads, first_head, code_ref, q_ref, *refs):
    *piece_refs, out_ref, store, sems = refs
    pairs = []
    start = 0
    for piece in piece_refs:
        pairs.append((piece, store.at[pl.ds(start, piece.shape[0])]))
        start += piece.shape[0]
    run_copies(pairs, sems)

    per_frame = BPF * pieces_of
    width = len(distances)

    def item(index, carry):
        frame = index // heads
        head = index - frame * heads
        columns = pl.ds(pl.multiple_of(head * HD, HD), HD)
        q_columns = pl.ds(pl.multiple_of((head + first_head) * HD, HD), HD)

        def block(kind, position, count):
            rows = store[pl.ds(position, count), kind, :, columns]
            return rows.reshape(rows.shape[0] * rows.shape[1], HD)

        places = []
        biases = []
        for place, distance in enumerate(distances):
            codes = [code_ref[(frame * BPF + b) * width + place] for b in range(BPF)]
            pick = jnp.maximum(codes[0], codes[1]) // 2
            relative = frame + (distance + REACH)
            position = relative * BPF - 1 + pick
            if distance == -REACH:
                position = jnp.where(relative == 0, 0, position)
            if distance == REACH:
                position = jnp.where(frame == frames - 1, relative * BPF - 1, position)
            places.append(position * pieces_of)
            biases.append([jnp.where(code > 0, 0.0, very_low).astype(jnp.float32) for code in codes])

        own = ((frame + REACH) * BPF - 1) * pieces_of
        queries = q_ref[pl.ds(frame * per_frame, per_frame), 0, :, q_columns].reshape(BPF * BLK, HD)

        def keys_or_values(kind):
            found = [block(kind, own, per_frame)]
            for a in range(0, width, 2):
                found.append(
                    jnp.concatenate([block(kind, places[a], pieces_of), block(kind, places[a + 1], pieces_of)], axis=0)
                )
            return found

        keys = keys_or_values(0)
        tiles = [[] for _ in range(BPF)]
        for pair, key in enumerate(keys):
            scores = lax.dot_general(queries, key, (((1,), (1,)), ((), ())), preferred_element_type=jnp.float32)
            for b in range(BPF):
                for side in range(2):
                    tile = scores[b * BLK : (b + 1) * BLK, side * BLK : (side + 1) * BLK]
                    if pair > 0:
                        tile = tile + biases[2 * (pair - 1) + side][b]
                    tiles[b].append(tile)
        weights = []
        totals = []
        for b in range(BPF):
            row_max = jnp.max(functools.reduce(jnp.maximum, tiles[b]), axis=1, keepdims=True)
            exps = [jnp.exp2((tile - row_max) * to_log2) for tile in tiles[b]]
            totals.append(jnp.sum(functools.reduce(jnp.add, exps), axis=1, keepdims=True))
            weights.append(jnp.concatenate([e.astype(jnp.bfloat16) for e in exps], axis=1))
        values = jnp.concatenate(keys_or_values(1), axis=0)
        mixed = jnp.dot(jnp.concatenate(weights, axis=0), values, preferred_element_type=jnp.float32)
        result = (mixed / jnp.concatenate(totals, axis=0)).astype(jnp.bfloat16)
        out_ref[pl.ds(frame * per_frame, per_frame), :, columns] = result.reshape(per_frame, BLK // pieces_of, HD)
        return carry

    lax.fori_loop(0, frames * heads, item, 0)


def attend(codes, queries, pieces, frames, first_head, after=()):
    members, _, rows, _ = queries.shape
    pieces_of = BLK // rows
    width = pieces[0].shape[3]
    heads = width // HD
    stored = sum(piece.shape[0] for piece in pieces)
    whole = pl.BlockSpec(memory_space=pltpu.VMEM)
    anywhere = pl.BlockSpec(memory_space=pl.ANY)
    pairs = frames * BPF * heads * (2 * REACH + BPF)

    def body(code_ref, q_ref, *refs):
        kept = refs[: len(pieces)] + refs[len(pieces) + len(after) :]
        attend_kernel(frames, pieces_of, heads, first_head, code_ref, q_ref, *kept)

    return pl.pallas_call(
        body,
        out_shape=jax.ShapeDtypeStruct((members, rows, width), jnp.bfloat16),
        in_specs=[pl.BlockSpec(memory_space=pltpu.SMEM), whole] + [anywhere] * (len(pieces) + len(after)),
        out_specs=whole,
        scratch_shapes=[
            pltpu.VMEM((stored, 2, rows, width), jnp.bfloat16),
            pltpu.SemaphoreType.DMA((len(pieces),)),
        ],
        compiler_params=pltpu.CompilerParams(vmem_limit_bytes=32 * 1024 * 1024),
        cost_estimate=pl.CostEstimate(
            flops=6 * pairs * 4 * BLK * BLK * HD,
            bytes_accessed=2 * (stored * 2 + 2 * members) * rows * width,
            transcendentals=pairs * BLK * BLK,
        ),
    )(codes, queries, *pieces, *after)


def on_device(outer, inner, q_proj, k_proj, v_proj, kv_list):
    frames = inner
    rows, model_width = q_proj.shape
    team = ("inner", "rep", "uly")
    team_size = frames * BPF * BLK // rows
    heads_here = model_width // HD // team_size
    pieces_of = BLK // rows
    per_frame = BPF * pieces_of
    my_group = lax.axis_index("outer")

    def rows_of(reader_frame, count):
        start = jnp.clip(reader_frame * BPF, 0, kv_list.shape[0] - count * BPF)
        return lax.dynamic_slice_in_dim(kv_list, start, count * BPF, 0)

    lists = rows_of(my_group * frames, frames).reshape(frames, BPF, 1, -1)
    first_ids = BPF * (
        my_group * frames + jnp.arange(frames, dtype=jnp.int32)[:, None] + jnp.array(distances, jnp.int32)[None, :]
    )[:, None, :, None]
    hits = jnp.where(lists == first_ids, 1, 0) + jnp.where(lists == first_ids + 1, 2, 0)
    codes = jnp.sum(jnp.where(lists >= 0, hits, 0), axis=-1).reshape(-1)

    def picked(reader_frame, holder_frame):
        return jnp.any(rows_of(reader_frame, 1) == holder_frame * BPF + 1).astype(jnp.int32)

    assert sum(CHUNKS) == heads_here
    widths = [heads * HD for heads in CHUNKS]
    lows = [sum(CHUNKS[:c]) for c in range(len(CHUNKS))]
    starts = [low * team_size * HD for low in lows]

    def exchange(array):
        return lax.all_to_all(array, team, split_axis=0, concat_axis=0, tiled=True)

    def shifted(array, heading):
        route = [(i, i + heading) for i in range(outer) if 0 <= i + heading < outer]
        return lax.ppermute(array, "outer", route)

    hops = -(-REACH // frames)

    def halo(own):
        found = {}
        held = {1: own, -1: own}
        held_frames = frames
        for hop in range(1, hops + 1):
            spare = hop * frames - REACH
            keep = frames - max(0, spare)
            single = spare >= 0
            whole = (keep - 1 if single else keep) * per_frame
            for heading in (1, -1):
                mine = held[heading]
                if single:
                    if heading == 1:
                        edge = mine.shape[0] - whole - per_frame
                        reader = (my_group + 1) * frames
                        holder = reader - REACH
                    else:
                        edge = whole
                        reader = my_group * frames - 1
                        holder = reader + REACH
                    place = (edge + pieces_of * picked(reader, holder)).reshape(1)
                    whole_start = mine.shape[0] - whole if heading == 1 else 0
                    mine = select(mine, place, pieces_of, whole_start, whole, heading)
                elif keep < held_frames:
                    mine = mine[mine.shape[0] - whole :] if heading == 1 else mine[:whole]
                held[heading] = shifted(mine, heading)
                found[heading, hop] = held[heading]
            held_frames = keep
        lefts = [found[1, hop] for hop in range(hops, 0, -1)]
        rights = [found[-1, hop] for hop in range(1, hops + 1)]
        return lefts + [own] + rights, found[1, 1]

    chunks = range(len(CHUNKS))
    owned = []
    pieces = []
    for c in chunks:
        after = [first_arrival] if c >= 2 else []
        packed = pack([k_proj, v_proj], [starts[c]], [widths[c]], team_size, after=after)
        owned.append(exchange(packed))
        near, arrival = halo(owned[c])
        pieces.append(near)
        if c == 0:
            first_arrival = arrival
    queries = exchange(pack([q_proj], starts, widths, team_size))

    outs = []
    results = []
    for c in chunks:
        results.append(attend(codes, queries, pieces[c], frames, lows[c], after=results[-1:]))
        outs.append(exchange(results[c]))
    return unpack(outs, starts, model_width)


def solution(mesh):
    sizes = dict(mesh.shape)
    members = sizes["uly"] * sizes["rep"]
    heads = 40
    inner = max(
        i for i in range(1, sizes["ctx"] + 1) if sizes["ctx"] % i == 0 and heads % (i * members) == 0
    )
    outer = sizes["ctx"] // inner
    finer = Mesh(
        mesh.devices.reshape(sizes["groups"], outer, inner, sizes["uly"], sizes["rep"]),
        ("groups", "outer", "inner", "uly", "rep"),
    )
    split = P(("groups", "outer", "inner", "rep", "uly"), None)
    return jax.shard_map(
        functools.partial(on_device, outer, inner),
        mesh=finer,
        in_specs=(split, split, split, P("groups", None)),
        out_specs=split,
        check_vma=False,
    )
```

```python
import functools
import math

import jax
import jax.numpy as jnp
from jax import lax
from jax.experimental import pallas as pl
from jax.experimental.pallas import tpu as pltpu
from jax.sharding import Mesh, PartitionSpec as P

HD = 128
BLK = 128
BPF = 2
REACH = 7
CHUNKS = (1, 2, 2)

very_low = -1e30
to_log2 = math.log2(math.e) * HD ** -0.5
distances = [d for d in range(-REACH, REACH + 1) if d != 0]


def run_copies(pairs, sems):
    copies = [pltpu.make_async_copy(source, target, sems.at[i]) for i, (source, target) in enumerate(pairs)]
    for copy in copies:
        copy.start()
    for copy in copies:
        copy.wait()


def copy_call(kernel, out_shape, copies, operands, scalars=(), after=()):
    anywhere = pl.BlockSpec(memory_space=pl.ANY)

    def body(*refs):
        used = refs[: len(scalars) + len(operands)]
        run_copies(kernel(*used, refs[-2]), refs[-1])

    return pl.pallas_call(
        body,
        out_shape=out_shape,
        in_specs=[pl.BlockSpec(memory_space=pltpu.SMEM)] * len(scalars) + [anywhere] * (len(operands) + len(after)),
        out_specs=pl.BlockSpec(memory_space=pltpu.VMEM),
        scratch_shapes=[pltpu.SemaphoreType.DMA((copies,))],
        compiler_params=pltpu.CompilerParams(vmem_limit_bytes=16 * 1024 * 1024),
        cost_estimate=pl.CostEstimate(flops=0, bytes_accessed=4 * math.prod(out_shape.shape), transcendentals=0),
    )(*scalars, *operands, *after)


def pack(arrays, starts, widths, team_size, after=()):
    rows = arrays[0].shape[0]

    def kernel(*refs):
        *sources, out = refs
        pairs = []
        for member in range(team_size):
            for kind, source in enumerate(sources):
                low = 0
                for start, width in zip(starts, widths):
                    pairs.append(
                        (
                            source.at[:, pl.ds(start + member * width, width)],
                            out.at[member, kind, :, pl.ds(low, width)],
                        )
                    )
                    low += width
        return pairs

    shape = jax.ShapeDtypeStruct((team_size, len(arrays), rows, sum(widths)), jnp.bfloat16)
    return copy_call(kernel, shape, team_size * len(arrays) * len(starts), arrays, after=after)


def unpack(parts, starts, model_width):
    def kernel(*refs):
        *sources, out = refs
        return [
            (source.at[member], out.at[:, pl.ds(start + member * source.shape[2], source.shape[2])])
            for start, source in zip(starts, sources)
            for member in range(source.shape[0])
        ]

    shape = jax.ShapeDtypeStruct((parts[0].shape[1], model_width), jnp.bfloat16)
    return copy_call(kernel, shape, sum(part.shape[0] for part in parts), parts)


def select(held, place, count, whole_start, whole, heading):
    def kernel(place_ref, source, out):
        one, rest = (0, count) if heading == 1 else (whole, 0)
        pairs = [(source.at[pl.ds(place_ref[0], count)], out.at[pl.ds(one, count)])]
        if whole > 0:
            pairs.append((source.at[pl.ds(whole_start, whole)], out.at[pl.ds(rest, whole)]))
        return pairs

    shape = jax.ShapeDtypeStruct((count + whole,) + held.shape[1:], held.dtype)
    return copy_call(kernel, shape, 2, [held], scalars=[place])


def attend_kernel(frames, pieces_of, heads, first_head, code_ref, q_ref, *refs):
    *piece_refs, out_ref, store, sems = refs
    pairs = []
    start = 0
    for piece in piece_refs:
        pairs.append((piece, store.at[pl.ds(start, piece.shape[0])]))
        start += piece.shape[0]
    run_copies(pairs, sems)

    per_frame = BPF * pieces_of
    width = len(distances)

    def item(index, carry):
        frame = index // heads
        head = index - frame * heads
        columns = pl.ds(pl.multiple_of(head * HD, HD), HD)
        q_columns = pl.ds(pl.multiple_of((head + first_head) * HD, HD), HD)

        def block(kind, position, count):
            rows = store[pl.ds(position, count), kind, :, columns]
            return rows.reshape(rows.shape[0] * rows.shape[1], HD)

        places = []
        biases = []
        for place, distance in enumerate(distances):
            codes = [code_ref[(frame * BPF + b) * width + place] for b in range(BPF)]
            pick = jnp.maximum(codes[0], codes[1]) // 2
            relative = frame + (distance + REACH)
            position = relative * BPF - 1 + pick
            if distance == -REACH:
                position = jnp.where(relative == 0, 0, position)
            if distance == REACH:
                position = jnp.where(frame == frames - 1, relative * BPF - 1, position)
            places.append(position * pieces_of)
            biases.append([jnp.where(code > 0, 0.0, very_low).astype(jnp.float32) for code in codes])

        own = ((frame + REACH) * BPF - 1) * pieces_of
        queries = q_ref[pl.ds(frame * per_frame, per_frame), 0, :, q_columns].reshape(BPF * BLK, HD)

        def keys_or_values(kind):
            found = [block(kind, own, per_frame)]
            for a in range(0, width, 2):
                found.append(
                    jnp.concatenate([block(kind, places[a], pieces_of), block(kind, places[a + 1], pieces_of)], axis=0)
                )
            return found

        keys = keys_or_values(0)
        tiles = [[] for _ in range(BPF)]
        for pair, key in enumerate(keys):
            scores = lax.dot_general(queries, key, (((1,), (1,)), ((), ())), preferred_element_type=jnp.float32)
            for b in range(BPF):
                for side in range(2):
                    tile = scores[b * BLK : (b + 1) * BLK, side * BLK : (side + 1) * BLK]
                    if pair > 0:
                        tile = tile + biases[2 * (pair - 1) + side][b]
                    tiles[b].append(tile)
        weights = []
        totals = []
        for b in range(BPF):
            row_max = jnp.max(functools.reduce(jnp.maximum, tiles[b]), axis=1, keepdims=True)
            exps = [jnp.exp2((tile - row_max) * to_log2) for tile in tiles[b]]
            totals.append(jnp.sum(functools.reduce(jnp.add, exps), axis=1, keepdims=True))
            weights.append(jnp.concatenate([e.astype(jnp.bfloat16) for e in exps], axis=1))
        values = jnp.concatenate(keys_or_values(1), axis=0)
        mixed = jnp.dot(jnp.concatenate(weights, axis=0), values, preferred_element_type=jnp.float32)
        result = (mixed / jnp.concatenate(totals, axis=0)).astype(jnp.bfloat16)
        out_ref[pl.ds(frame * per_frame, per_frame), :, columns] = result.reshape(per_frame, BLK // pieces_of, HD)
        return carry

    lax.fori_loop(0, frames * heads, item, 0)


def attend(codes, queries, pieces, frames, first_head, after=()):
    members, _, rows, _ = queries.shape
    pieces_of = BLK // rows
    width = pieces[0].shape[3]
    heads = width // HD
    stored = sum(piece.shape[0] for piece in pieces)
    whole = pl.BlockSpec(memory_space=pltpu.VMEM)
    anywhere = pl.BlockSpec(memory_space=pl.ANY)
    pairs = frames * BPF * heads * (2 * REACH + BPF)

    def body(code_ref, q_ref, *refs):
        kept = refs[: len(pieces)] + refs[len(pieces) + len(after) :]
        attend_kernel(frames, pieces_of, heads, first_head, code_ref, q_ref, *kept)

    return pl.pallas_call(
        body,
        out_shape=jax.ShapeDtypeStruct((members, rows, width), jnp.bfloat16),
        in_specs=[pl.BlockSpec(memory_space=pltpu.SMEM), whole] + [anywhere] * (len(pieces) + len(after)),
        out_specs=whole,
        scratch_shapes=[
            pltpu.VMEM((stored, 2, rows, width), jnp.bfloat16),
            pltpu.SemaphoreType.DMA((len(pieces),)),
        ],
        compiler_params=pltpu.CompilerParams(vmem_limit_bytes=32 * 1024 * 1024),
        cost_estimate=pl.CostEstimate(
            flops=6 * pairs * 4 * BLK * BLK * HD,
            bytes_accessed=2 * (stored * 2 + 2 * members) * rows * width,
            transcendentals=pairs * BLK * BLK,
        ),
    )(codes, queries, *pieces, *after)


def on_device(outer, inner, q_proj, k_proj, v_proj, kv_list):
    frames = inner
    rows, model_width = q_proj.shape
    team = ("inner", "rep", "uly")
    team_size = frames * BPF * BLK // rows
    heads_here = model_width // HD // team_size
    pieces_of = BLK // rows
    per_frame = BPF * pieces_of
    my_group = lax.axis_index("outer")

    def rows_of(reader_frame, count):
        start = jnp.clip(reader_frame * BPF, 0, kv_list.shape[0] - count * BPF)
        return lax.dynamic_slice_in_dim(kv_list, start, count * BPF, 0)

    lists = rows_of(my_group * frames, frames).reshape(frames, BPF, 1, -1)
    first_ids = BPF * (
        my_group * frames + jnp.arange(frames, dtype=jnp.int32)[:, None] + jnp.array(distances, jnp.int32)[None, :]
    )[:, None, :, None]
    hits = jnp.where(lists == first_ids, 1, 0) + jnp.where(lists == first_ids + 1, 2, 0)
    codes = jnp.sum(jnp.where(lists >= 0, hits, 0), axis=-1).reshape(-1)

    def picked(reader_frame, holder_frame):
        return jnp.any(rows_of(reader_frame, 1) == holder_frame * BPF + 1).astype(jnp.int32)

    assert sum(CHUNKS) == heads_here
    widths = [heads * HD for heads in CHUNKS]
    lows = [sum(CHUNKS[:c]) for c in range(len(CHUNKS))]
    starts = [low * team_size * HD for low in lows]

    def exchange(array):
        return lax.all_to_all(array, team, split_axis=0, concat_axis=0, tiled=True)

    def shifted(array, heading):
        route = [(i, i + heading) for i in range(outer) if 0 <= i + heading < outer]
        return lax.ppermute(array, "outer", route)

    hops = -(-REACH // frames)

    def halo(own):
        found = {}
        held = {1: own, -1: own}
        held_frames = frames
        for hop in range(1, hops + 1):
            spare = hop * frames - REACH
            keep = frames - max(0, spare)
            single = spare >= 0
            whole = (keep - 1 if single else keep) * per_frame
            for heading in (1, -1):
                mine = held[heading]
                if single:
                    if heading == 1:
                        edge = mine.shape[0] - whole - per_frame
                        reader = (my_group + 1) * frames
                        holder = reader - REACH
                    else:
                        edge = whole
                        reader = my_group * frames - 1
                        holder = reader + REACH
                    place = (edge + pieces_of * picked(reader, holder)).reshape(1)
                    whole_start = mine.shape[0] - whole if heading == 1 else 0
                    mine = select(mine, place, pieces_of, whole_start, whole, heading)
                elif keep < held_frames:
                    mine = mine[mine.shape[0] - whole :] if heading == 1 else mine[:whole]
                held[heading] = shifted(mine, heading)
                found[heading, hop] = held[heading]
            held_frames = keep
        lefts = [found[1, hop] for hop in range(hops, 0, -1)]
        rights = [found[-1, hop] for hop in range(1, hops + 1)]
        return lefts + [own] + rights, found[1, 1]

    chunks = range(len(CHUNKS))
    owned = []
    pieces = []
    for c in chunks:
        after = [first_arrival] if c >= 2 else []
        packed = pack([k_proj, v_proj], [starts[c]], [widths[c]], team_size, after=after)
        owned.append(exchange(packed))
        near, arrival = halo(owned[c])
        pieces.append(near)
        if c == 0:
            first_arrival = arrival
    queries = exchange(pack([q_proj], starts, widths, team_size))

    outs = []
    results = []
    for c in chunks:
        results.append(attend(codes, queries, pieces[c], frames, lows[c], after=results[-1:]))
        outs.append(exchange(results[c]))
    return unpack(outs, starts, model_width)


def solution(mesh):
    sizes = dict(mesh.shape)
    members = sizes["uly"] * sizes["rep"]
    heads = 40
    inner = max(
        i for i in range(1, sizes["ctx"] + 1) if sizes["ctx"] % i == 0 and heads % (i * members) == 0
    )
    outer = sizes["ctx"] // inner
    finer = Mesh(
        mesh.devices.reshape(sizes["groups"], outer, inner, sizes["uly"], sizes["rep"]),
        ("groups", "outer", "inner", "uly", "rep"),
    )
    split = P(("groups", "outer", "inner", "rep", "uly"), None)
    return jax.shard_map(
        functools.partial(on_device, outer, inner),
        mesh=finer,
        in_specs=(split, split, split, P("groups", None)),
        out_specs=split,
        check_vma=False,
    )
```

```python
import functools
import math

import jax
import jax.numpy as jnp
from jax import lax
from jax.experimental import pallas as pl
from jax.experimental.pallas import tpu as pltpu
from jax.sharding import Mesh, PartitionSpec as P

HD = 128
BLK = 128
BPF = 2
REACH = 7
CHUNKS = (1, 2, 2)

very_low = -1e30
to_log2 = math.log2(math.e) * HD ** -0.5
distances = [d for d in range(-REACH, REACH + 1) if d != 0]


def staged_copies(steps, sems):
    count = len(steps)
    fetches = [pltpu.make_async_copy(s, stage, sems.at[i]) for i, (s, stage, t) in enumerate(steps)]
    puts = [pltpu.make_async_copy(stage, t, sems.at[count + i]) for i, (s, stage, t) in enumerate(steps)]
    for fetch in fetches:
        fetch.start()
    for fetch, put in zip(fetches, puts):
        fetch.wait()
        put.start()
    for put in puts:
        put.wait()


in_hbm = pl.BlockSpec(memory_space=pltpu.HBM)


def copy_call(plan, shapes, count, operands, scalars=(), after=()):
    def body(*refs):
        first = len(scalars)
        last = first + len(operands)
        results = refs[last + len(after) :]
        n = len(shapes)
        staged_copies(plan(refs[:first], refs[first:last], results[:n], results[n : 2 * n]), results[2 * n])

    return pl.pallas_call(
        body,
        out_shape=shapes,
        in_specs=[pl.BlockSpec(memory_space=pltpu.SMEM)] * len(scalars) + [in_hbm] * (len(operands) + len(after)),
        out_specs=[in_hbm] * len(shapes),
        scratch_shapes=[pltpu.VMEM(s.shape, s.dtype) for s in shapes] + [pltpu.SemaphoreType.DMA((2 * count,))],
        compiler_params=pltpu.CompilerParams(vmem_limit_bytes=16 * 1024 * 1024),
        cost_estimate=pl.CostEstimate(
            flops=0, bytes_accessed=sum(4 * math.prod(s.shape) for s in shapes), transcendentals=0
        ),
    )(*scalars, *operands, *after)


def pack(arrays, starts, widths, team_size, after=()):
    rows = arrays[0].shape[0]

    def plan(scalars, sources, outs, stages):
        steps = []
        for member in range(team_size):
            for kind, source in enumerate(sources):
                low = 0
                for start, width in zip(starts, widths):
                    place = (member, kind, slice(None), pl.ds(low, width))
                    columns = pl.ds(start + member * width, width)
                    steps.append((source.at[:, columns], stages[0].at[place], outs[0].at[place]))
                    low += width
        return steps

    shape = jax.ShapeDtypeStruct((team_size, len(arrays), rows, sum(widths)), jnp.bfloat16)
    return copy_call(plan, [shape], team_size * len(arrays) * len(starts), arrays, after=after)[0]


def unpack(parts, starts, model_width):
    def plan(scalars, sources, outs, stages):
        steps = []
        for start, source in zip(starts, sources):
            for member in range(source.shape[0]):
                columns = pl.ds(start + member * source.shape[2], source.shape[2])
                steps.append((source.at[member], stages[0].at[:, columns], outs[0].at[:, columns]))
        return steps

    shape = jax.ShapeDtypeStruct((parts[0].shape[1], model_width), jnp.bfloat16)
    return copy_call(plan, [shape], sum(part.shape[0] for part in parts), parts)[0]


def select(held, places, count, whole, after=()):
    def plan(scalars, sources, outs, stages):
        (place_ref,) = scalars
        steps = []
        for side, (source, stage, out) in enumerate(zip(sources, stages, outs)):
            one = pl.ds(0 if side == 0 else whole, count)
            steps.append((source.at[pl.ds(place_ref[side], count)], stage.at[one], out.at[one]))
            if whole > 0:
                rest = pl.ds(count if side == 0 else 0, whole)
                kept = pl.ds(source.shape[0] - whole if side == 0 else 0, whole)
                steps.append((source.at[kept], stage.at[rest], out.at[rest]))
        return steps

    shapes = [jax.ShapeDtypeStruct((count + whole,) + array.shape[1:], array.dtype) for array in held]
    return copy_call(plan, shapes, 2 * (2 if whole > 0 else 1), held, scalars=[places], after=after)


def attend_kernel(frames, pieces_of, heads, first_head, code_ref, q_hbm, *refs):
    *piece_refs, out_hbm, q_ref, out_ref, store, sems = refs
    copies = []

    def fetch(source, target):
        copies.append(pltpu.make_async_copy(source, target, sems.at[len(copies)]))
        copies[-1].start()

    fetch(q_hbm.at[:, 0, :, pl.ds(first_head * HD, heads * HD)], q_ref)
    start = 0
    for piece in piece_refs:
        fetch(piece, store.at[pl.ds(start, piece.shape[0])])
        start += piece.shape[0]
    for copy in copies:
        copy.wait()

    per_frame = BPF * pieces_of
    width = len(distances)

    def item(frame, head):
        columns = pl.ds(pl.multiple_of(head * HD, HD), HD)

        def block(kind, position, count):
            rows = store[pl.ds(position, count), kind, :, columns]
            return rows.reshape(rows.shape[0] * rows.shape[1], HD)

        places = []
        biases = []
        for place, distance in enumerate(distances):
            codes = [code_ref[(frame * BPF + b) * width + place] for b in range(BPF)]
            pick = jnp.maximum(codes[0], codes[1]) // 2
            relative = frame + (distance + REACH)
            position = relative * BPF - 1 + pick
            if distance == -REACH:
                position = jnp.where(relative == 0, 0, position)
            if distance == REACH:
                position = jnp.where(frame == frames - 1, relative * BPF - 1, position)
            places.append(position * pieces_of)
            biases.append([jnp.where(code > 0, 0.0, very_low).astype(jnp.float32) for code in codes])

        own = ((frame + REACH) * BPF - 1) * pieces_of
        queries = q_ref[pl.ds(frame * per_frame, per_frame), :, columns].reshape(BPF * BLK, HD)

        def keys_or_values(kind):
            found = [block(kind, own, per_frame)]
            for a in range(0, width, 2):
                found.append(
                    jnp.concatenate([block(kind, places[a], pieces_of), block(kind, places[a + 1], pieces_of)], axis=0)
                )
            return found

        keys = keys_or_values(0)
        tiles = [[] for _ in range(BPF)]
        for pair, key in enumerate(keys):
            scores = lax.dot_general(queries, key, (((1,), (1,)), ((), ())), preferred_element_type=jnp.float32)
            for b in range(BPF):
                for side in range(2):
                    tile = scores[b * BLK : (b + 1) * BLK, side * BLK : (side + 1) * BLK]
                    if pair > 0:
                        tile = tile + biases[2 * (pair - 1) + side][b]
                    tiles[b].append(tile)
        weights = []
        totals = []
        for b in range(BPF):
            row_max = jnp.max(functools.reduce(jnp.maximum, tiles[b]), axis=1, keepdims=True)
            exps = [jnp.exp2((tile - row_max) * to_log2) for tile in tiles[b]]
            totals.append(jnp.sum(functools.reduce(jnp.add, exps), axis=1, keepdims=True))
            weights.append(jnp.concatenate([e.astype(jnp.bfloat16) for e in exps], axis=1))
        values = jnp.concatenate(keys_or_values(1), axis=0)
        mixed = jnp.dot(jnp.concatenate(weights, axis=0), values, preferred_element_type=jnp.float32)
        result = (mixed / jnp.concatenate(totals, axis=0)).astype(jnp.bfloat16)
        out_ref[pl.ds(frame * per_frame, per_frame), :, columns] = result.reshape(per_frame, BLK // pieces_of, HD)

    together = 2 if frames % 2 == 0 else 1
    steps = frames // together

    def step(index, carry):
        head = index // steps
        first = (index - head * steps) * together
        for offset in range(together):
            item(first + offset, head)
        return carry

    lax.fori_loop(0, steps * heads, step, 0)
    put = pltpu.make_async_copy(out_ref, out_hbm, sems.at[0])
    put.start()
    put.wait()


def attend(codes, queries, pieces, frames, first_head, after=()):
    members, _, rows, _ = queries.shape
    pieces_of = BLK // rows
    width = pieces[0].shape[3]
    heads = width // HD
    stored = sum(piece.shape[0] for piece in pieces)
    pairs = frames * BPF * heads * (2 * REACH + BPF)

    def body(code_ref, q_hbm, *refs):
        kept = refs[: len(pieces)] + refs[len(pieces) + len(after) :]
        attend_kernel(frames, pieces_of, heads, first_head, code_ref, q_hbm, *kept)

    return pl.pallas_call(
        body,
        out_shape=jax.ShapeDtypeStruct((members, rows, width), jnp.bfloat16),
        in_specs=[pl.BlockSpec(memory_space=pltpu.SMEM)] + [in_hbm] * (1 + len(pieces) + len(after)),
        out_specs=in_hbm,
        scratch_shapes=[
            pltpu.VMEM((members, rows, width), jnp.bfloat16),
            pltpu.VMEM((members, rows, width), jnp.bfloat16),
            pltpu.VMEM((stored, 2, rows, width), jnp.bfloat16),
            pltpu.SemaphoreType.DMA((1 + len(pieces),)),
        ],
        compiler_params=pltpu.CompilerParams(vmem_limit_bytes=32 * 1024 * 1024),
        cost_estimate=pl.CostEstimate(
            flops=6 * pairs * 4 * BLK * BLK * HD,
            bytes_accessed=2 * (stored * 2 + 2 * members) * rows * width,
            transcendentals=pairs * BLK * BLK,
        ),
    )(codes, queries, *pieces, *after)


def on_device(outer, inner, q_proj, k_proj, v_proj, kv_list):
    frames = inner
    rows, model_width = q_proj.shape
    team = ("inner", "rep", "uly")
    team_size = frames * BPF * BLK // rows
    heads_here = model_width // HD // team_size
    pieces_of = BLK // rows
    per_frame = BPF * pieces_of
    my_group = lax.axis_index("outer")

    def rows_of(reader_frame, count):
        start = jnp.clip(reader_frame * BPF, 0, kv_list.shape[0] - count * BPF)
        return lax.dynamic_slice_in_dim(kv_list, start, count * BPF, 0)

    lists = rows_of(my_group * frames, frames).reshape(frames, BPF, 1, -1)
    first_ids = BPF * (
        my_group * frames + jnp.arange(frames, dtype=jnp.int32)[:, None] + jnp.array(distances, jnp.int32)[None, :]
    )[:, None, :, None]
    hits = jnp.where(lists == first_ids, 1, 0) + jnp.where(lists == first_ids + 1, 2, 0)
    codes = jnp.sum(jnp.where(lists >= 0, hits, 0), axis=-1).reshape(-1)

    def picked(reader_frame, holder_frame):
        return jnp.any(rows_of(reader_frame, 1) == holder_frame * BPF + 1).astype(jnp.int32)

    assert sum(CHUNKS) == heads_here
    widths = [heads * HD for heads in CHUNKS]
    lows = [sum(CHUNKS[:c]) for c in range(len(CHUNKS))]
    starts = [low * team_size * HD for low in lows]

    def exchange(array):
        return lax.all_to_all(array, team, split_axis=0, concat_axis=0, tiled=True)

    def shifted(array, heading):
        route = [(i, i + heading) for i in range(outer) if 0 <= i + heading < outer]
        return lax.ppermute(array, "outer", route)

    hops = []
    for hop in range(1, -(-REACH // frames) + 1):
        spare = hop * frames - REACH
        hops.append((frames - max(0, spare), spare >= 0))

    def forwarded(held, held_frames, keep, single, after):
        whole = (keep - 1 if single else keep) * per_frame
        if single:
            from_left, from_right = (my_group + 1) * frames, my_group * frames - 1
            edges = held[0].shape[0] - whole - per_frame, whole
            places = jnp.stack(
                [
                    edges[0] + pieces_of * picked(from_left, from_left - REACH),
                    edges[1] + pieces_of * picked(from_right, from_right + REACH),
                ]
            )
            return list(select(held, places, pieces_of, whole, after))
        if keep < held_frames:
            return [held[0][held[0].shape[0] - whole :], held[1][:whole]]
        return held

    def first_hop(own):
        assert hops[0] == (frames, False)
        return [[shifted(own, 1), shifted(own, -1)]]

    def selected(arrivals, after=()):
        for hop in range(1, len(hops)):
            to_send = forwarded(arrivals[-1], hops[hop - 1][0], *hops[hop], after if hop == len(hops) - 1 else ())
            if hop < len(hops) - 1:
                arrivals.append([shifted(to_send[0], 1), shifted(to_send[1], -1)])
        return to_send

    def last_hop(arrivals, to_send):
        arrivals.append([shifted(to_send[0], 1), shifted(to_send[1], -1)])
        return arrivals[-1]

    chunks = range(len(CHUNKS))
    owned, arrivals, sent, results, outs = [], [], [], [], []

    def attend_chunk(c, after):
        order = [a[0] for a in arrivals[c][::-1]] + [owned[c]] + [a[1] for a in arrivals[c]]
        results.append(attend(codes, queries, order, frames, lows[c], after=after))
        outs.append(exchange(results[c]))

    last_arrival = []
    for c in chunks:
        packed = pack([k_proj, v_proj], [starts[c]], [widths[c]], team_size, after=sent[c - 2] if c >= 2 else ())
        if c == len(CHUNKS) - 1:
            queries = exchange(pack([q_proj], starts, widths, team_size, after=[packed]))
        owned.append(exchange(packed))
        arrivals.append(first_hop(owned[c]))
        sent.append(selected(arrivals[c], after=last_arrival))
        last_arrival = last_hop(arrivals[c], sent[c])
    for c in chunks:
        attend_chunk(c, after=results[-1:] + (sent[c + 1] if c + 1 < len(CHUNKS) else []))
    return unpack(outs, starts, model_width)


def solution(mesh):
    sizes = dict(mesh.shape)
    members = sizes["uly"] * sizes["rep"]
    heads = 40
    inner = max(
        i for i in range(1, sizes["ctx"] + 1) if sizes["ctx"] % i == 0 and heads % (i * members) == 0
    )
    outer = sizes["ctx"] // inner
    finer = Mesh(
        mesh.devices.reshape(sizes["groups"], outer, inner, sizes["uly"], sizes["rep"]),
        ("groups", "outer", "inner", "uly", "rep"),
    )
    split = P(("groups", "outer", "inner", "rep", "uly"), None)
    return jax.shard_map(
        functools.partial(on_device, outer, inner),
        mesh=finer,
        in_specs=(split, split, split, P("groups", None)),
        out_specs=split,
        check_vma=False,
    )
```

```python
import functools
import math

import jax
import jax.numpy as jnp
from jax import lax
from jax.experimental import pallas as pl
from jax.experimental.pallas import tpu as pltpu
from jax.sharding import Mesh, PartitionSpec as P

HD = 128
BLK = 128
BPF = 2
REACH = 7
CHUNKS = (3, 2)
VMEM_LIMIT = 60 * 1024 * 1024
little = dict(flops=1024, bytes_accessed=1024, transcendentals=0)

very_low = -1e30
to_log2 = math.log2(math.e) * HD ** -0.5
distances = [d for d in range(-REACH, REACH + 1) if d != 0]


def staged_copies(steps, sems):
    count = len(steps)
    fetches = [pltpu.make_async_copy(s, stage, sems.at[i]) for i, (s, stage, t) in enumerate(steps)]
    puts = [pltpu.make_async_copy(stage, t, sems.at[count + i]) for i, (s, stage, t) in enumerate(steps)]
    for fetch in fetches:
        fetch.start()
    for fetch, put in zip(fetches, puts):
        fetch.wait()
        put.start()
    for put in puts:
        put.wait()


in_hbm = pl.BlockSpec(memory_space=pltpu.HBM)


def copy_call(plan, shapes, count, operands, scalars=(), after=()):
    def body(*refs):
        first = len(scalars)
        last = first + len(operands)
        results = refs[last + len(after) :]
        n = len(shapes)
        staged_copies(plan(refs[:first], refs[first:last], results[:n], results[n : 2 * n]), results[2 * n])

    return pl.pallas_call(
        body,
        out_shape=shapes,
        in_specs=[pl.BlockSpec(memory_space=pltpu.SMEM)] * len(scalars) + [in_hbm] * (len(operands) + len(after)),
        out_specs=[in_hbm] * len(shapes),
        scratch_shapes=[pltpu.VMEM(s.shape, s.dtype) for s in shapes] + [pltpu.SemaphoreType.DMA((2 * count,))],
        compiler_params=pltpu.CompilerParams(vmem_limit_bytes=VMEM_LIMIT),
        cost_estimate=pl.CostEstimate(**little),
    )(*scalars, *operands, *after)


def pack(arrays, starts, widths, team_size, after=()):
    rows = arrays[0].shape[0]

    def plan(scalars, sources, outs, stages):
        steps = []
        for member in range(team_size):
            for kind, source in enumerate(sources):
                low = 0
                for start, width in zip(starts, widths):
                    place = (member, kind, slice(None), pl.ds(low, width))
                    columns = pl.ds(start + member * width, width)
                    steps.append((source.at[:, columns], stages[0].at[place], outs[0].at[place]))
                    low += width
        return steps

    shape = jax.ShapeDtypeStruct((team_size, len(arrays), rows, sum(widths)), jnp.bfloat16)
    return copy_call(plan, [shape], team_size * len(arrays) * len(starts), arrays, after=after)[0]


def unpack(parts, starts, model_width):
    def plan(scalars, sources, outs, stages):
        steps = []
        for start, source in zip(starts, sources):
            for member in range(source.shape[0]):
                columns = pl.ds(start + member * source.shape[2], source.shape[2])
                steps.append((source.at[member], stages[0].at[:, columns], outs[0].at[:, columns]))
        return steps

    shape = jax.ShapeDtypeStruct((parts[0].shape[1], model_width), jnp.bfloat16)
    return copy_call(plan, [shape], sum(part.shape[0] for part in parts), parts)[0]


def select(held, places, count, whole, after=()):
    def plan(scalars, sources, outs, stages):
        (place_ref,) = scalars
        steps = []
        for side, (source, stage, out) in enumerate(zip(sources, stages, outs)):
            one = pl.ds(0 if side == 0 else whole, count)
            steps.append((source.at[pl.ds(place_ref[side], count)], stage.at[one], out.at[one]))
            if whole > 0:
                rest = pl.ds(count if side == 0 else 0, whole)
                kept = pl.ds(source.shape[0] - whole if side == 0 else 0, whole)
                steps.append((source.at[kept], stage.at[rest], out.at[rest]))
        return steps

    shapes = [jax.ShapeDtypeStruct((count + whole,) + array.shape[1:], array.dtype) for array in held]
    return copy_call(plan, shapes, 2 * (2 if whole > 0 else 1), held, scalars=[places], after=after)


def attend_kernel(frames, pieces_of, heads, first_head, code_ref, q_hbm, *refs):
    *piece_refs, out_hbm, q_ref, out_ref, store, sems = refs
    copies = []

    def fetch(source, target):
        copies.append(pltpu.make_async_copy(source, target, sems.at[len(copies)]))
        copies[-1].start()

    fetch(q_hbm.at[:, 0, :, pl.ds(first_head * HD, heads * HD)], q_ref)
    start = 0
    for piece in piece_refs:
        fetch(piece, store.at[pl.ds(start, piece.shape[0])])
        start += piece.shape[0]
    for copy in copies:
        copy.wait()

    per_frame = BPF * pieces_of
    width = len(distances)

    def item(frame, head):
        columns = pl.ds(pl.multiple_of(head * HD, HD), HD)

        def block(kind, position, count):
            rows = store[pl.ds(position, count), kind, :, columns]
            return rows.reshape(rows.shape[0] * rows.shape[1], HD)

        places = []
        biases = []
        for place, distance in enumerate(distances):
            codes = [code_ref[(frame * BPF + b) * width + place] for b in range(BPF)]
            pick = jnp.maximum(codes[0], codes[1]) // 2
            relative = frame + (distance + REACH)
            position = relative * BPF - 1 + pick
            if distance == -REACH:
                position = jnp.where(relative == 0, 0, position)
            if distance == REACH:
                position = jnp.where(frame == frames - 1, relative * BPF - 1, position)
            places.append(position * pieces_of)
            biases.append([jnp.where(code > 0, 0.0, very_low).astype(jnp.float32) for code in codes])

        own = ((frame + REACH) * BPF - 1) * pieces_of
        queries = q_ref[pl.ds(frame * per_frame, per_frame), :, columns].reshape(BPF * BLK, HD)

        def keys_or_values(kind):
            found = [block(kind, own, per_frame)]
            for a in range(0, width, 2):
                found.append(
                    jnp.concatenate([block(kind, places[a], pieces_of), block(kind, places[a + 1], pieces_of)], axis=0)
                )
            return found

        keys = keys_or_values(0)
        tiles = [[] for _ in range(BPF)]
        for pair, key in enumerate(keys):
            scores = lax.dot_general(queries, key, (((1,), (1,)), ((), ())), preferred_element_type=jnp.float32)
            for b in range(BPF):
                for side in range(2):
                    tile = scores[b * BLK : (b + 1) * BLK, side * BLK : (side + 1) * BLK]
                    if pair > 0:
                        tile = tile + biases[2 * (pair - 1) + side][b]
                    tiles[b].append(tile)
        weights = []
        totals = []
        for b in range(BPF):
            row_max = jnp.max(functools.reduce(jnp.maximum, tiles[b]), axis=1, keepdims=True)
            exps = [jnp.exp2((tile - row_max) * to_log2) for tile in tiles[b]]
            totals.append(jnp.sum(functools.reduce(jnp.add, exps), axis=1, keepdims=True))
            weights.append(jnp.concatenate([e.astype(jnp.bfloat16) for e in exps], axis=1))
        values = jnp.concatenate(keys_or_values(1), axis=0)
        mixed = jnp.dot(jnp.concatenate(weights, axis=0), values, preferred_element_type=jnp.float32)
        result = (mixed / jnp.concatenate(totals, axis=0)).astype(jnp.bfloat16)
        out_ref[pl.ds(frame * per_frame, per_frame), :, columns] = result.reshape(per_frame, BLK // pieces_of, HD)

    together = 2 if frames % 2 == 0 else 1
    steps = frames // together

    def step(index, carry):
        head = index // steps
        first = (index - head * steps) * together
        for offset in range(together):
            item(first + offset, head)
        return carry

    lax.fori_loop(0, steps * heads, step, 0)
    put = pltpu.make_async_copy(out_ref, out_hbm, sems.at[0])
    put.start()
    put.wait()


def attend(codes, queries, pieces, frames, first_head, after=()):
    members, _, rows, _ = queries.shape
    pieces_of = BLK // rows
    width = pieces[0].shape[3]
    heads = width // HD
    stored = sum(piece.shape[0] for piece in pieces)

    def body(code_ref, q_hbm, *refs):
        kept = refs[: len(pieces)] + refs[len(pieces) + len(after) :]
        attend_kernel(frames, pieces_of, heads, first_head, code_ref, q_hbm, *kept)

    return pl.pallas_call(
        body,
        out_shape=jax.ShapeDtypeStruct((members, rows, width), jnp.bfloat16),
        in_specs=[pl.BlockSpec(memory_space=pltpu.SMEM)] + [in_hbm] * (1 + len(pieces) + len(after)),
        out_specs=in_hbm,
        scratch_shapes=[
            pltpu.VMEM((members, rows, width), jnp.bfloat16),
            pltpu.VMEM((members, rows, width), jnp.bfloat16),
            pltpu.VMEM((stored, 2, rows, width), jnp.bfloat16),
            pltpu.SemaphoreType.DMA((1 + len(pieces),)),
        ],
        compiler_params=pltpu.CompilerParams(vmem_limit_bytes=VMEM_LIMIT),
        cost_estimate=pl.CostEstimate(**little),
    )(codes, queries, *pieces, *after)


def on_device(outer, inner, q_proj, k_proj, v_proj, kv_list):
    frames = inner
    rows, model_width = q_proj.shape
    team = ("inner", "rep", "uly")
    team_size = frames * BPF * BLK // rows
    heads_here = model_width // HD // team_size
    pieces_of = BLK // rows
    per_frame = BPF * pieces_of
    my_group = lax.axis_index("outer")

    def rows_of(reader_frame, count):
        start = jnp.clip(reader_frame * BPF, 0, kv_list.shape[0] - count * BPF)
        return lax.dynamic_slice_in_dim(kv_list, start, count * BPF, 0)

    lists = rows_of(my_group * frames, frames).reshape(frames, BPF, 1, -1)
    first_ids = BPF * (
        my_group * frames + jnp.arange(frames, dtype=jnp.int32)[:, None] + jnp.array(distances, jnp.int32)[None, :]
    )[:, None, :, None]
    hits = jnp.where(lists == first_ids, 1, 0) + jnp.where(lists == first_ids + 1, 2, 0)
    codes = jnp.sum(jnp.where(lists >= 0, hits, 0), axis=-1).reshape(-1)

    def picked(reader_frame, holder_frame):
        return jnp.any(rows_of(reader_frame, 1) == holder_frame * BPF + 1).astype(jnp.int32)

    assert sum(CHUNKS) == heads_here
    widths = [heads * HD for heads in CHUNKS]
    lows = [sum(CHUNKS[:c]) for c in range(len(CHUNKS))]
    starts = [low * team_size * HD for low in lows]

    def exchange(array):
        return lax.all_to_all(array, team, split_axis=0, concat_axis=0, tiled=True)

    def shifted(array, heading):
        route = [(i, i + heading) for i in range(outer) if 0 <= i + heading < outer]
        return lax.ppermute(array, "outer", route)

    hops = []
    for hop in range(1, -(-REACH // frames) + 1):
        spare = hop * frames - REACH
        hops.append((frames - max(0, spare), spare >= 0))

    def forwarded(held, held_frames, keep, single, after):
        whole = (keep - 1 if single else keep) * per_frame
        if single:
            from_left, from_right = (my_group + 1) * frames, my_group * frames - 1
            edges = held[0].shape[0] - whole - per_frame, whole
            places = jnp.stack(
                [
                    edges[0] + pieces_of * picked(from_left, from_left - REACH),
                    edges[1] + pieces_of * picked(from_right, from_right + REACH),
                ]
            )
            return list(select(held, places, pieces_of, whole, after))
        if keep < held_frames:
            return [held[0][held[0].shape[0] - whole :], held[1][:whole]]
        return held

    def first_hop(own):
        assert hops[0] == (frames, False)
        return [[shifted(own, 1), shifted(own, -1)]]

    def selected(arrivals, after=()):
        for hop in range(1, len(hops)):
            to_send = forwarded(arrivals[-1], hops[hop - 1][0], *hops[hop], after if hop == len(hops) - 1 else ())
            if hop < len(hops) - 1:
                arrivals.append([shifted(to_send[0], 1), shifted(to_send[1], -1)])
        return to_send

    def last_hop(arrivals, to_send):
        arrivals.append([shifted(to_send[0], 1), shifted(to_send[1], -1)])
        return arrivals[-1]

    chunks = range(len(CHUNKS))
    owned, arrivals, sent, results, outs = [], [], [], [], []

    def attend_chunk(c, after):
        order = [a[0] for a in arrivals[c][::-1]] + [owned[c]] + [a[1] for a in arrivals[c]]
        results.append(attend(codes, queries, order, frames, lows[c], after=after))
        outs.append(exchange(results[c]))

    last_arrival = []
    for c in chunks:
        packed = pack([k_proj, v_proj], [starts[c]], [widths[c]], team_size, after=sent[c - 2] if c >= 2 else ())
        if c == len(CHUNKS) - 1:
            queries = exchange(pack([q_proj], starts, widths, team_size, after=[packed]))
        owned.append(exchange(packed))
        arrivals.append(first_hop(owned[c]))
        sent.append(selected(arrivals[c], after=last_arrival))
        last_arrival = last_hop(arrivals[c], sent[c])
    for c in chunks:
        attend_chunk(c, after=results[-1:] + (sent[c + 1] if c + 1 < len(CHUNKS) else []))
    return unpack(outs, starts, model_width)


def solution(mesh):
    sizes = dict(mesh.shape)
    members = sizes["uly"] * sizes["rep"]
    heads = 40
    inner = max(
        i for i in range(1, sizes["ctx"] + 1) if sizes["ctx"] % i == 0 and heads % (i * members) == 0
    )
    outer = sizes["ctx"] // inner
    finer = Mesh(
        mesh.devices.reshape(sizes["groups"], outer, inner, sizes["uly"], sizes["rep"]),
        ("groups", "outer", "inner", "uly", "rep"),
    )
    split = P(("groups", "outer", "inner", "rep", "uly"), None)
    return jax.shard_map(
        functools.partial(on_device, outer, inner),
        mesh=finer,
        in_specs=(split, split, split, P("groups", None)),
        out_specs=split,
        check_vma=False,
    )
```

```python
import functools
import math

import jax
import jax.numpy as jnp
from jax import lax
from jax.experimental import pallas as pl
from jax.experimental.pallas import tpu as pltpu
from jax.sharding import Mesh, PartitionSpec as P

HD = 128
BLK = 128
BPF = 2
REACH = 7
CHUNKS = (3, 2)
VMEM_LIMIT = 60 * 1024 * 1024
little = dict(flops=1024, bytes_accessed=1024, transcendentals=0)

very_low = -1e30
to_log2 = math.log2(math.e) * HD ** -0.5
distances = [d for d in range(-REACH, REACH + 1) if d != 0]


def staged_copies(steps, sems):
    count = len(steps)
    fetches = [pltpu.make_async_copy(s, stage, sems.at[i]) for i, (s, stage, t) in enumerate(steps)]
    puts = [pltpu.make_async_copy(stage, t, sems.at[count + i]) for i, (s, stage, t) in enumerate(steps)]
    for fetch in fetches:
        fetch.start()
    for fetch, put in zip(fetches, puts):
        fetch.wait()
        put.start()
    for put in puts:
        put.wait()


in_hbm = pl.BlockSpec(memory_space=pltpu.HBM)


def copy_call(plan, shapes, count, operands, scalars=(), after=()):
    def body(*refs):
        first = len(scalars)
        last = first + len(operands)
        results = refs[last + len(after) :]
        n = len(shapes)
        staged_copies(plan(refs[:first], refs[first:last], results[:n], results[n : 2 * n]), results[2 * n])

    return pl.pallas_call(
        body,
        out_shape=shapes,
        in_specs=[pl.BlockSpec(memory_space=pltpu.SMEM)] * len(scalars) + [in_hbm] * (len(operands) + len(after)),
        out_specs=[in_hbm] * len(shapes),
        scratch_shapes=[pltpu.VMEM(s.shape, s.dtype) for s in shapes] + [pltpu.SemaphoreType.DMA((2 * count,))],
        compiler_params=pltpu.CompilerParams(vmem_limit_bytes=VMEM_LIMIT),
        cost_estimate=pl.CostEstimate(**little),
    )(*scalars, *operands, *after)


def pack(arrays, starts, widths, team_size, after=()):
    rows = arrays[0].shape[0]

    def plan(scalars, sources, outs, stages):
        steps = []
        for member in range(team_size):
            for kind, source in enumerate(sources):
                low = 0
                for start, width in zip(starts, widths):
                    place = (member, kind, slice(None), pl.ds(low, width))
                    columns = pl.ds(start + member * width, width)
                    steps.append((source.at[:, columns], stages[0].at[place], outs[0].at[place]))
                    low += width
        return steps

    shape = jax.ShapeDtypeStruct((team_size, len(arrays), rows, sum(widths)), jnp.bfloat16)
    return copy_call(plan, [shape], team_size * len(arrays) * len(starts), arrays, after=after)[0]


def unpack(parts, starts, model_width):
    def plan(scalars, sources, outs, stages):
        steps = []
        for start, source in zip(starts, sources):
            for member in range(source.shape[0]):
                columns = pl.ds(start + member * source.shape[2], source.shape[2])
                steps.append((source.at[member], stages[0].at[:, columns], outs[0].at[:, columns]))
        return steps

    shape = jax.ShapeDtypeStruct((parts[0].shape[1], model_width), jnp.bfloat16)
    return copy_call(plan, [shape], sum(part.shape[0] for part in parts), parts)[0]


def select(held, places, count, whole, after=()):
    def plan(scalars, sources, outs, stages):
        (place_ref,) = scalars
        steps = []
        for side, (source, stage, out) in enumerate(zip(sources, stages, outs)):
            one = pl.ds(0 if side == 0 else whole, count)
            steps.append((source.at[pl.ds(place_ref[side], count)], stage.at[one], out.at[one]))
            if whole > 0:
                rest = pl.ds(count if side == 0 else 0, whole)
                kept = pl.ds(source.shape[0] - whole if side == 0 else 0, whole)
                steps.append((source.at[kept], stage.at[rest], out.at[rest]))
        return steps

    shapes = [jax.ShapeDtypeStruct((count + whole,) + array.shape[1:], array.dtype) for array in held]
    return copy_call(plan, shapes, 2 * (2 if whole > 0 else 1), held, scalars=[places], after=after)


def attend_kernel(frames, pieces_of, heads, first_head, code_ref, q_hbm, *refs):
    *piece_refs, out_hbm, q_ref, out_ref, store, sems = refs
    copies = []

    def fetch(source, target):
        copies.append(pltpu.make_async_copy(source, target, sems.at[len(copies)]))
        copies[-1].start()

    fetch(q_hbm.at[:, 0, :, pl.ds(first_head * HD, heads * HD)], q_ref)
    start = 0
    for piece in piece_refs:
        fetch(piece, store.at[pl.ds(start, piece.shape[0])])
        start += piece.shape[0]
    for copy in copies:
        copy.wait()

    per_frame = BPF * pieces_of
    width = len(distances)

    def item(frame, head):
        columns = pl.ds(pl.multiple_of(head * HD, HD), HD)

        def block(kind, position, count):
            rows = store[pl.ds(position, count), kind, :, columns]
            return rows.reshape(rows.shape[0] * rows.shape[1], HD)

        places = []
        biases = []
        for place, distance in enumerate(distances):
            codes = [code_ref[(frame * BPF + b) * width + place] for b in range(BPF)]
            pick = jnp.maximum(codes[0], codes[1]) // 2
            relative = frame + (distance + REACH)
            position = relative * BPF - 1 + pick
            if distance == -REACH:
                position = jnp.where(relative == 0, 0, position)
            if distance == REACH:
                position = jnp.where(frame == frames - 1, relative * BPF - 1, position)
            places.append(position * pieces_of)
            biases.append([jnp.where(code > 0, 0.0, very_low).astype(jnp.float32) for code in codes])

        own = ((frame + REACH) * BPF - 1) * pieces_of
        queries = q_ref[pl.ds(frame * per_frame, per_frame), :, columns].reshape(BPF * BLK, HD)

        def keys_or_values(kind):
            found = [block(kind, own, per_frame)]
            for a in range(0, width, 2):
                found.append(
                    jnp.concatenate([block(kind, places[a], pieces_of), block(kind, places[a + 1], pieces_of)], axis=0)
                )
            return found

        keys = keys_or_values(0)
        tiles = [[] for _ in range(BPF)]
        for pair, key in enumerate(keys):
            scores = lax.dot_general(queries, key, (((1,), (1,)), ((), ())), preferred_element_type=jnp.float32)
            for b in range(BPF):
                for side in range(2):
                    tile = scores[b * BLK : (b + 1) * BLK, side * BLK : (side + 1) * BLK]
                    if pair > 0:
                        tile = tile + biases[2 * (pair - 1) + side][b]
                    tiles[b].append(tile)
        weights = []
        totals = []
        for b in range(BPF):
            row_max = jnp.max(functools.reduce(jnp.maximum, tiles[b]), axis=1, keepdims=True)
            exps = [jnp.exp2((tile - row_max) * to_log2) for tile in tiles[b]]
            totals.append(jnp.sum(functools.reduce(jnp.add, exps), axis=1, keepdims=True))
            weights.append(jnp.concatenate([e.astype(jnp.bfloat16) for e in exps], axis=1))
        values = jnp.concatenate(keys_or_values(1), axis=0)
        mixed = jnp.dot(jnp.concatenate(weights, axis=0), values, preferred_element_type=jnp.float32)
        result = (mixed / jnp.concatenate(totals, axis=0)).astype(jnp.bfloat16)
        out_ref[pl.ds(frame * per_frame, per_frame), :, columns] = result.reshape(per_frame, BLK // pieces_of, HD)

    together = 2 if frames % 2 == 0 else 1
    steps = frames // together

    def step(index, carry):
        head = index // steps
        first = (index - head * steps) * together
        for offset in range(together):
            item(first + offset, head)
        return carry

    lax.fori_loop(0, steps * heads, step, 0)
    put = pltpu.make_async_copy(out_ref, out_hbm, sems.at[0])
    put.start()
    put.wait()


def attend(codes, queries, pieces, frames, first_head, after=()):
    members, _, rows, _ = queries.shape
    pieces_of = BLK // rows
    width = pieces[0].shape[3]
    heads = width // HD
    stored = sum(piece.shape[0] for piece in pieces)

    def body(code_ref, q_hbm, *refs):
        kept = refs[: len(pieces)] + refs[len(pieces) + len(after) :]
        attend_kernel(frames, pieces_of, heads, first_head, code_ref, q_hbm, *kept)

    return pl.pallas_call(
        body,
        out_shape=jax.ShapeDtypeStruct((members, rows, width), jnp.bfloat16),
        in_specs=[pl.BlockSpec(memory_space=pltpu.SMEM)] + [in_hbm] * (1 + len(pieces) + len(after)),
        out_specs=in_hbm,
        scratch_shapes=[
            pltpu.VMEM((members, rows, width), jnp.bfloat16),
            pltpu.VMEM((members, rows, width), jnp.bfloat16),
            pltpu.VMEM((stored, 2, rows, width), jnp.bfloat16),
            pltpu.SemaphoreType.DMA((1 + len(pieces),)),
        ],
        compiler_params=pltpu.CompilerParams(vmem_limit_bytes=VMEM_LIMIT),
        cost_estimate=pl.CostEstimate(
            flops=6 * frames * BPF * heads * len(distances) * 4 * BLK * BLK * HD, bytes_accessed=1024, transcendentals=0
        ),
    )(codes, queries, *pieces, *after)


def on_device(outer, inner, q_proj, k_proj, v_proj, kv_list):
    frames = inner
    rows, model_width = q_proj.shape
    team = ("inner", "rep", "uly")
    team_size = frames * BPF * BLK // rows
    heads_here = model_width // HD // team_size
    pieces_of = BLK // rows
    per_frame = BPF * pieces_of
    my_group = lax.axis_index("outer")

    def rows_of(reader_frame, count):
        start = jnp.clip(reader_frame * BPF, 0, kv_list.shape[0] - count * BPF)
        return lax.dynamic_slice_in_dim(kv_list, start, count * BPF, 0)

    lists = rows_of(my_group * frames, frames).reshape(frames, BPF, 1, -1)
    first_ids = BPF * (
        my_group * frames + jnp.arange(frames, dtype=jnp.int32)[:, None] + jnp.array(distances, jnp.int32)[None, :]
    )[:, None, :, None]
    hits = jnp.where(lists == first_ids, 1, 0) + jnp.where(lists == first_ids + 1, 2, 0)
    codes = jnp.sum(jnp.where(lists >= 0, hits, 0), axis=-1).reshape(-1)

    def picked(reader_frame, holder_frame):
        return jnp.any(rows_of(reader_frame, 1) == holder_frame * BPF + 1).astype(jnp.int32)

    assert sum(CHUNKS) == heads_here
    widths = [heads * HD for heads in CHUNKS]
    lows = [sum(CHUNKS[:c]) for c in range(len(CHUNKS))]
    starts = [low * team_size * HD for low in lows]

    def exchange(array):
        return lax.all_to_all(array, team, split_axis=0, concat_axis=0, tiled=True)

    def shifted(array, heading):
        route = [(i, i + heading) for i in range(outer) if 0 <= i + heading < outer]
        return lax.ppermute(array, "outer", route)

    hops = []
    for hop in range(1, -(-REACH // frames) + 1):
        spare = hop * frames - REACH
        hops.append((frames - max(0, spare), spare >= 0))

    def forwarded(held, held_frames, keep, single, after):
        whole = (keep - 1 if single else keep) * per_frame
        if single:
            from_left, from_right = (my_group + 1) * frames, my_group * frames - 1
            edges = held[0].shape[0] - whole - per_frame, whole
            places = jnp.stack(
                [
                    edges[0] + pieces_of * picked(from_left, from_left - REACH),
                    edges[1] + pieces_of * picked(from_right, from_right + REACH),
                ]
            )
            return list(select(held, places, pieces_of, whole, after))
        if keep < held_frames:
            return [held[0][held[0].shape[0] - whole :], held[1][:whole]]
        return held

    def first_hop(own):
        assert hops[0] == (frames, False)
        return [[shifted(own, 1), shifted(own, -1)]]

    def selected(arrivals, after=()):
        for hop in range(1, len(hops)):
            to_send = forwarded(arrivals[-1], hops[hop - 1][0], *hops[hop], after if hop == len(hops) - 1 else ())
            if hop < len(hops) - 1:
                arrivals.append([shifted(to_send[0], 1), shifted(to_send[1], -1)])
        return to_send

    def last_hop(arrivals, to_send):
        arrivals.append([shifted(to_send[0], 1), shifted(to_send[1], -1)])

    chunks = range(len(CHUNKS))
    owned, arrivals, sent, results, outs = [], [], [], [], []

    def attend_chunk(c, after):
        order = [a[0] for a in arrivals[c][::-1]] + [owned[c]] + [a[1] for a in arrivals[c]]
        results.append(attend(codes, queries, order, frames, lows[c], after=after))
        outs.append(exchange(results[c]))

    for c in chunks:
        packed = pack([k_proj, v_proj], [starts[c]], [widths[c]], team_size, after=sent[c - 2] if c >= 2 else ())
        if c == len(CHUNKS) - 1:
            queries = exchange(pack([q_proj], starts, widths, team_size, after=[packed]))
        owned.append(exchange(packed))
        arrivals.append(first_hop(owned[c]))
        sent.append(selected(arrivals[c], after=sent[-1] if sent else ()))
        last_hop(arrivals[c], sent[c])
    for c in chunks:
        attend_chunk(c, after=results[-1:] + (sent[c + 1] if c + 1 < len(CHUNKS) else []))
    return unpack(outs, starts, model_width)


def solution(mesh):
    sizes = dict(mesh.shape)
    members = sizes["uly"] * sizes["rep"]
    heads = 40
    inner = max(
        i for i in range(1, sizes["ctx"] + 1) if sizes["ctx"] % i == 0 and heads % (i * members) == 0
    )
    outer = sizes["ctx"] // inner
    finer = Mesh(
        mesh.devices.reshape(sizes["groups"], outer, inner, sizes["uly"], sizes["rep"]),
        ("groups", "outer", "inner", "uly", "rep"),
    )
    split = P(("groups", "outer", "inner", "rep", "uly"), None)
    return jax.shard_map(
        functools.partial(on_device, outer, inner),
        mesh=finer,
        in_specs=(split, split, split, P("groups", None)),
        out_specs=split,
        check_vma=False,
    )
```

```python
import functools
import math

import jax
import jax.numpy as jnp
from jax import lax
from jax.experimental import pallas as pl
from jax.experimental.pallas import tpu as pltpu
from jax.sharding import Mesh, PartitionSpec as P

HD = 128
BLK = 128
BPF = 2
REACH = 7
CHUNKS = (3, 2)
VMEM_LIMIT = 60 * 1024 * 1024
little = dict(flops=1024, bytes_accessed=1024, transcendentals=0)

very_low = -1e30
to_log2 = math.log2(math.e) * HD ** -0.5
distances = [d for d in range(-REACH, REACH + 1) if d != 0]


def staged_copies(steps, sems):
    count = len(steps)
    fetches = [pltpu.make_async_copy(s, stage, sems.at[i]) for i, (s, stage, t) in enumerate(steps)]
    puts = [pltpu.make_async_copy(stage, t, sems.at[count + i]) for i, (s, stage, t) in enumerate(steps)]
    for fetch in fetches:
        fetch.start()
    for fetch, put in zip(fetches, puts):
        fetch.wait()
        put.start()
    for put in puts:
        put.wait()


in_hbm = pl.BlockSpec(memory_space=pltpu.HBM)


def copy_call(plan, shapes, count, operands, scalars=(), after=()):
    def body(*refs):
        first = len(scalars)
        last = first + len(operands)
        results = refs[last + len(after) :]
        n = len(shapes)
        staged_copies(plan(refs[:first], refs[first:last], results[:n], results[n : 2 * n]), results[2 * n])

    return pl.pallas_call(
        body,
        out_shape=shapes,
        in_specs=[pl.BlockSpec(memory_space=pltpu.SMEM)] * len(scalars) + [in_hbm] * (len(operands) + len(after)),
        out_specs=[in_hbm] * len(shapes),
        scratch_shapes=[pltpu.VMEM(s.shape, s.dtype) for s in shapes] + [pltpu.SemaphoreType.DMA((2 * count,))],
        compiler_params=pltpu.CompilerParams(vmem_limit_bytes=VMEM_LIMIT),
        cost_estimate=pl.CostEstimate(**little),
    )(*scalars, *operands, *after)


def pack(arrays, starts, widths, team_size, after=()):
    rows = arrays[0].shape[0]

    def plan(scalars, sources, outs, stages):
        steps = []
        for member in range(team_size):
            for kind, source in enumerate(sources):
                low = 0
                for start, width in zip(starts, widths):
                    place = (member, kind, slice(None), pl.ds(low, width))
                    columns = pl.ds(start + member * width, width)
                    steps.append((source.at[:, columns], stages[0].at[place], outs[0].at[place]))
                    low += width
        return steps

    shape = jax.ShapeDtypeStruct((team_size, len(arrays), rows, sum(widths)), jnp.bfloat16)
    return copy_call(plan, [shape], team_size * len(arrays) * len(starts), arrays, after=after)[0]


def unpack(parts, starts, model_width):
    def plan(scalars, sources, outs, stages):
        steps = []
        for start, source in zip(starts, sources):
            for member in range(source.shape[0]):
                columns = pl.ds(start + member * source.shape[2], source.shape[2])
                steps.append((source.at[member], stages[0].at[:, columns], outs[0].at[:, columns]))
        return steps

    shape = jax.ShapeDtypeStruct((parts[0].shape[1], model_width), jnp.bfloat16)
    return copy_call(plan, [shape], sum(part.shape[0] for part in parts), parts)[0]


def select(held, places, count, whole, after=()):
    def plan(scalars, sources, outs, stages):
        (place_ref,) = scalars
        steps = []
        for side, (source, stage, out) in enumerate(zip(sources, stages, outs)):
            one = pl.ds(0 if side == 0 else whole, count)
            steps.append((source.at[pl.ds(place_ref[side], count)], stage.at[one], out.at[one]))
            if whole > 0:
                rest = pl.ds(count if side == 0 else 0, whole)
                kept = pl.ds(source.shape[0] - whole if side == 0 else 0, whole)
                steps.append((source.at[kept], stage.at[rest], out.at[rest]))
        return steps

    shapes = [jax.ShapeDtypeStruct((count + whole,) + array.shape[1:], array.dtype) for array in held]
    return copy_call(plan, shapes, 2 * (2 if whole > 0 else 1), held, scalars=[places], after=after)


def attend_kernel(frames, pieces_of, heads, first_head, code_ref, q_hbm, *refs):
    *piece_refs, out_hbm, q_ref, out_ref, store, sems, put_sems = refs
    per_frame = BPF * pieces_of
    width = len(distances)

    def columns_of(head):
        return pl.ds(pl.multiple_of(head * HD, HD), HD)

    def fetches(head):
        columns = columns_of(head)
        found = [(q_hbm.at[:, 0, :, columns_of(head + first_head)], q_ref.at[:, :, columns])]
        start = 0
        for piece in piece_refs:
            size = piece.shape[0]
            found.append((piece.at[:, :, :, columns], store.at[pl.ds(start, size), :, :, columns]))
            start += size
        return [pltpu.make_async_copy(a, b, sems.at[head, i]) for i, (a, b) in enumerate(found)]

    def put(head):
        columns = columns_of(head)
        return pltpu.make_async_copy(out_ref.at[:, :, columns], out_hbm.at[:, :, columns], put_sems.at[head])

    def item(frame, head):
        columns = columns_of(head)

        def block(kind, position, count):
            rows = store[pl.ds(position, count), kind, :, columns]
            return rows.reshape(rows.shape[0] * rows.shape[1], HD)

        own = ((frame + REACH) * BPF - 1) * pieces_of
        places = []
        biases = []
        for place, distance in enumerate(distances):
            codes = [code_ref[(frame * BPF + b) * width + place] for b in range(BPF)]
            pick = jnp.maximum(codes[0], codes[1]) // 2
            relative = frame + (distance + REACH)
            position = relative * BPF - 1 + pick
            if distance == -REACH:
                position = jnp.where(relative == 0, 0, position)
            if distance == REACH:
                position = jnp.where(frame == frames - 1, relative * BPF - 1, position)
            places.append(position * pieces_of)
            biases.append([jnp.where(code > 0, 0.0, very_low).astype(jnp.float32) for code in codes])

        def keys_or_values(kind):
            found = [block(kind, own, per_frame)] + [block(kind, place, pieces_of) for place in places]
            return jnp.concatenate(found, axis=0)

        queries = q_ref[pl.ds(frame * per_frame, per_frame), :, columns].reshape(BPF * BLK, HD)
        scores = lax.dot_general(
            keys_or_values(0), queries, (((1,), (1,)), ((), ())), preferred_element_type=jnp.float32
        )
        weights = []
        totals = []
        for b in range(BPF):
            tiles = []
            for j in range(BPF + width):
                tile = scores[j * BLK : (j + 1) * BLK, b * BLK : (b + 1) * BLK]
                tiles.append(tile if j < BPF else tile + biases[j - BPF][b])
            top = jnp.max(functools.reduce(jnp.maximum, tiles), axis=0, keepdims=True)
            exps = [jnp.exp2((tile - top) * to_log2) for tile in tiles]
            totals.append(jnp.sum(functools.reduce(jnp.add, exps), axis=0, keepdims=True))
            weights.append(jnp.concatenate([e.astype(jnp.bfloat16) for e in exps], axis=0))
        mixed = lax.dot_general(
            keys_or_values(1),
            jnp.concatenate(weights, axis=1),
            (((0,), (0,)), ((), ())),
            preferred_element_type=jnp.float32,
        )
        result = jnp.transpose(mixed / jnp.concatenate(totals, axis=1)).astype(jnp.bfloat16)
        out_ref[pl.ds(frame * per_frame, per_frame), :, columns] = result.reshape(per_frame, BLK // pieces_of, HD)

    together = 2 if frames % 2 == 0 else 1

    def one_head(head, carry):
        for fetch in fetches(head):
            fetch.wait()

        def step(index, carry):
            for offset in range(together):
                item(index * together + offset, head)
            return carry

        lax.fori_loop(0, frames // together, step, 0)
        put(head).start()
        return carry

    for head in range(heads):
        for fetch in fetches(head):
            fetch.start()
    lax.fori_loop(0, heads, one_head, 0)
    for head in range(heads):
        put(head).wait()


def attend(codes, queries, pieces, frames, first_head, after=()):
    members, _, rows, _ = queries.shape
    pieces_of = BLK // rows
    width = pieces[0].shape[3]
    heads = width // HD
    stored = sum(piece.shape[0] for piece in pieces)

    def body(code_ref, q_hbm, *refs):
        kept = refs[: len(pieces)] + refs[len(pieces) + len(after) :]
        attend_kernel(frames, pieces_of, heads, first_head, code_ref, q_hbm, *kept)

    return pl.pallas_call(
        body,
        out_shape=jax.ShapeDtypeStruct((members, rows, width), jnp.bfloat16),
        in_specs=[pl.BlockSpec(memory_space=pltpu.SMEM)] + [in_hbm] * (1 + len(pieces) + len(after)),
        out_specs=in_hbm,
        scratch_shapes=[
            pltpu.VMEM((members, rows, width), jnp.bfloat16),
            pltpu.VMEM((members, rows, width), jnp.bfloat16),
            pltpu.VMEM((stored, 2, rows, width), jnp.bfloat16),
            pltpu.SemaphoreType.DMA((heads, 1 + len(pieces))),
            pltpu.SemaphoreType.DMA((heads,)),
        ],
        compiler_params=pltpu.CompilerParams(vmem_limit_bytes=VMEM_LIMIT),
        cost_estimate=pl.CostEstimate(
            flops=6 * frames * BPF * heads * len(distances) * 4 * BLK * BLK * HD, bytes_accessed=1024, transcendentals=0
        ),
    )(codes, queries, *pieces, *after)


def on_device(outer, inner, q_proj, k_proj, v_proj, kv_list):
    frames = inner
    rows, model_width = q_proj.shape
    team = ("inner", "rep", "uly")
    team_size = frames * BPF * BLK // rows
    heads_here = model_width // HD // team_size
    pieces_of = BLK // rows
    per_frame = BPF * pieces_of
    my_group = lax.axis_index("outer")

    def rows_of(reader_frame, count):
        start = jnp.clip(reader_frame * BPF, 0, kv_list.shape[0] - count * BPF)
        return lax.dynamic_slice_in_dim(kv_list, start, count * BPF, 0)

    lists = rows_of(my_group * frames, frames).reshape(frames, BPF, 1, -1)
    first_ids = BPF * (
        my_group * frames + jnp.arange(frames, dtype=jnp.int32)[:, None] + jnp.array(distances, jnp.int32)[None, :]
    )[:, None, :, None]
    hits = jnp.where(lists == first_ids, 1, 0) + jnp.where(lists == first_ids + 1, 2, 0)
    codes = jnp.sum(jnp.where(lists >= 0, hits, 0), axis=-1).reshape(-1)

    def picked(reader_frame, holder_frame):
        return jnp.any(rows_of(reader_frame, 1) == holder_frame * BPF + 1).astype(jnp.int32)

    assert sum(CHUNKS) == heads_here
    widths = [heads * HD for heads in CHUNKS]
    lows = [sum(CHUNKS[:c]) for c in range(len(CHUNKS))]
    starts = [low * team_size * HD for low in lows]

    def exchange(array):
        return lax.all_to_all(array, team, split_axis=0, concat_axis=0, tiled=True)

    def shifted(array, heading):
        route = [(i, i + heading) for i in range(outer) if 0 <= i + heading < outer]
        return lax.ppermute(array, "outer", route)

    hops = []
    for hop in range(1, -(-REACH // frames) + 1):
        spare = hop * frames - REACH
        hops.append((frames - max(0, spare), spare >= 0))

    def forwarded(held, held_frames, keep, single, after):
        whole = (keep - 1 if single else keep) * per_frame
        if single:
            from_left, from_right = (my_group + 1) * frames, my_group * frames - 1
            edges = held[0].shape[0] - whole - per_frame, whole
            places = jnp.stack(
                [
                    edges[0] + pieces_of * picked(from_left, from_left - REACH),
                    edges[1] + pieces_of * picked(from_right, from_right + REACH),
                ]
            )
            return list(select(held, places, pieces_of, whole, after))
        if keep < held_frames:
            return [held[0][held[0].shape[0] - whole :], held[1][:whole]]
        return held

    def first_hop(own):
        assert hops[0] == (frames, False)
        return [[shifted(own, 1), shifted(own, -1)]]

    def selected(arrivals, after=()):
        for hop in range(1, len(hops)):
            to_send = forwarded(arrivals[-1], hops[hop - 1][0], *hops[hop], after if hop == len(hops) - 1 else ())
            if hop < len(hops) - 1:
                arrivals.append([shifted(to_send[0], 1), shifted(to_send[1], -1)])
        return to_send

    def last_hop(arrivals, to_send):
        arrivals.append([shifted(to_send[0], 1), shifted(to_send[1], -1)])

    chunks = range(len(CHUNKS))
    owned, arrivals, sent, results, outs = [], [], [], [], []

    def attend_chunk(c, after):
        order = [a[0] for a in arrivals[c][::-1]] + [owned[c]] + [a[1] for a in arrivals[c]]
        results.append(attend(codes, queries, order, frames, lows[c], after=after))
        result = results[c]
        if outs:
            result, outs[-1] = lax.optimization_barrier((result, outs[-1]))
        outs.append(exchange(result))

    for c in chunks:
        packed = pack([k_proj, v_proj], [starts[c]], [widths[c]], team_size, after=sent[c - 2] if c >= 2 else ())
        if c == len(CHUNKS) - 1:
            queries = exchange(pack([q_proj], starts, widths, team_size, after=[packed]))
        owned.append(exchange(packed))
        arrivals.append(first_hop(owned[c]))
        sent.append(selected(arrivals[c], after=sent[-1] if sent else ()))
        last_hop(arrivals[c], sent[c])
    for c in chunks:
        attend_chunk(c, after=results[-1:] + (sent[c + 1] if c + 1 < len(CHUNKS) else []))
    return unpack(outs, starts, model_width)


def solution(mesh):
    sizes = dict(mesh.shape)
    members = sizes["uly"] * sizes["rep"]
    heads = 40
    inner = max(
        i for i in range(1, sizes["ctx"] + 1) if sizes["ctx"] % i == 0 and heads % (i * members) == 0
    )
    outer = sizes["ctx"] // inner
    finer = Mesh(
        mesh.devices.reshape(sizes["groups"], outer, inner, sizes["uly"], sizes["rep"]),
        ("groups", "outer", "inner", "uly", "rep"),
    )
    split = P(("groups", "outer", "inner", "rep", "uly"), None)
    return jax.shard_map(
        functools.partial(on_device, outer, inner),
        mesh=finer,
        in_specs=(split, split, split, P("groups", None)),
        out_specs=split,
        check_vma=False,
    )
```

```python
import functools
import math

import jax
import jax.numpy as jnp
from jax import lax
from jax.experimental import pallas as pl
from jax.experimental.pallas import tpu as pltpu
from jax.sharding import Mesh, PartitionSpec as P

HD = 128
BLK = 128
BPF = 2
REACH = 7
CHUNKS = (3, 2)
VMEM_LIMIT = 60 * 1024 * 1024
little = dict(flops=1024, bytes_accessed=1024, transcendentals=0)

very_low = -1e30
to_log2 = math.log2(math.e) * HD ** -0.5


def staged_copies(steps, sems):
    count = len(steps)
    fetches = [pltpu.make_async_copy(s, stage, sems.at[i]) for i, (s, stage, t) in enumerate(steps)]
    puts = [pltpu.make_async_copy(stage, t, sems.at[count + i]) for i, (s, stage, t) in enumerate(steps)]
    for fetch in fetches:
        fetch.start()
    for fetch, put in zip(fetches, puts):
        fetch.wait()
        put.start()
    for put in puts:
        put.wait()


anywhere = pl.BlockSpec(memory_space=pl.ANY)


def copy_call(plan, shapes, count, operands, scalars=(), after=()):
    def body(*refs):
        first = len(scalars)
        last = first + len(operands)
        results = refs[last + len(after) :]
        n = len(shapes)
        staged_copies(plan(refs[:first], refs[first:last], results[:n], results[n : 2 * n]), results[2 * n])

    return pl.pallas_call(
        body,
        out_shape=shapes,
        in_specs=[pl.BlockSpec(memory_space=pltpu.SMEM)] * len(scalars) + [anywhere] * (len(operands) + len(after)),
        out_specs=[anywhere] * len(shapes),
        scratch_shapes=[pltpu.VMEM(s.shape, s.dtype) for s in shapes] + [pltpu.SemaphoreType.DMA((2 * count,))],
        compiler_params=pltpu.CompilerParams(vmem_limit_bytes=VMEM_LIMIT),
        cost_estimate=pl.CostEstimate(**little),
    )(*scalars, *operands, *after)


def pack(arrays, starts, widths, team_size, after=()):
    rows = arrays[0].shape[0]

    def plan(scalars, sources, outs, stages):
        steps = []
        for member in range(team_size):
            for kind, source in enumerate(sources):
                low = 0
                for start, width in zip(starts, widths):
                    place = (member, kind, slice(None), pl.ds(low, width))
                    columns = pl.ds(start + member * width, width)
                    steps.append((source.at[:, columns], stages[0].at[place], outs[0].at[place]))
                    low += width
        return steps

    shape = jax.ShapeDtypeStruct((team_size, len(arrays), rows, sum(widths)), jnp.bfloat16)
    return copy_call(plan, [shape], team_size * len(arrays) * len(starts), arrays, after=after)[0]


def unpack(parts, starts, model_width):
    def plan(scalars, sources, outs, stages):
        steps = []
        for start, source in zip(starts, sources):
            for member in range(source.shape[0]):
                columns = pl.ds(start + member * source.shape[2], source.shape[2])
                steps.append((source.at[member], stages[0].at[:, columns], outs[0].at[:, columns]))
        return steps

    shape = jax.ShapeDtypeStruct((parts[0].shape[1], model_width), jnp.bfloat16)
    return copy_call(plan, [shape], sum(part.shape[0] for part in parts), parts)[0]


def select(held, places, count, whole, after=()):
    def plan(scalars, sources, outs, stages):
        (place_ref,) = scalars
        steps = []
        for side, (source, stage, out) in enumerate(zip(sources, stages, outs)):
            one = pl.ds(0 if side == 0 else whole, count)
            steps.append((source.at[pl.ds(place_ref[side], count)], stage.at[one], out.at[one]))
            if whole > 0:
                rest = pl.ds(count if side == 0 else 0, whole)
                kept = pl.ds(source.shape[0] - whole if side == 0 else 0, whole)
                steps.append((source.at[kept], stage.at[rest], out.at[rest]))
        return steps

    shapes = [jax.ShapeDtypeStruct((count + whole,) + array.shape[1:], array.dtype) for array in held]
    return copy_call(plan, shapes, 2 * (2 if whole > 0 else 1), held, scalars=[places], after=after)


def columns_of(head):
    return pl.ds(pl.multiple_of(head * HD, HD), HD)


def flat(rows):
    return rows.reshape(rows.shape[0] * rows.shape[1], HD)


def masked_scores(queries, keys, masks):
    tiles = [[] for _ in range(BPF)]
    for first in range(0, len(keys), 2):
        some = jnp.concatenate(keys[first : first + 2], axis=0)
        scores = lax.dot_general(queries, some, (((1,), (1,)), ((), ())), preferred_element_type=jnp.float32)
        for side, mask in enumerate(masks[first : first + 2]):
            for b in range(BPF):
                tile = scores[b * BLK : (b + 1) * BLK, side * BLK : (side + 1) * BLK]
                tiles[b].append(tile if mask is None else tile + mask[b])
    return tiles


def largest(tiles):
    return jnp.max(functools.reduce(jnp.maximum, tiles), axis=1, keepdims=True)


def weighted(tiles, tops, values):
    totals, weights = [], []
    for b in range(BPF):
        exps = [jnp.exp2((tile - tops[b]) * to_log2) for tile in tiles[b]]
        totals.append(jnp.sum(functools.reduce(jnp.add, exps), axis=1, keepdims=True))
        weights.append(jnp.concatenate([e.astype(jnp.bfloat16) for e in exps], axis=1))
    mixed = jnp.dot(
        jnp.concatenate(weights, axis=0), jnp.concatenate(values, axis=0), preferred_element_type=jnp.float32
    )
    return mixed, jnp.concatenate(totals, axis=0)


def mask_of(codes):
    return [jnp.where(code > 0, 0.0, very_low).astype(jnp.float32) for code in codes]


def each_head(heads, fetches, puts, work):
    for head in range(heads):
        for fetch in fetches(head):
            fetch.start()

    def one_head(head, carry):
        for fetch in fetches(head):
            fetch.wait()
        work(head)
        for put in puts(head):
            put.start()
        return carry

    lax.fori_loop(0, heads, one_head, 0)
    for head in range(heads):
        for put in puts(head):
            put.wait()


def near_kernel(frames, near, pieces_of, heads, first_head, code_ref, q_hbm, *refs):
    *piece_refs, acc_hbm, stat_hbm, q_ref, store, acc_ref, stat_ref, sems, put_sems = refs
    per_frame = BPF * pieces_of
    width = frames + 2 * REACH

    def fetches(head):
        columns = columns_of(head)
        found = [(q_hbm.at[:, 0, :, columns_of(head + first_head)], q_ref.at[:, :, columns])]
        start = 0
        for piece in piece_refs:
            size = piece.shape[0]
            found.append((piece.at[:, :, :, columns], store.at[pl.ds(start, size), :, :, columns]))
            start += size
        return [pltpu.make_async_copy(a, b, sems.at[head, i]) for i, (a, b) in enumerate(found)]

    def puts(head):
        pairs = [(acc_ref, acc_hbm), (stat_ref, stat_hbm)]
        return [pltpu.make_async_copy(a.at[head], b.at[head], put_sems.at[head, i]) for i, (a, b) in enumerate(pairs)]

    def item(frame, head):
        columns = columns_of(head)
        own = (frame + near) * BPF * pieces_of
        keys, values, masks = [], [], []
        for b in range(BPF):
            keys.append(flat(store[pl.ds(own + b * pieces_of, pieces_of), 0, :, columns]))
            values.append(flat(store[pl.ds(own + b * pieces_of, pieces_of), 1, :, columns]))
            masks.append(None)
        for other in range(frames + 2 * near - 1):
            relative = other - near
            relative = relative + jnp.where(relative >= frame, 1, 0)
            codes = [code_ref[(frame * BPF + b) * width + relative + REACH] for b in range(BPF)]
            pick = jnp.maximum(codes[0], codes[1]) // 2
            place = ((relative + near) * BPF + pick) * pieces_of
            keys.append(flat(store[pl.ds(place, pieces_of), 0, :, columns]))
            values.append(flat(store[pl.ds(place, pieces_of), 1, :, columns]))
            masks.append(mask_of(codes))
        queries = flat(q_ref[pl.ds(frame * per_frame, per_frame), :, columns])
        tiles = masked_scores(queries, keys, masks)
        tops = [largest(tiles[b]) for b in range(BPF)]
        mixed, totals = weighted(tiles, tops, values)
        acc_ref[head, frame] = mixed
        lanes = lax.broadcasted_iota(jnp.int32, (BPF * BLK, HD), 1)
        stat_ref[head, frame] = jnp.where(lanes < HD // 2, jnp.concatenate(tops, axis=0), totals)

    together = 2 if frames % 2 == 0 else 1

    def work(head):
        def step(index, carry):
            for offset in range(together):
                item(index * together + offset, head)
            return carry

        lax.fori_loop(0, frames // together, step, 0)

    each_head(heads, fetches, puts, work)


def far_kernel(frames, near, pieces_of, heads, first_head, code_ref, q_hbm, *refs):
    left_hbm, right_hbm, acc_hbm, stat_hbm, out_hbm, q_ref, left, right, acc_ref, stat_ref, out_ref, sems, put_sems = refs
    per_frame = BPF * pieces_of
    width = frames + 2 * REACH

    def fetches(head):
        columns = columns_of(head)
        pairs = [
            (q_hbm.at[:, 0, :, columns_of(head + first_head)], q_ref.at[:, :, columns]),
            (left_hbm.at[:, :, :, columns], left.at[:, :, :, columns]),
            (right_hbm.at[:, :, :, columns], right.at[:, :, :, columns]),
            (acc_hbm.at[head], acc_ref.at[head]),
            (stat_hbm.at[head], stat_ref.at[head]),
        ]
        return [pltpu.make_async_copy(a, b, sems.at[head, i]) for i, (a, b) in enumerate(pairs)]

    def puts(head):
        columns = columns_of(head)
        return [pltpu.make_async_copy(out_ref.at[:, :, columns], out_hbm.at[:, :, columns], put_sems.at[head])]

    def item(frame, head):
        columns = columns_of(head)
        keys, values, masks = [], [], []
        for relative in [*range(-REACH, -near), *range(frames + near, frames + REACH)]:
            if abs(relative - frame) > REACH:
                continue
            codes = [code_ref[(frame * BPF + b) * width + relative + REACH] for b in range(BPF)]
            pick = jnp.maximum(codes[0], codes[1]) // 2
            if relative < 0:
                piece, place = left, (0 if relative == -REACH else (relative + REACH) * BPF - 1 + pick)
            else:
                first = (relative - frames - near) * BPF
                piece, place = right, (first if relative == frames + REACH - 1 else first + pick)
            keys.append(flat(piece[pl.ds(place * pieces_of, pieces_of), 0, :, columns]))
            values.append(flat(piece[pl.ds(place * pieces_of, pieces_of), 1, :, columns]))
            masks.append(mask_of(codes))
        queries = flat(q_ref[pl.ds(frame * per_frame, per_frame), :, columns])
        tiles = masked_scores(queries, keys, masks)
        stat = stat_ref[head, frame]
        near_top, near_total = stat[:, :1], stat[:, HD - 1 :]
        tops = [jnp.maximum(largest(tiles[b]), near_top[b * BLK : (b + 1) * BLK]) for b in range(BPF)]
        mixed, totals = weighted(tiles, tops, values)
        shrink = jnp.exp2((near_top - jnp.concatenate(tops, axis=0)) * to_log2)
        result = (acc_ref[head, frame] * shrink + mixed) / (near_total * shrink + totals)
        out_ref[pl.ds(frame * per_frame, per_frame), :, columns] = result.astype(jnp.bfloat16).reshape(
            per_frame, BLK // pieces_of, HD
        )

    def work(head):
        for frame in range(frames):
            item(frame, head)

    each_head(heads, fetches, puts, work)


def attend_near(codes, queries, pieces, frames, near, first_head, after=()):
    members, _, rows, _ = queries.shape
    pieces_of = BLK // rows
    width = pieces[0].shape[3]
    heads = width // HD
    stored = sum(piece.shape[0] for piece in pieces)

    def body(code_ref, q_hbm, *refs):
        kept = refs[: len(pieces)] + refs[len(pieces) + len(after) :]
        near_kernel(frames, near, pieces_of, heads, first_head, code_ref, q_hbm, *kept)

    partial = jax.ShapeDtypeStruct((heads, frames, BPF * BLK, HD), jnp.float32)
    return pl.pallas_call(
        body,
        out_shape=[partial, partial],
        in_specs=[pl.BlockSpec(memory_space=pltpu.SMEM)] + [anywhere] * (1 + len(pieces) + len(after)),
        out_specs=[anywhere, anywhere],
        scratch_shapes=[
            pltpu.VMEM((members, rows, width), jnp.bfloat16),
            pltpu.VMEM((stored, 2, rows, width), jnp.bfloat16),
            pltpu.VMEM(partial.shape, jnp.float32),
            pltpu.VMEM(partial.shape, jnp.float32),
            pltpu.SemaphoreType.DMA((heads, 1 + len(pieces))),
            pltpu.SemaphoreType.DMA((heads, 2)),
        ],
        compiler_params=pltpu.CompilerParams(vmem_limit_bytes=VMEM_LIMIT),
        cost_estimate=pl.CostEstimate(
            flops=6 * frames * heads * BPF * (frames + 2 * near + 1) * 4 * BLK * BLK * HD,
            bytes_accessed=1024,
            transcendentals=0,
        ),
    )(codes, queries, *pieces, *after)


def attend_far(codes, queries, far, partials, frames, near, first_head, after=()):
    members, _, rows, _ = queries.shape
    pieces_of = BLK // rows
    width = far[0].shape[3]
    heads = width // HD

    def body(code_ref, q_hbm, *refs):
        far_kernel(frames, near, pieces_of, heads, first_head, code_ref, q_hbm, *refs[:4], *refs[4 + len(after) :])

    result = jax.ShapeDtypeStruct((members, rows, width), jnp.bfloat16)
    return pl.pallas_call(
        body,
        out_shape=result,
        in_specs=[pl.BlockSpec(memory_space=pltpu.SMEM)] + [anywhere] * (5 + len(after)),
        out_specs=anywhere,
        scratch_shapes=[
            pltpu.VMEM(result.shape, result.dtype),
            *[pltpu.VMEM(array.shape, array.dtype) for array in (*far, *partials)],
            pltpu.VMEM(result.shape, result.dtype),
            pltpu.SemaphoreType.DMA((heads, 5)),
            pltpu.SemaphoreType.DMA((heads,)),
        ],
        compiler_params=pltpu.CompilerParams(vmem_limit_bytes=VMEM_LIMIT),
        cost_estimate=pl.CostEstimate(
            flops=6 * frames * heads * BPF * 4 * 4 * BLK * BLK * HD, bytes_accessed=1024, transcendentals=0
        ),
    )(codes, queries, *far, *partials, *after)


def on_device(outer, inner, q_proj, k_proj, v_proj, kv_list):
    frames = inner
    rows, model_width = q_proj.shape
    team = ("inner", "rep", "uly")
    team_size = frames * BPF * BLK // rows
    heads_here = model_width // HD // team_size
    pieces_of = BLK // rows
    per_frame = BPF * pieces_of
    my_group = lax.axis_index("outer")

    def rows_of(reader_frame, count):
        start = jnp.clip(reader_frame * BPF, 0, kv_list.shape[0] - count * BPF)
        return lax.dynamic_slice_in_dim(kv_list, start, count * BPF, 0)

    lists = rows_of(my_group * frames, frames).reshape(frames * BPF, 1, -1)
    first_ids = BPF * (my_group * frames - REACH + lax.broadcasted_iota(jnp.int32, (1, frames + 2 * REACH, 1), 1))
    hits = jnp.where(lists == first_ids, 1, 0) + jnp.where(lists == first_ids + 1, 2, 0)
    codes = jnp.sum(jnp.where(lists >= 0, hits, 0), axis=-1).reshape(-1)

    def picked(reader_frame, holder_frame):
        return jnp.any(rows_of(reader_frame, 1) == holder_frame * BPF + 1).astype(jnp.int32)

    assert sum(CHUNKS) == heads_here
    widths = [heads * HD for heads in CHUNKS]
    lows = [sum(CHUNKS[:c]) for c in range(len(CHUNKS))]
    starts = [low * team_size * HD for low in lows]

    def exchange(array):
        return lax.all_to_all(array, team, split_axis=0, concat_axis=0, tiled=True)

    def shifted(array, heading):
        route = [(i, i + heading) for i in range(outer) if 0 <= i + heading < outer]
        return lax.ppermute(array, "outer", route)

    hops = []
    for hop in range(1, -(-REACH // frames) + 1):
        spare = hop * frames - REACH
        hops.append((frames - max(0, spare), spare >= 0))

    def forwarded(held, held_frames, keep, single, after):
        whole = (keep - 1 if single else keep) * per_frame
        if single:
            from_left, from_right = (my_group + 1) * frames, my_group * frames - 1
            edges = held[0].shape[0] - whole - per_frame, whole
            places = jnp.stack(
                [
                    edges[0] + pieces_of * picked(from_left, from_left - REACH),
                    edges[1] + pieces_of * picked(from_right, from_right + REACH),
                ]
            )
            return list(select(held, places, pieces_of, whole, after))
        if keep < held_frames:
            return [held[0][held[0].shape[0] - whole :], held[1][:whole]]
        return held

    def first_hop(own):
        assert hops[0] == (frames, False)
        return [[shifted(own, 1), shifted(own, -1)]]

    def selected(arrivals, after=()):
        for hop in range(1, len(hops)):
            to_send = forwarded(arrivals[-1], hops[hop - 1][0], *hops[hop], after if hop == len(hops) - 1 else ())
            if hop < len(hops) - 1:
                arrivals.append([shifted(to_send[0], 1), shifted(to_send[1], -1)])
        return to_send

    def last_hop(arrivals, to_send):
        arrivals.append([shifted(to_send[0], 1), shifted(to_send[1], -1)])

    chunks = range(len(CHUNKS))
    near = (len(hops) - 1) * frames
    owned, arrivals, sent, partials, results, outs = [], [], [], [], [], []
    for c in chunks:
        packed = pack([k_proj, v_proj], [starts[c]], [widths[c]], team_size, after=sent[c - 2] if c >= 2 else ())
        if c == len(CHUNKS) - 1:
            queries = exchange(pack([q_proj], starts, widths, team_size, after=[packed]))
        owned.append(exchange(packed))
        arrivals.append(first_hop(owned[c]))
        sent.append(selected(arrivals[c], after=sent[-1] if sent else ()))
    for c in chunks:
        order = [a[0] for a in arrivals[c][::-1]] + [owned[c]] + [a[1] for a in arrivals[c]]
        last_hop(arrivals[c], sent[c])
        before = sent[c] + (partials[-1] if partials else [])
        partials.append(list(attend_near(codes, queries, order, frames, near, lows[c], after=before)))
    for c in chunks:
        before = results[-1:] if results else partials[-1]
        result = attend_far(codes, queries, arrivals[c][-1], partials[c], frames, near, lows[c], after=before)
        results.append(result)
        if outs:
            result, outs[-1] = lax.optimization_barrier((result, outs[-1]))
        outs.append(exchange(result))
    return unpack(outs, starts, model_width)


def solution(mesh):
    sizes = dict(mesh.shape)
    members = sizes["uly"] * sizes["rep"]
    heads = 40
    inner = max(
        i for i in range(1, sizes["ctx"] + 1) if sizes["ctx"] % i == 0 and heads % (i * members) == 0
    )
    outer = sizes["ctx"] // inner
    finer = Mesh(
        mesh.devices.reshape(sizes["groups"], outer, inner, sizes["uly"], sizes["rep"]),
        ("groups", "outer", "inner", "uly", "rep"),
    )
    split = P(("groups", "outer", "inner", "rep", "uly"), None)
    return jax.shard_map(
        functools.partial(on_device, outer, inner),
        mesh=finer,
        in_specs=(split, split, split, P("groups", None)),
        out_specs=split,
        check_vma=False,
    )
```

```python
import functools
import math

import jax
import jax.numpy as jnp
from jax import lax
from jax.experimental import pallas as pl
from jax.experimental.pallas import tpu as pltpu
from jax.sharding import Mesh, PartitionSpec as P

HD = 128
BLK = 128
BPF = 2
REACH = 7
CHUNKS = (3, 2)
VMEM_LIMIT = 60 * 1024 * 1024
little = dict(flops=1024, bytes_accessed=1024, transcendentals=0)

ROWS = 16

very_low = -1e30
to_log2 = math.log2(math.e) * HD ** -0.5


def staged_copies(steps, sems):
    count = len(steps)
    fetches = [pltpu.make_async_copy(s, stage, sems.at[i]) for i, (s, stage, t) in enumerate(steps)]
    puts = [pltpu.make_async_copy(stage, t, sems.at[count + i]) for i, (s, stage, t) in enumerate(steps)]
    for fetch in fetches:
        fetch.start()
    for fetch, put in zip(fetches, puts):
        fetch.wait()
        put.start()
    for put in puts:
        put.wait()


anywhere = pl.BlockSpec(memory_space=pl.ANY)


def copy_call(plan, shapes, count, operands, scalars=(), after=()):
    def body(*refs):
        first = len(scalars)
        last = first + len(operands)
        results = refs[last + len(after) :]
        n = len(shapes)
        staged_copies(plan(refs[:first], refs[first:last], results[:n], results[n : 2 * n]), results[2 * n])

    return pl.pallas_call(
        body,
        out_shape=shapes,
        in_specs=[pl.BlockSpec(memory_space=pltpu.SMEM)] * len(scalars) + [anywhere] * (len(operands) + len(after)),
        out_specs=[anywhere] * len(shapes),
        scratch_shapes=[pltpu.VMEM(s.shape, s.dtype) for s in shapes] + [pltpu.SemaphoreType.DMA((2 * count,))],
        compiler_params=pltpu.CompilerParams(vmem_limit_bytes=VMEM_LIMIT),
        cost_estimate=pl.CostEstimate(**little),
    )(*scalars, *operands, *after)


def pack(arrays, starts, widths, team_size, after=()):
    rows = arrays[0].shape[0]

    def plan(scalars, sources, outs, stages):
        steps = []
        for member in range(team_size):
            for kind, source in enumerate(sources):
                low = 0
                for start, width in zip(starts, widths):
                    place = (member, kind, slice(None), pl.ds(low, width))
                    columns = pl.ds(start + member * width, width)
                    steps.append((source.at[:, columns], stages[0].at[place], outs[0].at[place]))
                    low += width
        return steps

    shape = jax.ShapeDtypeStruct((team_size, len(arrays), rows, sum(widths)), jnp.bfloat16)
    return copy_call(plan, [shape], team_size * len(arrays) * len(starts), arrays, after=after)[0]


def unpack(parts, starts, model_width):
    def plan(scalars, sources, outs, stages):
        steps = []
        for start, source in zip(starts, sources):
            for member in range(source.shape[0]):
                columns = pl.ds(start + member * source.shape[2], source.shape[2])
                steps.append((source.at[member], stages[0].at[:, columns], outs[0].at[:, columns]))
        return steps

    shape = jax.ShapeDtypeStruct((parts[0].shape[1], model_width), jnp.bfloat16)
    return copy_call(plan, [shape], sum(part.shape[0] for part in parts), parts)[0]


def select(held, places, count, whole, after=()):
    def plan(scalars, sources, outs, stages):
        (place_ref,) = scalars
        steps = []
        for side, (source, stage, out) in enumerate(zip(sources, stages, outs)):
            one = pl.ds(0 if side == 0 else whole, count)
            steps.append((source.at[pl.ds(place_ref[side], count)], stage.at[one], out.at[one]))
            if whole > 0:
                rest = pl.ds(count if side == 0 else 0, whole)
                kept = pl.ds(source.shape[0] - whole if side == 0 else 0, whole)
                steps.append((source.at[kept], stage.at[rest], out.at[rest]))
        return steps

    shapes = [jax.ShapeDtypeStruct((count + whole,) + array.shape[1:], array.dtype) for array in held]
    return copy_call(plan, shapes, 2 * (2 if whole > 0 else 1), held, scalars=[places], after=after)


def columns_of(head):
    return pl.ds(pl.multiple_of(head * HD, HD), HD)


def flat(rows):
    return rows.reshape(rows.shape[0] * rows.shape[1], HD)


def attend_kernel(frames, pieces_of, heads, first_head, place_ref, mask_ref, q_hbm, *refs):
    *piece_refs, out_hbm, q_ref, out_ref, store, scores_a, scores_b, weights_a, weights_b, totals_a, totals_b, sems, put_sems = refs
    per_frame = BPF * pieces_of
    width = 2 * REACH
    items = frames * heads
    slots = [(scores_a, weights_a, totals_a), (scores_b, weights_b, totals_b)]

    def fetches(head):
        columns = columns_of(head)
        found = [(q_hbm.at[:, 0, :, columns_of(head + first_head)], q_ref.at[:, :, columns])]
        start = 0
        for piece in piece_refs:
            size = piece.shape[0]
            found.append((piece.at[:, :, :, columns], store.at[pl.ds(start, size), :, :, columns]))
            start += size
        return [pltpu.make_async_copy(a, b, sems.at[head, i]) for i, (a, b) in enumerate(found)]

    def put(head):
        columns = columns_of(head)
        return pltpu.make_async_copy(out_ref.at[:, :, columns], out_hbm.at[:, :, columns], put_sems.at[head])

    def keys_or_values(kind, frame, columns):
        own = ((frame + REACH) * BPF - 1) * pieces_of
        found = [flat(store[pl.ds(own, per_frame), kind, :, columns])]
        for pair in range(REACH):
            places = [place_ref[frame * width + 2 * pair + side] for side in range(2)]
            found.append(
                jnp.concatenate([flat(store[pl.ds(place, pieces_of), kind, :, columns]) for place in places], axis=0)
            )
        return found

    def score(item, scores_ref):
        head = item // frames
        frame = item - head * frames
        columns = columns_of(head)
        queries = flat(q_ref[pl.ds(frame * per_frame, per_frame), :, columns])
        for pair, keys in enumerate(keys_or_values(0, frame, columns)):
            scores = lax.dot_general(queries, keys, (((1,), (1,)), ((), ())), preferred_element_type=jnp.float32)
            for side in range(2):
                for b in range(BPF):
                    tile = scores[b * BLK : (b + 1) * BLK, side * BLK : (side + 1) * BLK]
                    if pair > 0:
                        tile = tile + mask_ref[(frame * BPF + b) * width + 2 * (pair - 1) + side]
                    scores_ref[b * BLK : (b + 1) * BLK, (2 * pair + side) * BLK : (2 * pair + side + 1) * BLK] = tile

    def soften(scores_ref, weights_ref, totals_ref):
        for low in range(0, BPF * BLK, ROWS):
            rows = slice(low, low + ROWS)
            tiles = [scores_ref[rows, j * BLK : (j + 1) * BLK] for j in range(BPF + width)]
            top = jnp.max(functools.reduce(jnp.maximum, tiles), axis=1, keepdims=True)
            total = None
            for j in range(BPF + width):
                exps = jnp.exp2((scores_ref[rows, j * BLK : (j + 1) * BLK] - top) * to_log2)
                total = exps if total is None else total + exps
                weights_ref[rows, j * BLK : (j + 1) * BLK] = exps.astype(jnp.bfloat16)
            totals_ref[rows, :] = jnp.broadcast_to(jnp.sum(total, axis=1, keepdims=True), (ROWS, HD))

    def product(item, weights_ref, totals_ref):
        head = item // frames
        frame = item - head * frames
        columns = columns_of(head)
        values = jnp.concatenate(keys_or_values(1, frame, columns), axis=0)
        mixed = jnp.dot(weights_ref[...], values, preferred_element_type=jnp.float32)
        result = (mixed / totals_ref[...]).astype(jnp.bfloat16)
        out_ref[pl.ds(frame * per_frame, per_frame), :, columns] = result.reshape(per_frame, BLK // pieces_of, HD)

    for head in range(heads):
        for fetch in fetches(head):
            fetch.start()
    for fetch in fetches(0):
        fetch.wait()
    weights_b[...] = jnp.zeros_like(weights_b)
    totals_b[...] = jnp.ones_like(totals_b)
    score(0, scores_a)

    def stages(item, here, there):
        after = jnp.minimum(item + 1, items - 1)

        @pl.when((after % frames == 0) & (after > item))
        def _():
            for fetch in fetches(after // frames):
                fetch.wait()

        score(after, there[0])
        soften(*here)
        product(jnp.maximum(item - 1, 0), *there[1:])

    def step(index, carry):
        stages(2 * index, slots[0], slots[1])
        stages(2 * index + 1, slots[1], slots[0])
        return carry

    lax.fori_loop(0, items // 2, step, 0)
    if items % 2 == 1:
        stages(items - 1, slots[0], slots[1])
    product(items - 1, *slots[(items - 1) % 2][1:])
    for head in range(heads):
        put(head).start()
    for head in range(heads):
        put(head).wait()


def attend(places, masks, queries, pieces, frames, first_head, after=()):
    members, _, rows, _ = queries.shape
    pieces_of = BLK // rows
    width = pieces[0].shape[3]
    heads = width // HD
    stored = sum(piece.shape[0] for piece in pieces)
    keys = (2 * REACH + BPF) * BLK

    def body(place_ref, mask_ref, q_hbm, *refs):
        kept = refs[: len(pieces)] + refs[len(pieces) + len(after) :]
        attend_kernel(frames, pieces_of, heads, first_head, place_ref, mask_ref, q_hbm, *kept)

    return pl.pallas_call(
        body,
        out_shape=jax.ShapeDtypeStruct((members, rows, width), jnp.bfloat16),
        in_specs=[pl.BlockSpec(memory_space=pltpu.SMEM)] * 2 + [anywhere] * (1 + len(pieces) + len(after)),
        out_specs=anywhere,
        scratch_shapes=[
            pltpu.VMEM((members, rows, width), jnp.bfloat16),
            pltpu.VMEM((members, rows, width), jnp.bfloat16),
            pltpu.VMEM((stored, 2, rows, width), jnp.bfloat16),
            *[pltpu.VMEM((BPF * BLK, keys), jnp.float32)] * 2,
            *[pltpu.VMEM((BPF * BLK, keys), jnp.bfloat16)] * 2,
            *[pltpu.VMEM((BPF * BLK, HD), jnp.float32)] * 2,
            pltpu.SemaphoreType.DMA((heads, 1 + len(pieces))),
            pltpu.SemaphoreType.DMA((heads,)),
        ],
        compiler_params=pltpu.CompilerParams(vmem_limit_bytes=VMEM_LIMIT),
        cost_estimate=pl.CostEstimate(
            flops=6 * frames * BPF * heads * 2 * REACH * 4 * BLK * BLK * HD, bytes_accessed=1024, transcendentals=0
        ),
    )(places, masks, queries, *pieces, *after)


def on_device(outer, inner, q_proj, k_proj, v_proj, kv_list):
    frames = inner
    rows, model_width = q_proj.shape
    team = ("inner", "rep", "uly")
    team_size = frames * BPF * BLK // rows
    heads_here = model_width // HD // team_size
    pieces_of = BLK // rows
    per_frame = BPF * pieces_of
    my_group = lax.axis_index("outer")

    def rows_of(reader_frame, count):
        start = jnp.clip(reader_frame * BPF, 0, kv_list.shape[0] - count * BPF)
        return lax.dynamic_slice_in_dim(kv_list, start, count * BPF, 0)

    lists = rows_of(my_group * frames, frames).reshape(frames, BPF, 1, -1)
    shape = (frames, 1, 2 * REACH, 1)
    steps = lax.broadcasted_iota(jnp.int32, shape, 2)
    relative = lax.broadcasted_iota(jnp.int32, shape, 0) + steps - REACH + jnp.where(steps >= REACH, 1, 0)
    first_ids = BPF * (my_group * frames + relative)
    hits = jnp.where(lists == first_ids, 1, 0) + jnp.where(lists == first_ids + 1, 2, 0)
    codes = jnp.sum(jnp.where(lists >= 0, hits, 0), axis=-1)
    masks = jnp.where(codes > 0, 0.0, very_low).astype(jnp.float32).reshape(-1)
    relative = relative.reshape(frames, 2 * REACH)
    picks = jnp.where(relative == frames - 1 + REACH, 0, jnp.max(codes, axis=1) // 2)
    places = pieces_of * jnp.maximum(BPF * (relative + REACH) - 1 + picks, 0)
    places = jnp.where(relative == -REACH, 0, places).reshape(-1)

    def picked(reader_frame, holder_frame):
        return jnp.any(rows_of(reader_frame, 1) == holder_frame * BPF + 1).astype(jnp.int32)

    assert sum(CHUNKS) == heads_here
    widths = [heads * HD for heads in CHUNKS]
    lows = [sum(CHUNKS[:c]) for c in range(len(CHUNKS))]
    starts = [low * team_size * HD for low in lows]

    def exchange(array):
        return lax.all_to_all(array, team, split_axis=0, concat_axis=0, tiled=True)

    def shifted(array, heading):
        route = [(i, i + heading) for i in range(outer) if 0 <= i + heading < outer]
        return lax.ppermute(array, "outer", route)

    hops = []
    for hop in range(1, -(-REACH // frames) + 1):
        spare = hop * frames - REACH
        hops.append((frames - max(0, spare), spare >= 0))

    def forwarded(held, held_frames, keep, single, after):
        whole = (keep - 1 if single else keep) * per_frame
        if single:
            from_left, from_right = (my_group + 1) * frames, my_group * frames - 1
            edges = held[0].shape[0] - whole - per_frame, whole
            edge_places = jnp.stack(
                [
                    edges[0] + pieces_of * picked(from_left, from_left - REACH),
                    edges[1] + pieces_of * picked(from_right, from_right + REACH),
                ]
            )
            return list(select(held, edge_places, pieces_of, whole, after))
        if keep < held_frames:
            return [held[0][held[0].shape[0] - whole :], held[1][:whole]]
        return held

    def first_hop(own):
        assert hops[0] == (frames, False)
        return [[shifted(own, 1), shifted(own, -1)]]

    def selected(arrivals, after=()):
        for hop in range(1, len(hops)):
            to_send = forwarded(arrivals[-1], hops[hop - 1][0], *hops[hop], after if hop == len(hops) - 1 else ())
            if hop < len(hops) - 1:
                arrivals.append([shifted(to_send[0], 1), shifted(to_send[1], -1)])
        return to_send

    def last_hop(arrivals, to_send):
        arrivals.append([shifted(to_send[0], 1), shifted(to_send[1], -1)])

    chunks = range(len(CHUNKS))
    owned, arrivals, sent, results, outs = [], [], [], [], []

    def attend_chunk(c, after):
        order = [a[0] for a in arrivals[c][::-1]] + [owned[c]] + [a[1] for a in arrivals[c]]
        results.append(attend(places, masks, queries, order, frames, lows[c], after=after))
        result = results[c]
        if outs:
            result, outs[-1] = lax.optimization_barrier((result, outs[-1]))
        outs.append(exchange(result))

    for c in chunks:
        packed = pack([k_proj, v_proj], [starts[c]], [widths[c]], team_size, after=sent[c - 2] if c >= 2 else ())
        if c == len(CHUNKS) - 1:
            queries = exchange(pack([q_proj], starts, widths, team_size, after=[packed]))
        owned.append(exchange(packed))
        arrivals.append(first_hop(owned[c]))
        sent.append(selected(arrivals[c], after=sent[-1] if sent else ()))
        last_hop(arrivals[c], sent[c])
    for c in chunks:
        attend_chunk(c, after=results[-1:] + (sent[c + 1] if c + 1 < len(CHUNKS) else []))
    return unpack(outs, starts, model_width)


def solution(mesh):
    sizes = dict(mesh.shape)
    members = sizes["uly"] * sizes["rep"]
    heads = 40
    inner = max(
        i for i in range(1, sizes["ctx"] + 1) if sizes["ctx"] % i == 0 and heads % (i * members) == 0
    )
    outer = sizes["ctx"] // inner
    finer = Mesh(
        mesh.devices.reshape(sizes["groups"], outer, inner, sizes["uly"], sizes["rep"]),
        ("groups", "outer", "inner", "uly", "rep"),
    )
    split = P(("groups", "outer", "inner", "rep", "uly"), None)
    return jax.shard_map(
        functools.partial(on_device, outer, inner),
        mesh=finer,
        in_specs=(split, split, split, P("groups", None)),
        out_specs=split,
        check_vma=False,
    )
```

```python
import functools
import math

import jax
import jax.numpy as jnp
from jax import lax
from jax.experimental import pallas as pl
from jax.experimental.pallas import tpu as pltpu
from jax.sharding import Mesh, PartitionSpec as P

HD = 128
BLK = 128
BPF = 2
REACH = 7
CHUNKS = (2, 2, 1)
VMEM_LIMIT = 60 * 1024 * 1024
little = dict(flops=1024, bytes_accessed=1024, transcendentals=0)

ROWS = 16

very_low = -1e30
to_log2 = math.log2(math.e) * HD ** -0.5


def staged_copies(steps, sems):
    count = len(steps)
    fetches = [pltpu.make_async_copy(s, stage, sems.at[i]) for i, (s, stage, t) in enumerate(steps)]
    puts = [pltpu.make_async_copy(stage, t, sems.at[count + i]) for i, (s, stage, t) in enumerate(steps)]
    for fetch in fetches:
        fetch.start()
    for fetch, put in zip(fetches, puts):
        fetch.wait()
        put.start()
    for put in puts:
        put.wait()


anywhere = pl.BlockSpec(memory_space=pl.ANY)


def copy_call(plan, shapes, count, operands, scalars=(), after=()):
    def body(*refs):
        first = len(scalars)
        last = first + len(operands)
        results = refs[last + len(after) :]
        n = len(shapes)
        staged_copies(plan(refs[:first], refs[first:last], results[:n], results[n : 2 * n]), results[2 * n])

    return pl.pallas_call(
        body,
        out_shape=shapes,
        in_specs=[pl.BlockSpec(memory_space=pltpu.SMEM)] * len(scalars) + [anywhere] * (len(operands) + len(after)),
        out_specs=[anywhere] * len(shapes),
        scratch_shapes=[pltpu.VMEM(s.shape, s.dtype) for s in shapes] + [pltpu.SemaphoreType.DMA((2 * count,))],
        compiler_params=pltpu.CompilerParams(vmem_limit_bytes=VMEM_LIMIT),
        cost_estimate=pl.CostEstimate(**little),
    )(*scalars, *operands, *after)


def pack(arrays, starts, widths, team_size, after=()):
    rows = arrays[0].shape[0]

    def plan(scalars, sources, outs, stages):
        steps = []
        for member in range(team_size):
            for kind, source in enumerate(sources):
                low = 0
                for start, width in zip(starts, widths):
                    place = (member, kind, slice(None), pl.ds(low, width))
                    columns = pl.ds(start + member * width, width)
                    steps.append((source.at[:, columns], stages[0].at[place], outs[0].at[place]))
                    low += width
        return steps

    shape = jax.ShapeDtypeStruct((team_size, len(arrays), rows, sum(widths)), jnp.bfloat16)
    return copy_call(plan, [shape], team_size * len(arrays) * len(starts), arrays, after=after)[0]


def unpack(parts, starts, model_width):
    def plan(scalars, sources, outs, stages):
        steps = []
        for start, source in zip(starts, sources):
            for member in range(source.shape[0]):
                columns = pl.ds(start + member * source.shape[2], source.shape[2])
                steps.append((source.at[member], stages[0].at[:, columns], outs[0].at[:, columns]))
        return steps

    shape = jax.ShapeDtypeStruct((parts[0].shape[1], model_width), jnp.bfloat16)
    return copy_call(plan, [shape], sum(part.shape[0] for part in parts), parts)[0]


def select(held, places, count, whole, after=()):
    def plan(scalars, sources, outs, stages):
        (place_ref,) = scalars
        steps = []
        for side, (source, stage, out) in enumerate(zip(sources, stages, outs)):
            one = pl.ds(0 if side == 0 else whole, count)
            steps.append((source.at[pl.ds(place_ref[side], count)], stage.at[one], out.at[one]))
            if whole > 0:
                rest = pl.ds(count if side == 0 else 0, whole)
                kept = pl.ds(source.shape[0] - whole if side == 0 else 0, whole)
                steps.append((source.at[kept], stage.at[rest], out.at[rest]))
        return steps

    shapes = [jax.ShapeDtypeStruct((count + whole,) + array.shape[1:], array.dtype) for array in held]
    return copy_call(plan, shapes, 2 * (2 if whole > 0 else 1), held, scalars=[places], after=after)


def columns_of(head):
    return pl.ds(pl.multiple_of(head * HD, HD), HD)


def flat(rows):
    return rows.reshape(rows.shape[0] * rows.shape[1], HD)


def attend_kernel(frames, pieces_of, heads, first_head, place_ref, mask_ref, q_hbm, *refs):
    *piece_refs, out_hbm, q_ref, out_ref, store, scores_a, scores_b, weights_a, weights_b, totals_a, totals_b, sems, put_sems = refs
    per_frame = BPF * pieces_of
    width = 2 * REACH
    items = frames * heads
    slots = [(scores_a, weights_a, totals_a), (scores_b, weights_b, totals_b)]

    def fetches(head):
        columns = columns_of(head)
        found = [(q_hbm.at[:, 0, :, columns_of(head + first_head)], q_ref.at[:, :, columns])]
        start = 0
        for piece in piece_refs:
            size = piece.shape[0]
            found.append((piece.at[:, :, :, columns], store.at[pl.ds(start, size), :, :, columns]))
            start += size
        return [pltpu.make_async_copy(a, b, sems.at[head, i]) for i, (a, b) in enumerate(found)]

    def put(head):
        columns = columns_of(head)
        return pltpu.make_async_copy(out_ref.at[:, :, columns], out_hbm.at[:, :, columns], put_sems.at[head])

    def keys_or_values(kind, frame, columns):
        own = ((frame + REACH) * BPF - 1) * pieces_of
        found = [flat(store[pl.ds(own, per_frame), kind, :, columns])]
        for pair in range(REACH):
            places = [place_ref[frame * width + 2 * pair + side] for side in range(2)]
            found.append(
                jnp.concatenate([flat(store[pl.ds(place, pieces_of), kind, :, columns]) for place in places], axis=0)
            )
        return found

    def score(item, scores_ref):
        head = item // frames
        frame = item - head * frames
        columns = columns_of(head)
        queries = flat(q_ref[pl.ds(frame * per_frame, per_frame), :, columns])
        for pair, keys in enumerate(keys_or_values(0, frame, columns)):
            scores = lax.dot_general(queries, keys, (((1,), (1,)), ((), ())), preferred_element_type=jnp.float32)
            for side in range(2):
                for b in range(BPF):
                    tile = scores[b * BLK : (b + 1) * BLK, side * BLK : (side + 1) * BLK]
                    if pair > 0:
                        tile = tile + mask_ref[(frame * BPF + b) * width + 2 * (pair - 1) + side]
                    scores_ref[b * BLK : (b + 1) * BLK, (2 * pair + side) * BLK : (2 * pair + side + 1) * BLK] = tile

    def soften(scores_ref, weights_ref, totals_ref):
        for low in range(0, BPF * BLK, ROWS):
            rows = slice(low, low + ROWS)
            tiles = [scores_ref[rows, j * BLK : (j + 1) * BLK] for j in range(BPF + width)]
            top = jnp.max(functools.reduce(jnp.maximum, tiles), axis=1, keepdims=True)
            total = None
            for j in range(BPF + width):
                exps = jnp.exp2((scores_ref[rows, j * BLK : (j + 1) * BLK] - top) * to_log2)
                total = exps if total is None else total + exps
                weights_ref[rows, j * BLK : (j + 1) * BLK] = exps.astype(jnp.bfloat16)
            totals_ref[rows, :] = jnp.broadcast_to(jnp.sum(total, axis=1, keepdims=True), (ROWS, HD))

    def product(item, weights_ref, totals_ref):
        head = item // frames
        frame = item - head * frames
        columns = columns_of(head)
        values = jnp.concatenate(keys_or_values(1, frame, columns), axis=0)
        mixed = jnp.dot(weights_ref[...], values, preferred_element_type=jnp.float32)
        result = (mixed / totals_ref[...]).astype(jnp.bfloat16)
        out_ref[pl.ds(frame * per_frame, per_frame), :, columns] = result.reshape(per_frame, BLK // pieces_of, HD)

    for head in range(heads):
        for fetch in fetches(head):
            fetch.start()
    for fetch in fetches(0):
        fetch.wait()
    weights_b[...] = jnp.zeros_like(weights_b)
    totals_b[...] = jnp.ones_like(totals_b)
    score(0, scores_a)

    def stages(item, here, there):
        after = jnp.minimum(item + 1, items - 1)

        @pl.when((after % frames == 0) & (after > item))
        def _():
            for fetch in fetches(after // frames):
                fetch.wait()

        score(after, there[0])
        soften(*here)
        product(jnp.maximum(item - 1, 0), *there[1:])

    def step(index, carry):
        stages(2 * index, slots[0], slots[1])
        stages(2 * index + 1, slots[1], slots[0])
        return carry

    lax.fori_loop(0, items // 2, step, 0)
    if items % 2 == 1:
        stages(items - 1, slots[0], slots[1])
    product(items - 1, *slots[(items - 1) % 2][1:])
    for head in range(heads):
        put(head).start()
    for head in range(heads):
        put(head).wait()


def attend(places, masks, queries, pieces, frames, first_head, after=()):
    members, _, rows, _ = queries.shape
    pieces_of = BLK // rows
    width = pieces[0].shape[3]
    heads = width // HD
    stored = sum(piece.shape[0] for piece in pieces)
    keys = (2 * REACH + BPF) * BLK

    def body(place_ref, mask_ref, q_hbm, *refs):
        kept = refs[: len(pieces)] + refs[len(pieces) + len(after) :]
        attend_kernel(frames, pieces_of, heads, first_head, place_ref, mask_ref, q_hbm, *kept)

    return pl.pallas_call(
        body,
        out_shape=jax.ShapeDtypeStruct((members, rows, width), jnp.bfloat16),
        in_specs=[pl.BlockSpec(memory_space=pltpu.SMEM)] * 2 + [anywhere] * (1 + len(pieces) + len(after)),
        out_specs=anywhere,
        scratch_shapes=[
            pltpu.VMEM((members, rows, width), jnp.bfloat16),
            pltpu.VMEM((members, rows, width), jnp.bfloat16),
            pltpu.VMEM((stored, 2, rows, width), jnp.bfloat16),
            *[pltpu.VMEM((BPF * BLK, keys), jnp.float32)] * 2,
            *[pltpu.VMEM((BPF * BLK, keys), jnp.bfloat16)] * 2,
            *[pltpu.VMEM((BPF * BLK, HD), jnp.float32)] * 2,
            pltpu.SemaphoreType.DMA((heads, 1 + len(pieces))),
            pltpu.SemaphoreType.DMA((heads,)),
        ],
        compiler_params=pltpu.CompilerParams(vmem_limit_bytes=VMEM_LIMIT),
        cost_estimate=pl.CostEstimate(
            flops=6 * frames * BPF * heads * 2 * REACH * 4 * BLK * BLK * HD, bytes_accessed=1024, transcendentals=0
        ),
    )(places, masks, queries, *pieces, *after)


def on_device(outer, inner, q_proj, k_proj, v_proj, kv_list):
    frames = inner
    rows, model_width = q_proj.shape
    team = ("inner", "rep", "uly")
    team_size = frames * BPF * BLK // rows
    heads_here = model_width // HD // team_size
    pieces_of = BLK // rows
    per_frame = BPF * pieces_of
    my_group = lax.axis_index("outer")

    def rows_of(reader_frame, count):
        start = jnp.clip(reader_frame * BPF, 0, kv_list.shape[0] - count * BPF)
        return lax.dynamic_slice_in_dim(kv_list, start, count * BPF, 0)

    lists = rows_of(my_group * frames, frames).reshape(frames, BPF, 1, -1)
    shape = (frames, 1, 2 * REACH, 1)
    steps = lax.broadcasted_iota(jnp.int32, shape, 2)
    relative = lax.broadcasted_iota(jnp.int32, shape, 0) + steps - REACH + jnp.where(steps >= REACH, 1, 0)
    first_ids = BPF * (my_group * frames + relative)
    hits = jnp.where(lists == first_ids, 1, 0) + jnp.where(lists == first_ids + 1, 2, 0)
    codes = jnp.sum(jnp.where(lists >= 0, hits, 0), axis=-1)
    masks = jnp.where(codes > 0, 0.0, very_low).astype(jnp.float32).reshape(-1)
    relative = relative.reshape(frames, 2 * REACH)
    picks = jnp.where(relative == frames - 1 + REACH, 0, jnp.max(codes, axis=1) // 2)
    places = pieces_of * jnp.maximum(BPF * (relative + REACH) - 1 + picks, 0)
    places = jnp.where(relative == -REACH, 0, places).reshape(-1)

    def picked(reader_frame, holder_frame):
        return jnp.any(rows_of(reader_frame, 1) == holder_frame * BPF + 1).astype(jnp.int32)

    assert sum(CHUNKS) == heads_here
    widths = [heads * HD for heads in CHUNKS]
    lows = [sum(CHUNKS[:c]) for c in range(len(CHUNKS))]
    starts = [low * team_size * HD for low in lows]

    def exchange(array):
        return lax.all_to_all(array, team, split_axis=0, concat_axis=0, tiled=True)

    def shifted(array, heading):
        route = [(i, i + heading) for i in range(outer) if 0 <= i + heading < outer]
        return lax.ppermute(array, "outer", route)

    hops = []
    for hop in range(1, -(-REACH // frames) + 1):
        spare = hop * frames - REACH
        hops.append((frames - max(0, spare), spare >= 0))

    def forwarded(held, held_frames, keep, single, after):
        whole = (keep - 1 if single else keep) * per_frame
        if single:
            from_left, from_right = (my_group + 1) * frames, my_group * frames - 1
            edges = held[0].shape[0] - whole - per_frame, whole
            edge_places = jnp.stack(
                [
                    edges[0] + pieces_of * picked(from_left, from_left - REACH),
                    edges[1] + pieces_of * picked(from_right, from_right + REACH),
                ]
            )
            return list(select(held, edge_places, pieces_of, whole, after))
        if keep < held_frames:
            return [held[0][held[0].shape[0] - whole :], held[1][:whole]]
        return held

    def first_hop(own):
        assert hops[0] == (frames, False)
        return [[shifted(own, 1), shifted(own, -1)]]

    def selected(arrivals, after=()):
        for hop in range(1, len(hops)):
            to_send = forwarded(arrivals[-1], hops[hop - 1][0], *hops[hop], after if hop == len(hops) - 1 else ())
            if hop < len(hops) - 1:
                arrivals.append([shifted(to_send[0], 1), shifted(to_send[1], -1)])
        return to_send

    def last_hop(arrivals, to_send):
        arrivals.append([shifted(to_send[0], 1), shifted(to_send[1], -1)])

    chunks = range(len(CHUNKS))
    owned, arrivals, sent, results, outs = [], [], [], [], []

    def attend_chunk(c, after):
        order = [a[0] for a in arrivals[c][::-1]] + [owned[c]] + [a[1] for a in arrivals[c]]
        results.append(attend(places, masks, queries, order, frames, lows[c], after=after))
        result = results[c]
        if outs:
            result, outs[-1] = lax.optimization_barrier((result, outs[-1]))
        outs.append(exchange(result))

    for c in chunks:
        packed = pack([k_proj, v_proj], [starts[c]], [widths[c]], team_size, after=sent[c - 2] if c >= 2 else ())
        if c == min(1, len(CHUNKS) - 1):
            queries = exchange(pack([q_proj], starts, widths, team_size, after=[packed]))
        owned.append(exchange(packed))
        arrivals.append(first_hop(owned[c]))
        sent.append(selected(arrivals[c], after=sent[-1] if sent else ()))
        last_hop(arrivals[c], sent[c])
    for c in chunks:
        attend_chunk(c, after=results[-1:] + (sent[c + 1] if c + 1 < len(CHUNKS) else []))
    return unpack(outs, starts, model_width)


def solution(mesh):
    sizes = dict(mesh.shape)
    members = sizes["uly"] * sizes["rep"]
    heads = 40
    inner = max(
        i for i in range(1, sizes["ctx"] + 1) if sizes["ctx"] % i == 0 and heads % (i * members) == 0
    )
    outer = sizes["ctx"] // inner
    finer = Mesh(
        mesh.devices.reshape(sizes["groups"], outer, inner, sizes["uly"], sizes["rep"]),
        ("groups", "outer", "inner", "uly", "rep"),
    )
    split = P(("groups", "outer", "inner", "rep", "uly"), None)
    return jax.shard_map(
        functools.partial(on_device, outer, inner),
        mesh=finer,
        in_specs=(split, split, split, P("groups", None)),
        out_specs=split,
        check_vma=False,
    )
```

```python
import functools
import math

import jax
import jax.numpy as jnp
from jax import lax
from jax.experimental import pallas as pl
from jax.experimental.pallas import tpu as pltpu
from jax.sharding import Mesh, PartitionSpec as P

HD = 128
BLK = 128
BPF = 2
REACH = 7
CHUNKS = (2, 3)
VMEM_LIMIT = 60 * 1024 * 1024
little = dict(flops=1024, bytes_accessed=1024, transcendentals=0)

ROWS = 16

very_low = -1e30
to_log2 = math.log2(math.e) * HD ** -0.5


def staged_copies(steps, sems):
    count = len(steps)
    fetches = [pltpu.make_async_copy(s, stage, sems.at[i]) for i, (s, stage, t) in enumerate(steps)]
    puts = [pltpu.make_async_copy(stage, t, sems.at[count + i]) for i, (s, stage, t) in enumerate(steps)]
    for fetch in fetches:
        fetch.start()
    for fetch, put in zip(fetches, puts):
        fetch.wait()
        put.start()
    for put in puts:
        put.wait()


anywhere = pl.BlockSpec(memory_space=pl.ANY)


def copy_call(plan, shapes, count, operands, scalars=(), after=()):
    def body(*refs):
        first = len(scalars)
        last = first + len(operands)
        results = refs[last + len(after) :]
        n = len(shapes)
        staged_copies(plan(refs[:first], refs[first:last], results[:n], results[n : 2 * n]), results[2 * n])

    return pl.pallas_call(
        body,
        out_shape=shapes,
        in_specs=[pl.BlockSpec(memory_space=pltpu.SMEM)] * len(scalars) + [anywhere] * (len(operands) + len(after)),
        out_specs=[anywhere] * len(shapes),
        scratch_shapes=[pltpu.VMEM(s.shape, s.dtype) for s in shapes] + [pltpu.SemaphoreType.DMA((2 * count,))],
        compiler_params=pltpu.CompilerParams(vmem_limit_bytes=VMEM_LIMIT),
        cost_estimate=pl.CostEstimate(**little),
    )(*scalars, *operands, *after)


def pack(arrays, starts, widths, team_size, after=()):
    rows = arrays[0].shape[0]

    def plan(scalars, sources, outs, stages):
        steps = []
        for member in range(team_size):
            for kind, source in enumerate(sources):
                low = 0
                for start, width in zip(starts, widths):
                    place = (member, kind, slice(None), pl.ds(low, width))
                    columns = pl.ds(start + member * width, width)
                    steps.append((source.at[:, columns], stages[0].at[place], outs[0].at[place]))
                    low += width
        return steps

    shape = jax.ShapeDtypeStruct((team_size, len(arrays), rows, sum(widths)), jnp.bfloat16)
    return copy_call(plan, [shape], team_size * len(arrays) * len(starts), arrays, after=after)[0]


def unpack(parts, starts, model_width):
    def plan(scalars, sources, outs, stages):
        steps = []
        for start, source in zip(starts, sources):
            for member in range(source.shape[0]):
                columns = pl.ds(start + member * source.shape[2], source.shape[2])
                steps.append((source.at[member], stages[0].at[:, columns], outs[0].at[:, columns]))
        return steps

    shape = jax.ShapeDtypeStruct((parts[0].shape[1], model_width), jnp.bfloat16)
    return copy_call(plan, [shape], sum(part.shape[0] for part in parts), parts)[0]


def select(held, places, count, whole, after=()):
    arrays, kinds = zip(*held)

    def plan(scalars, sources, outs, stages):
        (place_ref,) = scalars
        steps = []
        for side, (source, stage, out) in enumerate(zip(sources, stages, outs)):
            both = pl.ds(kinds[side], 2)
            one = pl.ds(0 if side == 0 else whole, count)
            steps.append((source.at[pl.ds(place_ref[side], count), both], stage.at[one], out.at[one]))
            if whole > 0:
                rest = pl.ds(count if side == 0 else 0, whole)
                kept = pl.ds(source.shape[0] - whole if side == 0 else 0, whole)
                steps.append((source.at[kept, both], stage.at[rest], out.at[rest]))
        return steps

    shapes = [jax.ShapeDtypeStruct((count + whole, 2) + array.shape[2:], array.dtype) for array in arrays]
    return copy_call(plan, shapes, 2 * (2 if whole > 0 else 1), arrays, scalars=[places], after=after)


def merge(arrays, after=()):
    def plan(scalars, sources, outs, stages):
        steps = []
        low = 0
        for source in sources:
            kinds = source.shape[1]
            for member in range(source.shape[0]):
                place = (member, pl.ds(low, kinds))
                steps.append((source.at[member], stages[0].at[place], outs[0].at[place]))
            low += kinds
        return steps

    members, _, rows, width = arrays[0].shape
    shape = jax.ShapeDtypeStruct((members, sum(a.shape[1] for a in arrays), rows, width), arrays[0].dtype)
    return copy_call(plan, [shape], members * len(arrays), arrays, after=after)[0]


def columns_of(head):
    return pl.ds(pl.multiple_of(head * HD, HD), HD)


def flat(rows):
    return rows.reshape(rows.shape[0] * rows.shape[1], HD)


def attend_kernel(frames, pieces_of, heads, first_head, kinds, place_ref, mask_ref, q_hbm, *refs):
    *piece_refs, out_hbm, q_ref, out_ref, store, scores_a, scores_b, weights_a, weights_b, totals_a, totals_b, sems, put_sems = refs
    per_frame = BPF * pieces_of
    width = 2 * REACH
    items = frames * heads
    slots = [(scores_a, weights_a, totals_a), (scores_b, weights_b, totals_b)]

    def fetches(head):
        columns = columns_of(head)
        found = [(q_hbm.at[:, 0, :, columns_of(head + first_head)], q_ref.at[:, :, columns])]
        start = 0
        for piece, kind in zip(piece_refs, kinds):
            size = piece.shape[0]
            found.append((piece.at[:, pl.ds(kind, 2), :, columns], store.at[pl.ds(start, size), :, :, columns]))
            start += size
        return [pltpu.make_async_copy(a, b, sems.at[head, i]) for i, (a, b) in enumerate(found)]

    def put(head):
        columns = columns_of(head)
        return pltpu.make_async_copy(out_ref.at[:, :, columns], out_hbm.at[:, :, columns], put_sems.at[head])

    def keys_or_values(kind, frame, columns):
        own = ((frame + REACH) * BPF - 1) * pieces_of
        found = [flat(store[pl.ds(own, per_frame), kind, :, columns])]
        for pair in range(REACH):
            places = [place_ref[frame * width + 2 * pair + side] for side in range(2)]
            found.append(
                jnp.concatenate([flat(store[pl.ds(place, pieces_of), kind, :, columns]) for place in places], axis=0)
            )
        return found

    def score(item, scores_ref):
        head = item // frames
        frame = item - head * frames
        columns = columns_of(head)
        queries = flat(q_ref[pl.ds(frame * per_frame, per_frame), :, columns])
        for pair, keys in enumerate(keys_or_values(0, frame, columns)):
            scores = lax.dot_general(queries, keys, (((1,), (1,)), ((), ())), preferred_element_type=jnp.float32)
            for side in range(2):
                for b in range(BPF):
                    tile = scores[b * BLK : (b + 1) * BLK, side * BLK : (side + 1) * BLK]
                    if pair > 0:
                        tile = tile + mask_ref[(frame * BPF + b) * width + 2 * (pair - 1) + side]
                    scores_ref[b * BLK : (b + 1) * BLK, (2 * pair + side) * BLK : (2 * pair + side + 1) * BLK] = tile

    def soften(scores_ref, weights_ref, totals_ref):
        for low in range(0, BPF * BLK, ROWS):
            rows = slice(low, low + ROWS)
            tiles = [scores_ref[rows, j * BLK : (j + 1) * BLK] for j in range(BPF + width)]
            top = jnp.max(functools.reduce(jnp.maximum, tiles), axis=1, keepdims=True)
            total = None
            for j in range(BPF + width):
                exps = jnp.exp2((scores_ref[rows, j * BLK : (j + 1) * BLK] - top) * to_log2)
                total = exps if total is None else total + exps
                weights_ref[rows, j * BLK : (j + 1) * BLK] = exps.astype(jnp.bfloat16)
            totals_ref[rows, :] = jnp.broadcast_to(jnp.sum(total, axis=1, keepdims=True), (ROWS, HD))

    def product(item, weights_ref, totals_ref):
        head = item // frames
        frame = item - head * frames
        columns = columns_of(head)
        values = jnp.concatenate(keys_or_values(1, frame, columns), axis=0)
        mixed = jnp.dot(weights_ref[...], values, preferred_element_type=jnp.float32)
        result = (mixed / totals_ref[...]).astype(jnp.bfloat16)
        out_ref[pl.ds(frame * per_frame, per_frame), :, columns] = result.reshape(per_frame, BLK // pieces_of, HD)

    for head in range(heads):
        for fetch in fetches(head):
            fetch.start()
    for fetch in fetches(0):
        fetch.wait()
    weights_b[...] = jnp.zeros_like(weights_b)
    totals_b[...] = jnp.ones_like(totals_b)
    score(0, scores_a)

    def stages(item, here, there):
        after = jnp.minimum(item + 1, items - 1)

        @pl.when((after % frames == 0) & (after > item))
        def _():
            for fetch in fetches(after // frames):
                fetch.wait()

        score(after, there[0])
        soften(*here)
        product(jnp.maximum(item - 1, 0), *there[1:])

    def step(index, carry):
        stages(2 * index, slots[0], slots[1])
        stages(2 * index + 1, slots[1], slots[0])
        return carry

    lax.fori_loop(0, items // 2, step, 0)
    if items % 2 == 1:
        stages(items - 1, slots[0], slots[1])
    product(items - 1, *slots[(items - 1) % 2][1:])
    for head in range(heads):
        put(head).start()
    for head in range(heads):
        put(head).wait()


def attend(places, masks, queries, pieces, frames, first_head, after=()):
    pieces, kinds = zip(*pieces)
    members, _, rows, _ = queries.shape
    pieces_of = BLK // rows
    width = pieces[0].shape[3]
    heads = width // HD
    stored = sum(piece.shape[0] for piece in pieces)
    keys = (2 * REACH + BPF) * BLK

    def body(place_ref, mask_ref, q_hbm, *refs):
        kept = refs[: len(pieces)] + refs[len(pieces) + len(after) :]
        attend_kernel(frames, pieces_of, heads, first_head, kinds, place_ref, mask_ref, q_hbm, *kept)

    return pl.pallas_call(
        body,
        out_shape=jax.ShapeDtypeStruct((members, rows, width), jnp.bfloat16),
        in_specs=[pl.BlockSpec(memory_space=pltpu.SMEM)] * 2 + [anywhere] * (1 + len(pieces) + len(after)),
        out_specs=anywhere,
        scratch_shapes=[
            pltpu.VMEM((members, rows, width), jnp.bfloat16),
            pltpu.VMEM((members, rows, width), jnp.bfloat16),
            pltpu.VMEM((stored, 2, rows, width), jnp.bfloat16),
            *[pltpu.VMEM((BPF * BLK, keys), jnp.float32)] * 2,
            *[pltpu.VMEM((BPF * BLK, keys), jnp.bfloat16)] * 2,
            *[pltpu.VMEM((BPF * BLK, HD), jnp.float32)] * 2,
            pltpu.SemaphoreType.DMA((heads, 1 + len(pieces))),
            pltpu.SemaphoreType.DMA((heads,)),
        ],
        compiler_params=pltpu.CompilerParams(vmem_limit_bytes=VMEM_LIMIT),
        cost_estimate=pl.CostEstimate(
            flops=6 * frames * BPF * heads * 2 * REACH * 4 * BLK * BLK * HD, bytes_accessed=1024, transcendentals=0
        ),
    )(places, masks, queries, *pieces, *after)


def on_device(outer, inner, q_proj, k_proj, v_proj, kv_list):
    frames = inner
    rows, model_width = q_proj.shape
    team = ("inner", "rep", "uly")
    team_size = frames * BPF * BLK // rows
    heads_here = model_width // HD // team_size
    pieces_of = BLK // rows
    per_frame = BPF * pieces_of
    my_group = lax.axis_index("outer")

    def rows_of(reader_frame, count):
        start = jnp.clip(reader_frame * BPF, 0, kv_list.shape[0] - count * BPF)
        return lax.dynamic_slice_in_dim(kv_list, start, count * BPF, 0)

    lists = rows_of(my_group * frames, frames).reshape(frames, BPF, 1, -1)
    shape = (frames, 1, 2 * REACH, 1)
    steps = lax.broadcasted_iota(jnp.int32, shape, 2)
    relative = lax.broadcasted_iota(jnp.int32, shape, 0) + steps - REACH + jnp.where(steps >= REACH, 1, 0)
    first_ids = BPF * (my_group * frames + relative)
    hits = jnp.where(lists == first_ids, 1, 0) + jnp.where(lists == first_ids + 1, 2, 0)
    codes = jnp.sum(jnp.where(lists >= 0, hits, 0), axis=-1)
    masks = jnp.where(codes > 0, 0.0, very_low).astype(jnp.float32).reshape(-1)
    relative = relative.reshape(frames, 2 * REACH)
    picks = jnp.where(relative == frames - 1 + REACH, 0, jnp.max(codes, axis=1) // 2)
    places = pieces_of * jnp.maximum(BPF * (relative + REACH) - 1 + picks, 0)
    places = jnp.where(relative == -REACH, 0, places).reshape(-1)

    def picked(reader_frame, holder_frame):
        return jnp.any(rows_of(reader_frame, 1) == holder_frame * BPF + 1).astype(jnp.int32)

    assert sum(CHUNKS) == heads_here
    widths = [heads * HD for heads in CHUNKS]
    lows = [sum(CHUNKS[:c]) for c in range(len(CHUNKS))]
    starts = [low * team_size * HD for low in lows]

    def exchange(array):
        return lax.all_to_all(array, team, split_axis=0, concat_axis=0, tiled=True)

    def shifted(array, heading):
        route = [(i, i + heading) for i in range(outer) if 0 <= i + heading < outer]
        return lax.ppermute(array, "outer", route)

    hops = []
    for hop in range(1, -(-REACH // frames) + 1):
        spare = hop * frames - REACH
        hops.append((frames - max(0, spare), spare >= 0))

    def forwarded(held, held_frames, keep, single, after):
        whole = (keep - 1 if single else keep) * per_frame
        if single:
            from_left, from_right = (my_group + 1) * frames, my_group * frames - 1
            edges = held[0][0].shape[0] - whole - per_frame, whole
            edge_places = jnp.stack(
                [
                    edges[0] + pieces_of * picked(from_left, from_left - REACH),
                    edges[1] + pieces_of * picked(from_right, from_right + REACH),
                ]
            )
            return list(select(held, edge_places, pieces_of, whole, after))
        left, right = [array[:, kind : kind + 2] for array, kind in held]
        if keep < held_frames:
            return [left[left.shape[0] - whole :], right[:whole]]
        return [left, right]

    def hop(to_send):
        return [(shifted(to_send[0], 1), 0), (shifted(to_send[1], -1), 0)]

    def to_last_hop(arrivals, after=()):
        for number in range(1, len(hops)):
            to_send = forwarded(
                arrivals[-1], hops[number - 1][0], *hops[number], after if number == len(hops) - 1 else ()
            )
            if number < len(hops) - 1:
                arrivals.append(hop(to_send))
        return to_send

    assert hops[0] == (frames, False)
    packed = [pack([k_proj, v_proj], [starts[c]], [widths[c]], team_size) for c in range(2)]
    early = hop([packed[0], packed[0]])
    owned = {1: (exchange(packed[1]), 0)}
    joined = exchange(merge([packed[0], early[0][0], early[1][0]], after=[owned[1][0]]))
    owned[0] = (joined, 0)
    arrivals = {0: [[(joined, 2), (joined, 4)]], 1: [hop([owned[1][0]] * 2)]}
    queries = exchange(pack([q_proj], starts, widths, team_size, after=[joined]))

    sent = {1: to_last_hop(arrivals[1])}
    arrivals[1].append(hop(sent[1]))
    sent[0] = to_last_hop(arrivals[0], after=sent[1])
    arrivals[0].append(hop(sent[0]))

    results, outs = {}, {}
    for c, after in ((1, sent[0]), (0, None)):
        order = [a[0] for a in arrivals[c][::-1]] + [owned[c]] + [a[1] for a in arrivals[c]]
        results[c] = attend(places, masks, queries, order, frames, lows[c], after=after or [results[1]])
    outs[1] = exchange(results[1])
    last, outs[1] = lax.optimization_barrier((results[0], outs[1]))
    outs[0] = exchange(last)
    return unpack([outs[0], outs[1]], starts, model_width)


def solution(mesh):
    sizes = dict(mesh.shape)
    members = sizes["uly"] * sizes["rep"]
    heads = 40
    inner = max(
        i for i in range(1, sizes["ctx"] + 1) if sizes["ctx"] % i == 0 and heads % (i * members) == 0
    )
    outer = sizes["ctx"] // inner
    finer = Mesh(
        mesh.devices.reshape(sizes["groups"], outer, inner, sizes["uly"], sizes["rep"]),
        ("groups", "outer", "inner", "uly", "rep"),
    )
    split = P(("groups", "outer", "inner", "rep", "uly"), None)
    return jax.shard_map(
        functools.partial(on_device, outer, inner),
        mesh=finer,
        in_specs=(split, split, split, P("groups", None)),
        out_specs=split,
        check_vma=False,
    )
```

```python
import functools
import math

import jax
import jax.numpy as jnp
from jax import lax
from jax.experimental import pallas as pl
from jax.experimental.pallas import tpu as pltpu
from jax.sharding import Mesh, PartitionSpec as P

HD = 128
BLK = 128
BPF = 2
REACH = 7
CHUNKS = (3, 2)
VMEM_LIMIT = 60 * 1024 * 1024
little = dict(flops=1024, bytes_accessed=1024, transcendentals=0)

ROWS = 16

very_low = -1e30
to_log2 = math.log2(math.e) * HD ** -0.5


def staged_copies(steps, sems):
    count = len(steps)
    fetches = [pltpu.make_async_copy(s, stage, sems.at[i]) for i, (s, stage, t) in enumerate(steps)]
    puts = [pltpu.make_async_copy(stage, t, sems.at[count + i]) for i, (s, stage, t) in enumerate(steps)]
    for fetch in fetches:
        fetch.start()
    for fetch, put in zip(fetches, puts):
        fetch.wait()
        put.start()
    for put in puts:
        put.wait()


anywhere = pl.BlockSpec(memory_space=pl.ANY)


def copy_call(plan, shapes, count, operands, scalars=(), after=()):
    def body(*refs):
        first = len(scalars)
        last = first + len(operands)
        results = refs[last + len(after) :]
        n = len(shapes)
        staged_copies(plan(refs[:first], refs[first:last], results[:n], results[n : 2 * n]), results[2 * n])

    return pl.pallas_call(
        body,
        out_shape=shapes,
        in_specs=[pl.BlockSpec(memory_space=pltpu.SMEM)] * len(scalars) + [anywhere] * (len(operands) + len(after)),
        out_specs=[anywhere] * len(shapes),
        scratch_shapes=[pltpu.VMEM(s.shape, s.dtype) for s in shapes] + [pltpu.SemaphoreType.DMA((2 * count,))],
        compiler_params=pltpu.CompilerParams(vmem_limit_bytes=VMEM_LIMIT),
        cost_estimate=pl.CostEstimate(**little),
    )(*scalars, *operands, *after)


def pack(arrays, starts, widths, team_size, after=()):
    rows = arrays[0].shape[0]

    def plan(scalars, sources, outs, stages):
        steps = []
        for member in range(team_size):
            for kind, source in enumerate(sources):
                low = 0
                for start, width in zip(starts, widths):
                    place = (member, kind, slice(None), pl.ds(low, width))
                    columns = pl.ds(start + member * width, width)
                    steps.append((source.at[:, columns], stages[0].at[place], outs[0].at[place]))
                    low += width
        return steps

    shape = jax.ShapeDtypeStruct((team_size, len(arrays), rows, sum(widths)), jnp.bfloat16)
    return copy_call(plan, [shape], team_size * len(arrays) * len(starts), arrays, after=after)[0]


def unpack(parts, starts, model_width):
    def plan(scalars, sources, outs, stages):
        steps = []
        for start, source in zip(starts, sources):
            for member in range(source.shape[0]):
                columns = pl.ds(start + member * source.shape[2], source.shape[2])
                steps.append((source.at[member], stages[0].at[:, columns], outs[0].at[:, columns]))
        return steps

    shape = jax.ShapeDtypeStruct((parts[0].shape[1], model_width), jnp.bfloat16)
    return copy_call(plan, [shape], sum(part.shape[0] for part in parts), parts)[0]


def select(held, places, count, whole, after=()):
    def plan(scalars, sources, outs, stages):
        (place_ref,) = scalars
        steps = []
        for side, (source, stage, out) in enumerate(zip(sources, stages, outs)):
            one = pl.ds(0 if side == 0 else whole, count)
            steps.append((source.at[pl.ds(place_ref[side], count)], stage.at[one], out.at[one]))
            if whole > 0:
                rest = pl.ds(count if side == 0 else 0, whole)
                kept = pl.ds(source.shape[0] - whole if side == 0 else 0, whole)
                steps.append((source.at[kept], stage.at[rest], out.at[rest]))
        return steps

    shapes = [jax.ShapeDtypeStruct((count + whole,) + array.shape[1:], array.dtype) for array in held]
    return copy_call(plan, shapes, 2 * (2 if whole > 0 else 1), held, scalars=[places], after=after)


def columns_of(head):
    return pl.ds(pl.multiple_of(head * HD, HD), HD)


def flat(rows):
    return rows.reshape(rows.shape[0] * rows.shape[1], HD)


def attend_kernel(frames, pieces_of, heads, first_head, place_ref, mask_ref, q_hbm, *refs):
    *piece_refs, out_hbm, q_ref, out_ref, store, scores_a, scores_b, weights_a, weights_b, sems, put_sems = refs
    per_frame = BPF * pieces_of
    width = 2 * REACH
    items = frames * heads
    slots = [(scores_a, weights_a), (scores_b, weights_b)]

    def fetches(head):
        columns = columns_of(head)
        found = [(q_hbm.at[:, 0, :, columns_of(head + first_head)], q_ref.at[:, :, columns])]
        start = 0
        for piece in piece_refs:
            size = piece.shape[0]
            found.append((piece.at[:, :, :, columns], store.at[pl.ds(start, size), :, :, columns]))
            start += size
        return [pltpu.make_async_copy(a, b, sems.at[head, i]) for i, (a, b) in enumerate(found)]

    def put(head):
        columns = columns_of(head)
        return pltpu.make_async_copy(out_ref.at[:, :, columns], out_hbm.at[:, :, columns], put_sems.at[head])

    def keys_or_values(kind, frame, columns):
        own = ((frame + REACH) * BPF - 1) * pieces_of
        found = [flat(store[pl.ds(own, per_frame), kind, :, columns])]
        for pair in range(REACH):
            places = [place_ref[frame * width + 2 * pair + side] for side in range(2)]
            found.append(
                jnp.concatenate([flat(store[pl.ds(place, pieces_of), kind, :, columns]) for place in places], axis=0)
            )
        return found

    def score(item, scores_ref):
        head = item // frames
        frame = item - head * frames
        columns = columns_of(head)
        queries = flat(q_ref[pl.ds(frame * per_frame, per_frame), :, columns])
        for pair, keys in enumerate(keys_or_values(0, frame, columns)):
            scores = lax.dot_general(queries, keys, (((1,), (1,)), ((), ())), preferred_element_type=jnp.float32)
            for side in range(2):
                for b in range(BPF):
                    tile = scores[b * BLK : (b + 1) * BLK, side * BLK : (side + 1) * BLK]
                    if pair > 0:
                        tile = tile + mask_ref[(frame * BPF + b) * width + 2 * (pair - 1) + side]
                    scores_ref[b * BLK : (b + 1) * BLK, (2 * pair + side) * BLK : (2 * pair + side + 1) * BLK] = tile

    def soften(scores_ref, weights_ref):
        for low in range(0, BPF * BLK, ROWS):
            rows = slice(low, low + ROWS)
            tiles = [scores_ref[rows, j * BLK : (j + 1) * BLK] for j in range(BPF + width)]
            top = jnp.max(functools.reduce(jnp.maximum, tiles), axis=1, keepdims=True)
            for j in range(BPF + width):
                below = (scores_ref[rows, j * BLK : (j + 1) * BLK] - top) * to_log2
                weights_ref[rows, j * BLK : (j + 1) * BLK] = jnp.exp2(below.astype(jnp.bfloat16))

    def product(item, weights_ref):
        head = item // frames
        frame = item - head * frames
        columns = columns_of(head)
        values = jnp.concatenate(keys_or_values(1, frame, columns), axis=0)
        values = jnp.concatenate([values, jnp.ones_like(values)], axis=1)
        mixed = jnp.dot(weights_ref[...], values, preferred_element_type=jnp.float32)
        result = (mixed[:, :HD] / mixed[:, HD:]).astype(jnp.bfloat16)
        out_ref[pl.ds(frame * per_frame, per_frame), :, columns] = result.reshape(per_frame, BLK // pieces_of, HD)

    for head in range(heads):
        for fetch in fetches(head):
            fetch.start()
    for fetch in fetches(0):
        fetch.wait()
    weights_b[...] = jnp.ones_like(weights_b)
    score(0, scores_a)

    def stages(item, here, there):
        after = jnp.minimum(item + 1, items - 1)

        @pl.when((after % frames == 0) & (after > item))
        def _():
            for fetch in fetches(after // frames):
                fetch.wait()

        score(after, there[0])
        soften(*here)
        product(jnp.maximum(item - 1, 0), there[1])

    def step(index, carry):
        stages(2 * index, slots[0], slots[1])
        stages(2 * index + 1, slots[1], slots[0])
        return carry

    lax.fori_loop(0, items // 2, step, 0)
    if items % 2 == 1:
        stages(items - 1, slots[0], slots[1])
    product(items - 1, slots[(items - 1) % 2][1])
    for head in range(heads):
        put(head).start()
    for head in range(heads):
        put(head).wait()


def attend(places, masks, queries, pieces, frames, first_head, after=()):
    members, _, rows, _ = queries.shape
    pieces_of = BLK // rows
    width = pieces[0].shape[3]
    heads = width // HD
    stored = sum(piece.shape[0] for piece in pieces)
    keys = (2 * REACH + BPF) * BLK

    def body(place_ref, mask_ref, q_hbm, *refs):
        kept = refs[: len(pieces)] + refs[len(pieces) + len(after) :]
        attend_kernel(frames, pieces_of, heads, first_head, place_ref, mask_ref, q_hbm, *kept)

    return pl.pallas_call(
        body,
        out_shape=jax.ShapeDtypeStruct((members, rows, width), jnp.bfloat16),
        in_specs=[pl.BlockSpec(memory_space=pltpu.SMEM)] * 2 + [anywhere] * (1 + len(pieces) + len(after)),
        out_specs=anywhere,
        scratch_shapes=[
            pltpu.VMEM((members, rows, width), jnp.bfloat16),
            pltpu.VMEM((members, rows, width), jnp.bfloat16),
            pltpu.VMEM((stored, 2, rows, width), jnp.bfloat16),
            *[pltpu.VMEM((BPF * BLK, keys), jnp.float32)] * 2,
            *[pltpu.VMEM((BPF * BLK, keys), jnp.bfloat16)] * 2,
            pltpu.SemaphoreType.DMA((heads, 1 + len(pieces))),
            pltpu.SemaphoreType.DMA((heads,)),
        ],
        compiler_params=pltpu.CompilerParams(vmem_limit_bytes=VMEM_LIMIT),
        cost_estimate=pl.CostEstimate(
            flops=6 * frames * BPF * heads * 2 * REACH * 4 * BLK * BLK * HD, bytes_accessed=1024, transcendentals=0
        ),
    )(places, masks, queries, *pieces, *after)


def on_device(outer, inner, q_proj, k_proj, v_proj, kv_list):
    frames = inner
    rows, model_width = q_proj.shape
    team = ("inner", "rep", "uly")
    team_size = frames * BPF * BLK // rows
    heads_here = model_width // HD // team_size
    pieces_of = BLK // rows
    per_frame = BPF * pieces_of
    my_group = lax.axis_index("outer")

    def rows_of(reader_frame, count):
        start = jnp.clip(reader_frame * BPF, 0, kv_list.shape[0] - count * BPF)
        return lax.dynamic_slice_in_dim(kv_list, start, count * BPF, 0)

    lists = rows_of(my_group * frames, frames).reshape(frames, BPF, 1, -1)
    shape = (frames, 1, 2 * REACH, 1)
    steps = lax.broadcasted_iota(jnp.int32, shape, 2)
    relative = lax.broadcasted_iota(jnp.int32, shape, 0) + steps - REACH + jnp.where(steps >= REACH, 1, 0)
    first_ids = BPF * (my_group * frames + relative)
    hits = jnp.where(lists == first_ids, 1, 0) + jnp.where(lists == first_ids + 1, 2, 0)
    codes = jnp.sum(jnp.where(lists >= 0, hits, 0), axis=-1)
    masks = jnp.where(codes > 0, 0.0, very_low).astype(jnp.float32).reshape(-1)
    relative = relative.reshape(frames, 2 * REACH)
    picks = jnp.where(relative == frames - 1 + REACH, 0, jnp.max(codes, axis=1) // 2)
    places = pieces_of * jnp.maximum(BPF * (relative + REACH) - 1 + picks, 0)
    places = jnp.where(relative == -REACH, 0, places).reshape(-1)

    def picked(reader_frame, holder_frame):
        return jnp.any(rows_of(reader_frame, 1) == holder_frame * BPF + 1).astype(jnp.int32)

    assert sum(CHUNKS) == heads_here
    widths = [heads * HD for heads in CHUNKS]
    lows = [sum(CHUNKS[:c]) for c in range(len(CHUNKS))]
    starts = [low * team_size * HD for low in lows]

    def exchange(array):
        return lax.all_to_all(array, team, split_axis=0, concat_axis=0, tiled=True)

    def shifted(array, heading):
        route = [(i, i + heading) for i in range(outer) if 0 <= i + heading < outer]
        return lax.ppermute(array, "outer", route)

    hops = []
    for hop in range(1, -(-REACH // frames) + 1):
        spare = hop * frames - REACH
        hops.append((frames - max(0, spare), spare >= 0))

    def forwarded(held, held_frames, keep, single, after):
        whole = (keep - 1 if single else keep) * per_frame
        if single:
            from_left, from_right = (my_group + 1) * frames, my_group * frames - 1
            edges = held[0].shape[0] - whole - per_frame, whole
            edge_places = jnp.stack(
                [
                    edges[0] + pieces_of * picked(from_left, from_left - REACH),
                    edges[1] + pieces_of * picked(from_right, from_right + REACH),
                ]
            )
            return list(select(held, edge_places, pieces_of, whole, after))
        if keep < held_frames:
            return [held[0][held[0].shape[0] - whole :], held[1][:whole]]
        return held

    def first_hop(own):
        assert hops[0] == (frames, False)
        return [[shifted(own, 1), shifted(own, -1)]]

    def selected(arrivals, after=()):
        for hop in range(1, len(hops)):
            to_send = forwarded(arrivals[-1], hops[hop - 1][0], *hops[hop], after if hop == len(hops) - 1 else ())
            if hop < len(hops) - 1:
                arrivals.append([shifted(to_send[0], 1), shifted(to_send[1], -1)])
        return to_send

    def last_hop(arrivals, to_send):
        arrivals.append([shifted(to_send[0], 1), shifted(to_send[1], -1)])

    chunks = range(len(CHUNKS))
    owned, arrivals, sent, results, outs = [], [], [], [], []

    def attend_chunk(c, after):
        order = [a[0] for a in arrivals[c][::-1]] + [owned[c]] + [a[1] for a in arrivals[c]]
        results.append(attend(places, masks, queries, order, frames, lows[c], after=after))
        result = results[c]
        if outs:
            result, outs[-1] = lax.optimization_barrier((result, outs[-1]))
        outs.append(exchange(result))

    for c in chunks:
        packed = pack([k_proj, v_proj], [starts[c]], [widths[c]], team_size, after=sent[c - 2] if c >= 2 else ())
        if c == len(CHUNKS) - 1:
            queries = exchange(pack([q_proj], starts, widths, team_size, after=[packed]))
        owned.append(exchange(packed))
        arrivals.append(first_hop(owned[c]))
        sent.append(selected(arrivals[c], after=sent[-1] if sent else ()))
        last_hop(arrivals[c], sent[c])
    for c in chunks:
        attend_chunk(c, after=results[-1:] + (sent[c + 1] if c + 1 < len(CHUNKS) else []))
    return unpack(outs, starts, model_width)


def solution(mesh):
    sizes = dict(mesh.shape)
    members = sizes["uly"] * sizes["rep"]
    heads = 40
    inner = max(
        i for i in range(1, sizes["ctx"] + 1) if sizes["ctx"] % i == 0 and heads % (i * members) == 0
    )
    outer = sizes["ctx"] // inner
    finer = Mesh(
        mesh.devices.reshape(sizes["groups"], outer, inner, sizes["uly"], sizes["rep"]),
        ("groups", "outer", "inner", "uly", "rep"),
    )
    split = P(("groups", "outer", "inner", "rep", "uly"), None)
    return jax.shard_map(
        functools.partial(on_device, outer, inner),
        mesh=finer,
        in_specs=(split, split, split, P("groups", None)),
        out_specs=split,
        check_vma=False,
    )
```

```python
import functools
import math

import jax
import jax.numpy as jnp
from jax import lax
from jax.experimental import pallas as pl
from jax.experimental.pallas import tpu as pltpu
from jax.sharding import Mesh, PartitionSpec as P

HD = 128
BLK = 128
BPF = 2
REACH = 7
CHUNKS = (3, 2)
VMEM_LIMIT = 60 * 1024 * 1024
little = dict(flops=1024, bytes_accessed=1024, transcendentals=0)

ROWS = 16

very_low = -1e30
to_log2 = math.log2(math.e) * HD ** -0.5


def staged_copies(steps, sems, turned=()):
    count = len(steps)
    fetches = [pltpu.make_async_copy(s, stage, sems.at[i]) for i, (s, stage, t) in enumerate(steps)]
    puts = [pltpu.make_async_copy(stage, t, sems.at[count + i]) for i, (s, stage, t) in enumerate(steps)]
    for fetch in fetches:
        fetch.start()
    for number, (fetch, put) in enumerate(zip(fetches, puts)):
        fetch.wait()
        if number in turned:
            stage = steps[number][1]
            for low in range(0, stage.shape[1], HD):
                stage[:, low : low + HD] = jnp.transpose(stage[:, low : low + HD])
        put.start()
    for put in puts:
        put.wait()


anywhere = pl.BlockSpec(memory_space=pl.ANY)


def copy_call(plan, shapes, count, operands, scalars=(), after=(), turned=()):
    def body(*refs):
        first = len(scalars)
        last = first + len(operands)
        results = refs[last + len(after) :]
        n = len(shapes)
        steps = plan(refs[:first], refs[first:last], results[:n], results[n : 2 * n])
        staged_copies(steps, results[2 * n], turned)

    return pl.pallas_call(
        body,
        out_shape=shapes,
        in_specs=[pl.BlockSpec(memory_space=pltpu.SMEM)] * len(scalars) + [anywhere] * (len(operands) + len(after)),
        out_specs=[anywhere] * len(shapes),
        scratch_shapes=[pltpu.VMEM(s.shape, s.dtype) for s in shapes] + [pltpu.SemaphoreType.DMA((2 * count,))],
        compiler_params=pltpu.CompilerParams(vmem_limit_bytes=VMEM_LIMIT),
        cost_estimate=pl.CostEstimate(**little),
    )(*scalars, *operands, *after)


def pack(arrays, starts, widths, team_size, after=(), turn_first=False):
    rows = arrays[0].shape[0]

    def plan(scalars, sources, outs, stages):
        steps = []
        for member in range(team_size):
            for kind, source in enumerate(sources):
                low = 0
                for start, width in zip(starts, widths):
                    place = (member, kind, slice(None), pl.ds(low, width))
                    columns = pl.ds(start + member * width, width)
                    steps.append((source.at[:, columns], stages[0].at[place], outs[0].at[place]))
                    low += width
        return steps

    shape = jax.ShapeDtypeStruct((team_size, len(arrays), rows, sum(widths)), jnp.bfloat16)
    count = team_size * len(arrays) * len(starts)
    turned = range(0, count, len(arrays)) if turn_first else ()
    return copy_call(plan, [shape], count, arrays, after=after, turned=turned)[0]


def unpack(parts, starts, model_width):
    def plan(scalars, sources, outs, stages):
        steps = []
        for start, source in zip(starts, sources):
            for member in range(source.shape[0]):
                columns = pl.ds(start + member * source.shape[2], source.shape[2])
                steps.append((source.at[member], stages[0].at[:, columns], outs[0].at[:, columns]))
        return steps

    shape = jax.ShapeDtypeStruct((parts[0].shape[1], model_width), jnp.bfloat16)
    return copy_call(plan, [shape], sum(part.shape[0] for part in parts), parts)[0]


def select(held, places, count, whole, after=()):
    def plan(scalars, sources, outs, stages):
        (place_ref,) = scalars
        steps = []
        for side, (source, stage, out) in enumerate(zip(sources, stages, outs)):
            one = pl.ds(0 if side == 0 else whole, count)
            steps.append((source.at[pl.ds(place_ref[side], count)], stage.at[one], out.at[one]))
            if whole > 0:
                rest = pl.ds(count if side == 0 else 0, whole)
                kept = pl.ds(source.shape[0] - whole if side == 0 else 0, whole)
                steps.append((source.at[kept], stage.at[rest], out.at[rest]))
        return steps

    shapes = [jax.ShapeDtypeStruct((count + whole,) + array.shape[1:], array.dtype) for array in held]
    return copy_call(plan, shapes, 2 * (2 if whole > 0 else 1), held, scalars=[places], after=after)


def columns_of(head):
    return pl.ds(pl.multiple_of(head * HD, HD), HD)


def flat(rows):
    return rows.reshape(rows.shape[0] * rows.shape[1], HD)


def attend_kernel(frames, pieces_of, heads, first_head, place_ref, mask_ref, q_hbm, *refs):
    *piece_refs, out_hbm, q_ref, out_ref, store, scores_a, scores_b, weights_a, weights_b, totals_a, totals_b, sems, put_sems = refs
    per_frame = BPF * pieces_of
    width = 2 * REACH
    items = frames * heads
    slots = [(scores_a, weights_a, totals_a), (scores_b, weights_b, totals_b)]

    def fetches(head):
        columns = columns_of(head)
        found = [(q_hbm.at[:, 0, :, columns_of(head + first_head)], q_ref.at[:, :, columns])]
        start = 0
        for piece in piece_refs:
            size = piece.shape[0]
            found.append((piece.at[:, :, :, columns], store.at[pl.ds(start, size), :, :, columns]))
            start += size
        return [pltpu.make_async_copy(a, b, sems.at[head, i]) for i, (a, b) in enumerate(found)]

    def put(head):
        columns = columns_of(head)
        return pltpu.make_async_copy(out_ref.at[:, :, columns], out_hbm.at[:, :, columns], put_sems.at[head])

    turned = pieces_of == 1

    def keys_or_values(kind, frame, columns):
        own = ((frame + REACH) * BPF - 1) * pieces_of
        places = [own, own + pieces_of] + [place_ref[frame * width + j] for j in range(width)]
        blocks = [flat(store[pl.ds(place, pieces_of), kind, :, columns]) for place in places]
        axis = 1 if turned and kind == 0 else 0
        return [jnp.concatenate(blocks[first : first + 2], axis=axis) for first in range(0, len(blocks), 2)]

    def score(item, scores_ref):
        head = item // frames
        frame = item - head * frames
        columns = columns_of(head)
        queries = flat(q_ref[pl.ds(frame * per_frame, per_frame), :, columns])
        for pair, keys in enumerate(keys_or_values(0, frame, columns)):
            if turned:
                scores = jnp.dot(queries, keys, preferred_element_type=jnp.float32)
            else:
                scores = lax.dot_general(queries, keys, (((1,), (1,)), ((), ())), preferred_element_type=jnp.float32)
            for side in range(2):
                for b in range(BPF):
                    tile = scores[b * BLK : (b + 1) * BLK, side * BLK : (side + 1) * BLK]
                    if pair > 0:
                        tile = tile + mask_ref[(frame * BPF + b) * width + 2 * (pair - 1) + side]
                    scores_ref[b * BLK : (b + 1) * BLK, (2 * pair + side) * BLK : (2 * pair + side + 1) * BLK] = tile

    def soften(scores_ref, weights_ref, totals_ref):
        for low in range(0, BPF * BLK, ROWS):
            rows = slice(low, low + ROWS)
            tiles = [scores_ref[rows, j * BLK : (j + 1) * BLK] for j in range(BPF + width)]
            top = jnp.max(functools.reduce(jnp.maximum, tiles), axis=1, keepdims=True)
            total = None
            for j in range(BPF + width):
                exps = jnp.exp2((scores_ref[rows, j * BLK : (j + 1) * BLK] - top) * to_log2)
                total = exps if total is None else total + exps
                weights_ref[rows, j * BLK : (j + 1) * BLK] = exps.astype(jnp.bfloat16)
            totals_ref[rows, :] = jnp.broadcast_to(jnp.sum(total, axis=1, keepdims=True), (ROWS, HD))

    def product(item, weights_ref, totals_ref):
        head = item // frames
        frame = item - head * frames
        columns = columns_of(head)
        values = jnp.concatenate(keys_or_values(1, frame, columns), axis=0)
        mixed = jnp.dot(weights_ref[...], values, preferred_element_type=jnp.float32)
        result = (mixed / totals_ref[...]).astype(jnp.bfloat16)
        out_ref[pl.ds(frame * per_frame, per_frame), :, columns] = result.reshape(per_frame, BLK // pieces_of, HD)

    for head in range(heads):
        for fetch in fetches(head):
            fetch.start()
    for fetch in fetches(0):
        fetch.wait()
    weights_b[...] = jnp.zeros_like(weights_b)
    totals_b[...] = jnp.ones_like(totals_b)
    score(0, scores_a)

    def stages(item, here, there):
        after = jnp.minimum(item + 1, items - 1)

        @pl.when((after % frames == 0) & (after > item))
        def _():
            for fetch in fetches(after // frames):
                fetch.wait()

        score(after, there[0])
        soften(*here)
        product(jnp.maximum(item - 1, 0), *there[1:])

    def step(index, carry):
        stages(2 * index, slots[0], slots[1])
        stages(2 * index + 1, slots[1], slots[0])
        return carry

    lax.fori_loop(0, items // 2, step, 0)
    if items % 2 == 1:
        stages(items - 1, slots[0], slots[1])
    product(items - 1, *slots[(items - 1) % 2][1:])
    for head in range(heads):
        put(head).start()
    for head in range(heads):
        put(head).wait()


def attend(places, masks, queries, pieces, frames, first_head, after=()):
    members, _, rows, _ = queries.shape
    pieces_of = BLK // rows
    width = pieces[0].shape[3]
    heads = width // HD
    stored = sum(piece.shape[0] for piece in pieces)
    keys = (2 * REACH + BPF) * BLK

    def body(place_ref, mask_ref, q_hbm, *refs):
        kept = refs[: len(pieces)] + refs[len(pieces) + len(after) :]
        attend_kernel(frames, pieces_of, heads, first_head, place_ref, mask_ref, q_hbm, *kept)

    return pl.pallas_call(
        body,
        out_shape=jax.ShapeDtypeStruct((members, rows, width), jnp.bfloat16),
        in_specs=[pl.BlockSpec(memory_space=pltpu.SMEM)] * 2 + [anywhere] * (1 + len(pieces) + len(after)),
        out_specs=anywhere,
        scratch_shapes=[
            pltpu.VMEM((members, rows, width), jnp.bfloat16),
            pltpu.VMEM((members, rows, width), jnp.bfloat16),
            pltpu.VMEM((stored, 2, rows, width), jnp.bfloat16),
            *[pltpu.VMEM((BPF * BLK, keys), jnp.float32)] * 2,
            *[pltpu.VMEM((BPF * BLK, keys), jnp.bfloat16)] * 2,
            *[pltpu.VMEM((BPF * BLK, HD), jnp.float32)] * 2,
            pltpu.SemaphoreType.DMA((heads, 1 + len(pieces))),
            pltpu.SemaphoreType.DMA((heads,)),
        ],
        compiler_params=pltpu.CompilerParams(vmem_limit_bytes=VMEM_LIMIT),
        cost_estimate=pl.CostEstimate(
            flops=6 * frames * BPF * heads * 2 * REACH * 4 * BLK * BLK * HD, bytes_accessed=1024, transcendentals=0
        ),
    )(places, masks, queries, *pieces, *after)


def on_device(outer, inner, q_proj, k_proj, v_proj, kv_list):
    frames = inner
    rows, model_width = q_proj.shape
    team = ("inner", "rep", "uly")
    team_size = frames * BPF * BLK // rows
    heads_here = model_width // HD // team_size
    pieces_of = BLK // rows
    per_frame = BPF * pieces_of
    my_group = lax.axis_index("outer")

    def rows_of(reader_frame, count):
        start = jnp.clip(reader_frame * BPF, 0, kv_list.shape[0] - count * BPF)
        return lax.dynamic_slice_in_dim(kv_list, start, count * BPF, 0)

    lists = rows_of(my_group * frames, frames).reshape(frames, BPF, 1, -1)
    shape = (frames, 1, 2 * REACH, 1)
    steps = lax.broadcasted_iota(jnp.int32, shape, 2)
    relative = lax.broadcasted_iota(jnp.int32, shape, 0) + steps - REACH + jnp.where(steps >= REACH, 1, 0)
    first_ids = BPF * (my_group * frames + relative)
    hits = jnp.where(lists == first_ids, 1, 0) + jnp.where(lists == first_ids + 1, 2, 0)
    codes = jnp.sum(jnp.where(lists >= 0, hits, 0), axis=-1)
    masks = jnp.where(codes > 0, 0.0, very_low).astype(jnp.float32).reshape(-1)
    relative = relative.reshape(frames, 2 * REACH)
    picks = jnp.where(relative == frames - 1 + REACH, 0, jnp.max(codes, axis=1) // 2)
    places = pieces_of * jnp.maximum(BPF * (relative + REACH) - 1 + picks, 0)
    places = jnp.where(relative == -REACH, 0, places).reshape(-1)

    def picked(reader_frame, holder_frame):
        return jnp.any(rows_of(reader_frame, 1) == holder_frame * BPF + 1).astype(jnp.int32)

    assert sum(CHUNKS) == heads_here
    widths = [heads * HD for heads in CHUNKS]
    lows = [sum(CHUNKS[:c]) for c in range(len(CHUNKS))]
    starts = [low * team_size * HD for low in lows]

    def exchange(array):
        return lax.all_to_all(array, team, split_axis=0, concat_axis=0, tiled=True)

    def shifted(array, heading):
        route = [(i, i + heading) for i in range(outer) if 0 <= i + heading < outer]
        return lax.ppermute(array, "outer", route)

    hops = []
    for hop in range(1, -(-REACH // frames) + 1):
        spare = hop * frames - REACH
        hops.append((frames - max(0, spare), spare >= 0))

    def forwarded(held, held_frames, keep, single, after):
        whole = (keep - 1 if single else keep) * per_frame
        if single:
            from_left, from_right = (my_group + 1) * frames, my_group * frames - 1
            edges = held[0].shape[0] - whole - per_frame, whole
            edge_places = jnp.stack(
                [
                    edges[0] + pieces_of * picked(from_left, from_left - REACH),
                    edges[1] + pieces_of * picked(from_right, from_right + REACH),
                ]
            )
            return list(select(held, edge_places, pieces_of, whole, after))
        if keep < held_frames:
            return [held[0][held[0].shape[0] - whole :], held[1][:whole]]
        return held

    def first_hop(own):
        assert hops[0] == (frames, False)
        return [[shifted(own, 1), shifted(own, -1)]]

    def selected(arrivals, after=()):
        for hop in range(1, len(hops)):
            to_send = forwarded(arrivals[-1], hops[hop - 1][0], *hops[hop], after if hop == len(hops) - 1 else ())
            if hop < len(hops) - 1:
                arrivals.append([shifted(to_send[0], 1), shifted(to_send[1], -1)])
        return to_send

    def last_hop(arrivals, to_send):
        arrivals.append([shifted(to_send[0], 1), shifted(to_send[1], -1)])

    chunks = range(len(CHUNKS))
    owned, arrivals, sent, results, outs = [], [], [], [], []

    def attend_chunk(c, after):
        order = [a[0] for a in arrivals[c][::-1]] + [owned[c]] + [a[1] for a in arrivals[c]]
        results.append(attend(places, masks, queries, order, frames, lows[c], after=after))
        result = results[c]
        if outs:
            result, outs[-1] = lax.optimization_barrier((result, outs[-1]))
        outs.append(exchange(result))

    for c in chunks:
        after = sent[c - 2] if c >= 2 else ()
        packed = pack([k_proj, v_proj], [starts[c]], [widths[c]], team_size, after, turn_first=rows == BLK)
        if c == len(CHUNKS) - 1:
            queries = exchange(pack([q_proj], starts, widths, team_size, after=[packed]))
        owned.append(exchange(packed))
        arrivals.append(first_hop(owned[c]))
        sent.append(selected(arrivals[c], after=sent[-1] if sent else ()))
        last_hop(arrivals[c], sent[c])
    for c in chunks:
        attend_chunk(c, after=results[-1:] + (sent[c + 1] if c + 1 < len(CHUNKS) else []))
    return unpack(outs, starts, model_width)


def solution(mesh):
    sizes = dict(mesh.shape)
    members = sizes["uly"] * sizes["rep"]
    heads = 40
    inner = max(
        i for i in range(1, sizes["ctx"] + 1) if sizes["ctx"] % i == 0 and heads % (i * members) == 0
    )
    outer = sizes["ctx"] // inner
    finer = Mesh(
        mesh.devices.reshape(sizes["groups"], outer, inner, sizes["uly"], sizes["rep"]),
        ("groups", "outer", "inner", "uly", "rep"),
    )
    split = P(("groups", "outer", "inner", "rep", "uly"), None)
    return jax.shard_map(
        functools.partial(on_device, outer, inner),
        mesh=finer,
        in_specs=(split, split, split, P("groups", None)),
        out_specs=split,
        check_vma=False,
    )
```

```python
import functools
import math

import jax
import jax.numpy as jnp
from jax import lax
from jax.experimental import pallas as pl
from jax.experimental.pallas import tpu as pltpu
from jax.sharding import Mesh, PartitionSpec as P

HD = 128
BLK = 128
BPF = 2
REACH = 7
CHUNKS = (2, 2, 1)
VMEM_LIMIT = 60 * 1024 * 1024
little = dict(flops=1024, bytes_accessed=1024, transcendentals=0)
much = dict(flops=100_000_000_000, bytes_accessed=1024, transcendentals=0)

ROWS = 16

very_low = -1e30
to_log2 = math.log2(math.e) * HD ** -0.5


def staged_copies(steps, sems):
    count = len(steps)
    fetches = [pltpu.make_async_copy(s, stage, sems.at[i]) for i, (s, stage, t) in enumerate(steps)]
    puts = [pltpu.make_async_copy(stage, t, sems.at[count + i]) for i, (s, stage, t) in enumerate(steps)]
    for fetch in fetches:
        fetch.start()
    for fetch, put in zip(fetches, puts):
        fetch.wait()
        put.start()
    for put in puts:
        put.wait()


anywhere = pl.BlockSpec(memory_space=pl.ANY)


def copy_call(plan, shapes, count, operands, scalars=(), after=(), cost=little):
    def body(*refs):
        first = len(scalars)
        last = first + len(operands)
        results = refs[last + len(after) :]
        n = len(shapes)
        staged_copies(plan(refs[:first], refs[first:last], results[:n], results[n : 2 * n]), results[2 * n])

    return pl.pallas_call(
        body,
        out_shape=shapes,
        in_specs=[pl.BlockSpec(memory_space=pltpu.SMEM)] * len(scalars) + [anywhere] * (len(operands) + len(after)),
        out_specs=[anywhere] * len(shapes),
        scratch_shapes=[pltpu.VMEM(s.shape, s.dtype) for s in shapes] + [pltpu.SemaphoreType.DMA((2 * count,))],
        compiler_params=pltpu.CompilerParams(vmem_limit_bytes=VMEM_LIMIT),
        cost_estimate=pl.CostEstimate(**cost),
    )(*scalars, *operands, *after)


def pack(arrays, starts, widths, team_size, after=()):
    rows = arrays[0].shape[0]

    def plan(scalars, sources, outs, stages):
        steps = []
        for member in range(team_size):
            for kind, source in enumerate(sources):
                low = 0
                for start, width in zip(starts, widths):
                    place = (member, kind, slice(None), pl.ds(low, width))
                    columns = pl.ds(start + member * width, width)
                    steps.append((source.at[:, columns], stages[0].at[place], outs[0].at[place]))
                    low += width
        return steps

    shape = jax.ShapeDtypeStruct((team_size, len(arrays), rows, sum(widths)), jnp.bfloat16)
    return copy_call(plan, [shape], team_size * len(arrays) * len(starts), arrays, after=after)[0]


def unpack(parts, starts, model_width):
    def plan(scalars, sources, outs, stages):
        steps = []
        for start, source in zip(starts, sources):
            for member in range(source.shape[0]):
                columns = pl.ds(start + member * source.shape[2], source.shape[2])
                steps.append((source.at[member], stages[0].at[:, columns], outs[0].at[:, columns]))
        return steps

    shape = jax.ShapeDtypeStruct((parts[0].shape[1], model_width), jnp.bfloat16)
    return copy_call(plan, [shape], sum(part.shape[0] for part in parts), parts)[0]


def select(held, places, count, whole, after=()):
    def plan(scalars, sources, outs, stages):
        (place_ref,) = scalars
        steps = []
        for side, (source, stage, out) in enumerate(zip(sources, stages, outs)):
            one = pl.ds(0 if side == 0 else whole, count)
            steps.append((source.at[pl.ds(place_ref[side], count)], stage.at[one], out.at[one]))
            if whole > 0:
                rest = pl.ds(count if side == 0 else 0, whole)
                kept = pl.ds(source.shape[0] - whole if side == 0 else 0, whole)
                steps.append((source.at[kept], stage.at[rest], out.at[rest]))
        return steps

    shapes = [jax.ShapeDtypeStruct((count + whole,) + array.shape[1:], array.dtype) for array in held]
    return copy_call(plan, shapes, 2 * (2 if whole > 0 else 1), held, scalars=[places], after=after, cost=much)


def columns_of(head):
    return pl.ds(pl.multiple_of(head * HD, HD), HD)


def flat(rows):
    return rows.reshape(rows.shape[0] * rows.shape[1], HD)


def attend_kernel(frames, pieces_of, heads, first_head, place_ref, mask_ref, q_hbm, *refs):
    *piece_refs, out_hbm, q_ref, out_ref, store, scores_a, scores_b, weights_a, weights_b, totals_a, totals_b, sems, put_sems = refs
    per_frame = BPF * pieces_of
    width = 2 * REACH
    items = frames * heads
    slots = [(scores_a, weights_a, totals_a), (scores_b, weights_b, totals_b)]

    def fetches(head):
        columns = columns_of(head)
        found = [(q_hbm.at[:, 0, :, columns_of(head + first_head)], q_ref.at[:, :, columns])]
        start = 0
        for piece in piece_refs:
            size = piece.shape[0]
            found.append((piece.at[:, :, :, columns], store.at[pl.ds(start, size), :, :, columns]))
            start += size
        return [pltpu.make_async_copy(a, b, sems.at[head, i]) for i, (a, b) in enumerate(found)]

    def put(head):
        columns = columns_of(head)
        return pltpu.make_async_copy(out_ref.at[:, :, columns], out_hbm.at[:, :, columns], put_sems.at[head])

    def keys_or_values(kind, frame, columns):
        own = ((frame + REACH) * BPF - 1) * pieces_of
        found = [flat(store[pl.ds(own, per_frame), kind, :, columns])]
        for pair in range(REACH):
            places = [place_ref[frame * width + 2 * pair + side] for side in range(2)]
            found.append(
                jnp.concatenate([flat(store[pl.ds(place, pieces_of), kind, :, columns]) for place in places], axis=0)
            )
        return found

    def score(item, scores_ref):
        head = item // frames
        frame = item - head * frames
        columns = columns_of(head)
        queries = flat(q_ref[pl.ds(frame * per_frame, per_frame), :, columns])
        for pair, keys in enumerate(keys_or_values(0, frame, columns)):
            scores = lax.dot_general(queries, keys, (((1,), (1,)), ((), ())), preferred_element_type=jnp.float32)
            for side in range(2):
                for b in range(BPF):
                    tile = scores[b * BLK : (b + 1) * BLK, side * BLK : (side + 1) * BLK]
                    if pair > 0:
                        tile = tile + mask_ref[(frame * BPF + b) * width + 2 * (pair - 1) + side]
                    scores_ref[b * BLK : (b + 1) * BLK, (2 * pair + side) * BLK : (2 * pair + side + 1) * BLK] = tile

    def soften(scores_ref, weights_ref, totals_ref):
        for low in range(0, BPF * BLK, ROWS):
            rows = slice(low, low + ROWS)
            tiles = [scores_ref[rows, j * BLK : (j + 1) * BLK] for j in range(BPF + width)]
            top = jnp.max(functools.reduce(jnp.maximum, tiles), axis=1, keepdims=True)
            total = None
            for j in range(BPF + width):
                exps = jnp.exp2((scores_ref[rows, j * BLK : (j + 1) * BLK] - top) * to_log2)
                total = exps if total is None else total + exps
                weights_ref[rows, j * BLK : (j + 1) * BLK] = exps.astype(jnp.bfloat16)
            totals_ref[rows, :] = jnp.broadcast_to(jnp.sum(total, axis=1, keepdims=True), (ROWS, HD))

    def product(item, weights_ref, totals_ref):
        head = item // frames
        frame = item - head * frames
        columns = columns_of(head)
        values = jnp.concatenate(keys_or_values(1, frame, columns), axis=0)
        mixed = jnp.dot(weights_ref[...], values, preferred_element_type=jnp.float32)
        result = (mixed / totals_ref[...]).astype(jnp.bfloat16)
        out_ref[pl.ds(frame * per_frame, per_frame), :, columns] = result.reshape(per_frame, BLK // pieces_of, HD)

    for fetch in fetches(0):
        fetch.start()
    for fetch in fetches(0):
        fetch.wait()
    if heads > 1:
        for fetch in fetches(1):
            fetch.start()
    weights_b[...] = jnp.zeros_like(weights_b)
    totals_b[...] = jnp.ones_like(totals_b)
    score(0, scores_a)

    def stages(item, here, there):
        after = jnp.minimum(item + 1, items - 1)

        @pl.when((after % frames == 0) & (after > item))
        def _():
            for fetch in fetches(after // frames):
                fetch.wait()

        @pl.when((after % frames == 0) & (after > item) & (after // frames + 1 < heads))
        def _():
            for fetch in fetches(jnp.minimum(after // frames + 1, heads - 1)):
                fetch.start()

        score(after, there[0])
        soften(*here)
        product(jnp.maximum(item - 1, 0), *there[1:])

        @pl.when((item % frames == 0) & (item > 0))
        def _():
            put(jnp.maximum(item // frames - 1, 0)).start()

    def step(index, carry):
        stages(2 * index, slots[0], slots[1])
        stages(2 * index + 1, slots[1], slots[0])
        return carry

    lax.fori_loop(0, items // 2, step, 0)
    if items % 2 == 1:
        stages(items - 1, slots[0], slots[1])
    product(items - 1, *slots[(items - 1) % 2][1:])
    put(heads - 1).start()
    for head in range(heads):
        put(head).wait()


def attend(places, masks, queries, pieces, frames, first_head, after=()):
    members, _, rows, _ = queries.shape
    pieces_of = BLK // rows
    width = pieces[0].shape[3]
    heads = width // HD
    stored = sum(piece.shape[0] for piece in pieces)
    keys = (2 * REACH + BPF) * BLK

    def body(place_ref, mask_ref, q_hbm, *refs):
        kept = refs[: len(pieces)] + refs[len(pieces) + len(after) :]
        attend_kernel(frames, pieces_of, heads, first_head, place_ref, mask_ref, q_hbm, *kept)

    return pl.pallas_call(
        body,
        out_shape=jax.ShapeDtypeStruct((members, rows, width), jnp.bfloat16),
        in_specs=[pl.BlockSpec(memory_space=pltpu.SMEM)] * 2 + [anywhere] * (1 + len(pieces) + len(after)),
        out_specs=anywhere,
        scratch_shapes=[
            pltpu.VMEM((members, rows, width), jnp.bfloat16),
            pltpu.VMEM((members, rows, width), jnp.bfloat16),
            pltpu.VMEM((stored, 2, rows, width), jnp.bfloat16),
            *[pltpu.VMEM((BPF * BLK, keys), jnp.float32)] * 2,
            *[pltpu.VMEM((BPF * BLK, keys), jnp.bfloat16)] * 2,
            *[pltpu.VMEM((BPF * BLK, HD), jnp.float32)] * 2,
            pltpu.SemaphoreType.DMA((heads, 1 + len(pieces))),
            pltpu.SemaphoreType.DMA((heads,)),
        ],
        compiler_params=pltpu.CompilerParams(vmem_limit_bytes=VMEM_LIMIT),
        cost_estimate=pl.CostEstimate(
            flops=6 * frames * BPF * heads * 2 * REACH * 4 * BLK * BLK * HD, bytes_accessed=1024, transcendentals=0
        ),
    )(places, masks, queries, *pieces, *after)


def on_device(outer, inner, q_proj, k_proj, v_proj, kv_list):
    frames = inner
    rows, model_width = q_proj.shape
    team = ("inner", "rep", "uly")
    team_size = frames * BPF * BLK // rows
    heads_here = model_width // HD // team_size
    pieces_of = BLK // rows
    per_frame = BPF * pieces_of
    my_group = lax.axis_index("outer")

    def rows_of(reader_frame, count):
        start = jnp.clip(reader_frame * BPF, 0, kv_list.shape[0] - count * BPF)
        return lax.dynamic_slice_in_dim(kv_list, start, count * BPF, 0)

    lists = rows_of(my_group * frames, frames).reshape(frames, BPF, 1, -1)
    shape = (frames, 1, 2 * REACH, 1)
    steps = lax.broadcasted_iota(jnp.int32, shape, 2)
    relative = lax.broadcasted_iota(jnp.int32, shape, 0) + steps - REACH + jnp.where(steps >= REACH, 1, 0)
    first_ids = BPF * (my_group * frames + relative)
    hits = jnp.where(lists == first_ids, 1, 0) + jnp.where(lists == first_ids + 1, 2, 0)
    codes = jnp.sum(jnp.where(lists >= 0, hits, 0), axis=-1)
    masks = jnp.where(codes > 0, 0.0, very_low).astype(jnp.float32).reshape(-1)
    relative = relative.reshape(frames, 2 * REACH)
    picks = jnp.where(relative == frames - 1 + REACH, 0, jnp.max(codes, axis=1) // 2)
    places = pieces_of * jnp.maximum(BPF * (relative + REACH) - 1 + picks, 0)
    places = jnp.where(relative == -REACH, 0, places).reshape(-1)

    def picked(reader_frame, holder_frame):
        return jnp.any(rows_of(reader_frame, 1) == holder_frame * BPF + 1).astype(jnp.int32)

    assert sum(CHUNKS) == heads_here
    widths = [heads * HD for heads in CHUNKS]
    lows = [sum(CHUNKS[:c]) for c in range(len(CHUNKS))]
    starts = [low * team_size * HD for low in lows]

    def exchange(array):
        return lax.all_to_all(array, team, split_axis=0, concat_axis=0, tiled=True)

    def shifted(array, heading):
        route = [(i, i + heading) for i in range(outer) if 0 <= i + heading < outer]
        return lax.ppermute(array, "outer", route)

    hops = []
    for hop in range(1, -(-REACH // frames) + 1):
        spare = hop * frames - REACH
        hops.append((frames - max(0, spare), spare >= 0))

    def forwarded(held, held_frames, keep, single, after):
        whole = (keep - 1 if single else keep) * per_frame
        if single:
            from_left, from_right = (my_group + 1) * frames, my_group * frames - 1
            edges = held[0].shape[0] - whole - per_frame, whole
            edge_places = jnp.stack(
                [
                    edges[0] + pieces_of * picked(from_left, from_left - REACH),
                    edges[1] + pieces_of * picked(from_right, from_right + REACH),
                ]
            )
            return list(select(held, edge_places, pieces_of, whole, after))
        if keep < held_frames:
            return [held[0][held[0].shape[0] - whole :], held[1][:whole]]
        return held

    def first_hop(own):
        assert hops[0] == (frames, False)
        return [[shifted(own, 1), shifted(own, -1)]]

    def selected(arrivals, after=()):
        for hop in range(1, len(hops)):
            to_send = forwarded(arrivals[-1], hops[hop - 1][0], *hops[hop], after if hop == len(hops) - 1 else ())
            if hop < len(hops) - 1:
                arrivals.append([shifted(to_send[0], 1), shifted(to_send[1], -1)])
        return to_send

    def last_hop(arrivals, to_send):
        arrivals.append([shifted(to_send[0], 1), shifted(to_send[1], -1)])

    chunks = range(len(CHUNKS))
    owned, arrivals, sent, results, outs = [], [], [], [], []

    def attend_chunk(c, after):
        order = [a[0] for a in arrivals[c][::-1]] + [owned[c]] + [a[1] for a in arrivals[c]]
        results.append(attend(places, masks, queries, order, frames, lows[c], after=after))
        result = results[c]
        if outs:
            result, outs[-1] = lax.optimization_barrier((result, outs[-1]))
        outs.append(exchange(result))

    for c in chunks:
        packed = pack([k_proj, v_proj], [starts[c]], [widths[c]], team_size, after=sent[c - 2] if c >= 2 else ())
        owned.append(exchange(packed))
        if c == len(CHUNKS) - 1:
            queries = exchange(pack([q_proj], starts, widths, team_size, after=[packed]))
        arrivals.append(first_hop(owned[c]))
        sent.append(selected(arrivals[c], after=sent[-1] if sent else ()))
        last_hop(arrivals[c], sent[c])
    for c in chunks:
        attend_chunk(c, after=results[-1:] + (sent[c + 1] if c + 1 < len(CHUNKS) else []))
    return unpack(outs, starts, model_width)


def solution(mesh):
    sizes = dict(mesh.shape)
    members = sizes["uly"] * sizes["rep"]
    heads = 40
    inner = max(
        i for i in range(1, sizes["ctx"] + 1) if sizes["ctx"] % i == 0 and heads % (i * members) == 0
    )
    outer = sizes["ctx"] // inner
    finer = Mesh(
        mesh.devices.reshape(sizes["groups"], outer, inner, sizes["uly"], sizes["rep"]),
        ("groups", "outer", "inner", "uly", "rep"),
    )
    split = P(("groups", "outer", "inner", "rep", "uly"), None)
    return jax.shard_map(
        functools.partial(on_device, outer, inner),
        mesh=finer,
        in_specs=(split, split, split, P("groups", None)),
        out_specs=split,
        check_vma=False,
    )
```

```python
import functools
import math

import jax
import jax.numpy as jnp
from jax import lax
from jax.experimental import pallas as pl
from jax.experimental.pallas import tpu as pltpu
from jax.sharding import Mesh, PartitionSpec as P

HD = 128
BLK = 128
BPF = 2
REACH = 7
CHUNKS = (3, 2)
VMEM_LIMIT = 60 * 1024 * 1024
little = dict(flops=1024, bytes_accessed=1024, transcendentals=0)
much = dict(flops=100_000_000_000, bytes_accessed=1024, transcendentals=0)

very_low = -1e30
to_log2 = math.log2(math.e) * HD ** -0.5


def staged_copies(steps, sems):
    count = len(steps)
    fetches = [pltpu.make_async_copy(s, stage, sems.at[i]) for i, (s, stage, t) in enumerate(steps)]
    puts = [pltpu.make_async_copy(stage, t, sems.at[count + i]) for i, (s, stage, t) in enumerate(steps)]
    for fetch in fetches:
        fetch.start()
    for fetch, put in zip(fetches, puts):
        fetch.wait()
        put.start()
    for put in puts:
        put.wait()


anywhere = pl.BlockSpec(memory_space=pl.ANY)


def copy_call(plan, shapes, count, operands, scalars=(), after=(), cost=little):
    def body(*refs):
        first = len(scalars)
        last = first + len(operands)
        results = refs[last + len(after) :]
        n = len(shapes)
        staged_copies(plan(refs[:first], refs[first:last], results[:n], results[n : 2 * n]), results[2 * n])

    return pl.pallas_call(
        body,
        out_shape=shapes,
        in_specs=[pl.BlockSpec(memory_space=pltpu.SMEM)] * len(scalars) + [anywhere] * (len(operands) + len(after)),
        out_specs=[anywhere] * len(shapes),
        scratch_shapes=[pltpu.VMEM(s.shape, s.dtype) for s in shapes] + [pltpu.SemaphoreType.DMA((2 * count,))],
        compiler_params=pltpu.CompilerParams(vmem_limit_bytes=VMEM_LIMIT),
        cost_estimate=pl.CostEstimate(**cost),
    )(*scalars, *operands, *after)


def pack(arrays, starts, widths, team_size, after=()):
    rows = arrays[0].shape[0]

    def plan(scalars, sources, outs, stages):
        steps = []
        for member in range(team_size):
            for kind, source in enumerate(sources):
                low = 0
                for start, width in zip(starts, widths):
                    place = (member, kind, slice(None), pl.ds(low, width))
                    columns = pl.ds(start + member * width, width)
                    steps.append((source.at[:, columns], stages[0].at[place], outs[0].at[place]))
                    low += width
        return steps

    shape = jax.ShapeDtypeStruct((team_size, len(arrays), rows, sum(widths)), jnp.bfloat16)
    return copy_call(plan, [shape], team_size * len(arrays) * len(starts), arrays, after=after)[0]


def unpack(parts, starts, model_width):
    def plan(scalars, sources, outs, stages):
        steps = []
        for start, source in zip(starts, sources):
            for member in range(source.shape[0]):
                columns = pl.ds(start + member * source.shape[2], source.shape[2])
                steps.append((source.at[member], stages[0].at[:, columns], outs[0].at[:, columns]))
        return steps

    shape = jax.ShapeDtypeStruct((parts[0].shape[1], model_width), jnp.bfloat16)
    return copy_call(plan, [shape], sum(part.shape[0] for part in parts), parts)[0]


def select(held, places, count, whole, after=()):
    def plan(scalars, sources, outs, stages):
        (place_ref,) = scalars
        steps = []
        for side, (source, stage, out) in enumerate(zip(sources, stages, outs)):
            one = pl.ds(0 if side == 0 else whole, count)
            steps.append((source.at[pl.ds(place_ref[side], count)], stage.at[one], out.at[one]))
            if whole > 0:
                rest = pl.ds(count if side == 0 else 0, whole)
                kept = pl.ds(source.shape[0] - whole if side == 0 else 0, whole)
                steps.append((source.at[kept], stage.at[rest], out.at[rest]))
        return steps

    shapes = [jax.ShapeDtypeStruct((count + whole,) + array.shape[1:], array.dtype) for array in held]
    return copy_call(plan, shapes, 2 * (2 if whole > 0 else 1), held, scalars=[places], after=after, cost=much)


def columns_of(head):
    return pl.ds(pl.multiple_of(head * HD, HD), HD)


def flat(rows):
    return rows.reshape(rows.shape[0] * rows.shape[1], HD)


def masked_scores(queries, keys, masks):
    tiles = [[] for _ in range(BPF)]
    for first in range(0, len(keys), 2):
        some = jnp.concatenate(keys[first : first + 2], axis=0)
        scores = lax.dot_general(queries, some, (((1,), (1,)), ((), ())), preferred_element_type=jnp.float32)
        for side, mask in enumerate(masks[first : first + 2]):
            for b in range(BPF):
                tile = scores[b * BLK : (b + 1) * BLK, side * BLK : (side + 1) * BLK]
                tiles[b].append(tile if mask is None else tile + mask[b])
    return tiles


def largest(tiles):
    return jnp.max(functools.reduce(jnp.maximum, tiles), axis=1, keepdims=True)


def weighted(tiles, tops, values):
    totals, weights = [], []
    for b in range(BPF):
        exps = [jnp.exp2((tile - tops[b]) * to_log2) for tile in tiles[b]]
        totals.append(jnp.sum(functools.reduce(jnp.add, exps), axis=1, keepdims=True))
        weights.append(jnp.concatenate([e.astype(jnp.bfloat16) for e in exps], axis=1))
    mixed = jnp.dot(
        jnp.concatenate(weights, axis=0), jnp.concatenate(values, axis=0), preferred_element_type=jnp.float32
    )
    return mixed, jnp.concatenate(totals, axis=0)


def mask_of(codes):
    return [jnp.where(code > 0, 0.0, very_low).astype(jnp.float32) for code in codes]


def each_head(heads, fetches, puts, work):
    for head in range(heads):
        for fetch in fetches(head):
            fetch.start()

    def one_head(head, carry):
        for fetch in fetches(head):
            fetch.wait()
        work(head)
        for put in puts(head):
            put.start()
        return carry

    lax.fori_loop(0, heads, one_head, 0)
    for head in range(heads):
        for put in puts(head):
            put.wait()


def near_kernel(frames, near, pieces_of, heads, first_head, code_ref, q_hbm, *refs):
    *piece_refs, acc_hbm, top_hbm, total_hbm, q_ref, store, acc_ref, top_ref, total_ref, sems, put_sems = refs
    per_frame = BPF * pieces_of
    width = frames + 2 * REACH

    def fetches(head):
        columns = columns_of(head)
        found = [(q_hbm.at[:, 0, :, columns_of(head + first_head)], q_ref.at[:, :, columns])]
        start = 0
        for piece in piece_refs:
            size = piece.shape[0]
            found.append((piece.at[:, :, :, columns], store.at[pl.ds(start, size), :, :, columns]))
            start += size
        return [pltpu.make_async_copy(a, b, sems.at[head, i]) for i, (a, b) in enumerate(found)]

    def puts(head):
        pairs = [(acc_ref, acc_hbm), (top_ref, top_hbm), (total_ref, total_hbm)]
        return [pltpu.make_async_copy(a.at[head], b.at[head], put_sems.at[head, i]) for i, (a, b) in enumerate(pairs)]

    def item(frame, head):
        columns = columns_of(head)
        own = (frame + near) * BPF * pieces_of
        keys, values, masks = [], [], []
        for b in range(BPF):
            keys.append(flat(store[pl.ds(own + b * pieces_of, pieces_of), 0, :, columns]))
            values.append(flat(store[pl.ds(own + b * pieces_of, pieces_of), 1, :, columns]))
            masks.append(None)
        for other in range(frames + 2 * near - 1):
            relative = other - near
            relative = relative + jnp.where(relative >= frame, 1, 0)
            codes = [code_ref[(frame * BPF + b) * width + relative + REACH] for b in range(BPF)]
            pick = jnp.maximum(codes[0], codes[1]) // 2
            place = ((relative + near) * BPF + pick) * pieces_of
            keys.append(flat(store[pl.ds(place, pieces_of), 0, :, columns]))
            values.append(flat(store[pl.ds(place, pieces_of), 1, :, columns]))
            masks.append(mask_of(codes))
        queries = flat(q_ref[pl.ds(frame * per_frame, per_frame), :, columns])
        tiles = masked_scores(queries, keys, masks)
        tops = [largest(tiles[b]) for b in range(BPF)]
        mixed, totals = weighted(tiles, tops, values)
        acc_ref[head, frame] = mixed
        top_ref[head, frame] = jnp.broadcast_to(jnp.concatenate(tops, axis=0), mixed.shape)
        total_ref[head, frame] = jnp.broadcast_to(totals, mixed.shape)

    together = 2 if frames % 2 == 0 else 1

    def work(head):
        def step(index, carry):
            for offset in range(together):
                item(index * together + offset, head)
            return carry

        lax.fori_loop(0, frames // together, step, 0)

    each_head(heads, fetches, puts, work)


def far_kernel(frames, near, pieces_of, heads, first_head, code_ref, q_hbm, *refs):
    left_hbm, right_hbm, acc_hbm, top_hbm, total_hbm, out_hbm, *scratch = refs
    q_ref, left, right, acc_ref, top_ref, total_ref, out_ref, sems, put_sems = scratch
    per_frame = BPF * pieces_of
    width = frames + 2 * REACH

    def fetches(head):
        columns = columns_of(head)
        pairs = [
            (q_hbm.at[:, 0, :, columns_of(head + first_head)], q_ref.at[:, :, columns]),
            (left_hbm.at[:, :, :, columns], left.at[:, :, :, columns]),
            (right_hbm.at[:, :, :, columns], right.at[:, :, :, columns]),
            (acc_hbm.at[head], acc_ref.at[head]),
            (top_hbm.at[head], top_ref.at[head]),
            (total_hbm.at[head], total_ref.at[head]),
        ]
        return [pltpu.make_async_copy(a, b, sems.at[head, i]) for i, (a, b) in enumerate(pairs)]

    def puts(head):
        columns = columns_of(head)
        return [pltpu.make_async_copy(out_ref.at[:, :, columns], out_hbm.at[:, :, columns], put_sems.at[head])]

    def item(frame, head):
        columns = columns_of(head)
        keys, values, masks = [], [], []
        for relative in [*range(-REACH, -near), *range(frames + near, frames + REACH)]:
            if abs(relative - frame) > REACH:
                continue
            codes = [code_ref[(frame * BPF + b) * width + relative + REACH] for b in range(BPF)]
            pick = jnp.maximum(codes[0], codes[1]) // 2
            if relative < 0:
                piece, place = left, (0 if relative == -REACH else (relative + REACH) * BPF - 1 + pick)
            else:
                first = (relative - frames - near) * BPF
                piece, place = right, (first if relative == frames + REACH - 1 else first + pick)
            keys.append(flat(piece[pl.ds(place * pieces_of, pieces_of), 0, :, columns]))
            values.append(flat(piece[pl.ds(place * pieces_of, pieces_of), 1, :, columns]))
            masks.append(mask_of(codes))
        queries = flat(q_ref[pl.ds(frame * per_frame, per_frame), :, columns])
        tiles = masked_scores(queries, keys, masks)
        near_top = top_ref[head, frame]
        tops = [jnp.maximum(largest(tiles[b]), near_top[b * BLK : (b + 1) * BLK]) for b in range(BPF)]
        mixed, totals = weighted(tiles, tops, values)
        shrink = jnp.exp2((near_top - jnp.concatenate(tops, axis=0)) * to_log2)
        result = (acc_ref[head, frame] * shrink + mixed) / (total_ref[head, frame] * shrink + totals)
        out_ref[pl.ds(frame * per_frame, per_frame), :, columns] = result.astype(jnp.bfloat16).reshape(
            per_frame, BLK // pieces_of, HD
        )

    def work(head):
        for frame in range(frames):
            item(frame, head)

    each_head(heads, fetches, puts, work)


def attend_near(codes, queries, pieces, frames, near, first_head, after=()):
    members, _, rows, _ = queries.shape
    pieces_of = BLK // rows
    width = pieces[0].shape[3]
    heads = width // HD
    stored = sum(piece.shape[0] for piece in pieces)

    def body(code_ref, q_hbm, *refs):
        kept = refs[: len(pieces)] + refs[len(pieces) + len(after) :]
        near_kernel(frames, near, pieces_of, heads, first_head, code_ref, q_hbm, *kept)

    partial = jax.ShapeDtypeStruct((heads, frames, BPF * BLK, HD), jnp.float32)
    return pl.pallas_call(
        body,
        out_shape=[partial] * 3,
        in_specs=[pl.BlockSpec(memory_space=pltpu.SMEM)] + [anywhere] * (1 + len(pieces) + len(after)),
        out_specs=[anywhere] * 3,
        scratch_shapes=[
            pltpu.VMEM((members, rows, width), jnp.bfloat16),
            pltpu.VMEM((stored, 2, rows, width), jnp.bfloat16),
            *[pltpu.VMEM(partial.shape, jnp.float32)] * 3,
            pltpu.SemaphoreType.DMA((heads, 1 + len(pieces))),
            pltpu.SemaphoreType.DMA((heads, 3)),
        ],
        compiler_params=pltpu.CompilerParams(vmem_limit_bytes=VMEM_LIMIT),
        cost_estimate=pl.CostEstimate(
            flops=6 * frames * heads * BPF * (frames + 2 * near + 1) * 4 * BLK * BLK * HD,
            bytes_accessed=1024,
            transcendentals=0,
        ),
    )(codes, queries, *pieces, *after)


def attend_far(codes, queries, far, partials, frames, near, first_head, after=()):
    members, _, rows, _ = queries.shape
    pieces_of = BLK // rows
    width = far[0].shape[3]
    heads = width // HD

    def body(code_ref, q_hbm, *refs):
        far_kernel(frames, near, pieces_of, heads, first_head, code_ref, q_hbm, *refs[:5], *refs[5 + len(after) :])

    result = jax.ShapeDtypeStruct((members, rows, width), jnp.bfloat16)
    return pl.pallas_call(
        body,
        out_shape=result,
        in_specs=[pl.BlockSpec(memory_space=pltpu.SMEM)] + [anywhere] * (6 + len(after)),
        out_specs=anywhere,
        scratch_shapes=[
            pltpu.VMEM(result.shape, result.dtype),
            *[pltpu.VMEM(array.shape, array.dtype) for array in (*far, *partials)],
            pltpu.VMEM(result.shape, result.dtype),
            pltpu.SemaphoreType.DMA((heads, 6)),
            pltpu.SemaphoreType.DMA((heads,)),
        ],
        compiler_params=pltpu.CompilerParams(vmem_limit_bytes=VMEM_LIMIT),
        cost_estimate=pl.CostEstimate(
            flops=6 * frames * heads * BPF * 4 * 4 * BLK * BLK * HD, bytes_accessed=1024, transcendentals=0
        ),
    )(codes, queries, *far, *partials, *after)


def on_device(outer, inner, q_proj, k_proj, v_proj, kv_list):
    frames = inner
    rows, model_width = q_proj.shape
    team = ("inner", "rep", "uly")
    team_size = frames * BPF * BLK // rows
    heads_here = model_width // HD // team_size
    pieces_of = BLK // rows
    per_frame = BPF * pieces_of
    my_group = lax.axis_index("outer")

    def rows_of(reader_frame, count):
        start = jnp.clip(reader_frame * BPF, 0, kv_list.shape[0] - count * BPF)
        return lax.dynamic_slice_in_dim(kv_list, start, count * BPF, 0)

    lists = rows_of(my_group * frames, frames).reshape(frames * BPF, 1, -1)
    first_ids = BPF * (my_group * frames - REACH + lax.broadcasted_iota(jnp.int32, (1, frames + 2 * REACH, 1), 1))
    hits = jnp.where(lists == first_ids, 1, 0) + jnp.where(lists == first_ids + 1, 2, 0)
    codes = jnp.sum(jnp.where(lists >= 0, hits, 0), axis=-1).reshape(-1)

    def picked(reader_frame, holder_frame):
        return jnp.any(rows_of(reader_frame, 1) == holder_frame * BPF + 1).astype(jnp.int32)

    assert sum(CHUNKS) == heads_here
    widths = [heads * HD for heads in CHUNKS]
    lows = [sum(CHUNKS[:c]) for c in range(len(CHUNKS))]
    starts = [low * team_size * HD for low in lows]

    def exchange(array):
        return lax.all_to_all(array, team, split_axis=0, concat_axis=0, tiled=True)

    def shifted(array, heading):
        route = [(i, i + heading) for i in range(outer) if 0 <= i + heading < outer]
        return lax.ppermute(array, "outer", route)

    hops = []
    for hop in range(1, -(-REACH // frames) + 1):
        spare = hop * frames - REACH
        hops.append((frames - max(0, spare), spare >= 0))

    def forwarded(held, held_frames, keep, single, after):
        whole = (keep - 1 if single else keep) * per_frame
        if single:
            from_left, from_right = (my_group + 1) * frames, my_group * frames - 1
            edges = held[0].shape[0] - whole - per_frame, whole
            edge_places = jnp.stack(
                [
                    edges[0] + pieces_of * picked(from_left, from_left - REACH),
                    edges[1] + pieces_of * picked(from_right, from_right + REACH),
                ]
            )
            return list(select(held, edge_places, pieces_of, whole, after))
        if keep < held_frames:
            return [held[0][held[0].shape[0] - whole :], held[1][:whole]]
        return held

    def first_hop(own):
        assert hops[0] == (frames, False)
        return [[shifted(own, 1), shifted(own, -1)]]

    def selected(arrivals, after=()):
        for hop in range(1, len(hops)):
            to_send = forwarded(arrivals[-1], hops[hop - 1][0], *hops[hop], after if hop == len(hops) - 1 else ())
            if hop < len(hops) - 1:
                arrivals.append([shifted(to_send[0], 1), shifted(to_send[1], -1)])
        return to_send

    def last_hop(arrivals, to_send):
        arrivals.append([shifted(to_send[0], 1), shifted(to_send[1], -1)])

    chunks = range(len(CHUNKS))
    near = (len(hops) - 1) * frames
    packed = [pack([k_proj, v_proj], [starts[c]], [widths[c]], team_size) for c in chunks]
    owned = [exchange(array) for array in packed]
    queries = exchange(pack([q_proj], starts, widths, team_size, after=packed[-1:]))
    arrivals, partials, outs = [], [], []
    before = ()
    for c in chunks:
        arrivals.append(first_hop(owned[c]))
        sent = selected(arrivals[c], after=before)
        order = [a[0] for a in arrivals[c][::-1]] + [owned[c]] + [a[1] for a in arrivals[c]]
        last_hop(arrivals[c], sent)
        partials.append(list(attend_near(codes, queries, order, frames, near, lows[c], after=sent)))
        before = partials[c]
    for c in chunks:
        result = attend_far(codes, queries, arrivals[c][-1], partials[c], frames, near, lows[c], after=before)
        before = [result]
        if outs:
            result, outs[-1] = lax.optimization_barrier((result, outs[-1]))
        outs.append(exchange(result))
    return unpack(outs, starts, model_width)


def solution(mesh):
    sizes = dict(mesh.shape)
    members = sizes["uly"] * sizes["rep"]
    heads = 40
    inner = max(
        i for i in range(1, sizes["ctx"] + 1) if sizes["ctx"] % i == 0 and heads % (i * members) == 0
    )
    outer = sizes["ctx"] // inner
    finer = Mesh(
        mesh.devices.reshape(sizes["groups"], outer, inner, sizes["uly"], sizes["rep"]),
        ("groups", "outer", "inner", "uly", "rep"),
    )
    split = P(("groups", "outer", "inner", "rep", "uly"), None)
    return jax.shard_map(
        functools.partial(on_device, outer, inner),
        mesh=finer,
        in_specs=(split, split, split, P("groups", None)),
        out_specs=split,
        check_vma=False,
    )
```

```python
import functools
import math

import jax
import jax.numpy as jnp
from jax import lax
from jax.experimental import pallas as pl
from jax.experimental.pallas import tpu as pltpu
from jax.sharding import Mesh, PartitionSpec as P

HD = 128
BLK = 128
BPF = 2
REACH = 7
CHUNKS = (3, 2)
VMEM_LIMIT = 28 * 1024 * 1024
little = dict(flops=1024, bytes_accessed=1024, transcendentals=0)
much = dict(flops=100_000_000_000, bytes_accessed=1024, transcendentals=0)

very_low = -1e30
to_log2 = math.log2(math.e) * HD ** -0.5


def staged_copies(steps, sems):
    count = len(steps)
    fetches = [pltpu.make_async_copy(s, stage, sems.at[i]) for i, (s, stage, t) in enumerate(steps)]
    puts = [pltpu.make_async_copy(stage, t, sems.at[count + i]) for i, (s, stage, t) in enumerate(steps)]
    for fetch in fetches:
        fetch.start()
    for fetch, put in zip(fetches, puts):
        fetch.wait()
        put.start()
    for put in puts:
        put.wait()


anywhere = pl.BlockSpec(memory_space=pl.ANY)
in_hbm = pl.BlockSpec(memory_space=pltpu.HBM)


def copy_call(plan, shapes, count, operands, scalars=(), after=(), cost=little, place=anywhere):
    def body(*refs):
        first = len(scalars)
        last = first + len(operands)
        results = refs[last + len(after) :]
        n = len(shapes)
        staged_copies(plan(refs[:first], refs[first:last], results[:n], results[n : 2 * n]), results[2 * n])

    return pl.pallas_call(
        body,
        out_shape=shapes,
        in_specs=[pl.BlockSpec(memory_space=pltpu.SMEM)] * len(scalars) + [place] * (len(operands) + len(after)),
        out_specs=[place] * len(shapes),
        scratch_shapes=[pltpu.VMEM(s.shape, s.dtype) for s in shapes] + [pltpu.SemaphoreType.DMA((2 * count,))],
        compiler_params=pltpu.CompilerParams(vmem_limit_bytes=VMEM_LIMIT),
        cost_estimate=pl.CostEstimate(**cost),
    )(*scalars, *operands, *after)


def pack(arrays, starts, widths, team_size, after=()):
    rows = arrays[0].shape[0]

    def plan(scalars, sources, outs, stages):
        steps = []
        for member in range(team_size):
            for kind, source in enumerate(sources):
                low = 0
                for start, width in zip(starts, widths):
                    place = (member, kind, slice(None), pl.ds(low, width))
                    columns = pl.ds(start + member * width, width)
                    steps.append((source.at[:, columns], stages[0].at[place], outs[0].at[place]))
                    low += width
        return steps

    shape = jax.ShapeDtypeStruct((team_size, len(arrays), rows, sum(widths)), jnp.bfloat16)
    return copy_call(plan, [shape], team_size * len(arrays) * len(starts), arrays, after=after, place=in_hbm)[0]


def unpack(parts, starts, model_width):
    members, rows, _ = parts[0].shape
    count = members * len(parts)

    def body(*refs):
        *sources, out, sems = refs
        puts = []
        for start, source in zip(starts, sources):
            width = source.shape[2]
            for member in range(members):
                columns = pl.ds(start + member * width, width)
                puts.append(pltpu.make_async_copy(source.at[member], out.at[:, columns], sems.at[len(puts)]))
                puts[-1].start()
        for put in puts:
            put.wait()

    return pl.pallas_call(
        body,
        out_shape=jax.ShapeDtypeStruct((rows, model_width), jnp.bfloat16),
        in_specs=[pl.BlockSpec(memory_space=pltpu.VMEM)] * len(parts),
        out_specs=in_hbm,
        scratch_shapes=[pltpu.SemaphoreType.DMA((count,))],
        compiler_params=pltpu.CompilerParams(vmem_limit_bytes=8 * 1024 * 1024),
        cost_estimate=pl.CostEstimate(**little),
    )(*parts)


def select(held, places, count, whole, after=()):
    def plan(scalars, sources, outs, stages):
        (place_ref,) = scalars
        steps = []
        for side, (source, stage, out) in enumerate(zip(sources, stages, outs)):
            one = pl.ds(0 if side == 0 else whole, count)
            steps.append((source.at[pl.ds(place_ref[side], count)], stage.at[one], out.at[one]))
            if whole > 0:
                rest = pl.ds(count if side == 0 else 0, whole)
                kept = pl.ds(source.shape[0] - whole if side == 0 else 0, whole)
                steps.append((source.at[kept], stage.at[rest], out.at[rest]))
        return steps

    shapes = [jax.ShapeDtypeStruct((count + whole,) + array.shape[1:], array.dtype) for array in held]
    return copy_call(plan, shapes, 2 * (2 if whole > 0 else 1), held, scalars=[places], after=after, cost=much)


def columns_of(head):
    return pl.ds(pl.multiple_of(head * HD, HD), HD)


def flat(rows):
    return rows.reshape(rows.shape[0] * rows.shape[1], HD)


def masked_scores(queries, keys, masks):
    tiles = [[] for _ in range(BPF)]
    for first in range(0, len(keys), 2):
        some = jnp.concatenate(keys[first : first + 2], axis=0)
        scores = lax.dot_general(queries, some, (((1,), (1,)), ((), ())), preferred_element_type=jnp.float32)
        for side, mask in enumerate(masks[first : first + 2]):
            for b in range(BPF):
                tile = scores[b * BLK : (b + 1) * BLK, side * BLK : (side + 1) * BLK]
                tiles[b].append(tile if mask is None else tile + mask[b])
    return tiles


def largest(tiles):
    return jnp.max(functools.reduce(jnp.maximum, tiles), axis=1, keepdims=True)


def weighted(tiles, tops, values):
    totals, weights = [], []
    for b in range(BPF):
        exps = [jnp.exp2((tile - tops[b]) * to_log2) for tile in tiles[b]]
        totals.append(jnp.sum(functools.reduce(jnp.add, exps), axis=1, keepdims=True))
        weights.append(jnp.concatenate([e.astype(jnp.bfloat16) for e in exps], axis=1))
    mixed = jnp.dot(
        jnp.concatenate(weights, axis=0), jnp.concatenate(values, axis=0), preferred_element_type=jnp.float32
    )
    return mixed, jnp.concatenate(totals, axis=0)


def mask_of(codes):
    return [jnp.where(code > 0, 0.0, very_low).astype(jnp.float32) for code in codes]


def each_head(heads, fetches, puts, work):
    for head in range(heads):
        for fetch in fetches(head):
            fetch.start()

    def one_head(head, carry):
        for fetch in fetches(head):
            fetch.wait()
        work(head)
        for put in puts(head):
            put.start()
        return carry

    lax.fori_loop(0, heads, one_head, 0)
    for head in range(heads):
        for put in puts(head):
            put.wait()


def near_kernel(frames, near, pieces_of, heads, first_head, code_ref, q_hbm, *refs):
    *piece_refs, acc_hbm, top_hbm, total_hbm, q_ref, store, acc_ref, top_ref, total_ref, sems, put_sems = refs
    per_frame = BPF * pieces_of
    width = frames + 2 * REACH

    def fetches(head):
        columns = columns_of(head)
        found = [(q_hbm.at[:, 0, :, columns_of(head + first_head)], q_ref.at[:, :, columns])]
        start = 0
        for piece in piece_refs:
            size = piece.shape[0]
            found.append((piece.at[:, :, :, columns], store.at[pl.ds(start, size), :, :, columns]))
            start += size
        return [pltpu.make_async_copy(a, b, sems.at[head, i]) for i, (a, b) in enumerate(found)]

    def puts(head):
        pairs = [(acc_ref, acc_hbm), (top_ref, top_hbm), (total_ref, total_hbm)]
        return [pltpu.make_async_copy(a.at[head], b.at[head], put_sems.at[head, i]) for i, (a, b) in enumerate(pairs)]

    def item(frame, head):
        columns = columns_of(head)
        own = (frame + near) * BPF * pieces_of
        keys, values, masks = [], [], []
        for b in range(BPF):
            keys.append(flat(store[pl.ds(own + b * pieces_of, pieces_of), 0, :, columns]))
            values.append(flat(store[pl.ds(own + b * pieces_of, pieces_of), 1, :, columns]))
            masks.append(None)
        for other in range(frames + 2 * near - 1):
            relative = other - near
            relative = relative + jnp.where(relative >= frame, 1, 0)
            codes = [code_ref[(frame * BPF + b) * width + relative + REACH] for b in range(BPF)]
            pick = jnp.maximum(codes[0], codes[1]) // 2
            place = ((relative + near) * BPF + pick) * pieces_of
            keys.append(flat(store[pl.ds(place, pieces_of), 0, :, columns]))
            values.append(flat(store[pl.ds(place, pieces_of), 1, :, columns]))
            masks.append(mask_of(codes))
        queries = flat(q_ref[pl.ds(frame * per_frame, per_frame), :, columns])
        tiles = masked_scores(queries, keys, masks)
        tops = [largest(tiles[b]) for b in range(BPF)]
        mixed, totals = weighted(tiles, tops, values)
        acc_ref[head, frame] = mixed
        top_ref[head, frame] = jnp.broadcast_to(jnp.concatenate(tops, axis=0), mixed.shape)
        total_ref[head, frame] = jnp.broadcast_to(totals, mixed.shape)

    together = 2 if frames % 2 == 0 else 1

    def work(head):
        def step(index, carry):
            for offset in range(together):
                item(index * together + offset, head)
            return carry

        lax.fori_loop(0, frames // together, step, 0)

    each_head(heads, fetches, puts, work)


def far_kernel(frames, near, pieces_of, heads, first_head, code_ref, q_hbm, *refs):
    left_hbm, right_hbm, acc_hbm, top_hbm, total_hbm, out_hbm, *scratch = refs
    q_ref, left, right, acc_ref, top_ref, total_ref, out_ref, sems, put_sems = scratch
    per_frame = BPF * pieces_of
    width = frames + 2 * REACH

    def fetches(head):
        columns = columns_of(head)
        pairs = [
            (q_hbm.at[:, 0, :, columns_of(head + first_head)], q_ref.at[:, :, columns]),
            (left_hbm.at[:, :, :, columns], left.at[:, :, :, columns]),
            (right_hbm.at[:, :, :, columns], right.at[:, :, :, columns]),
            (acc_hbm.at[head], acc_ref.at[head]),
            (top_hbm.at[head], top_ref.at[head]),
            (total_hbm.at[head], total_ref.at[head]),
        ]
        return [pltpu.make_async_copy(a, b, sems.at[head, i]) for i, (a, b) in enumerate(pairs)]

    def puts(head):
        columns = columns_of(head)
        return [pltpu.make_async_copy(out_ref.at[:, :, columns], out_hbm.at[:, :, columns], put_sems.at[head])]

    def item(frame, head):
        columns = columns_of(head)
        keys, values, masks = [], [], []
        for relative in [*range(-REACH, -near), *range(frames + near, frames + REACH)]:
            if abs(relative - frame) > REACH:
                continue
            codes = [code_ref[(frame * BPF + b) * width + relative + REACH] for b in range(BPF)]
            pick = jnp.maximum(codes[0], codes[1]) // 2
            if relative < 0:
                piece, place = left, (0 if relative == -REACH else (relative + REACH) * BPF - 1 + pick)
            else:
                first = (relative - frames - near) * BPF
                piece, place = right, (first if relative == frames + REACH - 1 else first + pick)
            keys.append(flat(piece[pl.ds(place * pieces_of, pieces_of), 0, :, columns]))
            values.append(flat(piece[pl.ds(place * pieces_of, pieces_of), 1, :, columns]))
            masks.append(mask_of(codes))
        queries = flat(q_ref[pl.ds(frame * per_frame, per_frame), :, columns])
        tiles = masked_scores(queries, keys, masks)
        near_top = top_ref[head, frame]
        tops = [jnp.maximum(largest(tiles[b]), near_top[b * BLK : (b + 1) * BLK]) for b in range(BPF)]
        mixed, totals = weighted(tiles, tops, values)
        shrink = jnp.exp2((near_top - jnp.concatenate(tops, axis=0)) * to_log2)
        result = (acc_ref[head, frame] * shrink + mixed) / (total_ref[head, frame] * shrink + totals)
        out_ref[pl.ds(frame * per_frame, per_frame), :, columns] = result.astype(jnp.bfloat16).reshape(
            per_frame, BLK // pieces_of, HD
        )

    def work(head):
        for frame in range(frames):
            item(frame, head)

    each_head(heads, fetches, puts, work)


def attend_near(codes, queries, pieces, frames, near, first_head, after=()):
    members, _, rows, _ = queries.shape
    pieces_of = BLK // rows
    width = pieces[0].shape[3]
    heads = width // HD
    stored = sum(piece.shape[0] for piece in pieces)

    def body(code_ref, q_hbm, *refs):
        kept = refs[: len(pieces)] + refs[len(pieces) + len(after) :]
        near_kernel(frames, near, pieces_of, heads, first_head, code_ref, q_hbm, *kept)

    partial = jax.ShapeDtypeStruct((heads, frames, BPF * BLK, HD), jnp.float32)
    return pl.pallas_call(
        body,
        out_shape=[partial] * 3,
        in_specs=[pl.BlockSpec(memory_space=pltpu.SMEM)] + [anywhere] * (1 + len(pieces) + len(after)),
        out_specs=[anywhere] * 3,
        scratch_shapes=[
            pltpu.VMEM((members, rows, width), jnp.bfloat16),
            pltpu.VMEM((stored, 2, rows, width), jnp.bfloat16),
            *[pltpu.VMEM(partial.shape, jnp.float32)] * 3,
            pltpu.SemaphoreType.DMA((heads, 1 + len(pieces))),
            pltpu.SemaphoreType.DMA((heads, 3)),
        ],
        compiler_params=pltpu.CompilerParams(vmem_limit_bytes=VMEM_LIMIT),
        cost_estimate=pl.CostEstimate(
            flops=6 * frames * heads * BPF * (frames + 2 * near + 1) * 4 * BLK * BLK * HD,
            bytes_accessed=1024,
            transcendentals=0,
        ),
    )(codes, queries, *pieces, *after)


def attend_far(codes, queries, far, partials, frames, near, first_head, after=()):
    members, _, rows, _ = queries.shape
    pieces_of = BLK // rows
    width = far[0].shape[3]
    heads = width // HD

    def body(code_ref, q_hbm, *refs):
        far_kernel(frames, near, pieces_of, heads, first_head, code_ref, q_hbm, *refs[:5], *refs[5 + len(after) :])

    result = jax.ShapeDtypeStruct((members, rows, width), jnp.bfloat16)
    return pl.pallas_call(
        body,
        out_shape=result,
        in_specs=[pl.BlockSpec(memory_space=pltpu.SMEM)] + [anywhere] * (6 + len(after)),
        out_specs=in_hbm,
        scratch_shapes=[
            pltpu.VMEM(result.shape, result.dtype),
            *[pltpu.VMEM(array.shape, array.dtype) for array in (*far, *partials)],
            pltpu.VMEM(result.shape, result.dtype),
            pltpu.SemaphoreType.DMA((heads, 6)),
            pltpu.SemaphoreType.DMA((heads,)),
        ],
        compiler_params=pltpu.CompilerParams(vmem_limit_bytes=VMEM_LIMIT),
        cost_estimate=pl.CostEstimate(
            flops=6 * frames * heads * BPF * 4 * 4 * BLK * BLK * HD, bytes_accessed=1024, transcendentals=0
        ),
    )(codes, queries, *far, *partials, *after)


def on_device(outer, inner, q_proj, k_proj, v_proj, kv_list):
    frames = inner
    rows, model_width = q_proj.shape
    team = ("inner", "rep", "uly")
    team_size = frames * BPF * BLK // rows
    heads_here = model_width // HD // team_size
    pieces_of = BLK // rows
    per_frame = BPF * pieces_of
    my_group = lax.axis_index("outer")

    def rows_of(reader_frame, count):
        start = jnp.clip(reader_frame * BPF, 0, kv_list.shape[0] - count * BPF)
        return lax.dynamic_slice_in_dim(kv_list, start, count * BPF, 0)

    lists = rows_of(my_group * frames, frames).reshape(frames * BPF, 1, -1)
    first_ids = BPF * (my_group * frames - REACH + lax.broadcasted_iota(jnp.int32, (1, frames + 2 * REACH, 1), 1))
    hits = jnp.where(lists == first_ids, 1, 0) + jnp.where(lists == first_ids + 1, 2, 0)
    codes = jnp.sum(jnp.where(lists >= 0, hits, 0), axis=-1).reshape(-1)

    def picked(reader_frame, holder_frame):
        return jnp.any(rows_of(reader_frame, 1) == holder_frame * BPF + 1).astype(jnp.int32)

    assert sum(CHUNKS) == heads_here
    widths = [heads * HD for heads in CHUNKS]
    lows = [sum(CHUNKS[:c]) for c in range(len(CHUNKS))]
    starts = [low * team_size * HD for low in lows]

    def exchange(array):
        return lax.all_to_all(array, team, split_axis=0, concat_axis=0, tiled=True)

    def shifted(array, heading, hop):
        places = range(outer)
        route = [(i, i + heading) for i in places if i + heading in places and i - (hop - 1) * heading in places]
        return lax.ppermute(array, "outer", route)

    hops = []
    for hop in range(1, -(-REACH // frames) + 1):
        spare = hop * frames - REACH
        hops.append((frames - max(0, spare), spare >= 0))

    def forwarded(held, held_frames, keep, single, after):
        whole = (keep - 1 if single else keep) * per_frame
        if single:
            from_left, from_right = (my_group + 1) * frames, my_group * frames - 1
            edges = held[0].shape[0] - whole - per_frame, whole
            edge_places = jnp.stack(
                [
                    edges[0] + pieces_of * picked(from_left, from_left - REACH),
                    edges[1] + pieces_of * picked(from_right, from_right + REACH),
                ]
            )
            return list(select(held, edge_places, pieces_of, whole, after))
        if keep < held_frames:
            return [held[0][held[0].shape[0] - whole :], held[1][:whole]]
        return held

    def first_hop(own):
        assert hops[0] == (frames, False)
        return [[shifted(own, 1, 1), shifted(own, -1, 1)]]

    def selected(arrivals, after=()):
        for hop in range(1, len(hops)):
            to_send = forwarded(arrivals[-1], hops[hop - 1][0], *hops[hop], after if hop == len(hops) - 1 else ())
            if hop < len(hops) - 1:
                arrivals.append([shifted(to_send[0], 1, hop + 1), shifted(to_send[1], -1, hop + 1)])
        return to_send

    def last_hop(arrivals, to_send):
        arrivals.append([shifted(to_send[0], 1, len(hops)), shifted(to_send[1], -1, len(hops))])

    chunks = range(len(CHUNKS))
    near = (len(hops) - 1) * frames
    packed = [pack([k_proj, v_proj], [starts[c]], [widths[c]], team_size) for c in chunks]
    owned = [exchange(array) for array in packed]
    queries = exchange(pack([q_proj], starts, widths, team_size, after=packed[-1:]))
    arrivals, partials, outs = [], [], []
    before = ()
    for c in chunks:
        arrivals.append(first_hop(owned[c]))
        sent = selected(arrivals[c], after=before)
        order = [a[0] for a in arrivals[c][::-1]] + [owned[c]] + [a[1] for a in arrivals[c]]
        last_hop(arrivals[c], sent)
        partials.append(list(attend_near(codes, queries, order, frames, near, lows[c], after=sent)))
        before = partials[c]
    for c in chunks:
        result = attend_far(codes, queries, arrivals[c][-1], partials[c], frames, near, lows[c], after=before)
        before = [result]
        if outs:
            result, outs[-1] = lax.optimization_barrier((result, outs[-1]))
        outs.append(exchange(result))
    return unpack(outs, starts, model_width)


def solution(mesh):
    sizes = dict(mesh.shape)
    members = sizes["uly"] * sizes["rep"]
    heads = 40
    inner = max(
        i for i in range(1, sizes["ctx"] + 1) if sizes["ctx"] % i == 0 and heads % (i * members) == 0
    )
    outer = sizes["ctx"] // inner
    finer = Mesh(
        mesh.devices.reshape(sizes["groups"], outer, inner, sizes["uly"], sizes["rep"]),
        ("groups", "outer", "inner", "uly", "rep"),
    )
    split = P(("groups", "outer", "inner", "rep", "uly"), None)
    return jax.shard_map(
        functools.partial(on_device, outer, inner),
        mesh=finer,
        in_specs=(split, split, split, P("groups", None)),
        out_specs=split,
        check_vma=False,
    )
```

```python
import functools
import math

import jax
import jax.numpy as jnp
from jax import lax
from jax.experimental import pallas as pl
from jax.experimental.pallas import tpu as pltpu
from jax.sharding import Mesh, PartitionSpec as P

HD = 128
BLK = 128
BPF = 2
REACH = 7
CHUNKS = (2, 3)
VMEM_LIMIT = 60 * 1024 * 1024
NEAR_VMEM_LIMIT = 28 * 1024 * 1024
little = dict(flops=1024, bytes_accessed=1024, transcendentals=0)
some = dict(flops=20_000_000_000, bytes_accessed=1024, transcendentals=0)
much = dict(flops=100_000_000_000, bytes_accessed=1024, transcendentals=0)

very_low = -1e30
to_log2 = math.log2(math.e) * HD ** -0.5


def staged_copies(steps, sems):
    count = len(steps)
    fetches = [pltpu.make_async_copy(s, stage, sems.at[i]) for i, (s, stage, t) in enumerate(steps)]
    puts = [pltpu.make_async_copy(stage, t, sems.at[count + i]) for i, (s, stage, t) in enumerate(steps)]
    for fetch in fetches:
        fetch.start()
    for fetch, put in zip(fetches, puts):
        fetch.wait()
        put.start()
    for put in puts:
        put.wait()


anywhere = pl.BlockSpec(memory_space=pl.ANY)
in_hbm = pl.BlockSpec(memory_space=pltpu.HBM)


def copy_call(plan, shapes, count, operands, scalars=(), after=(), cost=little):
    def body(*refs):
        first = len(scalars)
        last = first + len(operands)
        results = refs[last + len(after) :]
        n = len(shapes)
        staged_copies(plan(refs[:first], refs[first:last], results[:n], results[n : 2 * n]), results[2 * n])

    return pl.pallas_call(
        body,
        out_shape=shapes,
        in_specs=[pl.BlockSpec(memory_space=pltpu.SMEM)] * len(scalars) + [anywhere] * (len(operands) + len(after)),
        out_specs=[anywhere] * len(shapes),
        scratch_shapes=[pltpu.VMEM(s.shape, s.dtype) for s in shapes] + [pltpu.SemaphoreType.DMA((2 * count,))],
        compiler_params=pltpu.CompilerParams(vmem_limit_bytes=VMEM_LIMIT),
        cost_estimate=pl.CostEstimate(**cost),
    )(*scalars, *operands, *after)


def pack(arrays, starts, widths, team_size, after=()):
    rows = arrays[0].shape[0]

    def plan(scalars, sources, outs, stages):
        steps = []
        for member in range(team_size):
            for kind, source in enumerate(sources):
                low = 0
                for start, width in zip(starts, widths):
                    place = (member, kind, slice(None), pl.ds(low, width))
                    columns = pl.ds(start + member * width, width)
                    steps.append((source.at[:, columns], stages[0].at[place], outs[0].at[place]))
                    low += width
        return steps

    shape = jax.ShapeDtypeStruct((team_size, len(arrays), rows, sum(widths)), jnp.bfloat16)
    return copy_call(plan, [shape], team_size * len(arrays) * len(starts), arrays, after=after, cost=some)[0]


def unpack(parts, starts, model_width):
    members, rows, _ = parts[0].shape
    count = members * len(parts)

    def body(*refs):
        *sources, out, sems = refs
        puts = []
        for start, source in zip(starts, sources):
            width = source.shape[2]
            for member in range(members):
                columns = pl.ds(start + member * width, width)
                puts.append(pltpu.make_async_copy(source.at[member], out.at[:, columns], sems.at[len(puts)]))
                puts[-1].start()
        for put in puts:
            put.wait()

    return pl.pallas_call(
        body,
        out_shape=jax.ShapeDtypeStruct((rows, model_width), jnp.bfloat16),
        in_specs=[pl.BlockSpec(memory_space=pltpu.VMEM)] * len(parts),
        out_specs=in_hbm,
        scratch_shapes=[pltpu.SemaphoreType.DMA((count,))],
        compiler_params=pltpu.CompilerParams(vmem_limit_bytes=8 * 1024 * 1024),
        cost_estimate=pl.CostEstimate(**little),
    )(*parts)


def select(held, places, count, whole, after=()):
    def plan(scalars, sources, outs, stages):
        (place_ref,) = scalars
        steps = []
        for side, (source, stage, out) in enumerate(zip(sources, stages, outs)):
            one = pl.ds(0 if side == 0 else whole, count)
            steps.append((source.at[pl.ds(place_ref[side], count)], stage.at[one], out.at[one]))
            if whole > 0:
                rest = pl.ds(count if side == 0 else 0, whole)
                kept = pl.ds(source.shape[0] - whole if side == 0 else 0, whole)
                steps.append((source.at[kept], stage.at[rest], out.at[rest]))
        return steps

    shapes = [jax.ShapeDtypeStruct((count + whole,) + array.shape[1:], array.dtype) for array in held]
    return copy_call(plan, shapes, 2 * (2 if whole > 0 else 1), held, scalars=[places], after=after, cost=much)


def columns_of(head):
    return pl.ds(pl.multiple_of(head * HD, HD), HD)


def flat(rows):
    return rows.reshape(rows.shape[0] * rows.shape[1], HD)


def masked_scores(queries, keys, masks):
    tiles = [[] for _ in range(BPF)]
    for first in range(0, len(keys), 2):
        some = jnp.concatenate(keys[first : first + 2], axis=0)
        scores = lax.dot_general(queries, some, (((1,), (1,)), ((), ())), preferred_element_type=jnp.float32)
        for side, mask in enumerate(masks[first : first + 2]):
            for b in range(BPF):
                tile = scores[b * BLK : (b + 1) * BLK, side * BLK : (side + 1) * BLK]
                tiles[b].append(tile if mask is None else tile + mask[b])
    return tiles


def largest(tiles):
    return jnp.max(functools.reduce(jnp.maximum, tiles), axis=1, keepdims=True)


def weighted(tiles, tops, values):
    totals, weights = [], []
    for b in range(BPF):
        exps = [jnp.exp2((tile - tops[b]) * to_log2) for tile in tiles[b]]
        totals.append(jnp.sum(functools.reduce(jnp.add, exps), axis=1, keepdims=True))
        weights.append(jnp.concatenate([e.astype(jnp.bfloat16) for e in exps], axis=1))
    mixed = jnp.dot(
        jnp.concatenate(weights, axis=0), jnp.concatenate(values, axis=0), preferred_element_type=jnp.float32
    )
    return mixed, jnp.concatenate(totals, axis=0)


def mask_of(codes):
    return [jnp.where(code > 0, 0.0, very_low).astype(jnp.float32) for code in codes]


def each_head(heads, fetches, puts, work):
    for head in range(heads):
        for fetch in fetches(head):
            fetch.start()

    def one_head(head, carry):
        for fetch in fetches(head):
            fetch.wait()
        work(head)
        for put in puts(head):
            put.start()
        return carry

    lax.fori_loop(0, heads, one_head, 0)
    for head in range(heads):
        for put in puts(head):
            put.wait()


def near_kernel(frames, near, pieces_of, heads, first_head, code_ref, q_hbm, *refs):
    *piece_refs, acc_hbm, top_hbm, total_hbm, q_ref, store, acc_ref, top_ref, total_ref, sems, put_sems = refs
    per_frame = BPF * pieces_of
    width = frames + 2 * REACH

    def fetches(head):
        columns = columns_of(head)
        found = [(q_hbm.at[:, 0, :, columns_of(head + first_head)], q_ref.at[:, :, columns])]
        start = 0
        for piece in piece_refs:
            size = piece.shape[0]
            found.append((piece.at[:, :, :, columns], store.at[pl.ds(start, size), :, :, columns]))
            start += size
        return [pltpu.make_async_copy(a, b, sems.at[head, i]) for i, (a, b) in enumerate(found)]

    def puts(head):
        pairs = [(acc_ref, acc_hbm), (top_ref, top_hbm), (total_ref, total_hbm)]
        return [pltpu.make_async_copy(a.at[head], b.at[head], put_sems.at[head, i]) for i, (a, b) in enumerate(pairs)]

    def item(frame, head):
        columns = columns_of(head)
        own = (frame + near) * BPF * pieces_of
        keys, values, masks = [], [], []
        for b in range(BPF):
            keys.append(flat(store[pl.ds(own + b * pieces_of, pieces_of), 0, :, columns]))
            values.append(flat(store[pl.ds(own + b * pieces_of, pieces_of), 1, :, columns]))
            masks.append(None)
        for other in range(frames + 2 * near - 1):
            relative = other - near
            relative = relative + jnp.where(relative >= frame, 1, 0)
            codes = [code_ref[(frame * BPF + b) * width + relative + REACH] for b in range(BPF)]
            pick = jnp.maximum(codes[0], codes[1]) // 2
            place = ((relative + near) * BPF + pick) * pieces_of
            keys.append(flat(store[pl.ds(place, pieces_of), 0, :, columns]))
            values.append(flat(store[pl.ds(place, pieces_of), 1, :, columns]))
            masks.append(mask_of(codes))
        queries = flat(q_ref[pl.ds(frame * per_frame, per_frame), :, columns])
        tiles = masked_scores(queries, keys, masks)
        tops = [largest(tiles[b]) for b in range(BPF)]
        mixed, totals = weighted(tiles, tops, values)
        acc_ref[head, frame] = mixed
        top_ref[head, frame] = jnp.broadcast_to(jnp.concatenate(tops, axis=0), mixed.shape)
        total_ref[head, frame] = jnp.broadcast_to(totals, mixed.shape)

    together = 2 if frames % 2 == 0 else 1

    def work(head):
        def step(index, carry):
            for offset in range(together):
                item(index * together + offset, head)
            return carry

        lax.fori_loop(0, frames // together, step, 0)

    each_head(heads, fetches, puts, work)


def far_kernel(frames, near, pieces_of, heads, first_head, code_ref, q_hbm, *refs):
    left_hbm, right_hbm, acc_hbm, top_hbm, total_hbm, out_hbm, *scratch = refs
    q_ref, left, right, acc_ref, top_ref, total_ref, out_ref, sems, put_sems = scratch
    per_frame = BPF * pieces_of
    width = frames + 2 * REACH

    def fetches(head):
        columns = columns_of(head)
        pairs = [
            (q_hbm.at[:, 0, :, columns_of(head + first_head)], q_ref.at[:, :, columns]),
            (left_hbm.at[:, :, :, columns], left.at[:, :, :, columns]),
            (right_hbm.at[:, :, :, columns], right.at[:, :, :, columns]),
            (acc_hbm.at[head], acc_ref.at[head]),
            (top_hbm.at[head], top_ref.at[head]),
            (total_hbm.at[head], total_ref.at[head]),
        ]
        return [pltpu.make_async_copy(a, b, sems.at[head, i]) for i, (a, b) in enumerate(pairs)]

    def puts(head):
        columns = columns_of(head)
        return [pltpu.make_async_copy(out_ref.at[:, :, columns], out_hbm.at[:, :, columns], put_sems.at[head])]

    def item(frame, head):
        columns = columns_of(head)
        keys, values, masks = [], [], []
        for relative in [*range(-REACH, -near), *range(frames + near, frames + REACH)]:
            if abs(relative - frame) > REACH:
                continue
            codes = [code_ref[(frame * BPF + b) * width + relative + REACH] for b in range(BPF)]
            pick = jnp.maximum(codes[0], codes[1]) // 2
            if relative < 0:
                piece, place = left, (0 if relative == -REACH else (relative + REACH) * BPF - 1 + pick)
            else:
                first = (relative - frames - near) * BPF
                piece, place = right, (first if relative == frames + REACH - 1 else first + pick)
            keys.append(flat(piece[pl.ds(place * pieces_of, pieces_of), 0, :, columns]))
            values.append(flat(piece[pl.ds(place * pieces_of, pieces_of), 1, :, columns]))
            masks.append(mask_of(codes))
        queries = flat(q_ref[pl.ds(frame * per_frame, per_frame), :, columns])
        tiles = masked_scores(queries, keys, masks)
        near_top = top_ref[head, frame]
        tops = [jnp.maximum(largest(tiles[b]), near_top[b * BLK : (b + 1) * BLK]) for b in range(BPF)]
        mixed, totals = weighted(tiles, tops, values)
        shrink = jnp.exp2((near_top - jnp.concatenate(tops, axis=0)) * to_log2)
        result = (acc_ref[head, frame] * shrink + mixed) / (total_ref[head, frame] * shrink + totals)
        out_ref[pl.ds(frame * per_frame, per_frame), :, columns] = result.astype(jnp.bfloat16).reshape(
            per_frame, BLK // pieces_of, HD
        )

    def work(head):
        for frame in range(frames):
            item(frame, head)

    each_head(heads, fetches, puts, work)


def attend_near(codes, queries, pieces, frames, near, first_head, after=()):
    members, _, rows, _ = queries.shape
    pieces_of = BLK // rows
    width = pieces[0].shape[3]
    heads = width // HD
    stored = sum(piece.shape[0] for piece in pieces)

    def body(code_ref, q_hbm, *refs):
        kept = refs[: len(pieces)] + refs[len(pieces) + len(after) :]
        near_kernel(frames, near, pieces_of, heads, first_head, code_ref, q_hbm, *kept)

    partial = jax.ShapeDtypeStruct((heads, frames, BPF * BLK, HD), jnp.float32)
    return pl.pallas_call(
        body,
        out_shape=[partial] * 3,
        in_specs=[pl.BlockSpec(memory_space=pltpu.SMEM)] + [anywhere] * (1 + len(pieces) + len(after)),
        out_specs=[anywhere] * 3,
        scratch_shapes=[
            pltpu.VMEM((members, rows, width), jnp.bfloat16),
            pltpu.VMEM((stored, 2, rows, width), jnp.bfloat16),
            *[pltpu.VMEM(partial.shape, jnp.float32)] * 3,
            pltpu.SemaphoreType.DMA((heads, 1 + len(pieces))),
            pltpu.SemaphoreType.DMA((heads, 3)),
        ],
        compiler_params=pltpu.CompilerParams(vmem_limit_bytes=NEAR_VMEM_LIMIT),
        cost_estimate=pl.CostEstimate(
            flops=6 * frames * heads * BPF * (frames + 2 * near + 1) * 4 * BLK * BLK * HD,
            bytes_accessed=1024,
            transcendentals=0,
        ),
    )(codes, queries, *pieces, *after)


def attend_far(codes, queries, far, partials, frames, near, first_head, after=()):
    members, _, rows, _ = queries.shape
    pieces_of = BLK // rows
    width = far[0].shape[3]
    heads = width // HD

    def body(code_ref, q_hbm, *refs):
        far_kernel(frames, near, pieces_of, heads, first_head, code_ref, q_hbm, *refs[:5], *refs[5 + len(after) :])

    result = jax.ShapeDtypeStruct((members, rows, width), jnp.bfloat16)
    return pl.pallas_call(
        body,
        out_shape=result,
        in_specs=[pl.BlockSpec(memory_space=pltpu.SMEM)] + [anywhere] * (6 + len(after)),
        out_specs=anywhere,
        scratch_shapes=[
            pltpu.VMEM(result.shape, result.dtype),
            *[pltpu.VMEM(array.shape, array.dtype) for array in (*far, *partials)],
            pltpu.VMEM(result.shape, result.dtype),
            pltpu.SemaphoreType.DMA((heads, 6)),
            pltpu.SemaphoreType.DMA((heads,)),
        ],
        compiler_params=pltpu.CompilerParams(vmem_limit_bytes=VMEM_LIMIT),
        cost_estimate=pl.CostEstimate(
            flops=6 * frames * heads * BPF * 4 * 4 * BLK * BLK * HD, bytes_accessed=1024, transcendentals=0
        ),
    )(codes, queries, *far, *partials, *after)


def on_device(outer, inner, q_proj, k_proj, v_proj, kv_list):
    frames = inner
    rows, model_width = q_proj.shape
    team = ("inner", "rep", "uly")
    team_size = frames * BPF * BLK // rows
    heads_here = model_width // HD // team_size
    pieces_of = BLK // rows
    per_frame = BPF * pieces_of
    my_group = lax.axis_index("outer")

    def rows_of(reader_frame, count):
        start = jnp.clip(reader_frame * BPF, 0, kv_list.shape[0] - count * BPF)
        return lax.dynamic_slice_in_dim(kv_list, start, count * BPF, 0)

    lists = rows_of(my_group * frames, frames).reshape(frames * BPF, 1, -1)
    first_ids = BPF * (my_group * frames - REACH + lax.broadcasted_iota(jnp.int32, (1, frames + 2 * REACH, 1), 1))
    hits = jnp.where(lists == first_ids, 1, 0) + jnp.where(lists == first_ids + 1, 2, 0)
    codes = jnp.sum(jnp.where(lists >= 0, hits, 0), axis=-1).reshape(-1)

    def picked(reader_frame, holder_frame):
        return jnp.any(rows_of(reader_frame, 1) == holder_frame * BPF + 1).astype(jnp.int32)

    assert sum(CHUNKS) == heads_here
    widths = [heads * HD for heads in CHUNKS]
    lows = [sum(CHUNKS[:c]) for c in range(len(CHUNKS))]
    starts = [low * team_size * HD for low in lows]

    def exchange(array):
        return lax.all_to_all(array, team, split_axis=0, concat_axis=0, tiled=True)

    def shifted(array, heading, hop):
        places = range(outer)
        route = [(i, i + heading) for i in places if i + heading in places and i - (hop - 1) * heading in places]
        return lax.ppermute(array, "outer", route)

    hops = []
    for hop in range(1, -(-REACH // frames) + 1):
        spare = hop * frames - REACH
        hops.append((frames - max(0, spare), spare >= 0))

    def forwarded(held, held_frames, keep, single, after):
        whole = (keep - 1 if single else keep) * per_frame
        if single:
            from_left, from_right = (my_group + 1) * frames, my_group * frames - 1
            edges = held[0].shape[0] - whole - per_frame, whole
            edge_places = jnp.stack(
                [
                    edges[0] + pieces_of * picked(from_left, from_left - REACH),
                    edges[1] + pieces_of * picked(from_right, from_right + REACH),
                ]
            )
            return list(select(held, edge_places, pieces_of, whole, after))
        if keep < held_frames:
            return [held[0][held[0].shape[0] - whole :], held[1][:whole]]
        return held

    def first_hop(own):
        assert hops[0] == (frames, False)
        return [[shifted(own, 1, 1), shifted(own, -1, 1)]]

    def selected(arrivals, after=()):
        for hop in range(1, len(hops)):
            to_send = forwarded(arrivals[-1], hops[hop - 1][0], *hops[hop], after if hop == len(hops) - 1 else ())
            if hop < len(hops) - 1:
                arrivals.append([shifted(to_send[0], 1, hop + 1), shifted(to_send[1], -1, hop + 1)])
        return to_send

    def last_hop(arrivals, to_send):
        arrivals.append([shifted(to_send[0], 1, len(hops)), shifted(to_send[1], -1, len(hops))])

    chunks = range(len(CHUNKS))
    near = (len(hops) - 1) * frames
    packed = [pack([k_proj, v_proj], [starts[c]], [widths[c]], team_size) for c in chunks]
    owned = [exchange(array) for array in packed]
    queries = exchange(pack([q_proj], starts, widths, team_size, after=packed[-1:]))
    arrivals, partials, outs = [], [], []
    before = ()
    for c in chunks:
        arrivals.append(first_hop(owned[c]))
        sent = selected(arrivals[c], after=before)
        order = [a[0] for a in arrivals[c][::-1]] + [owned[c]] + [a[1] for a in arrivals[c]]
        last_hop(arrivals[c], sent)
        partials.append(list(attend_near(codes, queries, order, frames, near, lows[c], after=sent)))
        before = partials[c]
    for c in chunks:
        result = attend_far(codes, queries, arrivals[c][-1], partials[c], frames, near, lows[c], after=before)
        before = [result]
        if outs:
            result, outs[-1] = lax.optimization_barrier((result, outs[-1]))
        outs.append(exchange(result))
    return unpack(outs, starts, model_width)


def solution(mesh):
    sizes = dict(mesh.shape)
    members = sizes["uly"] * sizes["rep"]
    heads = 40
    inner = max(
        i for i in range(1, sizes["ctx"] + 1) if sizes["ctx"] % i == 0 and heads % (i * members) == 0
    )
    outer = sizes["ctx"] // inner
    finer = Mesh(
        mesh.devices.reshape(sizes["groups"], outer, inner, sizes["uly"], sizes["rep"]),
        ("groups", "outer", "inner", "uly", "rep"),
    )
    split = P(("groups", "outer", "inner", "rep", "uly"), None)
    return jax.shard_map(
        functools.partial(on_device, outer, inner),
        mesh=finer,
        in_specs=(split, split, split, P("groups", None)),
        out_specs=split,
        check_vma=False,
    )
```

```python
import functools
import math

import jax
import jax.numpy as jnp
from jax import lax
from jax.experimental import pallas as pl
from jax.experimental.pallas import tpu as pltpu
from jax.sharding import Mesh, PartitionSpec as P

HD = 128
BLK = 128
BPF = 2
REACH = 7
CHUNKS = (3, 2)
PACK_VMEM = 60 * 1024 * 1024
NEAR_VMEM = 24 * 1024 * 1024
OTHER_VMEM = 14 * 1024 * 1024
little = dict(flops=1024, bytes_accessed=1024, transcendentals=0)
much = dict(flops=100_000_000_000, bytes_accessed=1024, transcendentals=0)

very_low = -1e30
to_log2 = math.log2(math.e) * HD ** -0.5


def staged_copies(steps, sems):
    count = len(steps)
    fetches = [pltpu.make_async_copy(s, stage, sems.at[i]) for i, (s, stage, t) in enumerate(steps)]
    puts = [pltpu.make_async_copy(stage, t, sems.at[count + i]) for i, (s, stage, t) in enumerate(steps)]
    for fetch in fetches:
        fetch.start()
    for fetch, put in zip(fetches, puts):
        fetch.wait()
        put.start()
    for put in puts:
        put.wait()


anywhere = pl.BlockSpec(memory_space=pl.ANY)
in_hbm = pl.BlockSpec(memory_space=pltpu.HBM)
in_vmem = pl.BlockSpec(memory_space=pltpu.VMEM)


def copy_call(plan, shapes, count, operands, scalars=(), after=(), cost=little, limit=OTHER_VMEM):
    def body(*refs):
        first = len(scalars)
        last = first + len(operands)
        results = refs[last + len(after) :]
        n = len(shapes)
        staged_copies(plan(refs[:first], refs[first:last], results[:n], results[n : 2 * n]), results[2 * n])

    return pl.pallas_call(
        body,
        out_shape=shapes,
        in_specs=[pl.BlockSpec(memory_space=pltpu.SMEM)] * len(scalars) + [anywhere] * (len(operands) + len(after)),
        out_specs=[anywhere] * len(shapes),
        scratch_shapes=[pltpu.VMEM(s.shape, s.dtype) for s in shapes] + [pltpu.SemaphoreType.DMA((2 * count,))],
        compiler_params=pltpu.CompilerParams(vmem_limit_bytes=limit),
        cost_estimate=pl.CostEstimate(**cost),
    )(*scalars, *operands, *after)


def pack(arrays, starts, widths, team_size, after=()):
    rows = arrays[0].shape[0]

    def plan(scalars, sources, outs, stages):
        steps = []
        for member in range(team_size):
            for kind, source in enumerate(sources):
                low = 0
                for start, width in zip(starts, widths):
                    place = (member, kind, slice(None), pl.ds(low, width))
                    columns = pl.ds(start + member * width, width)
                    steps.append((source.at[:, columns], stages[0].at[place], outs[0].at[place]))
                    low += width
        return steps

    shape = jax.ShapeDtypeStruct((team_size, len(arrays), rows, sum(widths)), jnp.bfloat16)
    return copy_call(plan, [shape], team_size * len(arrays) * len(starts), arrays, after=after, limit=PACK_VMEM)[0]


def unpack(parts, starts, model_width):
    members, rows, _ = parts[0].shape
    count = members * len(parts)

    def body(*refs):
        *sources, out, sems = refs
        puts = []
        for start, source in zip(starts, sources):
            width = source.shape[2]
            for member in range(members):
                columns = pl.ds(start + member * width, width)
                puts.append(pltpu.make_async_copy(source.at[member], out.at[:, columns], sems.at[len(puts)]))
                puts[-1].start()
        for put in puts:
            put.wait()

    return pl.pallas_call(
        body,
        out_shape=jax.ShapeDtypeStruct((rows, model_width), jnp.bfloat16),
        in_specs=[pl.BlockSpec(memory_space=pltpu.VMEM)] * len(parts),
        out_specs=in_hbm,
        scratch_shapes=[pltpu.SemaphoreType.DMA((count,))],
        compiler_params=pltpu.CompilerParams(vmem_limit_bytes=8 * 1024 * 1024),
        cost_estimate=pl.CostEstimate(**little),
    )(*parts)


def select(held, places, count, whole, after=()):
    def plan(scalars, sources, outs, stages):
        (place_ref,) = scalars
        steps = []
        for side, (source, stage, out) in enumerate(zip(sources, stages, outs)):
            one = pl.ds(0 if side == 0 else whole, count)
            steps.append((source.at[pl.ds(place_ref[side], count)], stage.at[one], out.at[one]))
            if whole > 0:
                rest = pl.ds(count if side == 0 else 0, whole)
                kept = pl.ds(source.shape[0] - whole if side == 0 else 0, whole)
                steps.append((source.at[kept], stage.at[rest], out.at[rest]))
        return steps

    shapes = [jax.ShapeDtypeStruct((count + whole,) + array.shape[1:], array.dtype) for array in held]
    return copy_call(plan, shapes, 2 * (2 if whole > 0 else 1), held, scalars=[places], after=after, cost=much)


def columns_of(head):
    return pl.ds(pl.multiple_of(head * HD, HD), HD)


def flat(rows):
    return rows.reshape(rows.shape[0] * rows.shape[1], HD)


def masked_scores(queries, keys, masks):
    tiles = [[] for _ in range(BPF)]
    for first in range(0, len(keys), 2):
        some = jnp.concatenate(keys[first : first + 2], axis=0)
        scores = lax.dot_general(queries, some, (((1,), (1,)), ((), ())), preferred_element_type=jnp.float32)
        for side, mask in enumerate(masks[first : first + 2]):
            for b in range(BPF):
                tile = scores[b * BLK : (b + 1) * BLK, side * BLK : (side + 1) * BLK]
                tiles[b].append(tile if mask is None else tile + mask[b])
    return tiles


def largest(tiles):
    return jnp.max(functools.reduce(jnp.maximum, tiles), axis=1, keepdims=True)


def weighted(tiles, tops, values):
    totals, weights = [], []
    for b in range(BPF):
        exps = [jnp.exp2((tile - tops[b]) * to_log2) for tile in tiles[b]]
        totals.append(jnp.sum(functools.reduce(jnp.add, exps), axis=1, keepdims=True))
        weights.append(jnp.concatenate([e.astype(jnp.bfloat16) for e in exps], axis=1))
    mixed = jnp.dot(
        jnp.concatenate(weights, axis=0), jnp.concatenate(values, axis=0), preferred_element_type=jnp.float32
    )
    return mixed, jnp.concatenate(totals, axis=0)


def mask_of(codes):
    return [jnp.where(code > 0, 0.0, very_low).astype(jnp.float32) for code in codes]


def each_head(heads, fetches, puts, work):
    for head in range(heads):
        for fetch in fetches(head):
            fetch.start()

    def one_head(head, carry):
        for fetch in fetches(head):
            fetch.wait()
        work(head)
        for put in puts(head):
            put.start()
        return carry

    lax.fori_loop(0, heads, one_head, 0)
    for head in range(heads):
        for put in puts(head):
            put.wait()


def near_kernel(frames, near, pieces_of, heads, first_head, code_ref, q_hbm, *refs):
    *piece_refs, acc_ref, top_ref, total_ref, q_ref, store, sems = refs
    per_frame = BPF * pieces_of
    width = frames + 2 * REACH

    def fetches(head):
        columns = columns_of(head)
        found = [(q_hbm.at[:, 0, :, columns_of(head + first_head)], q_ref.at[:, :, columns])]
        start = 0
        for piece in piece_refs:
            size = piece.shape[0]
            found.append((piece.at[:, :, :, columns], store.at[pl.ds(start, size), :, :, columns]))
            start += size
        return [pltpu.make_async_copy(a, b, sems.at[head, i]) for i, (a, b) in enumerate(found)]

    def item(frame, head):
        columns = columns_of(head)
        own = (frame + near) * BPF * pieces_of
        keys, values, masks = [], [], []
        for b in range(BPF):
            keys.append(flat(store[pl.ds(own + b * pieces_of, pieces_of), 0, :, columns]))
            values.append(flat(store[pl.ds(own + b * pieces_of, pieces_of), 1, :, columns]))
            masks.append(None)
        for other in range(frames + 2 * near - 1):
            relative = other - near
            relative = relative + jnp.where(relative >= frame, 1, 0)
            codes = [code_ref[(frame * BPF + b) * width + relative + REACH] for b in range(BPF)]
            pick = jnp.maximum(codes[0], codes[1]) // 2
            place = ((relative + near) * BPF + pick) * pieces_of
            keys.append(flat(store[pl.ds(place, pieces_of), 0, :, columns]))
            values.append(flat(store[pl.ds(place, pieces_of), 1, :, columns]))
            masks.append(mask_of(codes))
        queries = flat(q_ref[pl.ds(frame * per_frame, per_frame), :, columns])
        tiles = masked_scores(queries, keys, masks)
        tops = [largest(tiles[b]) for b in range(BPF)]
        mixed, totals = weighted(tiles, tops, values)
        acc_ref[head, frame] = mixed
        top_ref[head, frame] = jnp.broadcast_to(jnp.concatenate(tops, axis=0), mixed.shape)
        total_ref[head, frame] = jnp.broadcast_to(totals, mixed.shape)

    together = 2 if frames % 2 == 0 else 1

    def work(head):
        def step(index, carry):
            for offset in range(together):
                item(index * together + offset, head)
            return carry

        lax.fori_loop(0, frames // together, step, 0)

    each_head(heads, fetches, lambda head: [], work)


def far_kernel(frames, near, pieces_of, heads, first_head, code_ref, q_hbm, *refs):
    left_hbm, right_hbm, acc_ref, top_ref, total_ref, out_hbm, q_ref, left, right, out_ref, sems, put_sems = refs
    per_frame = BPF * pieces_of
    width = frames + 2 * REACH

    def fetches(head):
        columns = columns_of(head)
        pairs = [
            (q_hbm.at[:, 0, :, columns_of(head + first_head)], q_ref.at[:, :, columns]),
            (left_hbm.at[:, :, :, columns], left.at[:, :, :, columns]),
            (right_hbm.at[:, :, :, columns], right.at[:, :, :, columns]),
        ]
        return [pltpu.make_async_copy(a, b, sems.at[head, i]) for i, (a, b) in enumerate(pairs)]

    def puts(head):
        columns = columns_of(head)
        return [pltpu.make_async_copy(out_ref.at[:, :, columns], out_hbm.at[:, :, columns], put_sems.at[head])]

    def item(frame, head):
        columns = columns_of(head)
        keys, values, masks = [], [], []
        for relative in [*range(-REACH, -near), *range(frames + near, frames + REACH)]:
            if abs(relative - frame) > REACH:
                continue
            codes = [code_ref[(frame * BPF + b) * width + relative + REACH] for b in range(BPF)]
            pick = jnp.maximum(codes[0], codes[1]) // 2
            if relative < 0:
                piece, place = left, (0 if relative == -REACH else (relative + REACH) * BPF - 1 + pick)
            else:
                first = (relative - frames - near) * BPF
                piece, place = right, (first if relative == frames + REACH - 1 else first + pick)
            keys.append(flat(piece[pl.ds(place * pieces_of, pieces_of), 0, :, columns]))
            values.append(flat(piece[pl.ds(place * pieces_of, pieces_of), 1, :, columns]))
            masks.append(mask_of(codes))
        queries = flat(q_ref[pl.ds(frame * per_frame, per_frame), :, columns])
        tiles = masked_scores(queries, keys, masks)
        near_top = top_ref[head, frame]
        tops = [jnp.maximum(largest(tiles[b]), near_top[b * BLK : (b + 1) * BLK]) for b in range(BPF)]
        mixed, totals = weighted(tiles, tops, values)
        shrink = jnp.exp2((near_top - jnp.concatenate(tops, axis=0)) * to_log2)
        result = (acc_ref[head, frame] * shrink + mixed) / (total_ref[head, frame] * shrink + totals)
        out_ref[pl.ds(frame * per_frame, per_frame), :, columns] = result.astype(jnp.bfloat16).reshape(
            per_frame, BLK // pieces_of, HD
        )

    def work(head):
        for frame in range(frames):
            item(frame, head)

    each_head(heads, fetches, puts, work)


def attend_near(codes, queries, pieces, frames, near, first_head, after=()):
    members, _, rows, _ = queries.shape
    pieces_of = BLK // rows
    width = pieces[0].shape[3]
    heads = width // HD
    stored = sum(piece.shape[0] for piece in pieces)

    def body(code_ref, q_hbm, *refs):
        kept = refs[: len(pieces)] + refs[len(pieces) + len(after) :]
        near_kernel(frames, near, pieces_of, heads, first_head, code_ref, q_hbm, *kept)

    partial = jax.ShapeDtypeStruct((heads, frames, BPF * BLK, HD), jnp.float32)
    return pl.pallas_call(
        body,
        out_shape=[partial] * 3,
        in_specs=[pl.BlockSpec(memory_space=pltpu.SMEM)] + [anywhere] * (1 + len(pieces) + len(after)),
        out_specs=[in_vmem] * 3,
        scratch_shapes=[
            pltpu.VMEM((members, rows, width), jnp.bfloat16),
            pltpu.VMEM((stored, 2, rows, width), jnp.bfloat16),
            pltpu.SemaphoreType.DMA((heads, 1 + len(pieces))),
        ],
        compiler_params=pltpu.CompilerParams(vmem_limit_bytes=NEAR_VMEM),
        cost_estimate=pl.CostEstimate(
            flops=6 * frames * heads * BPF * (frames + 2 * near + 1) * 4 * BLK * BLK * HD,
            bytes_accessed=1024,
            transcendentals=0,
        ),
    )(codes, queries, *pieces, *after)


def attend_far(codes, queries, far, partials, frames, near, first_head, after=()):
    members, _, rows, _ = queries.shape
    pieces_of = BLK // rows
    width = far[0].shape[3]
    heads = width // HD

    def body(code_ref, q_hbm, *refs):
        far_kernel(frames, near, pieces_of, heads, first_head, code_ref, q_hbm, *refs[:5], *refs[5 + len(after) :])

    result = jax.ShapeDtypeStruct((members, rows, width), jnp.bfloat16)
    return pl.pallas_call(
        body,
        out_shape=result,
        in_specs=[pl.BlockSpec(memory_space=pltpu.SMEM)] + [anywhere] * 3 + [in_vmem] * 3 + [anywhere] * len(after),
        out_specs=in_hbm,
        scratch_shapes=[
            pltpu.VMEM(result.shape, result.dtype),
            *[pltpu.VMEM(array.shape, array.dtype) for array in far],
            pltpu.VMEM(result.shape, result.dtype),
            pltpu.SemaphoreType.DMA((heads, 3)),
            pltpu.SemaphoreType.DMA((heads,)),
        ],
        compiler_params=pltpu.CompilerParams(vmem_limit_bytes=OTHER_VMEM),
        cost_estimate=pl.CostEstimate(
            flops=6 * frames * heads * BPF * 4 * 4 * BLK * BLK * HD, bytes_accessed=1024, transcendentals=0
        ),
    )(codes, queries, *far, *partials, *after)


def on_device(outer, inner, q_proj, k_proj, v_proj, kv_list):
    frames = inner
    rows, model_width = q_proj.shape
    team = ("inner", "rep", "uly")
    team_size = frames * BPF * BLK // rows
    heads_here = model_width // HD // team_size
    pieces_of = BLK // rows
    per_frame = BPF * pieces_of
    my_group = lax.axis_index("outer")

    def rows_of(reader_frame, count):
        start = jnp.clip(reader_frame * BPF, 0, kv_list.shape[0] - count * BPF)
        return lax.dynamic_slice_in_dim(kv_list, start, count * BPF, 0)

    lists = rows_of(my_group * frames, frames).reshape(frames * BPF, 1, -1)
    first_ids = BPF * (my_group * frames - REACH + lax.broadcasted_iota(jnp.int32, (1, frames + 2 * REACH, 1), 1))
    hits = jnp.where(lists == first_ids, 1, 0) + jnp.where(lists == first_ids + 1, 2, 0)
    codes = jnp.sum(jnp.where(lists >= 0, hits, 0), axis=-1).reshape(-1)

    def picked(reader_frame, holder_frame):
        return jnp.any(rows_of(reader_frame, 1) == holder_frame * BPF + 1).astype(jnp.int32)

    assert sum(CHUNKS) == heads_here
    widths = [heads * HD for heads in CHUNKS]
    lows = [sum(CHUNKS[:c]) for c in range(len(CHUNKS))]
    starts = [low * team_size * HD for low in lows]

    def exchange(array):
        return lax.all_to_all(array, team, split_axis=0, concat_axis=0, tiled=True)

    def shifted(array, heading, hop):
        places = range(outer)
        route = [(i, i + heading) for i in places if i + heading in places and i - (hop - 1) * heading in places]
        return lax.ppermute(array, "outer", route)

    hops = []
    for hop in range(1, -(-REACH // frames) + 1):
        spare = hop * frames - REACH
        hops.append((frames - max(0, spare), spare >= 0))

    def forwarded(held, held_frames, keep, single, after):
        whole = (keep - 1 if single else keep) * per_frame
        if single:
            from_left, from_right = (my_group + 1) * frames, my_group * frames - 1
            edges = held[0].shape[0] - whole - per_frame, whole
            edge_places = jnp.stack(
                [
                    edges[0] + pieces_of * picked(from_left, from_left - REACH),
                    edges[1] + pieces_of * picked(from_right, from_right + REACH),
                ]
            )
            return list(select(held, edge_places, pieces_of, whole, after))
        if keep < held_frames:
            return [held[0][held[0].shape[0] - whole :], held[1][:whole]]
        return held

    def first_hop(own):
        assert hops[0] == (frames, False)
        return [[shifted(own, 1, 1), shifted(own, -1, 1)]]

    def selected(arrivals, after=()):
        for hop in range(1, len(hops)):
            to_send = forwarded(arrivals[-1], hops[hop - 1][0], *hops[hop], after if hop == len(hops) - 1 else ())
            if hop < len(hops) - 1:
                arrivals.append([shifted(to_send[0], 1, hop + 1), shifted(to_send[1], -1, hop + 1)])
        return to_send

    def last_hop(arrivals, to_send):
        arrivals.append([shifted(to_send[0], 1, len(hops)), shifted(to_send[1], -1, len(hops))])

    chunks = range(len(CHUNKS))
    near = (len(hops) - 1) * frames
    packed = [pack([k_proj, v_proj], [starts[c]], [widths[c]], team_size) for c in chunks]
    owned = [exchange(array) for array in packed]
    queries = exchange(pack([q_proj], starts, widths, team_size, after=packed[-1:]))
    arrivals, partials, outs = [], [], []
    before = ()
    for c in chunks:
        arrivals.append(first_hop(owned[c]))
        sent = selected(arrivals[c], after=before)
        order = [a[0] for a in arrivals[c][::-1]] + [owned[c]] + [a[1] for a in arrivals[c]]
        last_hop(arrivals[c], sent)
        partials.append(list(attend_near(codes, queries, order, frames, near, lows[c], after=sent)))
        before = partials[c]
    for c in chunks:
        result = attend_far(codes, queries, arrivals[c][-1], partials[c], frames, near, lows[c], after=before)
        before = [result]
        if outs:
            result, outs[-1] = lax.optimization_barrier((result, outs[-1]))
        outs.append(exchange(result))
    return unpack(outs, starts, model_width)


def solution(mesh):
    sizes = dict(mesh.shape)
    members = sizes["uly"] * sizes["rep"]
    heads = 40
    inner = max(
        i for i in range(1, sizes["ctx"] + 1) if sizes["ctx"] % i == 0 and heads % (i * members) == 0
    )
    outer = sizes["ctx"] // inner
    finer = Mesh(
        mesh.devices.reshape(sizes["groups"], outer, inner, sizes["uly"], sizes["rep"]),
        ("groups", "outer", "inner", "uly", "rep"),
    )
    split = P(("groups", "outer", "inner", "rep", "uly"), None)
    return jax.shard_map(
        functools.partial(on_device, outer, inner),
        mesh=finer,
        in_specs=(split, split, split, P("groups", None)),
        out_specs=split,
        check_vma=False,
    )
```

```python
import functools
import math

import jax
import jax.numpy as jnp
from jax import lax
from jax.experimental import pallas as pl
from jax.experimental.pallas import tpu as pltpu
from jax.sharding import Mesh, PartitionSpec as P

HD = 128
BLK = 128
BPF = 2
REACH = 7
CHUNKS = (3, 2)
PACK_VMEM = 60 * 1024 * 1024
NEAR_VMEM = 24 * 1024 * 1024
OTHER_VMEM = 14 * 1024 * 1024
BESIDE_KEPT = 57 * 1024 * 1024
little = dict(flops=1024, bytes_accessed=1024, transcendentals=0)
much = dict(flops=100_000_000_000, bytes_accessed=1024, transcendentals=0)

very_low = -1e30
to_log2 = math.log2(math.e) * HD ** -0.5


def staged_copies(steps, sems):
    count = len(steps)
    fetches = [pltpu.make_async_copy(s, stage, sems.at[i]) for i, (s, stage, t) in enumerate(steps)]
    puts = [pltpu.make_async_copy(stage, t, sems.at[count + i]) for i, (s, stage, t) in enumerate(steps)]
    for fetch in fetches:
        fetch.start()
    for fetch, put in zip(fetches, puts):
        fetch.wait()
        put.start()
    for put in puts:
        put.wait()


anywhere = pl.BlockSpec(memory_space=pl.ANY)
in_hbm = pl.BlockSpec(memory_space=pltpu.HBM)
in_vmem = pl.BlockSpec(memory_space=pltpu.VMEM)


def copy_call(plan, shapes, count, operands, scalars=(), after=(), cost=little, limit=OTHER_VMEM):
    def body(*refs):
        first = len(scalars)
        last = first + len(operands)
        results = refs[last + len(after) :]
        n = len(shapes)
        staged_copies(plan(refs[:first], refs[first:last], results[:n], results[n : 2 * n]), results[2 * n])

    return pl.pallas_call(
        body,
        out_shape=shapes,
        in_specs=[pl.BlockSpec(memory_space=pltpu.SMEM)] * len(scalars) + [anywhere] * (len(operands) + len(after)),
        out_specs=[anywhere] * len(shapes),
        scratch_shapes=[pltpu.VMEM(s.shape, s.dtype) for s in shapes] + [pltpu.SemaphoreType.DMA((2 * count,))],
        compiler_params=pltpu.CompilerParams(vmem_limit_bytes=limit),
        cost_estimate=pl.CostEstimate(**cost),
    )(*scalars, *operands, *after)


def pack(arrays, starts, widths, team_size, after=()):
    rows = arrays[0].shape[0]

    def plan(scalars, sources, outs, stages):
        steps = []
        for member in range(team_size):
            for kind, source in enumerate(sources):
                low = 0
                for start, width in zip(starts, widths):
                    place = (member, kind, slice(None), pl.ds(low, width))
                    columns = pl.ds(start + member * width, width)
                    steps.append((source.at[:, columns], stages[0].at[place], outs[0].at[place]))
                    low += width
        return steps

    shape = jax.ShapeDtypeStruct((team_size, len(arrays), rows, sum(widths)), jnp.bfloat16)
    return copy_call(plan, [shape], team_size * len(arrays) * len(starts), arrays, after=after, limit=PACK_VMEM)[0]


def unpack(parts, starts, model_width):
    members, rows, _ = parts[0].shape
    count = members * len(parts)

    def body(*refs):
        *sources, out, sems = refs
        puts = []
        for start, source in zip(starts, sources):
            width = source.shape[2]
            for member in range(members):
                columns = pl.ds(start + member * width, width)
                puts.append(pltpu.make_async_copy(source.at[member], out.at[:, columns], sems.at[len(puts)]))
                puts[-1].start()
        for put in puts:
            put.wait()

    return pl.pallas_call(
        body,
        out_shape=jax.ShapeDtypeStruct((rows, model_width), jnp.bfloat16),
        in_specs=[pl.BlockSpec(memory_space=pltpu.VMEM)] * len(parts),
        out_specs=in_hbm,
        scratch_shapes=[pltpu.SemaphoreType.DMA((count,))],
        compiler_params=pltpu.CompilerParams(vmem_limit_bytes=8 * 1024 * 1024),
        cost_estimate=pl.CostEstimate(**little),
    )(*parts)


def select(held, places, count, whole, after=()):
    def plan(scalars, sources, outs, stages):
        (place_ref,) = scalars
        steps = []
        for side, (source, stage, out) in enumerate(zip(sources, stages, outs)):
            one = pl.ds(0 if side == 0 else whole, count)
            steps.append((source.at[pl.ds(place_ref[side], count)], stage.at[one], out.at[one]))
            if whole > 0:
                rest = pl.ds(count if side == 0 else 0, whole)
                kept = pl.ds(source.shape[0] - whole if side == 0 else 0, whole)
                steps.append((source.at[kept], stage.at[rest], out.at[rest]))
        return steps

    shapes = [jax.ShapeDtypeStruct((count + whole,) + array.shape[1:], array.dtype) for array in held]
    return copy_call(plan, shapes, 2 * (2 if whole > 0 else 1), held, scalars=[places], after=after, cost=much)


def columns_of(head):
    return pl.ds(pl.multiple_of(head * HD, HD), HD)


def flat(rows):
    return rows.reshape(rows.shape[0] * rows.shape[1], HD)


def masked_scores(queries, keys, masks):
    tiles = [[] for _ in range(BPF)]
    for first in range(0, len(keys), 2):
        some = jnp.concatenate(keys[first : first + 2], axis=0)
        scores = lax.dot_general(queries, some, (((1,), (1,)), ((), ())), preferred_element_type=jnp.float32)
        for side, mask in enumerate(masks[first : first + 2]):
            for b in range(BPF):
                tile = scores[b * BLK : (b + 1) * BLK, side * BLK : (side + 1) * BLK]
                tiles[b].append(tile if mask is None else tile + mask[b])
    return tiles


def largest(tiles):
    return jnp.max(functools.reduce(jnp.maximum, tiles), axis=1, keepdims=True)


def weighted(tiles, tops, values):
    totals, weights = [], []
    for b in range(BPF):
        exps = [jnp.exp2((tile - tops[b]) * to_log2) for tile in tiles[b]]
        totals.append(jnp.sum(functools.reduce(jnp.add, exps), axis=1, keepdims=True))
        weights.append(jnp.concatenate([e.astype(jnp.bfloat16) for e in exps], axis=1))
    mixed = jnp.dot(
        jnp.concatenate(weights, axis=0), jnp.concatenate(values, axis=0), preferred_element_type=jnp.float32
    )
    return mixed, jnp.concatenate(totals, axis=0)


def mask_of(codes):
    return [jnp.where(code > 0, 0.0, very_low).astype(jnp.float32) for code in codes]


def each_head(heads, fetches, puts, work):
    for head in range(heads):
        for fetch in fetches(head):
            fetch.start()

    def one_head(head, carry):
        for fetch in fetches(head):
            fetch.wait()
        work(head)
        for put in puts(head):
            put.start()
        return carry

    lax.fori_loop(0, heads, one_head, 0)
    for head in range(heads):
        for put in puts(head):
            put.wait()


def near_kernel(frames, near, pieces_of, heads, first_head, keep, code_ref, q_hbm, *refs):
    if keep:
        *piece_refs, acc_ref, top_ref, total_ref, q_ref, store, sems = refs
    else:
        *piece_refs, acc_hbm, top_hbm, total_hbm, q_ref, store, acc_ref, top_ref, total_ref, sems, put_sems = refs
    per_frame = BPF * pieces_of
    width = frames + 2 * REACH

    def fetches(head):
        columns = columns_of(head)
        found = [(q_hbm.at[:, 0, :, columns_of(head + first_head)], q_ref.at[:, :, columns])]
        start = 0
        for piece in piece_refs:
            size = piece.shape[0]
            found.append((piece.at[:, :, :, columns], store.at[pl.ds(start, size), :, :, columns]))
            start += size
        return [pltpu.make_async_copy(a, b, sems.at[head, i]) for i, (a, b) in enumerate(found)]

    def puts(head):
        if keep:
            return []
        pairs = [(acc_ref, acc_hbm), (top_ref, top_hbm), (total_ref, total_hbm)]
        return [pltpu.make_async_copy(a.at[head], b.at[head], put_sems.at[head, i]) for i, (a, b) in enumerate(pairs)]

    def item(frame, head):
        columns = columns_of(head)
        own = (frame + near) * BPF * pieces_of
        keys, values, masks = [], [], []
        for b in range(BPF):
            keys.append(flat(store[pl.ds(own + b * pieces_of, pieces_of), 0, :, columns]))
            values.append(flat(store[pl.ds(own + b * pieces_of, pieces_of), 1, :, columns]))
            masks.append(None)
        for other in range(frames + 2 * near - 1):
            relative = other - near
            relative = relative + jnp.where(relative >= frame, 1, 0)
            codes = [code_ref[(frame * BPF + b) * width + relative + REACH] for b in range(BPF)]
            pick = jnp.maximum(codes[0], codes[1]) // 2
            place = ((relative + near) * BPF + pick) * pieces_of
            keys.append(flat(store[pl.ds(place, pieces_of), 0, :, columns]))
            values.append(flat(store[pl.ds(place, pieces_of), 1, :, columns]))
            masks.append(mask_of(codes))
        queries = flat(q_ref[pl.ds(frame * per_frame, per_frame), :, columns])
        tiles = masked_scores(queries, keys, masks)
        tops = [largest(tiles[b]) for b in range(BPF)]
        mixed, totals = weighted(tiles, tops, values)
        acc_ref[head, frame] = mixed
        top_ref[head, frame] = jnp.broadcast_to(jnp.concatenate(tops, axis=0), mixed.shape)
        total_ref[head, frame] = jnp.broadcast_to(totals, mixed.shape)

    together = 2 if frames % 2 == 0 else 1

    def work(head):
        def step(index, carry):
            for offset in range(together):
                item(index * together + offset, head)
            return carry

        lax.fori_loop(0, frames // together, step, 0)

    each_head(heads, fetches, puts, work)


def far_kernel(frames, near, pieces_of, heads, first_head, keep, code_ref, q_hbm, *refs):
    left_hbm, right_hbm, *partials, out_hbm, q_ref, left, right, acc_ref, top_ref, total_ref, out_ref, sems, put_sems = (
        refs if not keep else refs[:9] + refs[2:5] + refs[9:]
    )
    per_frame = BPF * pieces_of
    width = frames + 2 * REACH

    def fetches(head):
        columns = columns_of(head)
        pairs = [
            (q_hbm.at[:, 0, :, columns_of(head + first_head)], q_ref.at[:, :, columns]),
            (left_hbm.at[:, :, :, columns], left.at[:, :, :, columns]),
            (right_hbm.at[:, :, :, columns], right.at[:, :, :, columns]),
        ]
        if not keep:
            pairs += [(a.at[head], b.at[head]) for a, b in zip(partials, (acc_ref, top_ref, total_ref))]
        return [pltpu.make_async_copy(a, b, sems.at[head, i]) for i, (a, b) in enumerate(pairs)]

    def puts(head):
        columns = columns_of(head)
        return [pltpu.make_async_copy(out_ref.at[:, :, columns], out_hbm.at[:, :, columns], put_sems.at[head])]

    def item(frame, head):
        columns = columns_of(head)
        keys, values, masks = [], [], []
        for relative in [*range(-REACH, -near), *range(frames + near, frames + REACH)]:
            if abs(relative - frame) > REACH:
                continue
            codes = [code_ref[(frame * BPF + b) * width + relative + REACH] for b in range(BPF)]
            pick = jnp.maximum(codes[0], codes[1]) // 2
            if relative < 0:
                piece, place = left, (0 if relative == -REACH else (relative + REACH) * BPF - 1 + pick)
            else:
                first = (relative - frames - near) * BPF
                piece, place = right, (first if relative == frames + REACH - 1 else first + pick)
            keys.append(flat(piece[pl.ds(place * pieces_of, pieces_of), 0, :, columns]))
            values.append(flat(piece[pl.ds(place * pieces_of, pieces_of), 1, :, columns]))
            masks.append(mask_of(codes))
        queries = flat(q_ref[pl.ds(frame * per_frame, per_frame), :, columns])
        tiles = masked_scores(queries, keys, masks)
        near_top = top_ref[head, frame]
        tops = [jnp.maximum(largest(tiles[b]), near_top[b * BLK : (b + 1) * BLK]) for b in range(BPF)]
        mixed, totals = weighted(tiles, tops, values)
        shrink = jnp.exp2((near_top - jnp.concatenate(tops, axis=0)) * to_log2)
        result = (acc_ref[head, frame] * shrink + mixed) / (total_ref[head, frame] * shrink + totals)
        out_ref[pl.ds(frame * per_frame, per_frame), :, columns] = result.astype(jnp.bfloat16).reshape(
            per_frame, BLK // pieces_of, HD
        )

    def work(head):
        for frame in range(frames):
            item(frame, head)

    each_head(heads, fetches, puts, work)


def attend_near(codes, queries, pieces, frames, near, first_head, keep, after=()):
    members, _, rows, _ = queries.shape
    pieces_of = BLK // rows
    width = pieces[0].shape[3]
    heads = width // HD
    stored = sum(piece.shape[0] for piece in pieces)

    def body(code_ref, q_hbm, *refs):
        kept = refs[: len(pieces)] + refs[len(pieces) + len(after) :]
        near_kernel(frames, near, pieces_of, heads, first_head, keep, code_ref, q_hbm, *kept)

    partial = jax.ShapeDtypeStruct((heads, frames, BPF * BLK, HD), jnp.float32)
    return pl.pallas_call(
        body,
        out_shape=[partial] * 3,
        in_specs=[pl.BlockSpec(memory_space=pltpu.SMEM)] + [anywhere] * (1 + len(pieces) + len(after)),
        out_specs=[in_vmem if keep else anywhere] * 3,
        scratch_shapes=[
            pltpu.VMEM((members, rows, width), jnp.bfloat16),
            pltpu.VMEM((stored, 2, rows, width), jnp.bfloat16),
            *[pltpu.VMEM(partial.shape, jnp.float32)] * (0 if keep else 3),
            pltpu.SemaphoreType.DMA((heads, 1 + len(pieces))),
            *[pltpu.SemaphoreType.DMA((heads, 3))] * (0 if keep else 1),
        ],
        compiler_params=pltpu.CompilerParams(vmem_limit_bytes=NEAR_VMEM if keep else BESIDE_KEPT),
        cost_estimate=pl.CostEstimate(
            flops=6 * frames * heads * BPF * (frames + 2 * near + 1) * 4 * BLK * BLK * HD,
            bytes_accessed=1024,
            transcendentals=0,
        ),
    )(codes, queries, *pieces, *after)


def attend_far(codes, queries, far, partials, frames, near, first_head, keep, after=()):
    members, _, rows, _ = queries.shape
    pieces_of = BLK // rows
    width = far[0].shape[3]
    heads = width // HD

    def body(code_ref, q_hbm, *refs):
        far_kernel(frames, near, pieces_of, heads, first_head, keep, code_ref, q_hbm, *refs[:5], *refs[5 + len(after) :])

    result = jax.ShapeDtypeStruct((members, rows, width), jnp.bfloat16)
    return pl.pallas_call(
        body,
        out_shape=result,
        in_specs=[pl.BlockSpec(memory_space=pltpu.SMEM)] + [anywhere] * 3 + [in_vmem if keep else anywhere] * 3 + [anywhere] * len(after),
        out_specs=in_hbm,
        scratch_shapes=[
            pltpu.VMEM(result.shape, result.dtype),
            *[pltpu.VMEM(array.shape, array.dtype) for array in (*far, *(() if keep else partials))],
            pltpu.VMEM(result.shape, result.dtype),
            pltpu.SemaphoreType.DMA((heads, 6)),
            pltpu.SemaphoreType.DMA((heads,)),
        ],
        compiler_params=pltpu.CompilerParams(vmem_limit_bytes=OTHER_VMEM if keep else PACK_VMEM),
        cost_estimate=pl.CostEstimate(
            flops=6 * frames * heads * BPF * 4 * 4 * BLK * BLK * HD, bytes_accessed=1024, transcendentals=0
        ),
    )(codes, queries, *far, *partials, *after)


def on_device(outer, inner, q_proj, k_proj, v_proj, kv_list):
    frames = inner
    rows, model_width = q_proj.shape
    team = ("inner", "rep", "uly")
    team_size = frames * BPF * BLK // rows
    heads_here = model_width // HD // team_size
    pieces_of = BLK // rows
    per_frame = BPF * pieces_of
    my_group = lax.axis_index("outer")

    def rows_of(reader_frame, count):
        start = jnp.clip(reader_frame * BPF, 0, kv_list.shape[0] - count * BPF)
        return lax.dynamic_slice_in_dim(kv_list, start, count * BPF, 0)

    lists = rows_of(my_group * frames, frames).reshape(frames * BPF, 1, -1)
    first_ids = BPF * (my_group * frames - REACH + lax.broadcasted_iota(jnp.int32, (1, frames + 2 * REACH, 1), 1))
    hits = jnp.where(lists == first_ids, 1, 0) + jnp.where(lists == first_ids + 1, 2, 0)
    codes = jnp.sum(jnp.where(lists >= 0, hits, 0), axis=-1).reshape(-1)

    def picked(reader_frame, holder_frame):
        return jnp.any(rows_of(reader_frame, 1) == holder_frame * BPF + 1).astype(jnp.int32)

    assert sum(CHUNKS) == heads_here
    widths = [heads * HD for heads in CHUNKS]
    lows = [sum(CHUNKS[:c]) for c in range(len(CHUNKS))]
    starts = [low * team_size * HD for low in lows]

    def exchange(array):
        return lax.all_to_all(array, team, split_axis=0, concat_axis=0, tiled=True)

    def shifted(array, heading, hop):
        places = range(outer)
        route = [(i, i + heading) for i in places if i + heading in places and i - (hop - 1) * heading in places]
        return lax.ppermute(array, "outer", route)

    hops = []
    for hop in range(1, -(-REACH // frames) + 1):
        spare = hop * frames - REACH
        hops.append((frames - max(0, spare), spare >= 0))

    def forwarded(held, held_frames, keep, single, after):
        whole = (keep - 1 if single else keep) * per_frame
        if single:
            from_left, from_right = (my_group + 1) * frames, my_group * frames - 1
            edges = held[0].shape[0] - whole - per_frame, whole
            edge_places = jnp.stack(
                [
                    edges[0] + pieces_of * picked(from_left, from_left - REACH),
                    edges[1] + pieces_of * picked(from_right, from_right + REACH),
                ]
            )
            return list(select(held, edge_places, pieces_of, whole, after))
        if keep < held_frames:
            return [held[0][held[0].shape[0] - whole :], held[1][:whole]]
        return held

    def first_hop(own):
        assert hops[0] == (frames, False)
        return [[shifted(own, 1, 1), shifted(own, -1, 1)]]

    def selected(arrivals, after=()):
        for hop in range(1, len(hops)):
            to_send = forwarded(arrivals[-1], hops[hop - 1][0], *hops[hop], after if hop == len(hops) - 1 else ())
            if hop < len(hops) - 1:
                arrivals.append([shifted(to_send[0], 1, hop + 1), shifted(to_send[1], -1, hop + 1)])
        return to_send

    def last_hop(arrivals, to_send):
        arrivals.append([shifted(to_send[0], 1, len(hops)), shifted(to_send[1], -1, len(hops))])

    chunks = range(len(CHUNKS))
    near = (len(hops) - 1) * frames
    packed = [pack([k_proj, v_proj], [starts[c]], [widths[c]], team_size) for c in chunks]
    owned = [exchange(array) for array in packed]
    queries = exchange(pack([q_proj], starts, widths, team_size, after=packed[-1:]))
    arrivals, partials, outs = [], [], []
    before = ()
    for c in chunks:
        arrivals.append(first_hop(owned[c]))
        sent = selected(arrivals[c], after=before)
        order = [a[0] for a in arrivals[c][::-1]] + [owned[c]] + [a[1] for a in arrivals[c]]
        last_hop(arrivals[c], sent)
        partials.append(list(attend_near(codes, queries, order, frames, near, lows[c], c == 0, after=sent)))
        before = partials[c]
    for c in chunks:
        result = attend_far(codes, queries, arrivals[c][-1], partials[c], frames, near, lows[c], c == 0, after=before)
        before = [result]
        if outs:
            result, outs[-1] = lax.optimization_barrier((result, outs[-1]))
        outs.append(exchange(result))
    return unpack(outs, starts, model_width)


def solution(mesh):
    sizes = dict(mesh.shape)
    members = sizes["uly"] * sizes["rep"]
    heads = 40
    inner = max(
        i for i in range(1, sizes["ctx"] + 1) if sizes["ctx"] % i == 0 and heads % (i * members) == 0
    )
    outer = sizes["ctx"] // inner
    finer = Mesh(
        mesh.devices.reshape(sizes["groups"], outer, inner, sizes["uly"], sizes["rep"]),
        ("groups", "outer", "inner", "uly", "rep"),
    )
    split = P(("groups", "outer", "inner", "rep", "uly"), None)
    return jax.shard_map(
        functools.partial(on_device, outer, inner),
        mesh=finer,
        in_specs=(split, split, split, P("groups", None)),
        out_specs=split,
        check_vma=False,
    )
```

```python
import functools
import math

import jax
import jax.numpy as jnp
from jax import lax
from jax.experimental import pallas as pl
from jax.experimental.pallas import tpu as pltpu
from jax.sharding import Mesh, PartitionSpec as P

HD = 128
BLK = 128
BPF = 2
REACH = 7
CHUNKS = (2, 3)
PACK_VMEM = 60 * 1024 * 1024
NEAR_VMEM = 24 * 1024 * 1024
OTHER_VMEM = 14 * 1024 * 1024
little = dict(flops=1024, bytes_accessed=1024, transcendentals=0)
some = dict(flops=20_000_000_000, bytes_accessed=1024, transcendentals=0)
much = dict(flops=100_000_000_000, bytes_accessed=1024, transcendentals=0)

very_low = -1e30
to_log2 = math.log2(math.e) * HD ** -0.5


def staged_copies(steps, sems):
    count = len(steps)
    fetches = [pltpu.make_async_copy(s, stage, sems.at[i]) for i, (s, stage, t) in enumerate(steps)]
    puts = [pltpu.make_async_copy(stage, t, sems.at[count + i]) for i, (s, stage, t) in enumerate(steps)]
    for fetch in fetches:
        fetch.start()
    for fetch, put in zip(fetches, puts):
        fetch.wait()
        put.start()
    for put in puts:
        put.wait()


anywhere = pl.BlockSpec(memory_space=pl.ANY)
in_hbm = pl.BlockSpec(memory_space=pltpu.HBM)
in_vmem = pl.BlockSpec(memory_space=pltpu.VMEM)


def copy_call(plan, shapes, count, operands, scalars=(), after=(), cost=little, limit=OTHER_VMEM):
    def body(*refs):
        first = len(scalars)
        last = first + len(operands)
        results = refs[last + len(after) :]
        n = len(shapes)
        staged_copies(plan(refs[:first], refs[first:last], results[:n], results[n : 2 * n]), results[2 * n])

    return pl.pallas_call(
        body,
        out_shape=shapes,
        in_specs=[pl.BlockSpec(memory_space=pltpu.SMEM)] * len(scalars) + [anywhere] * (len(operands) + len(after)),
        out_specs=[anywhere] * len(shapes),
        scratch_shapes=[pltpu.VMEM(s.shape, s.dtype) for s in shapes] + [pltpu.SemaphoreType.DMA((2 * count,))],
        compiler_params=pltpu.CompilerParams(vmem_limit_bytes=limit),
        cost_estimate=pl.CostEstimate(**cost),
    )(*scalars, *operands, *after)


def pack(arrays, starts, widths, team_size, after=()):
    rows = arrays[0].shape[0]

    def plan(scalars, sources, outs, stages):
        steps = []
        for member in range(team_size):
            for kind, source in enumerate(sources):
                low = 0
                for start, width in zip(starts, widths):
                    place = (member, kind, slice(None), pl.ds(low, width))
                    columns = pl.ds(start + member * width, width)
                    steps.append((source.at[:, columns], stages[0].at[place], outs[0].at[place]))
                    low += width
        return steps

    shape = jax.ShapeDtypeStruct((team_size, len(arrays), rows, sum(widths)), jnp.bfloat16)
    return copy_call(plan, [shape], team_size * len(arrays) * len(starts), arrays, after=after, cost=some, limit=PACK_VMEM)[0]


def unpack(parts, starts, model_width):
    members, rows, _ = parts[0].shape
    count = members * len(parts)

    def body(*refs):
        *sources, out, sems = refs
        puts = []
        for start, source in zip(starts, sources):
            width = source.shape[2]
            for member in range(members):
                columns = pl.ds(start + member * width, width)
                puts.append(pltpu.make_async_copy(source.at[member], out.at[:, columns], sems.at[len(puts)]))
                puts[-1].start()
        for put in puts:
            put.wait()

    return pl.pallas_call(
        body,
        out_shape=jax.ShapeDtypeStruct((rows, model_width), jnp.bfloat16),
        in_specs=[pl.BlockSpec(memory_space=pltpu.VMEM)] * len(parts),
        out_specs=in_hbm,
        scratch_shapes=[pltpu.SemaphoreType.DMA((count,))],
        compiler_params=pltpu.CompilerParams(vmem_limit_bytes=8 * 1024 * 1024),
        cost_estimate=pl.CostEstimate(**little),
    )(*parts)


def select(held, places, count, whole, after=()):
    def plan(scalars, sources, outs, stages):
        (place_ref,) = scalars
        steps = []
        for side, (source, stage, out) in enumerate(zip(sources, stages, outs)):
            one = pl.ds(0 if side == 0 else whole, count)
            steps.append((source.at[pl.ds(place_ref[side], count)], stage.at[one], out.at[one]))
            if whole > 0:
                rest = pl.ds(count if side == 0 else 0, whole)
                kept = pl.ds(source.shape[0] - whole if side == 0 else 0, whole)
                steps.append((source.at[kept], stage.at[rest], out.at[rest]))
        return steps

    shapes = [jax.ShapeDtypeStruct((count + whole,) + array.shape[1:], array.dtype) for array in held]
    return copy_call(plan, shapes, 2 * (2 if whole > 0 else 1), held, scalars=[places], after=after, cost=much)


def columns_of(head):
    return pl.ds(pl.multiple_of(head * HD, HD), HD)


def flat(rows):
    return rows.reshape(rows.shape[0] * rows.shape[1], HD)


def masked_scores(queries, keys, masks):
    tiles = [[] for _ in range(BPF)]
    for first in range(0, len(keys), 2):
        some = jnp.concatenate(keys[first : first + 2], axis=0)
        scores = lax.dot_general(queries, some, (((1,), (1,)), ((), ())), preferred_element_type=jnp.float32)
        for side, mask in enumerate(masks[first : first + 2]):
            for b in range(BPF):
                tile = scores[b * BLK : (b + 1) * BLK, side * BLK : (side + 1) * BLK]
                tiles[b].append(tile if mask is None else tile + mask[b])
    return tiles


def largest(tiles):
    return jnp.max(functools.reduce(jnp.maximum, tiles), axis=1, keepdims=True)


def weighted(tiles, tops, values):
    totals, weights = [], []
    for b in range(BPF):
        exps = [jnp.exp2((tile - tops[b]) * to_log2) for tile in tiles[b]]
        totals.append(jnp.sum(functools.reduce(jnp.add, exps), axis=1, keepdims=True))
        weights.append(jnp.concatenate([e.astype(jnp.bfloat16) for e in exps], axis=1))
    mixed = jnp.dot(
        jnp.concatenate(weights, axis=0), jnp.concatenate(values, axis=0), preferred_element_type=jnp.float32
    )
    return mixed, jnp.concatenate(totals, axis=0)


def mask_of(codes):
    return [jnp.where(code > 0, 0.0, very_low).astype(jnp.float32) for code in codes]


def each_head(heads, fetches, puts, work):
    for head in range(heads):
        for fetch in fetches(head):
            fetch.start()

    def one_head(head, carry):
        for fetch in fetches(head):
            fetch.wait()
        work(head)
        for put in puts(head):
            put.start()
        return carry

    lax.fori_loop(0, heads, one_head, 0)
    for head in range(heads):
        for put in puts(head):
            put.wait()


def near_kernel(frames, near, pieces_of, heads, first_head, code_ref, q_hbm, *refs):
    *piece_refs, acc_ref, top_ref, total_ref, q_ref, store, sems = refs
    per_frame = BPF * pieces_of
    width = frames + 2 * REACH

    def fetches(head):
        columns = columns_of(head)
        found = [(q_hbm.at[:, 0, :, columns_of(head + first_head)], q_ref.at[:, :, columns])]
        start = 0
        for piece in piece_refs:
            size = piece.shape[0]
            found.append((piece.at[:, :, :, columns], store.at[pl.ds(start, size), :, :, columns]))
            start += size
        return [pltpu.make_async_copy(a, b, sems.at[head, i]) for i, (a, b) in enumerate(found)]

    def item(frame, head):
        columns = columns_of(head)
        own = (frame + near) * BPF * pieces_of
        keys, values, masks = [], [], []
        for b in range(BPF):
            keys.append(flat(store[pl.ds(own + b * pieces_of, pieces_of), 0, :, columns]))
            values.append(flat(store[pl.ds(own + b * pieces_of, pieces_of), 1, :, columns]))
            masks.append(None)
        for other in range(frames + 2 * near - 1):
            relative = other - near
            relative = relative + jnp.where(relative >= frame, 1, 0)
            codes = [code_ref[(frame * BPF + b) * width + relative + REACH] for b in range(BPF)]
            pick = jnp.maximum(codes[0], codes[1]) // 2
            place = ((relative + near) * BPF + pick) * pieces_of
            keys.append(flat(store[pl.ds(place, pieces_of), 0, :, columns]))
            values.append(flat(store[pl.ds(place, pieces_of), 1, :, columns]))
            masks.append(mask_of(codes))
        queries = flat(q_ref[pl.ds(frame * per_frame, per_frame), :, columns])
        tiles = masked_scores(queries, keys, masks)
        tops = [largest(tiles[b]) for b in range(BPF)]
        mixed, totals = weighted(tiles, tops, values)
        acc_ref[head, frame] = mixed
        top_ref[head, frame] = jnp.broadcast_to(jnp.concatenate(tops, axis=0), mixed.shape)
        total_ref[head, frame] = jnp.broadcast_to(totals, mixed.shape)

    together = 2 if frames % 2 == 0 else 1

    def work(head):
        def step(index, carry):
            for offset in range(together):
                item(index * together + offset, head)
            return carry

        lax.fori_loop(0, frames // together, step, 0)

    each_head(heads, fetches, lambda head: [], work)


def far_kernel(frames, near, pieces_of, heads, first_head, code_ref, q_hbm, *refs):
    left_hbm, right_hbm, acc_ref, top_ref, total_ref, out_hbm, q_ref, left, right, out_ref, sems, put_sems = refs
    per_frame = BPF * pieces_of
    width = frames + 2 * REACH

    def fetches(head):
        columns = columns_of(head)
        pairs = [
            (q_hbm.at[:, 0, :, columns_of(head + first_head)], q_ref.at[:, :, columns]),
            (left_hbm.at[:, :, :, columns], left.at[:, :, :, columns]),
            (right_hbm.at[:, :, :, columns], right.at[:, :, :, columns]),
        ]
        return [pltpu.make_async_copy(a, b, sems.at[head, i]) for i, (a, b) in enumerate(pairs)]

    def puts(head):
        columns = columns_of(head)
        return [pltpu.make_async_copy(out_ref.at[:, :, columns], out_hbm.at[:, :, columns], put_sems.at[head])]

    def item(frame, head):
        columns = columns_of(head)
        keys, values, masks = [], [], []
        for relative in [*range(-REACH, -near), *range(frames + near, frames + REACH)]:
            if abs(relative - frame) > REACH:
                continue
            codes = [code_ref[(frame * BPF + b) * width + relative + REACH] for b in range(BPF)]
            pick = jnp.maximum(codes[0], codes[1]) // 2
            if relative < 0:
                piece, place = left, (0 if relative == -REACH else (relative + REACH) * BPF - 1 + pick)
            else:
                first = (relative - frames - near) * BPF
                piece, place = right, (first if relative == frames + REACH - 1 else first + pick)
            keys.append(flat(piece[pl.ds(place * pieces_of, pieces_of), 0, :, columns]))
            values.append(flat(piece[pl.ds(place * pieces_of, pieces_of), 1, :, columns]))
            masks.append(mask_of(codes))
        queries = flat(q_ref[pl.ds(frame * per_frame, per_frame), :, columns])
        tiles = masked_scores(queries, keys, masks)
        near_top = top_ref[head, frame]
        tops = [jnp.maximum(largest(tiles[b]), near_top[b * BLK : (b + 1) * BLK]) for b in range(BPF)]
        mixed, totals = weighted(tiles, tops, values)
        shrink = jnp.exp2((near_top - jnp.concatenate(tops, axis=0)) * to_log2)
        result = (acc_ref[head, frame] * shrink + mixed) / (total_ref[head, frame] * shrink + totals)
        out_ref[pl.ds(frame * per_frame, per_frame), :, columns] = result.astype(jnp.bfloat16).reshape(
            per_frame, BLK // pieces_of, HD
        )

    def work(head):
        for frame in range(frames):
            item(frame, head)

    each_head(heads, fetches, puts, work)


def measured_cost(blocks):
    return dict(flops=6 * blocks * BPF * 4 * BLK * BLK * HD, bytes_accessed=1024, transcendentals=0)


def attend_near(codes, queries, pieces, frames, near, first_head, cost=None, after=()):
    members, _, rows, _ = queries.shape
    pieces_of = BLK // rows
    width = pieces[0].shape[3]
    heads = width // HD
    stored = sum(piece.shape[0] for piece in pieces)

    def body(code_ref, q_hbm, *refs):
        kept = refs[: len(pieces)] + refs[len(pieces) + len(after) :]
        near_kernel(frames, near, pieces_of, heads, first_head, code_ref, q_hbm, *kept)

    partial = jax.ShapeDtypeStruct((heads, frames, BPF * BLK, HD), jnp.float32)
    return pl.pallas_call(
        body,
        out_shape=[partial] * 3,
        in_specs=[pl.BlockSpec(memory_space=pltpu.SMEM)] + [anywhere] * (1 + len(pieces) + len(after)),
        out_specs=[in_vmem] * 3,
        scratch_shapes=[
            pltpu.VMEM((members, rows, width), jnp.bfloat16),
            pltpu.VMEM((stored, 2, rows, width), jnp.bfloat16),
            pltpu.SemaphoreType.DMA((heads, 1 + len(pieces))),
        ],
        compiler_params=pltpu.CompilerParams(vmem_limit_bytes=NEAR_VMEM),
        cost_estimate=pl.CostEstimate(**(cost or measured_cost(frames * heads * (frames + 2 * near + 1)))),
    )(codes, queries, *pieces, *after)


def attend_far(codes, queries, far, partials, frames, near, first_head, cost=None, after=()):
    members, _, rows, _ = queries.shape
    pieces_of = BLK // rows
    width = far[0].shape[3]
    heads = width // HD

    def body(code_ref, q_hbm, *refs):
        far_kernel(frames, near, pieces_of, heads, first_head, code_ref, q_hbm, *refs[:5], *refs[5 + len(after) :])

    result = jax.ShapeDtypeStruct((members, rows, width), jnp.bfloat16)
    return pl.pallas_call(
        body,
        out_shape=result,
        in_specs=[pl.BlockSpec(memory_space=pltpu.SMEM)] + [anywhere] * 3 + [in_vmem] * 3 + [anywhere] * len(after),
        out_specs=in_hbm,
        scratch_shapes=[
            pltpu.VMEM(result.shape, result.dtype),
            *[pltpu.VMEM(array.shape, array.dtype) for array in far],
            pltpu.VMEM(result.shape, result.dtype),
            pltpu.SemaphoreType.DMA((heads, 3)),
            pltpu.SemaphoreType.DMA((heads,)),
        ],
        compiler_params=pltpu.CompilerParams(vmem_limit_bytes=OTHER_VMEM),
        cost_estimate=pl.CostEstimate(**(cost or measured_cost(frames * heads * 4))),
    )(codes, queries, *far, *partials, *after)


def on_device(outer, inner, q_proj, k_proj, v_proj, kv_list):
    frames = inner
    rows, model_width = q_proj.shape
    team = ("inner", "rep", "uly")
    team_size = frames * BPF * BLK // rows
    heads_here = model_width // HD // team_size
    pieces_of = BLK // rows
    per_frame = BPF * pieces_of
    my_group = lax.axis_index("outer")

    def rows_of(reader_frame, count):
        start = jnp.clip(reader_frame * BPF, 0, kv_list.shape[0] - count * BPF)
        return lax.dynamic_slice_in_dim(kv_list, start, count * BPF, 0)

    lists = rows_of(my_group * frames, frames).reshape(frames * BPF, 1, -1)
    first_ids = BPF * (my_group * frames - REACH + lax.broadcasted_iota(jnp.int32, (1, frames + 2 * REACH, 1), 1))
    hits = jnp.where(lists == first_ids, 1, 0) + jnp.where(lists == first_ids + 1, 2, 0)
    codes = jnp.sum(jnp.where(lists >= 0, hits, 0), axis=-1).reshape(-1)

    def picked(reader_frame, holder_frame):
        return jnp.any(rows_of(reader_frame, 1) == holder_frame * BPF + 1).astype(jnp.int32)

    assert sum(CHUNKS) == heads_here
    widths = [heads * HD for heads in CHUNKS]
    lows = [sum(CHUNKS[:c]) for c in range(len(CHUNKS))]
    starts = [low * team_size * HD for low in lows]

    def exchange(array):
        return lax.all_to_all(array, team, split_axis=0, concat_axis=0, tiled=True)

    def shifted(array, heading, hop):
        places = range(outer)
        route = [(i, i + heading) for i in places if i + heading in places and i - (hop - 1) * heading in places]
        return lax.ppermute(array, "outer", route)

    hops = []
    for hop in range(1, -(-REACH // frames) + 1):
        spare = hop * frames - REACH
        hops.append((frames - max(0, spare), spare >= 0))

    def forwarded(held, held_frames, keep, single, after):
        whole = (keep - 1 if single else keep) * per_frame
        if single:
            from_left, from_right = (my_group + 1) * frames, my_group * frames - 1
            edges = held[0].shape[0] - whole - per_frame, whole
            edge_places = jnp.stack(
                [
                    edges[0] + pieces_of * picked(from_left, from_left - REACH),
                    edges[1] + pieces_of * picked(from_right, from_right + REACH),
                ]
            )
            return list(select(held, edge_places, pieces_of, whole, after))
        if keep < held_frames:
            return [held[0][held[0].shape[0] - whole :], held[1][:whole]]
        return held

    def first_hop(own):
        assert hops[0] == (frames, False)
        return [[shifted(own, 1, 1), shifted(own, -1, 1)]]

    def selected(arrivals, after=()):
        for hop in range(1, len(hops)):
            to_send = forwarded(arrivals[-1], hops[hop - 1][0], *hops[hop], after if hop == len(hops) - 1 else ())
            if hop < len(hops) - 1:
                arrivals.append([shifted(to_send[0], 1, hop + 1), shifted(to_send[1], -1, hop + 1)])
        return to_send

    def last_hop(arrivals, to_send):
        arrivals.append([shifted(to_send[0], 1, len(hops)), shifted(to_send[1], -1, len(hops))])

    chunks = range(len(CHUNKS))
    near = (len(hops) - 1) * frames
    packed = [pack([k_proj, v_proj], [starts[c]], [widths[c]], team_size) for c in chunks]
    owned = [exchange(array) for array in packed]
    queries = exchange(pack([q_proj], starts, widths, team_size, after=packed[-1:]))
    arrivals, sent, results, outs = [], [], [], []
    partials = {}

    def attend_rest(c, after, cost):
        result = attend_far(codes, queries, arrivals[c][-1], partials[c], frames, near, lows[c], cost, after=after)
        results.append(result)
        if outs:
            result, outs[-1] = lax.optimization_barrier((result, outs[-1]))
        outs.append(exchange(result))

    for c in chunks:
        arrivals.append(first_hop(owned[c]))
        sent.append(selected(arrivals[c], after=partials[c - 1] if c > 0 else ()))
        order = [a[0] for a in arrivals[c][::-1]] + [owned[c]] + [a[1] for a in arrivals[c]]
        last_hop(arrivals[c], sent[c])
        if c > 0:
            attend_rest(c - 1, sent[c], None)
        after = sent[c] + results[-1:]
        cost = little if c == len(CHUNKS) - 1 else None
        partials[c] = list(attend_near(codes, queries, order, frames, near, lows[c], cost, after=after))
    attend_rest(chunks[-1], (), little)
    return unpack(outs, starts, model_width)


def solution(mesh):
    sizes = dict(mesh.shape)
    members = sizes["uly"] * sizes["rep"]
    heads = 40
    inner = max(
        i for i in range(1, sizes["ctx"] + 1) if sizes["ctx"] % i == 0 and heads % (i * members) == 0
    )
    outer = sizes["ctx"] // inner
    finer = Mesh(
        mesh.devices.reshape(sizes["groups"], outer, inner, sizes["uly"], sizes["rep"]),
        ("groups", "outer", "inner", "uly", "rep"),
    )
    split = P(("groups", "outer", "inner", "rep", "uly"), None)
    return jax.shard_map(
        functools.partial(on_device, outer, inner),
        mesh=finer,
        in_specs=(split, split, split, P("groups", None)),
        out_specs=split,
        check_vma=False,
    )
```

```python
import functools
import math

import jax
import jax.numpy as jnp
from jax import lax
from jax.experimental import pallas as pl
from jax.experimental.pallas import tpu as pltpu
from jax.sharding import Mesh, PartitionSpec as P

HD = 128
BLK = 128
BPF = 2
REACH = 7
CHUNKS = (2, 3)
PACK_VMEM = 60 * 1024 * 1024
NEAR_VMEM = 24 * 1024 * 1024
OTHER_VMEM = 14 * 1024 * 1024
little = dict(flops=1024, bytes_accessed=1024, transcendentals=0)
some = dict(flops=20_000_000_000, bytes_accessed=1024, transcendentals=0)
much = dict(flops=100_000_000_000, bytes_accessed=1024, transcendentals=0)

very_low = -1e30
to_log2 = math.log2(math.e) * HD ** -0.5


def staged_copies(steps, sems):
    count = len(steps)
    fetches = [pltpu.make_async_copy(s, stage, sems.at[i]) for i, (s, stage, t) in enumerate(steps)]
    puts = [pltpu.make_async_copy(stage, t, sems.at[count + i]) for i, (s, stage, t) in enumerate(steps)]
    for fetch in fetches:
        fetch.start()
    for fetch, put in zip(fetches, puts):
        fetch.wait()
        put.start()
    for put in puts:
        put.wait()


anywhere = pl.BlockSpec(memory_space=pl.ANY)
in_hbm = pl.BlockSpec(memory_space=pltpu.HBM)
in_vmem = pl.BlockSpec(memory_space=pltpu.VMEM)


def copy_call(plan, shapes, count, operands, scalars=(), after=(), cost=little):
    def body(*refs):
        first = len(scalars)
        last = first + len(operands)
        results = refs[last + len(after) :]
        n = len(shapes)
        staged_copies(plan(refs[:first], refs[first:last], results[:n], results[n : 2 * n]), results[2 * n])

    return pl.pallas_call(
        body,
        out_shape=shapes,
        in_specs=[pl.BlockSpec(memory_space=pltpu.SMEM)] * len(scalars) + [anywhere] * (len(operands) + len(after)),
        out_specs=[anywhere] * len(shapes),
        scratch_shapes=[pltpu.VMEM(s.shape, s.dtype) for s in shapes] + [pltpu.SemaphoreType.DMA((2 * count,))],
        compiler_params=pltpu.CompilerParams(vmem_limit_bytes=OTHER_VMEM),
        cost_estimate=pl.CostEstimate(**cost),
    )(*scalars, *operands, *after)


def pack(arrays, starts, widths, team_size, after=()):
    rows = arrays[0].shape[0]
    lows = [sum(widths[:i]) for i in range(len(widths))]
    count = len(arrays) * len(starts)

    def body(*refs):
        sources = refs[: len(arrays)]
        out, *stages, sems = refs[len(arrays) + len(after) :]
        fetches, puts = [], []
        for kind, source in enumerate(sources):
            for number, (start, width, low) in enumerate(zip(starts, widths, lows)):
                stage = stages[number].at[kind]
                place = len(fetches)
                columns = pl.ds(start, team_size * width)
                fetches.append(pltpu.make_async_copy(source.at[:, columns], stage, sems.at[place, team_size]))
                puts.append(
                    [
                        pltpu.make_async_copy(
                            stage.at[:, pl.ds(member * width, width)],
                            out.at[member, kind, :, pl.ds(low, width)],
                            sems.at[place, member],
                        )
                        for member in range(team_size)
                    ]
                )
        for fetch in fetches:
            fetch.start()
        for fetch, some_puts in zip(fetches, puts):
            fetch.wait()
            for put in some_puts:
                put.start()
        for some_puts in puts:
            for put in some_puts:
                put.wait()

    return pl.pallas_call(
        body,
        out_shape=jax.ShapeDtypeStruct((team_size, len(arrays), rows, sum(widths)), jnp.bfloat16),
        in_specs=[anywhere] * (len(arrays) + len(after)),
        out_specs=anywhere,
        scratch_shapes=[
            *[pltpu.VMEM((len(arrays), rows, team_size * width), jnp.bfloat16) for width in widths],
            pltpu.SemaphoreType.DMA((count, team_size + 1)),
        ],
        compiler_params=pltpu.CompilerParams(vmem_limit_bytes=PACK_VMEM),
        cost_estimate=pl.CostEstimate(**some),
    )(*arrays, *after)


def unpack(parts, starts, model_width):
    members, rows, _ = parts[0].shape
    count = members * len(parts)

    def body(*refs):
        *sources, out, sems = refs
        puts = []
        for start, source in zip(starts, sources):
            width = source.shape[2]
            for member in range(members):
                columns = pl.ds(start + member * width, width)
                puts.append(pltpu.make_async_copy(source.at[member], out.at[:, columns], sems.at[len(puts)]))
                puts[-1].start()
        for put in puts:
            put.wait()

    return pl.pallas_call(
        body,
        out_shape=jax.ShapeDtypeStruct((rows, model_width), jnp.bfloat16),
        in_specs=[pl.BlockSpec(memory_space=pltpu.VMEM)] * len(parts),
        out_specs=in_hbm,
        scratch_shapes=[pltpu.SemaphoreType.DMA((count,))],
        compiler_params=pltpu.CompilerParams(vmem_limit_bytes=8 * 1024 * 1024),
        cost_estimate=pl.CostEstimate(**little),
    )(*parts)


def select(held, places, count, whole, after=()):
    def plan(scalars, sources, outs, stages):
        (place_ref,) = scalars
        steps = []
        for side, (source, stage, out) in enumerate(zip(sources, stages, outs)):
            one = pl.ds(0 if side == 0 else whole, count)
            steps.append((source.at[pl.ds(place_ref[side], count)], stage.at[one], out.at[one]))
            if whole > 0:
                rest = pl.ds(count if side == 0 else 0, whole)
                kept = pl.ds(source.shape[0] - whole if side == 0 else 0, whole)
                steps.append((source.at[kept], stage.at[rest], out.at[rest]))
        return steps

    shapes = [jax.ShapeDtypeStruct((count + whole,) + array.shape[1:], array.dtype) for array in held]
    return copy_call(plan, shapes, 2 * (2 if whole > 0 else 1), held, scalars=[places], after=after, cost=much)


def columns_of(head):
    return pl.ds(pl.multiple_of(head * HD, HD), HD)


def flat(rows):
    return rows.reshape(rows.shape[0] * rows.shape[1], HD)


def masked_scores(queries, keys, masks):
    tiles = [[] for _ in range(BPF)]
    for first in range(0, len(keys), 2):
        some = jnp.concatenate(keys[first : first + 2], axis=0)
        scores = lax.dot_general(queries, some, (((1,), (1,)), ((), ())), preferred_element_type=jnp.float32)
        for side, mask in enumerate(masks[first : first + 2]):
            for b in range(BPF):
                tile = scores[b * BLK : (b + 1) * BLK, side * BLK : (side + 1) * BLK]
                tiles[b].append(tile if mask is None else tile + mask[b])
    return tiles


def largest(tiles):
    return jnp.max(functools.reduce(jnp.maximum, tiles), axis=1, keepdims=True)


def weighted(tiles, tops, values):
    totals, weights = [], []
    for b in range(BPF):
        exps = [jnp.exp2((tile - tops[b]) * to_log2) for tile in tiles[b]]
        totals.append(jnp.sum(functools.reduce(jnp.add, exps), axis=1, keepdims=True))
        weights.append(jnp.concatenate([e.astype(jnp.bfloat16) for e in exps], axis=1))
    mixed = jnp.dot(
        jnp.concatenate(weights, axis=0), jnp.concatenate(values, axis=0), preferred_element_type=jnp.float32
    )
    return mixed, jnp.concatenate(totals, axis=0)


def mask_of(codes):
    return [jnp.where(code > 0, 0.0, very_low).astype(jnp.float32) for code in codes]


def each_head(heads, fetches, puts, work):
    for head in range(heads):
        for fetch in fetches(head):
            fetch.start()

    def one_head(head, carry):
        for fetch in fetches(head):
            fetch.wait()
        work(head)
        for put in puts(head):
            put.start()
        return carry

    lax.fori_loop(0, heads, one_head, 0)
    for head in range(heads):
        for put in puts(head):
            put.wait()


def near_kernel(frames, near, pieces_of, heads, first_head, code_ref, q_hbm, *refs):
    *piece_refs, acc_ref, top_ref, total_ref, q_ref, store, sems = refs
    per_frame = BPF * pieces_of
    width = frames + 2 * REACH

    def fetches(head):
        columns = columns_of(head)
        found = [(q_hbm.at[:, 0, :, columns_of(head + first_head)], q_ref.at[:, :, columns])]
        start = 0
        for piece in piece_refs:
            size = piece.shape[0]
            found.append((piece.at[:, :, :, columns], store.at[pl.ds(start, size), :, :, columns]))
            start += size
        return [pltpu.make_async_copy(a, b, sems.at[head, i]) for i, (a, b) in enumerate(found)]

    def item(frame, head):
        columns = columns_of(head)
        own = (frame + near) * BPF * pieces_of
        keys, values, masks = [], [], []
        for b in range(BPF):
            keys.append(flat(store[pl.ds(own + b * pieces_of, pieces_of), 0, :, columns]))
            values.append(flat(store[pl.ds(own + b * pieces_of, pieces_of), 1, :, columns]))
            masks.append(None)
        for other in range(frames + 2 * near - 1):
            relative = other - near
            relative = relative + jnp.where(relative >= frame, 1, 0)
            codes = [code_ref[(frame * BPF + b) * width + relative + REACH] for b in range(BPF)]
            pick = jnp.maximum(codes[0], codes[1]) // 2
            place = ((relative + near) * BPF + pick) * pieces_of
            keys.append(flat(store[pl.ds(place, pieces_of), 0, :, columns]))
            values.append(flat(store[pl.ds(place, pieces_of), 1, :, columns]))
            masks.append(mask_of(codes))
        queries = flat(q_ref[pl.ds(frame * per_frame, per_frame), :, columns])
        tiles = masked_scores(queries, keys, masks)
        tops = [largest(tiles[b]) for b in range(BPF)]
        mixed, totals = weighted(tiles, tops, values)
        acc_ref[head, frame] = mixed
        top_ref[head, frame] = jnp.broadcast_to(jnp.concatenate(tops, axis=0), mixed.shape)
        total_ref[head, frame] = jnp.broadcast_to(totals, mixed.shape)

    together = 2 if frames % 2 == 0 else 1

    def work(head):
        def step(index, carry):
            for offset in range(together):
                item(index * together + offset, head)
            return carry

        lax.fori_loop(0, frames // together, step, 0)

    each_head(heads, fetches, lambda head: [], work)


def far_kernel(frames, near, pieces_of, heads, first_head, code_ref, q_hbm, *refs):
    left_hbm, right_hbm, acc_ref, top_ref, total_ref, out_hbm, token, q_ref, left, right, out_ref, sems, put_sems = refs
    token[...] = jnp.zeros_like(token)
    per_frame = BPF * pieces_of
    width = frames + 2 * REACH

    def fetches(head):
        columns = columns_of(head)
        pairs = [
            (q_hbm.at[:, 0, :, columns_of(head + first_head)], q_ref.at[:, :, columns]),
            (left_hbm.at[:, :, :, columns], left.at[:, :, :, columns]),
            (right_hbm.at[:, :, :, columns], right.at[:, :, :, columns]),
        ]
        return [pltpu.make_async_copy(a, b, sems.at[head, i]) for i, (a, b) in enumerate(pairs)]

    def puts(head):
        columns = columns_of(head)
        return [pltpu.make_async_copy(out_ref.at[:, :, columns], out_hbm.at[:, :, columns], put_sems.at[head])]

    def item(frame, head):
        columns = columns_of(head)
        keys, values, masks = [], [], []
        for relative in [*range(-REACH, -near), *range(frames + near, frames + REACH)]:
            if abs(relative - frame) > REACH:
                continue
            codes = [code_ref[(frame * BPF + b) * width + relative + REACH] for b in range(BPF)]
            pick = jnp.maximum(codes[0], codes[1]) // 2
            if relative < 0:
                piece, place = left, (0 if relative == -REACH else (relative + REACH) * BPF - 1 + pick)
            else:
                first = (relative - frames - near) * BPF
                piece, place = right, (first if relative == frames + REACH - 1 else first + pick)
            keys.append(flat(piece[pl.ds(place * pieces_of, pieces_of), 0, :, columns]))
            values.append(flat(piece[pl.ds(place * pieces_of, pieces_of), 1, :, columns]))
            masks.append(mask_of(codes))
        queries = flat(q_ref[pl.ds(frame * per_frame, per_frame), :, columns])
        tiles = masked_scores(queries, keys, masks)
        near_top = top_ref[head, frame]
        tops = [jnp.maximum(largest(tiles[b]), near_top[b * BLK : (b + 1) * BLK]) for b in range(BPF)]
        mixed, totals = weighted(tiles, tops, values)
        shrink = jnp.exp2((near_top - jnp.concatenate(tops, axis=0)) * to_log2)
        result = (acc_ref[head, frame] * shrink + mixed) / (total_ref[head, frame] * shrink + totals)
        out_ref[pl.ds(frame * per_frame, per_frame), :, columns] = result.astype(jnp.bfloat16).reshape(
            per_frame, BLK // pieces_of, HD
        )

    def work(head):
        for frame in range(frames):
            item(frame, head)

    each_head(heads, fetches, puts, work)


def measured_cost(blocks):
    return dict(flops=6 * blocks * BPF * 4 * BLK * BLK * HD, bytes_accessed=1024, transcendentals=0)


def attend_near(codes, queries, pieces, frames, near, first_head, cost=None, after=()):
    members, _, rows, _ = queries.shape
    pieces_of = BLK // rows
    width = pieces[0].shape[3]
    heads = width // HD
    stored = sum(piece.shape[0] for piece in pieces)

    def body(code_ref, q_hbm, *refs):
        kept = refs[: len(pieces)] + refs[len(pieces) + len(after) :]
        near_kernel(frames, near, pieces_of, heads, first_head, code_ref, q_hbm, *kept)

    partial = jax.ShapeDtypeStruct((heads, frames, BPF * BLK, HD), jnp.float32)
    return pl.pallas_call(
        body,
        out_shape=[partial] * 3,
        in_specs=[pl.BlockSpec(memory_space=pltpu.SMEM)] + [anywhere] * (1 + len(pieces) + len(after)),
        out_specs=[in_vmem] * 3,
        scratch_shapes=[
            pltpu.VMEM((members, rows, width), jnp.bfloat16),
            pltpu.VMEM((stored, 2, rows, width), jnp.bfloat16),
            pltpu.SemaphoreType.DMA((heads, 1 + len(pieces))),
        ],
        compiler_params=pltpu.CompilerParams(vmem_limit_bytes=NEAR_VMEM),
        cost_estimate=pl.CostEstimate(**(cost or measured_cost(frames * heads * (frames + 2 * near + 1)))),
    )(codes, queries, *pieces, *after)


def attend_far(codes, queries, far, partials, frames, near, first_head, cost=None, after=()):
    members, _, rows, _ = queries.shape
    pieces_of = BLK // rows
    width = far[0].shape[3]
    heads = width // HD

    def body(code_ref, q_hbm, *refs):
        far_kernel(frames, near, pieces_of, heads, first_head, code_ref, q_hbm, *refs[:5], *refs[5 + len(after) :])

    result = jax.ShapeDtypeStruct((members, rows, width), jnp.bfloat16)
    return pl.pallas_call(
        body,
        out_shape=[result, jax.ShapeDtypeStruct((8, 128), jnp.float32)],
        in_specs=[pl.BlockSpec(memory_space=pltpu.SMEM)] + [anywhere] * 3 + [in_vmem] * 3 + [anywhere] * len(after),
        out_specs=[in_hbm, in_vmem],
        scratch_shapes=[
            pltpu.VMEM(result.shape, result.dtype),
            *[pltpu.VMEM(array.shape, array.dtype) for array in far],
            pltpu.VMEM(result.shape, result.dtype),
            pltpu.SemaphoreType.DMA((heads, 3)),
            pltpu.SemaphoreType.DMA((heads,)),
        ],
        compiler_params=pltpu.CompilerParams(vmem_limit_bytes=OTHER_VMEM),
        cost_estimate=pl.CostEstimate(**(cost or measured_cost(frames * heads * 4))),
    )(codes, queries, *far, *partials, *after)


def on_device(outer, inner, q_proj, k_proj, v_proj, kv_list):
    frames = inner
    rows, model_width = q_proj.shape
    team = ("inner", "rep", "uly")
    team_size = frames * BPF * BLK // rows
    heads_here = model_width // HD // team_size
    pieces_of = BLK // rows
    per_frame = BPF * pieces_of
    my_group = lax.axis_index("outer")

    def rows_of(reader_frame, count):
        start = jnp.clip(reader_frame * BPF, 0, kv_list.shape[0] - count * BPF)
        return lax.dynamic_slice_in_dim(kv_list, start, count * BPF, 0)

    lists = rows_of(my_group * frames, frames).reshape(frames * BPF, 1, -1)
    first_ids = BPF * (my_group * frames - REACH + lax.broadcasted_iota(jnp.int32, (1, frames + 2 * REACH, 1), 1))
    hits = jnp.where(lists == first_ids, 1, 0) + jnp.where(lists == first_ids + 1, 2, 0)
    codes = jnp.sum(jnp.where(lists >= 0, hits, 0), axis=-1).reshape(-1)

    def picked(reader_frame, holder_frame):
        return jnp.any(rows_of(reader_frame, 1) == holder_frame * BPF + 1).astype(jnp.int32)

    assert sum(CHUNKS) == heads_here
    widths = [heads * HD for heads in CHUNKS]
    lows = [sum(CHUNKS[:c]) for c in range(len(CHUNKS))]
    starts = [low * team_size * HD for low in lows]

    def exchange(array):
        return lax.all_to_all(array, team, split_axis=0, concat_axis=0, tiled=True)

    def shifted(array, heading, hop):
        places = range(outer)
        route = [(i, i + heading) for i in places if i + heading in places and i - (hop - 1) * heading in places]
        return lax.ppermute(array, "outer", route)

    hops = []
    for hop in range(1, -(-REACH // frames) + 1):
        spare = hop * frames - REACH
        hops.append((frames - max(0, spare), spare >= 0))

    def forwarded(held, held_frames, keep, single, after):
        whole = (keep - 1 if single else keep) * per_frame
        if single:
            from_left, from_right = (my_group + 1) * frames, my_group * frames - 1
            edges = held[0].shape[0] - whole - per_frame, whole
            edge_places = jnp.stack(
                [
                    edges[0] + pieces_of * picked(from_left, from_left - REACH),
                    edges[1] + pieces_of * picked(from_right, from_right + REACH),
                ]
            )
            return list(select(held, edge_places, pieces_of, whole, after))
        if keep < held_frames:
            return [held[0][held[0].shape[0] - whole :], held[1][:whole]]
        return held

    def first_hop(own):
        assert hops[0] == (frames, False)
        return [[shifted(own, 1, 1), shifted(own, -1, 1)]]

    def selected(arrivals, after=()):
        for hop in range(1, len(hops)):
            to_send = forwarded(arrivals[-1], hops[hop - 1][0], *hops[hop], after if hop == len(hops) - 1 else ())
            if hop < len(hops) - 1:
                arrivals.append([shifted(to_send[0], 1, hop + 1), shifted(to_send[1], -1, hop + 1)])
        return to_send

    def last_hop(arrivals, to_send):
        arrivals.append([shifted(to_send[0], 1, len(hops)), shifted(to_send[1], -1, len(hops))])

    chunks = range(len(CHUNKS))
    near = (len(hops) - 1) * frames
    packed = [pack([k_proj, v_proj], [starts[c]], [widths[c]], team_size) for c in chunks]
    owned = [exchange(array) for array in packed]
    queries = exchange(pack([q_proj], starts, widths, team_size, after=packed[-1:]))
    arrivals, sent, tokens, outs = [], [], [], []
    partials = {}

    def attend_rest(c, after, cost):
        far = arrivals[c][-1]
        result, token = attend_far(codes, queries, far, partials[c], frames, near, lows[c], cost, after=after)
        tokens.append(token)
        if outs:
            result, outs[-1] = lax.optimization_barrier((result, outs[-1]))
        outs.append(exchange(result))

    for c in chunks:
        arrivals.append(first_hop(owned[c]))
        sent.append(selected(arrivals[c], after=partials[c - 1] if c > 0 else ()))
        order = [a[0] for a in arrivals[c][::-1]] + [owned[c]] + [a[1] for a in arrivals[c]]
        last_hop(arrivals[c], sent[c])
        if c > 0:
            attend_rest(c - 1, sent[c], None)
        after = sent[c] + tokens[-1:]
        cost = little if c == len(CHUNKS) - 1 else None
        partials[c] = list(attend_near(codes, queries, order, frames, near, lows[c], cost, after=after))
    attend_rest(chunks[-1], (), little)
    return unpack(outs, starts, model_width)


def solution(mesh):
    sizes = dict(mesh.shape)
    members = sizes["uly"] * sizes["rep"]
    heads = 40
    inner = max(
        i for i in range(1, sizes["ctx"] + 1) if sizes["ctx"] % i == 0 and heads % (i * members) == 0
    )
    outer = sizes["ctx"] // inner
    finer = Mesh(
        mesh.devices.reshape(sizes["groups"], outer, inner, sizes["uly"], sizes["rep"]),
        ("groups", "outer", "inner", "uly", "rep"),
    )
    split = P(("groups", "outer", "inner", "rep", "uly"), None)
    return jax.shard_map(
        functools.partial(on_device, outer, inner),
        mesh=finer,
        in_specs=(split, split, split, P("groups", None)),
        out_specs=split,
        check_vma=False,
    )
```

```python
import functools
import math

import jax
import jax.numpy as jnp
from jax import lax
from jax.experimental import pallas as pl
from jax.experimental.pallas import tpu as pltpu
from jax.sharding import Mesh, PartitionSpec as P

HD = 128
BLK = 128
BPF = 2
REACH = 7
CHUNKS = (2, 3)
PACK_VMEM = 60 * 1024 * 1024
NEAR_VMEM = 24 * 1024 * 1024
OTHER_VMEM = 14 * 1024 * 1024
little = dict(flops=1024, bytes_accessed=1024, transcendentals=0)
some = dict(flops=20_000_000_000, bytes_accessed=1024, transcendentals=0)
much = dict(flops=100_000_000_000, bytes_accessed=1024, transcendentals=0)

very_low = -1e30
to_log2 = math.log2(math.e) * HD ** -0.5


def staged_copies(steps, sems):
    count = len(steps)
    fetches = [pltpu.make_async_copy(s, stage, sems.at[i]) for i, (s, stage, t) in enumerate(steps)]
    puts = [pltpu.make_async_copy(stage, t, sems.at[count + i]) for i, (s, stage, t) in enumerate(steps)]
    for fetch in fetches:
        fetch.start()
    for fetch, put in zip(fetches, puts):
        fetch.wait()
        put.start()
    for put in puts:
        put.wait()


anywhere = pl.BlockSpec(memory_space=pl.ANY)
in_hbm = pl.BlockSpec(memory_space=pltpu.HBM)
in_vmem = pl.BlockSpec(memory_space=pltpu.VMEM)


def copy_call(plan, shapes, count, operands, scalars=(), after=(), cost=little):
    def body(*refs):
        first = len(scalars)
        last = first + len(operands)
        results = refs[last + len(after) :]
        n = len(shapes)
        staged_copies(plan(refs[:first], refs[first:last], results[:n], results[n : 2 * n]), results[2 * n])

    return pl.pallas_call(
        body,
        out_shape=shapes,
        in_specs=[pl.BlockSpec(memory_space=pltpu.SMEM)] * len(scalars) + [anywhere] * (len(operands) + len(after)),
        out_specs=[anywhere] * len(shapes),
        scratch_shapes=[pltpu.VMEM(s.shape, s.dtype) for s in shapes] + [pltpu.SemaphoreType.DMA((2 * count,))],
        compiler_params=pltpu.CompilerParams(vmem_limit_bytes=OTHER_VMEM),
        cost_estimate=pl.CostEstimate(**cost),
    )(*scalars, *operands, *after)


def pack(arrays, starts, widths, team_size, after=()):
    rows = arrays[0].shape[0]
    lows = [sum(widths[:i]) for i in range(len(widths))]
    count = len(arrays) * len(starts)

    def body(*refs):
        sources = refs[: len(arrays)]
        out, *stages, sems = refs[len(arrays) + len(after) :]
        fetches, puts = [], []
        for kind, source in enumerate(sources):
            for number, (start, width, low) in enumerate(zip(starts, widths, lows)):
                stage = stages[number].at[kind]
                place = len(fetches)
                columns = pl.ds(start, team_size * width)
                fetches.append(pltpu.make_async_copy(source.at[:, columns], stage, sems.at[place, team_size]))
                puts.append(
                    [
                        pltpu.make_async_copy(
                            stage.at[:, pl.ds(member * width, width)],
                            out.at[member, kind, :, pl.ds(low, width)],
                            sems.at[place, member],
                        )
                        for member in range(team_size)
                    ]
                )
        for fetch in fetches:
            fetch.start()
        for fetch, some_puts in zip(fetches, puts):
            fetch.wait()
            for put in some_puts:
                put.start()
        for some_puts in puts:
            for put in some_puts:
                put.wait()

    return pl.pallas_call(
        body,
        out_shape=jax.ShapeDtypeStruct((team_size, len(arrays), rows, sum(widths)), jnp.bfloat16),
        in_specs=[anywhere] * (len(arrays) + len(after)),
        out_specs=anywhere,
        scratch_shapes=[
            *[pltpu.VMEM((len(arrays), rows, team_size * width), jnp.bfloat16) for width in widths],
            pltpu.SemaphoreType.DMA((count, team_size + 1)),
        ],
        compiler_params=pltpu.CompilerParams(vmem_limit_bytes=PACK_VMEM),
        cost_estimate=pl.CostEstimate(**some),
    )(*arrays, *after)


def unpack(parts, starts, model_width):
    members, rows, _ = parts[0].shape
    count = members * len(parts)

    def body(*refs):
        *sources, out, sems = refs
        puts = []
        for start, source in zip(starts, sources):
            width = source.shape[2]
            for member in range(members):
                columns = pl.ds(start + member * width, width)
                puts.append(pltpu.make_async_copy(source.at[member], out.at[:, columns], sems.at[len(puts)]))
                puts[-1].start()
        for put in puts:
            put.wait()

    return pl.pallas_call(
        body,
        out_shape=jax.ShapeDtypeStruct((rows, model_width), jnp.bfloat16),
        in_specs=[pl.BlockSpec(memory_space=pltpu.VMEM)] * len(parts),
        out_specs=in_hbm,
        scratch_shapes=[pltpu.SemaphoreType.DMA((count,))],
        compiler_params=pltpu.CompilerParams(vmem_limit_bytes=8 * 1024 * 1024),
        cost_estimate=pl.CostEstimate(**little),
    )(*parts)


def select(held, places, count, whole, after=()):
    def plan(scalars, sources, outs, stages):
        (place_ref,) = scalars
        steps = []
        for side, (source, stage, out) in enumerate(zip(sources, stages, outs)):
            one = pl.ds(0 if side == 0 else whole, count)
            steps.append((source.at[pl.ds(place_ref[side], count)], stage.at[one], out.at[one]))
            for low in range(0, whole, count):
                rest = pl.ds(low + (count if side == 0 else 0), count)
                kept = pl.ds(low + (source.shape[0] - whole if side == 0 else 0), count)
                steps.append((source.at[kept], stage.at[rest], out.at[rest]))
        return steps

    shapes = [jax.ShapeDtypeStruct((count + whole,) + array.shape[1:], array.dtype) for array in held]
    return copy_call(plan, shapes, 2 * (1 + whole // count), held, scalars=[places], after=after, cost=much)


def columns_of(head):
    return pl.ds(pl.multiple_of(head * HD, HD), HD)


def flat(rows):
    return rows.reshape(rows.shape[0] * rows.shape[1], HD)


def masked_scores(queries, keys, masks):
    tiles = [[] for _ in range(BPF)]
    for first in range(0, len(keys), 2):
        some = jnp.concatenate(keys[first : first + 2], axis=0)
        scores = lax.dot_general(queries, some, (((1,), (1,)), ((), ())), preferred_element_type=jnp.float32)
        for side, mask in enumerate(masks[first : first + 2]):
            for b in range(BPF):
                tile = scores[b * BLK : (b + 1) * BLK, side * BLK : (side + 1) * BLK]
                tiles[b].append(tile if mask is None else tile + mask[b])
    return tiles


def largest(tiles):
    return jnp.max(functools.reduce(jnp.maximum, tiles), axis=1, keepdims=True)


def weighted(tiles, tops, values):
    totals, weights = [], []
    for b in range(BPF):
        exps = [jnp.exp2((tile - tops[b]) * to_log2) for tile in tiles[b]]
        totals.append(jnp.sum(functools.reduce(jnp.add, exps), axis=1, keepdims=True))
        weights.append(jnp.concatenate([e.astype(jnp.bfloat16) for e in exps], axis=1))
    mixed = jnp.dot(
        jnp.concatenate(weights, axis=0), jnp.concatenate(values, axis=0), preferred_element_type=jnp.float32
    )
    return mixed, jnp.concatenate(totals, axis=0)


def mask_of(codes):
    return [jnp.where(code > 0, 0.0, very_low).astype(jnp.float32) for code in codes]


def each_head(heads, fetches, puts, work):
    for head in range(heads):
        for fetch in fetches(head):
            fetch.start()

    def one_head(head, carry):
        for fetch in fetches(head):
            fetch.wait()
        work(head)
        for put in puts(head):
            put.start()
        return carry

    lax.fori_loop(0, heads, one_head, 0)
    for head in range(heads):
        for put in puts(head):
            put.wait()


def near_kernel(frames, near, pieces_of, heads, first_head, code_ref, q_hbm, *refs):
    *piece_refs, acc_ref, top_ref, total_ref, q_ref, store, sems = refs
    per_frame = BPF * pieces_of
    width = frames + 2 * REACH

    def fetches(head):
        columns = columns_of(head)
        found = [(q_hbm.at[:, 0, :, columns_of(head + first_head)], q_ref.at[:, :, columns])]
        start = 0
        for piece in piece_refs:
            size = piece.shape[0]
            found.append((piece.at[:, :, :, columns], store.at[pl.ds(start, size), :, :, columns]))
            start += size
        return [pltpu.make_async_copy(a, b, sems.at[head, i]) for i, (a, b) in enumerate(found)]

    def item(frame, head):
        columns = columns_of(head)
        own = (frame + near) * BPF * pieces_of
        keys, values, masks = [], [], []
        for b in range(BPF):
            keys.append(flat(store[pl.ds(own + b * pieces_of, pieces_of), 0, :, columns]))
            values.append(flat(store[pl.ds(own + b * pieces_of, pieces_of), 1, :, columns]))
            masks.append(None)
        for other in range(frames + 2 * near - 1):
            relative = other - near
            relative = relative + jnp.where(relative >= frame, 1, 0)
            codes = [code_ref[(frame * BPF + b) * width + relative + REACH] for b in range(BPF)]
            pick = jnp.maximum(codes[0], codes[1]) // 2
            place = ((relative + near) * BPF + pick) * pieces_of
            keys.append(flat(store[pl.ds(place, pieces_of), 0, :, columns]))
            values.append(flat(store[pl.ds(place, pieces_of), 1, :, columns]))
            masks.append(mask_of(codes))
        queries = flat(q_ref[pl.ds(frame * per_frame, per_frame), :, columns])
        tiles = masked_scores(queries, keys, masks)
        tops = [largest(tiles[b]) for b in range(BPF)]
        mixed, totals = weighted(tiles, tops, values)
        acc_ref[head, frame] = mixed
        top_ref[head, frame] = jnp.broadcast_to(jnp.concatenate(tops, axis=0), mixed.shape)
        total_ref[head, frame] = jnp.broadcast_to(totals, mixed.shape)

    together = math.gcd(frames, 4)

    def work(head):
        def step(index, carry):
            for offset in range(together):
                item(index * together + offset, head)
            return carry

        lax.fori_loop(0, frames // together, step, 0)

    each_head(heads, fetches, lambda head: [], work)


def far_kernel(frames, near, pieces_of, heads, first_head, code_ref, q_hbm, *refs):
    left_hbm, right_hbm, acc_ref, top_ref, total_ref, out_hbm, token, q_ref, left, right, out_ref, sems, put_sems = refs
    token[...] = jnp.zeros_like(token)
    per_frame = BPF * pieces_of
    width = frames + 2 * REACH

    def fetches(head):
        columns = columns_of(head)
        pairs = [
            (q_hbm.at[:, 0, :, columns_of(head + first_head)], q_ref.at[:, :, columns]),
            (left_hbm.at[:, :, :, columns], left.at[:, :, :, columns]),
            (right_hbm.at[:, :, :, columns], right.at[:, :, :, columns]),
        ]
        return [pltpu.make_async_copy(a, b, sems.at[head, i]) for i, (a, b) in enumerate(pairs)]

    def puts(head):
        columns = columns_of(head)
        return [pltpu.make_async_copy(out_ref.at[:, :, columns], out_hbm.at[:, :, columns], put_sems.at[head])]

    def item(frame, head):
        columns = columns_of(head)
        keys, values, masks = [], [], []
        for relative in [*range(-REACH, -near), *range(frames + near, frames + REACH)]:
            if abs(relative - frame) > REACH:
                continue
            codes = [code_ref[(frame * BPF + b) * width + relative + REACH] for b in range(BPF)]
            pick = jnp.maximum(codes[0], codes[1]) // 2
            if relative < 0:
                piece, place = left, (0 if relative == -REACH else (relative + REACH) * BPF - 1 + pick)
            else:
                first = (relative - frames - near) * BPF
                piece, place = right, (first if relative == frames + REACH - 1 else first + pick)
            keys.append(flat(piece[pl.ds(place * pieces_of, pieces_of), 0, :, columns]))
            values.append(flat(piece[pl.ds(place * pieces_of, pieces_of), 1, :, columns]))
            masks.append(mask_of(codes))
        queries = flat(q_ref[pl.ds(frame * per_frame, per_frame), :, columns])
        tiles = masked_scores(queries, keys, masks)
        near_top = top_ref[head, frame]
        tops = [jnp.maximum(largest(tiles[b]), near_top[b * BLK : (b + 1) * BLK]) for b in range(BPF)]
        mixed, totals = weighted(tiles, tops, values)
        shrink = jnp.exp2((near_top - jnp.concatenate(tops, axis=0)) * to_log2)
        result = (acc_ref[head, frame] * shrink + mixed) / (total_ref[head, frame] * shrink + totals)
        out_ref[pl.ds(frame * per_frame, per_frame), :, columns] = result.astype(jnp.bfloat16).reshape(
            per_frame, BLK // pieces_of, HD
        )

    def work(head):
        for frame in range(frames):
            item(frame, head)

    each_head(heads, fetches, puts, work)


def measured_cost(blocks):
    return dict(flops=6 * blocks * BPF * 4 * BLK * BLK * HD, bytes_accessed=1024, transcendentals=0)


def attend_near(codes, queries, pieces, frames, near, first_head, cost=None, after=()):
    members, _, rows, _ = queries.shape
    pieces_of = BLK // rows
    width = pieces[0].shape[3]
    heads = width // HD
    stored = sum(piece.shape[0] for piece in pieces)

    def body(code_ref, q_hbm, *refs):
        kept = refs[: len(pieces)] + refs[len(pieces) + len(after) :]
        near_kernel(frames, near, pieces_of, heads, first_head, code_ref, q_hbm, *kept)

    partial = jax.ShapeDtypeStruct((heads, frames, BPF * BLK, HD), jnp.float32)
    return pl.pallas_call(
        body,
        out_shape=[partial] * 3,
        in_specs=[pl.BlockSpec(memory_space=pltpu.SMEM)] + [anywhere] * (1 + len(pieces) + len(after)),
        out_specs=[in_vmem] * 3,
        scratch_shapes=[
            pltpu.VMEM((members, rows, width), jnp.bfloat16),
            pltpu.VMEM((stored, 2, rows, width), jnp.bfloat16),
            pltpu.SemaphoreType.DMA((heads, 1 + len(pieces))),
        ],
        compiler_params=pltpu.CompilerParams(vmem_limit_bytes=NEAR_VMEM),
        cost_estimate=pl.CostEstimate(**(cost or measured_cost(frames * heads * (frames + 2 * near + 1)))),
    )(codes, queries, *pieces, *after)


def attend_far(codes, queries, far, partials, frames, near, first_head, cost=None, after=()):
    members, _, rows, _ = queries.shape
    pieces_of = BLK // rows
    width = far[0].shape[3]
    heads = width // HD

    def body(code_ref, q_hbm, *refs):
        far_kernel(frames, near, pieces_of, heads, first_head, code_ref, q_hbm, *refs[:5], *refs[5 + len(after) :])

    result = jax.ShapeDtypeStruct((members, rows, width), jnp.bfloat16)
    return pl.pallas_call(
        body,
        out_shape=[result, jax.ShapeDtypeStruct((8, 128), jnp.float32)],
        in_specs=[pl.BlockSpec(memory_space=pltpu.SMEM)] + [anywhere] * 3 + [in_vmem] * 3 + [anywhere] * len(after),
        out_specs=[in_hbm, in_vmem],
        scratch_shapes=[
            pltpu.VMEM(result.shape, result.dtype),
            *[pltpu.VMEM(array.shape, array.dtype) for array in far],
            pltpu.VMEM(result.shape, result.dtype),
            pltpu.SemaphoreType.DMA((heads, 3)),
            pltpu.SemaphoreType.DMA((heads,)),
        ],
        compiler_params=pltpu.CompilerParams(vmem_limit_bytes=OTHER_VMEM),
        cost_estimate=pl.CostEstimate(**(cost or measured_cost(frames * heads * 4))),
    )(codes, queries, *far, *partials, *after)


def on_device(outer, inner, q_proj, k_proj, v_proj, kv_list):
    frames = inner
    rows, model_width = q_proj.shape
    team = ("inner", "rep", "uly")
    team_size = frames * BPF * BLK // rows
    heads_here = model_width // HD // team_size
    pieces_of = BLK // rows
    per_frame = BPF * pieces_of
    my_group = lax.axis_index("outer")

    def rows_of(reader_frame, count):
        start = jnp.clip(reader_frame * BPF, 0, kv_list.shape[0] - count * BPF)
        return lax.dynamic_slice_in_dim(kv_list, start, count * BPF, 0)

    lists = rows_of(my_group * frames, frames).reshape(frames * BPF, 1, -1)
    first_ids = BPF * (my_group * frames - REACH + lax.broadcasted_iota(jnp.int32, (1, frames + 2 * REACH, 1), 1))
    hits = jnp.where(lists == first_ids, 1, 0) + jnp.where(lists == first_ids + 1, 2, 0)
    codes = jnp.sum(jnp.where(lists >= 0, hits, 0), axis=-1).reshape(-1)

    def picked(reader_frame, holder_frame):
        return jnp.any(rows_of(reader_frame, 1) == holder_frame * BPF + 1).astype(jnp.int32)

    assert sum(CHUNKS) == heads_here
    widths = [heads * HD for heads in CHUNKS]
    lows = [sum(CHUNKS[:c]) for c in range(len(CHUNKS))]
    starts = [low * team_size * HD for low in lows]

    def exchange(array):
        return lax.all_to_all(array, team, split_axis=0, concat_axis=0, tiled=True)

    def shifted(array, heading, hop):
        places = range(outer)
        route = [(i, i + heading) for i in places if i + heading in places and i - (hop - 1) * heading in places]
        return lax.ppermute(array, "outer", route)

    hops = []
    for hop in range(1, -(-REACH // frames) + 1):
        spare = hop * frames - REACH
        hops.append((frames - max(0, spare), spare >= 0))

    def forwarded(held, held_frames, keep, single, after):
        whole = (keep - 1 if single else keep) * per_frame
        if single:
            from_left, from_right = (my_group + 1) * frames, my_group * frames - 1
            edges = held[0].shape[0] - whole - per_frame, whole
            edge_places = jnp.stack(
                [
                    edges[0] + pieces_of * picked(from_left, from_left - REACH),
                    edges[1] + pieces_of * picked(from_right, from_right + REACH),
                ]
            )
            return list(select(held, edge_places, pieces_of, whole, after))
        if keep < held_frames:
            return [held[0][held[0].shape[0] - whole :], held[1][:whole]]
        return held

    def first_hop(own):
        assert hops[0] == (frames, False)
        return [[shifted(own, 1, 1), shifted(own, -1, 1)]]

    def selected(arrivals, after=()):
        for hop in range(1, len(hops)):
            to_send = forwarded(arrivals[-1], hops[hop - 1][0], *hops[hop], after if hop == len(hops) - 1 else ())
            if hop < len(hops) - 1:
                arrivals.append([shifted(to_send[0], 1, hop + 1), shifted(to_send[1], -1, hop + 1)])
        return to_send

    def last_hop(arrivals, to_send):
        arrivals.append([shifted(to_send[0], 1, len(hops)), shifted(to_send[1], -1, len(hops))])

    chunks = range(len(CHUNKS))
    near = (len(hops) - 1) * frames
    packed = [pack([k_proj, v_proj], [starts[c]], [widths[c]], team_size) for c in chunks]
    owned = [exchange(array) for array in packed]
    queries = exchange(pack([q_proj], starts, widths, team_size, after=packed[-1:]))
    arrivals, sent, tokens, outs = [], [], [], []
    partials = {}

    def attend_rest(c, after, cost):
        far = arrivals[c][-1]
        result, token = attend_far(codes, queries, far, partials[c], frames, near, lows[c], cost, after=after)
        tokens.append(token)
        if outs:
            result, outs[-1] = lax.optimization_barrier((result, outs[-1]))
        outs.append(exchange(result))

    for c in chunks:
        arrivals.append(first_hop(owned[c]))
        sent.append(selected(arrivals[c], after=partials[c - 1] if c > 0 else ()))
        order = [a[0] for a in arrivals[c][::-1]] + [owned[c]] + [a[1] for a in arrivals[c]]
        last_hop(arrivals[c], sent[c])
        if c > 0:
            attend_rest(c - 1, sent[c], None)
        after = sent[c] + tokens[-1:]
        cost = little if c == len(CHUNKS) - 1 else None
        partials[c] = list(attend_near(codes, queries, order, frames, near, lows[c], cost, after=after))
    attend_rest(chunks[-1], (), little)
    return unpack(outs, starts, model_width)


def solution(mesh):
    sizes = dict(mesh.shape)
    members = sizes["uly"] * sizes["rep"]
    heads = 40
    inner = max(
        i for i in range(1, sizes["ctx"] + 1) if sizes["ctx"] % i == 0 and heads % (i * members) == 0
    )
    outer = sizes["ctx"] // inner
    finer = Mesh(
        mesh.devices.reshape(sizes["groups"], outer, inner, sizes["uly"], sizes["rep"]),
        ("groups", "outer", "inner", "uly", "rep"),
    )
    split = P(("groups", "outer", "inner", "rep", "uly"), None)
    return jax.shard_map(
        functools.partial(on_device, outer, inner),
        mesh=finer,
        in_specs=(split, split, split, P("groups", None)),
        out_specs=split,
        check_vma=False,
    )
```

```python
import functools
import math

import jax
import jax.numpy as jnp
from jax import lax
from jax.experimental import pallas as pl
from jax.experimental.pallas import tpu as pltpu
from jax.sharding import Mesh, PartitionSpec as P

HD = 128
BLK = 128
BPF = 2
REACH = 7
CHUNKS = (2, 3)
PACK_VMEM = 60 * 1024 * 1024
NEAR_VMEM = 24 * 1024 * 1024
OTHER_VMEM = 14 * 1024 * 1024
FAR_VMEM = 58 * 1024 * 1024 + 512 * 1024
little = dict(flops=1024, bytes_accessed=1024, transcendentals=0)
some = dict(flops=20_000_000_000, bytes_accessed=1024, transcendentals=0)
much = dict(flops=100_000_000_000, bytes_accessed=1024, transcendentals=0)

very_low = -1e30
to_log2 = math.log2(math.e) * HD ** -0.5


def staged_copies(steps, sems):
    count = len(steps)
    fetches = [pltpu.make_async_copy(s, stage, sems.at[i]) for i, (s, stage, t) in enumerate(steps)]
    puts = [pltpu.make_async_copy(stage, t, sems.at[count + i]) for i, (s, stage, t) in enumerate(steps)]
    for fetch in fetches:
        fetch.start()
    for fetch, put in zip(fetches, puts):
        fetch.wait()
        put.start()
    for put in puts:
        put.wait()


anywhere = pl.BlockSpec(memory_space=pl.ANY)
in_hbm = pl.BlockSpec(memory_space=pltpu.HBM)
in_vmem = pl.BlockSpec(memory_space=pltpu.VMEM)


def copy_call(plan, shapes, count, operands, scalars=(), after=(), cost=little):
    def body(*refs):
        first = len(scalars)
        last = first + len(operands)
        results = refs[last + len(after) :]
        n = len(shapes)
        staged_copies(plan(refs[:first], refs[first:last], results[:n], results[n : 2 * n]), results[2 * n])

    return pl.pallas_call(
        body,
        out_shape=shapes,
        in_specs=[pl.BlockSpec(memory_space=pltpu.SMEM)] * len(scalars) + [anywhere] * (len(operands) + len(after)),
        out_specs=[anywhere] * len(shapes),
        scratch_shapes=[pltpu.VMEM(s.shape, s.dtype) for s in shapes] + [pltpu.SemaphoreType.DMA((2 * count,))],
        compiler_params=pltpu.CompilerParams(vmem_limit_bytes=OTHER_VMEM),
        cost_estimate=pl.CostEstimate(**cost),
    )(*scalars, *operands, *after)


def pack(arrays, starts, widths, team_size, after=()):
    rows = arrays[0].shape[0]
    lows = [sum(widths[:i]) for i in range(len(widths))]
    count = len(arrays) * len(starts)

    def body(*refs):
        sources = refs[: len(arrays)]
        out, *stages, sems = refs[len(arrays) + len(after) :]
        fetches, puts = [], []
        for kind, source in enumerate(sources):
            for number, (start, width, low) in enumerate(zip(starts, widths, lows)):
                stage = stages[number].at[kind]
                place = len(fetches)
                columns = pl.ds(start, team_size * width)
                fetches.append(pltpu.make_async_copy(source.at[:, columns], stage, sems.at[place, team_size]))
                puts.append(
                    [
                        pltpu.make_async_copy(
                            stage.at[:, pl.ds(member * width, width)],
                            out.at[member, kind, :, pl.ds(low, width)],
                            sems.at[place, member],
                        )
                        for member in range(team_size)
                    ]
                )
        for fetch in fetches:
            fetch.start()
        for fetch, some_puts in zip(fetches, puts):
            fetch.wait()
            for put in some_puts:
                put.start()
        for some_puts in puts:
            for put in some_puts:
                put.wait()

    return pl.pallas_call(
        body,
        out_shape=jax.ShapeDtypeStruct((team_size, len(arrays), rows, sum(widths)), jnp.bfloat16),
        in_specs=[anywhere] * (len(arrays) + len(after)),
        out_specs=anywhere,
        scratch_shapes=[
            *[pltpu.VMEM((len(arrays), rows, team_size * width), jnp.bfloat16) for width in widths],
            pltpu.SemaphoreType.DMA((count, team_size + 1)),
        ],
        compiler_params=pltpu.CompilerParams(vmem_limit_bytes=PACK_VMEM),
        cost_estimate=pl.CostEstimate(**some),
    )(*arrays, *after)


def unpack(parts, starts, model_width):
    members, rows, _ = parts[0].shape
    count = members * len(parts)

    def body(*refs):
        *sources, out, sems = refs
        puts = []
        for start, source in zip(starts, sources):
            width = source.shape[2]
            for member in range(members):
                columns = pl.ds(start + member * width, width)
                puts.append(pltpu.make_async_copy(source.at[member], out.at[:, columns], sems.at[len(puts)]))
                puts[-1].start()
        for put in puts:
            put.wait()

    return pl.pallas_call(
        body,
        out_shape=jax.ShapeDtypeStruct((rows, model_width), jnp.bfloat16),
        in_specs=[pl.BlockSpec(memory_space=pltpu.VMEM)] * len(parts),
        out_specs=in_hbm,
        scratch_shapes=[pltpu.SemaphoreType.DMA((count,))],
        compiler_params=pltpu.CompilerParams(vmem_limit_bytes=8 * 1024 * 1024),
        cost_estimate=pl.CostEstimate(**little),
    )(*parts)


def select(held, places, count, whole, after=()):
    def plan(scalars, sources, outs, stages):
        (place_ref,) = scalars
        steps = []
        for side, (source, stage, out) in enumerate(zip(sources, stages, outs)):
            one = pl.ds(0 if side == 0 else whole, count)
            steps.append((source.at[pl.ds(place_ref[side], count)], stage.at[one], out.at[one]))
            for low in range(0, whole, count):
                rest = pl.ds(low + (count if side == 0 else 0), count)
                kept = pl.ds(low + (source.shape[0] - whole if side == 0 else 0), count)
                steps.append((source.at[kept], stage.at[rest], out.at[rest]))
        return steps

    shapes = [jax.ShapeDtypeStruct((count + whole,) + array.shape[1:], array.dtype) for array in held]
    return copy_call(plan, shapes, 2 * (1 + whole // count), held, scalars=[places], after=after, cost=much)


def columns_of(head):
    return pl.ds(pl.multiple_of(head * HD, HD), HD)


def flat(rows):
    return rows.reshape(rows.shape[0] * rows.shape[1], HD)


def masked_scores(queries, keys, masks):
    tiles = [[] for _ in range(BPF)]
    for first in range(0, len(keys), 2):
        some = jnp.concatenate(keys[first : first + 2], axis=0)
        scores = lax.dot_general(queries, some, (((1,), (1,)), ((), ())), preferred_element_type=jnp.float32)
        for side, mask in enumerate(masks[first : first + 2]):
            for b in range(BPF):
                tile = scores[b * BLK : (b + 1) * BLK, side * BLK : (side + 1) * BLK]
                tiles[b].append(tile if mask is None else tile + mask[b])
    return tiles


def largest(tiles):
    return jnp.max(functools.reduce(jnp.maximum, tiles), axis=1, keepdims=True)


def weighted(tiles, tops, values):
    totals, weights = [], []
    for b in range(BPF):
        exps = [jnp.exp2((tile - tops[b]) * to_log2) for tile in tiles[b]]
        totals.append(jnp.sum(functools.reduce(jnp.add, exps), axis=1, keepdims=True))
        weights.append(jnp.concatenate([e.astype(jnp.bfloat16) for e in exps], axis=1))
    mixed = jnp.dot(
        jnp.concatenate(weights, axis=0), jnp.concatenate(values, axis=0), preferred_element_type=jnp.float32
    )
    return mixed, jnp.concatenate(totals, axis=0)


def mask_of(codes):
    return [jnp.where(code > 0, 0.0, very_low).astype(jnp.float32) for code in codes]


def each_head(heads, fetches, puts, work):
    for head in range(heads):
        for fetch in fetches(head):
            fetch.start()

    def one_head(head, carry):
        for fetch in fetches(head):
            fetch.wait()
        work(head)
        for put in puts(head):
            put.start()
        return carry

    lax.fori_loop(0, heads, one_head, 0)
    for head in range(heads):
        for put in puts(head):
            put.wait()


def near_kernel(frames, near, pieces_of, heads, first_head, code_ref, q_hbm, *refs):
    *piece_refs, acc_ref, top_ref, total_ref, q_ref, store, sems = refs
    per_frame = BPF * pieces_of
    width = frames + 2 * REACH

    def fetches(head):
        columns = columns_of(head)
        found = [(q_hbm.at[:, 0, :, columns_of(head + first_head)], q_ref.at[:, :, columns])]
        start = 0
        for piece in piece_refs:
            size = piece.shape[0]
            found.append((piece.at[:, :, :, columns], store.at[pl.ds(start, size), :, :, columns]))
            start += size
        return [pltpu.make_async_copy(a, b, sems.at[head, i]) for i, (a, b) in enumerate(found)]

    def item(frame, head):
        columns = columns_of(head)
        own = (frame + near) * BPF * pieces_of
        keys, values, masks = [], [], []
        for b in range(BPF):
            keys.append(flat(store[pl.ds(own + b * pieces_of, pieces_of), 0, :, columns]))
            values.append(flat(store[pl.ds(own + b * pieces_of, pieces_of), 1, :, columns]))
            masks.append(None)
        for other in range(frames + 2 * near - 1):
            relative = other - near
            relative = relative + jnp.where(relative >= frame, 1, 0)
            codes = [code_ref[(frame * BPF + b) * width + relative + REACH] for b in range(BPF)]
            pick = jnp.maximum(codes[0], codes[1]) // 2
            place = ((relative + near) * BPF + pick) * pieces_of
            keys.append(flat(store[pl.ds(place, pieces_of), 0, :, columns]))
            values.append(flat(store[pl.ds(place, pieces_of), 1, :, columns]))
            masks.append(mask_of(codes))
        queries = flat(q_ref[pl.ds(frame * per_frame, per_frame), :, columns])
        tiles = masked_scores(queries, keys, masks)
        tops = [largest(tiles[b]) for b in range(BPF)]
        mixed, totals = weighted(tiles, tops, values)
        acc_ref[head, frame] = mixed
        top_ref[head, frame] = jnp.broadcast_to(jnp.concatenate(tops, axis=0), mixed.shape)
        total_ref[head, frame] = jnp.broadcast_to(totals, mixed.shape)

    together = math.gcd(frames, 4)

    def work(head):
        def step(index, carry):
            for offset in range(together):
                item(index * together + offset, head)
            return carry

        lax.fori_loop(0, frames // together, step, 0)

    each_head(heads, fetches, lambda head: [], work)


def far_kernel(frames, near, pieces_of, heads, first_head, code_ref, q_hbm, *refs):
    left_hbm, right_hbm, acc_ref, top_ref, total_ref, out_hbm, token, q_ref, left, right, out_ref, sems, put_sems = refs
    token[...] = jnp.zeros_like(token)
    per_frame = BPF * pieces_of
    width = frames + 2 * REACH

    def fetches(head):
        columns = columns_of(head)
        pairs = [
            (q_hbm.at[:, 0, :, columns_of(head + first_head)], q_ref.at[:, :, columns]),
            (left_hbm.at[:, :, :, columns], left.at[:, :, :, columns]),
            (right_hbm.at[:, :, :, columns], right.at[:, :, :, columns]),
        ]
        return [pltpu.make_async_copy(a, b, sems.at[head, i]) for i, (a, b) in enumerate(pairs)]

    def puts(head):
        columns = columns_of(head)
        return [pltpu.make_async_copy(out_ref.at[:, :, columns], out_hbm.at[:, :, columns], put_sems.at[head])]

    def item(frame, head):
        columns = columns_of(head)
        keys, values, masks = [], [], []
        for relative in [*range(-REACH, -near), *range(frames + near, frames + REACH)]:
            if abs(relative - frame) > REACH:
                continue
            codes = [code_ref[(frame * BPF + b) * width + relative + REACH] for b in range(BPF)]
            pick = jnp.maximum(codes[0], codes[1]) // 2
            if relative < 0:
                piece, place = left, (0 if relative == -REACH else (relative + REACH) * BPF - 1 + pick)
            else:
                first = (relative - frames - near) * BPF
                piece, place = right, (first if relative == frames + REACH - 1 else first + pick)
            keys.append(flat(piece[pl.ds(place * pieces_of, pieces_of), 0, :, columns]))
            values.append(flat(piece[pl.ds(place * pieces_of, pieces_of), 1, :, columns]))
            masks.append(mask_of(codes))
        queries = flat(q_ref[pl.ds(frame * per_frame, per_frame), :, columns])
        tiles = masked_scores(queries, keys, masks)
        near_top = top_ref[head, frame]
        tops = [jnp.maximum(largest(tiles[b]), near_top[b * BLK : (b + 1) * BLK]) for b in range(BPF)]
        mixed, totals = weighted(tiles, tops, values)
        shrink = jnp.exp2((near_top - jnp.concatenate(tops, axis=0)) * to_log2)
        result = (acc_ref[head, frame] * shrink + mixed) / (total_ref[head, frame] * shrink + totals)
        out_ref[pl.ds(frame * per_frame, per_frame), :, columns] = result.astype(jnp.bfloat16).reshape(
            per_frame, BLK // pieces_of, HD
        )

    def work(head):
        for frame in range(frames):
            item(frame, head)

    each_head(heads, fetches, puts, work)


def measured_cost(blocks):
    return dict(flops=6 * blocks * BPF * 4 * BLK * BLK * HD, bytes_accessed=1024, transcendentals=0)


def attend_near(codes, queries, pieces, frames, near, first_head, cost=None, after=()):
    members, _, rows, _ = queries.shape
    pieces_of = BLK // rows
    width = pieces[0].shape[3]
    heads = width // HD
    stored = sum(piece.shape[0] for piece in pieces)

    def body(code_ref, q_hbm, *refs):
        kept = refs[: len(pieces)] + refs[len(pieces) + len(after) :]
        near_kernel(frames, near, pieces_of, heads, first_head, code_ref, q_hbm, *kept)

    partial = jax.ShapeDtypeStruct((heads, frames, BPF * BLK, HD), jnp.float32)
    return pl.pallas_call(
        body,
        out_shape=[partial] * 3,
        in_specs=[pl.BlockSpec(memory_space=pltpu.SMEM)] + [anywhere] * (1 + len(pieces) + len(after)),
        out_specs=[in_vmem] * 3,
        scratch_shapes=[
            pltpu.VMEM((members, rows, width), jnp.bfloat16),
            pltpu.VMEM((stored, 2, rows, width), jnp.bfloat16),
            pltpu.SemaphoreType.DMA((heads, 1 + len(pieces))),
        ],
        compiler_params=pltpu.CompilerParams(vmem_limit_bytes=NEAR_VMEM),
        cost_estimate=pl.CostEstimate(**(cost or measured_cost(frames * heads * (frames + 2 * near + 1)))),
    )(codes, queries, *pieces, *after)


def attend_far(codes, queries, far, partials, frames, near, first_head, cost=None, after=()):
    members, _, rows, _ = queries.shape
    pieces_of = BLK // rows
    width = far[0].shape[3]
    heads = width // HD

    def body(code_ref, q_hbm, *refs):
        far_kernel(frames, near, pieces_of, heads, first_head, code_ref, q_hbm, *refs[:5], *refs[5 + len(after) :])

    result = jax.ShapeDtypeStruct((members, rows, width), jnp.bfloat16)
    return pl.pallas_call(
        body,
        out_shape=[result, jax.ShapeDtypeStruct((8, 128), jnp.float32)],
        in_specs=[pl.BlockSpec(memory_space=pltpu.SMEM)] + [anywhere] * 3 + [in_vmem] * 3 + [anywhere] * len(after),
        out_specs=[in_hbm, in_vmem],
        scratch_shapes=[
            pltpu.VMEM(result.shape, result.dtype),
            *[pltpu.VMEM(array.shape, array.dtype) for array in far],
            pltpu.VMEM(result.shape, result.dtype),
            pltpu.SemaphoreType.DMA((heads, 3)),
            pltpu.SemaphoreType.DMA((heads,)),
        ],
        compiler_params=pltpu.CompilerParams(vmem_limit_bytes=FAR_VMEM),
        cost_estimate=pl.CostEstimate(**(cost or measured_cost(frames * heads * 4))),
    )(codes, queries, *far, *partials, *after)


def on_device(outer, inner, q_proj, k_proj, v_proj, kv_list):
    frames = inner
    rows, model_width = q_proj.shape
    team = ("inner", "rep", "uly")
    team_size = frames * BPF * BLK // rows
    heads_here = model_width // HD // team_size
    pieces_of = BLK // rows
    per_frame = BPF * pieces_of
    my_group = lax.axis_index("outer")

    def rows_of(reader_frame, count):
        start = jnp.clip(reader_frame * BPF, 0, kv_list.shape[0] - count * BPF)
        return lax.dynamic_slice_in_dim(kv_list, start, count * BPF, 0)

    lists = rows_of(my_group * frames, frames).reshape(frames * BPF, 1, -1)
    first_ids = BPF * (my_group * frames - REACH + lax.broadcasted_iota(jnp.int32, (1, frames + 2 * REACH, 1), 1))
    hits = jnp.where(lists == first_ids, 1, 0) + jnp.where(lists == first_ids + 1, 2, 0)
    codes = jnp.sum(jnp.where(lists >= 0, hits, 0), axis=-1).reshape(-1)

    def picked(reader_frame, holder_frame):
        return jnp.any(rows_of(reader_frame, 1) == holder_frame * BPF + 1).astype(jnp.int32)

    assert sum(CHUNKS) == heads_here
    widths = [heads * HD for heads in CHUNKS]
    lows = [sum(CHUNKS[:c]) for c in range(len(CHUNKS))]
    starts = [low * team_size * HD for low in lows]

    def exchange(array):
        return lax.all_to_all(array, team, split_axis=0, concat_axis=0, tiled=True)

    def shifted(array, heading, hop):
        places = range(outer)
        route = [(i, i + heading) for i in places if i + heading in places and i - (hop - 1) * heading in places]
        return lax.ppermute(array, "outer", route)

    hops = []
    for hop in range(1, -(-REACH // frames) + 1):
        spare = hop * frames - REACH
        hops.append((frames - max(0, spare), spare >= 0))

    def forwarded(held, held_frames, keep, single, after):
        whole = (keep - 1 if single else keep) * per_frame
        if single:
            from_left, from_right = (my_group + 1) * frames, my_group * frames - 1
            edges = held[0].shape[0] - whole - per_frame, whole
            edge_places = jnp.stack(
                [
                    edges[0] + pieces_of * picked(from_left, from_left - REACH),
                    edges[1] + pieces_of * picked(from_right, from_right + REACH),
                ]
            )
            return list(select(held, edge_places, pieces_of, whole, after))
        if keep < held_frames:
            return [held[0][held[0].shape[0] - whole :], held[1][:whole]]
        return held

    def first_hop(own):
        assert hops[0] == (frames, False)
        return [[shifted(own, 1, 1), shifted(own, -1, 1)]]

    def selected(arrivals, after=()):
        for hop in range(1, len(hops)):
            to_send = forwarded(arrivals[-1], hops[hop - 1][0], *hops[hop], after if hop == len(hops) - 1 else ())
            if hop < len(hops) - 1:
                arrivals.append([shifted(to_send[0], 1, hop + 1), shifted(to_send[1], -1, hop + 1)])
        return to_send

    def last_hop(arrivals, to_send):
        arrivals.append([shifted(to_send[0], 1, len(hops)), shifted(to_send[1], -1, len(hops))])

    chunks = range(len(CHUNKS))
    near = (len(hops) - 1) * frames
    packed = [pack([k_proj, v_proj], [starts[c]], [widths[c]], team_size) for c in chunks]
    owned = [exchange(array) for array in packed]
    queries = exchange(pack([q_proj], starts, widths, team_size, after=packed[-1:]))
    arrivals, sent, tokens, outs = [], [], [], []
    partials = {}

    def attend_rest(c, after, cost):
        far = arrivals[c][-1]
        result, token = attend_far(codes, queries, far, partials[c], frames, near, lows[c], cost, after=after)
        tokens.append(token)
        if outs:
            result, outs[-1] = lax.optimization_barrier((result, outs[-1]))
        outs.append(exchange(result))

    for c in chunks:
        arrivals.append(first_hop(owned[c]))
        sent.append(selected(arrivals[c], after=partials[c - 1] if c > 0 else ()))
        order = [a[0] for a in arrivals[c][::-1]] + [owned[c]] + [a[1] for a in arrivals[c]]
        last_hop(arrivals[c], sent[c])
        if c > 0:
            attend_rest(c - 1, sent[c], None)
        after = sent[c] + tokens[-1:]
        cost = little if c == len(CHUNKS) - 1 else None
        partials[c] = list(attend_near(codes, queries, order, frames, near, lows[c], cost, after=after))
    attend_rest(chunks[-1], (), little)
    return unpack(outs, starts, model_width)


def solution(mesh):
    sizes = dict(mesh.shape)
    members = sizes["uly"] * sizes["rep"]
    heads = 40
    inner = max(
        i for i in range(1, sizes["ctx"] + 1) if sizes["ctx"] % i == 0 and heads % (i * members) == 0
    )
    outer = sizes["ctx"] // inner
    finer = Mesh(
        mesh.devices.reshape(sizes["groups"], outer, inner, sizes["uly"], sizes["rep"]),
        ("groups", "outer", "inner", "uly", "rep"),
    )
    split = P(("groups", "outer", "inner", "rep", "uly"), None)
    return jax.shard_map(
        functools.partial(on_device, outer, inner),
        mesh=finer,
        in_specs=(split, split, split, P("groups", None)),
        out_specs=split,
        check_vma=False,
    )
```

```python
import functools
import math

import jax
import jax.numpy as jnp
from jax import lax
from jax.experimental import pallas as pl
from jax.experimental.pallas import tpu as pltpu
from jax.sharding import Mesh, PartitionSpec as P

HD = 128
BLK = 128
BPF = 2
REACH = 7
CHUNKS = (3, 2)
PACK_VMEM = 60 * 1024 * 1024
NEAR_VMEM = 24 * 1024 * 1024
OTHER_VMEM = 14 * 1024 * 1024
little = dict(flops=1024, bytes_accessed=1024, transcendentals=0)
much = dict(flops=100_000_000_000, bytes_accessed=1024, transcendentals=0)

very_low = -1e30
to_log2 = math.log2(math.e) * HD ** -0.5


def staged_copies(steps, sems):
    count = len(steps)
    fetches = [pltpu.make_async_copy(s, stage, sems.at[i]) for i, (s, stage, t) in enumerate(steps)]
    puts = [pltpu.make_async_copy(stage, t, sems.at[count + i]) for i, (s, stage, t) in enumerate(steps)]
    for fetch in fetches:
        fetch.start()
    for fetch, put in zip(fetches, puts):
        fetch.wait()
        put.start()
    for put in puts:
        put.wait()


anywhere = pl.BlockSpec(memory_space=pl.ANY)
in_hbm = pl.BlockSpec(memory_space=pltpu.HBM)
in_vmem = pl.BlockSpec(memory_space=pltpu.VMEM)


def copy_call(plan, shapes, count, operands, scalars=(), after=(), cost=little):
    def body(*refs):
        first = len(scalars)
        last = first + len(operands)
        results = refs[last + len(after) :]
        n = len(shapes)
        staged_copies(plan(refs[:first], refs[first:last], results[:n], results[n : 2 * n]), results[2 * n])

    return pl.pallas_call(
        body,
        out_shape=shapes,
        in_specs=[pl.BlockSpec(memory_space=pltpu.SMEM)] * len(scalars) + [anywhere] * (len(operands) + len(after)),
        out_specs=[anywhere] * len(shapes),
        scratch_shapes=[pltpu.VMEM(s.shape, s.dtype) for s in shapes] + [pltpu.SemaphoreType.DMA((2 * count,))],
        compiler_params=pltpu.CompilerParams(vmem_limit_bytes=OTHER_VMEM),
        cost_estimate=pl.CostEstimate(**cost),
    )(*scalars, *operands, *after)


def pack(arrays, starts, widths, team_size, after=()):
    rows = arrays[0].shape[0]
    lows = [sum(widths[:i]) for i in range(len(widths))]
    count = len(arrays) * len(starts)

    def body(*refs):
        sources = refs[: len(arrays)]
        out, *stages, sems = refs[len(arrays) + len(after) :]
        fetches, puts = [], []
        for kind, source in enumerate(sources):
            for number, (start, width, low) in enumerate(zip(starts, widths, lows)):
                stage = stages[number].at[kind]
                place = len(fetches)
                columns = pl.ds(start, team_size * width)
                fetches.append(pltpu.make_async_copy(source.at[:, columns], stage, sems.at[place, team_size]))
                puts.append(
                    [
                        pltpu.make_async_copy(
                            stage.at[:, pl.ds(member * width, width)],
                            out.at[member, kind, :, pl.ds(low, width)],
                            sems.at[place, member],
                        )
                        for member in range(team_size)
                    ]
                )
        for fetch in fetches:
            fetch.start()
        for fetch, some_puts in zip(fetches, puts):
            fetch.wait()
            for put in some_puts:
                put.start()
        for some_puts in puts:
            for put in some_puts:
                put.wait()

    return pl.pallas_call(
        body,
        out_shape=jax.ShapeDtypeStruct((team_size, len(arrays), rows, sum(widths)), jnp.bfloat16),
        in_specs=[anywhere] * (len(arrays) + len(after)),
        out_specs=anywhere,
        scratch_shapes=[
            *[pltpu.VMEM((len(arrays), rows, team_size * width), jnp.bfloat16) for width in widths],
            pltpu.SemaphoreType.DMA((count, team_size + 1)),
        ],
        compiler_params=pltpu.CompilerParams(vmem_limit_bytes=PACK_VMEM),
        cost_estimate=pl.CostEstimate(**little),
    )(*arrays, *after)


def unpack(parts, starts, model_width):
    members, rows, _ = parts[0].shape
    count = members * len(parts)

    def body(*refs):
        *sources, out, sems = refs
        puts = []
        for start, source in zip(starts, sources):
            width = source.shape[2]
            for member in range(members):
                columns = pl.ds(start + member * width, width)
                puts.append(pltpu.make_async_copy(source.at[member], out.at[:, columns], sems.at[len(puts)]))
                puts[-1].start()
        for put in puts:
            put.wait()

    return pl.pallas_call(
        body,
        out_shape=jax.ShapeDtypeStruct((rows, model_width), jnp.bfloat16),
        in_specs=[pl.BlockSpec(memory_space=pltpu.VMEM)] * len(parts),
        out_specs=in_hbm,
        scratch_shapes=[pltpu.SemaphoreType.DMA((count,))],
        compiler_params=pltpu.CompilerParams(vmem_limit_bytes=8 * 1024 * 1024),
        cost_estimate=pl.CostEstimate(**little),
    )(*parts)


def select(held, places, count, whole, after=()):
    def plan(scalars, sources, outs, stages):
        (place_ref,) = scalars
        steps = []
        for side, (source, stage, out) in enumerate(zip(sources, stages, outs)):
            one = pl.ds(0 if side == 0 else whole, count)
            steps.append((source.at[pl.ds(place_ref[side], count)], stage.at[one], out.at[one]))
            for low in range(0, whole, count):
                rest = pl.ds(low + (count if side == 0 else 0), count)
                kept = pl.ds(low + (source.shape[0] - whole if side == 0 else 0), count)
                steps.append((source.at[kept], stage.at[rest], out.at[rest]))
        return steps

    shapes = [jax.ShapeDtypeStruct((count + whole,) + array.shape[1:], array.dtype) for array in held]
    return copy_call(plan, shapes, 2 * (1 + whole // count), held, scalars=[places], after=after, cost=much)


def columns_of(head):
    return pl.ds(pl.multiple_of(head * HD, HD), HD)


def flat(rows):
    return rows.reshape(rows.shape[0] * rows.shape[1], HD)


def masked_scores(queries, keys, masks):
    tiles = [[] for _ in range(BPF)]
    for first in range(0, len(keys), 2):
        some = jnp.concatenate(keys[first : first + 2], axis=0)
        scores = lax.dot_general(queries, some, (((1,), (1,)), ((), ())), preferred_element_type=jnp.float32)
        for side, mask in enumerate(masks[first : first + 2]):
            for b in range(BPF):
                tile = scores[b * BLK : (b + 1) * BLK, side * BLK : (side + 1) * BLK]
                tiles[b].append(tile if mask is None else tile + mask[b])
    return tiles


def largest(tiles):
    return jnp.max(functools.reduce(jnp.maximum, tiles), axis=1, keepdims=True)


def weighted(tiles, tops, values):
    totals, weights = [], []
    for b in range(BPF):
        exps = [jnp.exp2((tile - tops[b]) * to_log2) for tile in tiles[b]]
        totals.append(jnp.sum(functools.reduce(jnp.add, exps), axis=1, keepdims=True))
        weights.append(jnp.concatenate([e.astype(jnp.bfloat16) for e in exps], axis=1))
    mixed = jnp.dot(
        jnp.concatenate(weights, axis=0), jnp.concatenate(values, axis=0), preferred_element_type=jnp.float32
    )
    return mixed, jnp.concatenate(totals, axis=0)


def mask_of(codes):
    return [jnp.where(code > 0, 0.0, very_low).astype(jnp.float32) for code in codes]


def each_head(heads, fetches, puts, work):
    for head in range(heads):
        for fetch in fetches(head):
            fetch.start()

    def one_head(head, carry):
        for fetch in fetches(head):
            fetch.wait()
        work(head)
        for put in puts(head):
            put.start()
        return carry

    lax.fori_loop(0, heads, one_head, 0)
    for head in range(heads):
        for put in puts(head):
            put.wait()


def near_kernel(frames, near, pieces_of, heads, first_head, code_ref, q_hbm, *refs):
    *piece_refs, acc_ref, top_ref, total_ref, q_ref, store, sems = refs
    per_frame = BPF * pieces_of
    width = frames + 2 * REACH

    def fetches(head):
        columns = columns_of(head)
        found = [(q_hbm.at[:, 0, :, columns_of(head + first_head)], q_ref.at[:, :, columns])]
        start = 0
        for piece in piece_refs:
            size = piece.shape[0]
            found.append((piece.at[:, :, :, columns], store.at[pl.ds(start, size), :, :, columns]))
            start += size
        return [pltpu.make_async_copy(a, b, sems.at[head, i]) for i, (a, b) in enumerate(found)]

    def item(frame, head):
        columns = columns_of(head)
        own = (frame + near) * BPF * pieces_of
        keys, values, masks = [], [], []
        for b in range(BPF):
            keys.append(flat(store[pl.ds(own + b * pieces_of, pieces_of), 0, :, columns]))
            values.append(flat(store[pl.ds(own + b * pieces_of, pieces_of), 1, :, columns]))
            masks.append(None)
        for other in range(frames + 2 * near - 1):
            relative = other - near
            relative = relative + jnp.where(relative >= frame, 1, 0)
            codes = [code_ref[(frame * BPF + b) * width + relative + REACH] for b in range(BPF)]
            pick = jnp.maximum(codes[0], codes[1]) // 2
            place = ((relative + near) * BPF + pick) * pieces_of
            keys.append(flat(store[pl.ds(place, pieces_of), 0, :, columns]))
            values.append(flat(store[pl.ds(place, pieces_of), 1, :, columns]))
            masks.append(mask_of(codes))
        queries = flat(q_ref[pl.ds(frame * per_frame, per_frame), :, columns])
        tiles = masked_scores(queries, keys, masks)
        tops = [largest(tiles[b]) for b in range(BPF)]
        mixed, totals = weighted(tiles, tops, values)
        acc_ref[head, frame] = mixed
        top_ref[head, frame] = jnp.broadcast_to(jnp.concatenate(tops, axis=0), mixed.shape)
        total_ref[head, frame] = jnp.broadcast_to(totals, mixed.shape)

    together = math.gcd(frames, 4)

    def work(head):
        def step(index, carry):
            for offset in range(together):
                item(index * together + offset, head)
            return carry

        lax.fori_loop(0, frames // together, step, 0)

    each_head(heads, fetches, lambda head: [], work)


def far_kernel(frames, near, pieces_of, heads, first_head, code_ref, q_hbm, *refs):
    left_hbm, right_hbm, acc_ref, top_ref, total_ref, out_hbm, token, q_ref, left, right, out_ref, sems, put_sems = refs
    token[...] = jnp.zeros_like(token)
    per_frame = BPF * pieces_of
    width = frames + 2 * REACH

    def fetches(head):
        columns = columns_of(head)
        pairs = [
            (q_hbm.at[:, 0, :, columns_of(head + first_head)], q_ref.at[:, :, columns]),
            (left_hbm.at[:, :, :, columns], left.at[:, :, :, columns]),
            (right_hbm.at[:, :, :, columns], right.at[:, :, :, columns]),
        ]
        return [pltpu.make_async_copy(a, b, sems.at[head, i]) for i, (a, b) in enumerate(pairs)]

    def puts(head):
        columns = columns_of(head)
        return [pltpu.make_async_copy(out_ref.at[:, :, columns], out_hbm.at[:, :, columns], put_sems.at[head])]

    def item(frame, head):
        columns = columns_of(head)
        keys, values, masks = [], [], []
        for relative in [*range(-REACH, -near), *range(frames + near, frames + REACH)]:
            if abs(relative - frame) > REACH:
                continue
            codes = [code_ref[(frame * BPF + b) * width + relative + REACH] for b in range(BPF)]
            pick = jnp.maximum(codes[0], codes[1]) // 2
            if relative < 0:
                piece, place = left, (0 if relative == -REACH else (relative + REACH) * BPF - 1 + pick)
            else:
                first = (relative - frames - near) * BPF
                piece, place = right, (first if relative == frames + REACH - 1 else first + pick)
            keys.append(flat(piece[pl.ds(place * pieces_of, pieces_of), 0, :, columns]))
            values.append(flat(piece[pl.ds(place * pieces_of, pieces_of), 1, :, columns]))
            masks.append(mask_of(codes))
        queries = flat(q_ref[pl.ds(frame * per_frame, per_frame), :, columns])
        tiles = masked_scores(queries, keys, masks)
        near_top = top_ref[head, frame]
        tops = [jnp.maximum(largest(tiles[b]), near_top[b * BLK : (b + 1) * BLK]) for b in range(BPF)]
        mixed, totals = weighted(tiles, tops, values)
        shrink = jnp.exp2((near_top - jnp.concatenate(tops, axis=0)) * to_log2)
        result = (acc_ref[head, frame] * shrink + mixed) / (total_ref[head, frame] * shrink + totals)
        out_ref[pl.ds(frame * per_frame, per_frame), :, columns] = result.astype(jnp.bfloat16).reshape(
            per_frame, BLK // pieces_of, HD
        )

    def work(head):
        for frame in range(frames):
            item(frame, head)

    each_head(heads, fetches, puts, work)


def measured_cost(blocks):
    return dict(flops=6 * blocks * BPF * 4 * BLK * BLK * HD, bytes_accessed=1024, transcendentals=0)


def attend_near(codes, queries, pieces, frames, near, first_head, cost=None, after=()):
    members, _, rows, _ = queries.shape
    pieces_of = BLK // rows
    width = pieces[0].shape[3]
    heads = width // HD
    stored = sum(piece.shape[0] for piece in pieces)

    def body(code_ref, q_hbm, *refs):
        kept = refs[: len(pieces)] + refs[len(pieces) + len(after) :]
        near_kernel(frames, near, pieces_of, heads, first_head, code_ref, q_hbm, *kept)

    partial = jax.ShapeDtypeStruct((heads, frames, BPF * BLK, HD), jnp.float32)
    return pl.pallas_call(
        body,
        out_shape=[partial] * 3,
        in_specs=[pl.BlockSpec(memory_space=pltpu.SMEM)] + [anywhere] * (1 + len(pieces) + len(after)),
        out_specs=[in_vmem] * 3,
        scratch_shapes=[
            pltpu.VMEM((members, rows, width), jnp.bfloat16),
            pltpu.VMEM((stored, 2, rows, width), jnp.bfloat16),
            pltpu.SemaphoreType.DMA((heads, 1 + len(pieces))),
        ],
        compiler_params=pltpu.CompilerParams(vmem_limit_bytes=NEAR_VMEM),
        cost_estimate=pl.CostEstimate(**(cost or measured_cost(frames * heads * (frames + 2 * near + 1)))),
    )(codes, queries, *pieces, *after)


def attend_far(codes, queries, far, partials, frames, near, first_head, cost=None, after=()):
    members, _, rows, _ = queries.shape
    pieces_of = BLK // rows
    width = far[0].shape[3]
    heads = width // HD

    def body(code_ref, q_hbm, *refs):
        far_kernel(frames, near, pieces_of, heads, first_head, code_ref, q_hbm, *refs[:5], *refs[5 + len(after) :])

    result = jax.ShapeDtypeStruct((members, rows, width), jnp.bfloat16)
    return pl.pallas_call(
        body,
        out_shape=[result, jax.ShapeDtypeStruct((8, 128), jnp.float32)],
        in_specs=[pl.BlockSpec(memory_space=pltpu.SMEM)] + [anywhere] * 3 + [in_vmem] * 3 + [anywhere] * len(after),
        out_specs=[in_hbm, in_vmem],
        scratch_shapes=[
            pltpu.VMEM(result.shape, result.dtype),
            *[pltpu.VMEM(array.shape, array.dtype) for array in far],
            pltpu.VMEM(result.shape, result.dtype),
            pltpu.SemaphoreType.DMA((heads, 3)),
            pltpu.SemaphoreType.DMA((heads,)),
        ],
        compiler_params=pltpu.CompilerParams(vmem_limit_bytes=OTHER_VMEM),
        cost_estimate=pl.CostEstimate(**(cost or measured_cost(frames * heads * 4))),
    )(codes, queries, *far, *partials, *after)


def on_device(outer, inner, q_proj, k_proj, v_proj, kv_list):
    frames = inner
    rows, model_width = q_proj.shape
    team = ("inner", "rep", "uly")
    team_size = frames * BPF * BLK // rows
    heads_here = model_width // HD // team_size
    pieces_of = BLK // rows
    per_frame = BPF * pieces_of
    my_group = lax.axis_index("outer")

    def rows_of(reader_frame, count):
        start = jnp.clip(reader_frame * BPF, 0, kv_list.shape[0] - count * BPF)
        return lax.dynamic_slice_in_dim(kv_list, start, count * BPF, 0)

    lists = rows_of(my_group * frames, frames).reshape(frames * BPF, 1, -1)
    first_ids = BPF * (my_group * frames - REACH + lax.broadcasted_iota(jnp.int32, (1, frames + 2 * REACH, 1), 1))
    hits = jnp.where(lists == first_ids, 1, 0) + jnp.where(lists == first_ids + 1, 2, 0)
    codes = jnp.sum(jnp.where(lists >= 0, hits, 0), axis=-1).reshape(-1)

    def picked(reader_frame, holder_frame):
        return jnp.any(rows_of(reader_frame, 1) == holder_frame * BPF + 1).astype(jnp.int32)

    assert sum(CHUNKS) == heads_here
    widths = [heads * HD for heads in CHUNKS]
    lows = [sum(CHUNKS[:c]) for c in range(len(CHUNKS))]
    starts = [low * team_size * HD for low in lows]

    def exchange(array):
        return lax.all_to_all(array, team, split_axis=0, concat_axis=0, tiled=True)

    def shifted(array, heading, hop):
        places = range(outer)
        route = [(i, i + heading) for i in places if i + heading in places and i - (hop - 1) * heading in places]
        return lax.ppermute(array, "outer", route)

    hops = []
    for hop in range(1, -(-REACH // frames) + 1):
        spare = hop * frames - REACH
        hops.append((frames - max(0, spare), spare >= 0))

    def forwarded(held, held_frames, keep, single, after):
        whole = (keep - 1 if single else keep) * per_frame
        if single:
            from_left, from_right = (my_group + 1) * frames, my_group * frames - 1
            edges = held[0].shape[0] - whole - per_frame, whole
            edge_places = jnp.stack(
                [
                    edges[0] + pieces_of * picked(from_left, from_left - REACH),
                    edges[1] + pieces_of * picked(from_right, from_right + REACH),
                ]
            )
            return list(select(held, edge_places, pieces_of, whole, after))
        if keep < held_frames:
            return [held[0][held[0].shape[0] - whole :], held[1][:whole]]
        return held

    def first_hop(own):
        assert hops[0] == (frames, False)
        return [[shifted(own, 1, 1), shifted(own, -1, 1)]]

    def selected(arrivals, after=()):
        for hop in range(1, len(hops)):
            to_send = forwarded(arrivals[-1], hops[hop - 1][0], *hops[hop], after if hop == len(hops) - 1 else ())
            if hop < len(hops) - 1:
                arrivals.append([shifted(to_send[0], 1, hop + 1), shifted(to_send[1], -1, hop + 1)])
        return to_send

    def last_hop(arrivals, to_send):
        arrivals.append([shifted(to_send[0], 1, len(hops)), shifted(to_send[1], -1, len(hops))])

    chunks = range(len(CHUNKS))
    near = (len(hops) - 1) * frames
    packed = [pack([k_proj, v_proj], [starts[c]], [widths[c]], team_size) for c in chunks]
    owned = [exchange(array) for array in packed]
    queries = exchange(pack([q_proj], starts, widths, team_size, after=packed[-1:]))
    arrivals, sent, tokens, outs = [], [], [], []
    partials = {}

    def attend_rest(c, after, cost):
        far = arrivals[c][-1]
        result, token = attend_far(codes, queries, far, partials[c], frames, near, lows[c], cost, after=after)
        tokens.append(token)
        if outs:
            result, outs[-1] = lax.optimization_barrier((result, outs[-1]))
        outs.append(exchange(result))

    for c in chunks:
        arrivals.append(first_hop(owned[c]))
        sent.append(selected(arrivals[c], after=partials[c - 1] if c > 0 else ()))
        order = [a[0] for a in arrivals[c][::-1]] + [owned[c]] + [a[1] for a in arrivals[c]]
        last_hop(arrivals[c], sent[c])
        if c > 0:
            attend_rest(c - 1, sent[c], None)
        after = sent[c] + tokens[-1:]
        cost = little if c == len(CHUNKS) - 1 else None
        partials[c] = list(attend_near(codes, queries, order, frames, near, lows[c], cost, after=after))
    attend_rest(chunks[-1], (), little)
    return unpack(outs, starts, model_width)


def solution(mesh):
    sizes = dict(mesh.shape)
    members = sizes["uly"] * sizes["rep"]
    heads = 40
    inner = max(
        i for i in range(1, sizes["ctx"] + 1) if sizes["ctx"] % i == 0 and heads % (i * members) == 0
    )
    outer = sizes["ctx"] // inner
    finer = Mesh(
        mesh.devices.reshape(sizes["groups"], outer, inner, sizes["uly"], sizes["rep"]),
        ("groups", "outer", "inner", "uly", "rep"),
    )
    split = P(("groups", "outer", "inner", "rep", "uly"), None)
    return jax.shard_map(
        functools.partial(on_device, outer, inner),
        mesh=finer,
        in_specs=(split, split, split, P("groups", None)),
        out_specs=split,
        check_vma=False,
    )
```

```python
import functools
import math

import jax
import jax.numpy as jnp
from jax import lax
from jax.experimental import pallas as pl
from jax.experimental.pallas import tpu as pltpu
from jax.sharding import Mesh, PartitionSpec as P

HD = 128
BLK = 128
BPF = 2
REACH = 7
CHUNKS = (2, 3)
PACK_VMEM = 60 * 1024 * 1024
NEAR_VMEM = 24 * 1024 * 1024
OTHER_VMEM = 14 * 1024 * 1024
little = dict(flops=1024, bytes_accessed=1024, transcendentals=0)
some = dict(flops=20_000_000_000, bytes_accessed=1024, transcendentals=0)
much = dict(flops=100_000_000_000, bytes_accessed=1024, transcendentals=0)

very_low = -1e30
to_log2 = math.log2(math.e) * HD ** -0.5


def staged_copies(steps, sems):
    count = len(steps)
    fetches = [pltpu.make_async_copy(s, stage, sems.at[i]) for i, (s, stage, t) in enumerate(steps)]
    puts = [pltpu.make_async_copy(stage, t, sems.at[count + i]) for i, (s, stage, t) in enumerate(steps)]
    for fetch in fetches:
        fetch.start()
    for fetch, put in zip(fetches, puts):
        fetch.wait()
        put.start()
    for put in puts:
        put.wait()


anywhere = pl.BlockSpec(memory_space=pl.ANY)
in_hbm = pl.BlockSpec(memory_space=pltpu.HBM)
in_vmem = pl.BlockSpec(memory_space=pltpu.VMEM)


def copy_call(plan, shapes, count, operands, scalars=(), after=(), cost=little):
    def body(*refs):
        first = len(scalars)
        last = first + len(operands)
        results = refs[last + len(after) :]
        n = len(shapes)
        staged_copies(plan(refs[:first], refs[first:last], results[:n], results[n : 2 * n]), results[2 * n])

    return pl.pallas_call(
        body,
        out_shape=shapes,
        in_specs=[pl.BlockSpec(memory_space=pltpu.SMEM)] * len(scalars) + [anywhere] * (len(operands) + len(after)),
        out_specs=[anywhere] * len(shapes),
        scratch_shapes=[pltpu.VMEM(s.shape, s.dtype) for s in shapes] + [pltpu.SemaphoreType.DMA((2 * count,))],
        compiler_params=pltpu.CompilerParams(vmem_limit_bytes=OTHER_VMEM),
        cost_estimate=pl.CostEstimate(**cost),
    )(*scalars, *operands, *after)


def pack(arrays, starts, widths, team_size, after=()):
    rows = arrays[0].shape[0]
    lows = [sum(widths[:i]) for i in range(len(widths))]
    count = len(arrays) * len(starts)

    def body(*refs):
        sources = refs[: len(arrays)]
        out, *stages, sems = refs[len(arrays) + len(after) :]
        fetches, puts = [], []
        for kind, source in enumerate(sources):
            for number, (start, width, low) in enumerate(zip(starts, widths, lows)):
                stage = stages[number].at[kind]
                place = len(fetches)
                columns = pl.ds(start, team_size * width)
                fetches.append(pltpu.make_async_copy(source.at[:, columns], stage, sems.at[place, team_size]))
                puts.append(
                    [
                        pltpu.make_async_copy(
                            stage.at[:, pl.ds(member * width, width)],
                            out.at[member, kind, :, pl.ds(low, width)],
                            sems.at[place, member],
                        )
                        for member in range(team_size)
                    ]
                )
        for fetch in fetches:
            fetch.start()
        for fetch, some_puts in zip(fetches, puts):
            fetch.wait()
            for put in some_puts:
                put.start()
        for some_puts in puts:
            for put in some_puts:
                put.wait()

    return pl.pallas_call(
        body,
        out_shape=jax.ShapeDtypeStruct((team_size, len(arrays), rows, sum(widths)), jnp.bfloat16),
        in_specs=[anywhere] * (len(arrays) + len(after)),
        out_specs=anywhere,
        scratch_shapes=[
            *[pltpu.VMEM((len(arrays), rows, team_size * width), jnp.bfloat16) for width in widths],
            pltpu.SemaphoreType.DMA((count, team_size + 1)),
        ],
        compiler_params=pltpu.CompilerParams(vmem_limit_bytes=PACK_VMEM),
        cost_estimate=pl.CostEstimate(**some),
    )(*arrays, *after)


def unpack(parts, starts, model_width):
    members, rows, _ = parts[0].shape
    count = members * len(parts)

    def body(*refs):
        *sources, out, sems = refs
        puts = []
        for start, source in zip(starts, sources):
            width = source.shape[2]
            for member in range(members):
                columns = pl.ds(start + member * width, width)
                puts.append(pltpu.make_async_copy(source.at[member], out.at[:, columns], sems.at[len(puts)]))
                puts[-1].start()
        for put in puts:
            put.wait()

    return pl.pallas_call(
        body,
        out_shape=jax.ShapeDtypeStruct((rows, model_width), jnp.bfloat16),
        in_specs=[pl.BlockSpec(memory_space=pltpu.VMEM)] * len(parts),
        out_specs=in_hbm,
        scratch_shapes=[pltpu.SemaphoreType.DMA((count,))],
        compiler_params=pltpu.CompilerParams(vmem_limit_bytes=8 * 1024 * 1024),
        cost_estimate=pl.CostEstimate(**little),
    )(*parts)


def select(held, places, count, whole, after=()):
    def plan(scalars, sources, outs, stages):
        (place_ref,) = scalars
        steps = []
        for side, (source, stage, out) in enumerate(zip(sources, stages, outs)):
            one = pl.ds(0 if side == 0 else whole, count)
            steps.append((source.at[pl.ds(place_ref[side], count)], stage.at[one], out.at[one]))
            for low in range(0, whole, count):
                rest = pl.ds(low + (count if side == 0 else 0), count)
                kept = pl.ds(low + (source.shape[0] - whole if side == 0 else 0), count)
                steps.append((source.at[kept], stage.at[rest], out.at[rest]))
        return steps

    shapes = [jax.ShapeDtypeStruct((count + whole,) + array.shape[1:], array.dtype) for array in held]
    return copy_call(plan, shapes, 2 * (1 + whole // count), held, scalars=[places], after=after, cost=much)


def columns_of(head):
    return pl.ds(pl.multiple_of(head * HD, HD), HD)


def flat(rows):
    return rows.reshape(rows.shape[0] * rows.shape[1], HD)


def masked_scores(queries, keys, masks):
    tiles = [[] for _ in range(BPF)]
    for first in range(0, len(keys), 2):
        some = jnp.concatenate(keys[first : first + 2], axis=0)
        scores = lax.dot_general(queries, some, (((1,), (1,)), ((), ())), preferred_element_type=jnp.float32)
        for side, mask in enumerate(masks[first : first + 2]):
            for b in range(BPF):
                tile = scores[b * BLK : (b + 1) * BLK, side * BLK : (side + 1) * BLK]
                tiles[b].append(tile if mask is None else tile + mask[b])
    return tiles


def largest(tiles):
    return jnp.max(functools.reduce(jnp.maximum, tiles), axis=1, keepdims=True)


def weighted(tiles, tops, values):
    totals, weights = [], []
    for b in range(BPF):
        exps = [jnp.exp2((tile - tops[b]) * to_log2) for tile in tiles[b]]
        totals.append(jnp.sum(functools.reduce(jnp.add, exps), axis=1, keepdims=True))
        weights.append(jnp.concatenate([e.astype(jnp.bfloat16) for e in exps], axis=1))
    mixed = jnp.dot(
        jnp.concatenate(weights, axis=0), jnp.concatenate(values, axis=0), preferred_element_type=jnp.float32
    )
    return mixed, jnp.concatenate(totals, axis=0)


def mask_of(codes):
    return [jnp.where(code > 0, 0.0, very_low).astype(jnp.float32) for code in codes]


def each_head(heads, fetches, puts, work):
    for head in range(heads):
        for fetch in fetches(head):
            fetch.start()

    def one_head(head, carry):
        for fetch in fetches(head):
            fetch.wait()
        work(head)
        for put in puts(head):
            put.start()
        return carry

    lax.fori_loop(0, heads, one_head, 0)
    for head in range(heads):
        for put in puts(head):
            put.wait()


def near_kernel(frames, near, pieces_of, heads, first_head, code_ref, q_hbm, *refs):
    *piece_refs, acc_ref, top_ref, total_ref, q_ref, store, sems = refs
    per_frame = BPF * pieces_of
    width = frames + 2 * REACH

    def fetches(head):
        columns = columns_of(head)
        found = [(q_hbm.at[:, 0, :, columns_of(head + first_head)], q_ref.at[:, :, columns])]
        start = 0
        for piece in piece_refs:
            size = piece.shape[0]
            found.append((piece.at[:, :, :, columns], store.at[pl.ds(start, size), :, :, columns]))
            start += size
        return [pltpu.make_async_copy(a, b, sems.at[head, i]) for i, (a, b) in enumerate(found)]

    def item(frame, head):
        columns = columns_of(head)
        own = (frame + near) * BPF * pieces_of
        keys, values, masks = [], [], []
        for b in range(BPF):
            keys.append(flat(store[pl.ds(own + b * pieces_of, pieces_of), 0, :, columns]))
            values.append(flat(store[pl.ds(own + b * pieces_of, pieces_of), 1, :, columns]))
            masks.append(None)
        for other in range(frames + 2 * near - 1):
            relative = other - near
            relative = relative + jnp.where(relative >= frame, 1, 0)
            codes = [code_ref[(frame * BPF + b) * width + relative + REACH] for b in range(BPF)]
            pick = jnp.maximum(codes[0], codes[1]) // 2
            place = ((relative + near) * BPF + pick) * pieces_of
            keys.append(flat(store[pl.ds(place, pieces_of), 0, :, columns]))
            values.append(flat(store[pl.ds(place, pieces_of), 1, :, columns]))
            masks.append(mask_of(codes))
        queries = flat(q_ref[pl.ds(frame * per_frame, per_frame), :, columns])
        tiles = masked_scores(queries, keys, masks)
        tops = [largest(tiles[b]) for b in range(BPF)]
        mixed, totals = weighted(tiles, tops, values)
        acc_ref[head, frame] = mixed
        top_ref[head, frame] = jnp.broadcast_to(jnp.concatenate(tops, axis=0), mixed.shape)
        total_ref[head, frame] = jnp.broadcast_to(totals, mixed.shape)

    together = math.gcd(frames, 4)

    def work(head):
        def step(index, carry):
            for offset in range(together):
                item(index * together + offset, head)
            return carry

        lax.fori_loop(0, frames // together, step, 0)

    each_head(heads, fetches, lambda head: [], work)


def far_kernel(frames, near, pieces_of, heads, first_head, code_ref, q_hbm, *refs):
    left_hbm, right_hbm, acc_ref, top_ref, total_ref, out_hbm, token, q_ref, left, right, out_ref, sems, put_sems = refs
    token[...] = jnp.zeros_like(token)
    per_frame = BPF * pieces_of
    width = frames + 2 * REACH

    def fetches(head):
        columns = columns_of(head)
        pairs = [
            (q_hbm.at[:, 0, :, columns_of(head + first_head)], q_ref.at[:, :, columns]),
            (left_hbm.at[:, :, :, columns], left.at[:, :, :, columns]),
            (right_hbm.at[:, :, :, columns], right.at[:, :, :, columns]),
        ]
        return [pltpu.make_async_copy(a, b, sems.at[head, i]) for i, (a, b) in enumerate(pairs)]

    def puts(head):
        columns = columns_of(head)
        return [pltpu.make_async_copy(out_ref.at[:, :, columns], out_hbm.at[:, :, columns], put_sems.at[head])]

    def item(frame, head):
        columns = columns_of(head)
        keys, values, masks = [], [], []
        for relative in [*range(-REACH, -near), *range(frames + near, frames + REACH)]:
            if abs(relative - frame) > REACH:
                continue
            codes = [code_ref[(frame * BPF + b) * width + relative + REACH] for b in range(BPF)]
            pick = jnp.maximum(codes[0], codes[1]) // 2
            if relative < 0:
                piece, place = left, (0 if relative == -REACH else (relative + REACH) * BPF - 1 + pick)
            else:
                first = (relative - frames - near) * BPF
                piece, place = right, (first if relative == frames + REACH - 1 else first + pick)
            keys.append(flat(piece[pl.ds(place * pieces_of, pieces_of), 0, :, columns]))
            values.append(flat(piece[pl.ds(place * pieces_of, pieces_of), 1, :, columns]))
            masks.append(mask_of(codes))
        queries = flat(q_ref[pl.ds(frame * per_frame, per_frame), :, columns])
        tiles = masked_scores(queries, keys, masks)
        near_top = top_ref[head, frame]
        tops = [jnp.maximum(largest(tiles[b]), near_top[b * BLK : (b + 1) * BLK]) for b in range(BPF)]
        weights = [
            jnp.concatenate([jnp.exp2((tile - tops[b]) * to_log2).astype(jnp.bfloat16) for tile in tiles[b]], axis=1)
            for b in range(BPF)
        ]
        values = jnp.concatenate(values, axis=0)
        values = jnp.concatenate([values, jnp.ones_like(values)], axis=1)
        product = jnp.dot(jnp.concatenate(weights, axis=0), values, preferred_element_type=jnp.float32)
        mixed, totals = product[:, :HD], product[:, HD:]
        shrink = jnp.exp2((near_top - jnp.concatenate(tops, axis=0)) * to_log2)
        result = (acc_ref[head, frame] * shrink + mixed) / (total_ref[head, frame] * shrink + totals)
        out_ref[pl.ds(frame * per_frame, per_frame), :, columns] = result.astype(jnp.bfloat16).reshape(
            per_frame, BLK // pieces_of, HD
        )

    def work(head):
        for frame in range(frames):
            item(frame, head)

    each_head(heads, fetches, puts, work)


def measured_cost(blocks):
    return dict(flops=6 * blocks * BPF * 4 * BLK * BLK * HD, bytes_accessed=1024, transcendentals=0)


def attend_near(codes, queries, pieces, frames, near, first_head, cost=None, after=()):
    members, _, rows, _ = queries.shape
    pieces_of = BLK // rows
    width = pieces[0].shape[3]
    heads = width // HD
    stored = sum(piece.shape[0] for piece in pieces)

    def body(code_ref, q_hbm, *refs):
        kept = refs[: len(pieces)] + refs[len(pieces) + len(after) :]
        near_kernel(frames, near, pieces_of, heads, first_head, code_ref, q_hbm, *kept)

    partial = jax.ShapeDtypeStruct((heads, frames, BPF * BLK, HD), jnp.float32)
    return pl.pallas_call(
        body,
        out_shape=[partial] * 3,
        in_specs=[pl.BlockSpec(memory_space=pltpu.SMEM)] + [anywhere] * (1 + len(pieces) + len(after)),
        out_specs=[in_vmem] * 3,
        scratch_shapes=[
            pltpu.VMEM((members, rows, width), jnp.bfloat16),
            pltpu.VMEM((stored, 2, rows, width), jnp.bfloat16),
            pltpu.SemaphoreType.DMA((heads, 1 + len(pieces))),
        ],
        compiler_params=pltpu.CompilerParams(vmem_limit_bytes=NEAR_VMEM),
        cost_estimate=pl.CostEstimate(**(cost or measured_cost(frames * heads * (frames + 2 * near + 1)))),
    )(codes, queries, *pieces, *after)


def attend_far(codes, queries, far, partials, frames, near, first_head, cost=None, after=()):
    members, _, rows, _ = queries.shape
    pieces_of = BLK // rows
    width = far[0].shape[3]
    heads = width // HD

    def body(code_ref, q_hbm, *refs):
        far_kernel(frames, near, pieces_of, heads, first_head, code_ref, q_hbm, *refs[:5], *refs[5 + len(after) :])

    result = jax.ShapeDtypeStruct((members, rows, width), jnp.bfloat16)
    return pl.pallas_call(
        body,
        out_shape=[result, jax.ShapeDtypeStruct((8, 128), jnp.float32)],
        in_specs=[pl.BlockSpec(memory_space=pltpu.SMEM)] + [anywhere] * 3 + [in_vmem] * 3 + [anywhere] * len(after),
        out_specs=[in_hbm, in_vmem],
        scratch_shapes=[
            pltpu.VMEM(result.shape, result.dtype),
            *[pltpu.VMEM(array.shape, array.dtype) for array in far],
            pltpu.VMEM(result.shape, result.dtype),
            pltpu.SemaphoreType.DMA((heads, 3)),
            pltpu.SemaphoreType.DMA((heads,)),
        ],
        compiler_params=pltpu.CompilerParams(vmem_limit_bytes=OTHER_VMEM),
        cost_estimate=pl.CostEstimate(**(cost or measured_cost(frames * heads * 4))),
    )(codes, queries, *far, *partials, *after)


def on_device(outer, inner, q_proj, k_proj, v_proj, kv_list):
    frames = inner
    rows, model_width = q_proj.shape
    team = ("inner", "rep", "uly")
    team_size = frames * BPF * BLK // rows
    heads_here = model_width // HD // team_size
    pieces_of = BLK // rows
    per_frame = BPF * pieces_of
    my_group = lax.axis_index("outer")

    def rows_of(reader_frame, count):
        start = jnp.clip(reader_frame * BPF, 0, kv_list.shape[0] - count * BPF)
        return lax.dynamic_slice_in_dim(kv_list, start, count * BPF, 0)

    lists = rows_of(my_group * frames, frames).reshape(frames * BPF, 1, -1)
    first_ids = BPF * (my_group * frames - REACH + lax.broadcasted_iota(jnp.int32, (1, frames + 2 * REACH, 1), 1))
    hits = jnp.where(lists == first_ids, 1, 0) + jnp.where(lists == first_ids + 1, 2, 0)
    codes = jnp.sum(jnp.where(lists >= 0, hits, 0), axis=-1).reshape(-1)

    def picked(reader_frame, holder_frame):
        return jnp.any(rows_of(reader_frame, 1) == holder_frame * BPF + 1).astype(jnp.int32)

    assert sum(CHUNKS) == heads_here
    widths = [heads * HD for heads in CHUNKS]
    lows = [sum(CHUNKS[:c]) for c in range(len(CHUNKS))]
    starts = [low * team_size * HD for low in lows]

    def exchange(array):
        return lax.all_to_all(array, team, split_axis=0, concat_axis=0, tiled=True)

    def shifted(array, heading, hop):
        places = range(outer)
        route = [(i, i + heading) for i in places if i + heading in places and i - (hop - 1) * heading in places]
        return lax.ppermute(array, "outer", route)

    hops = []
    for hop in range(1, -(-REACH // frames) + 1):
        spare = hop * frames - REACH
        hops.append((frames - max(0, spare), spare >= 0))

    def forwarded(held, held_frames, keep, single, after):
        whole = (keep - 1 if single else keep) * per_frame
        if single:
            from_left, from_right = (my_group + 1) * frames, my_group * frames - 1
            edges = held[0].shape[0] - whole - per_frame, whole
            edge_places = jnp.stack(
                [
                    edges[0] + pieces_of * picked(from_left, from_left - REACH),
                    edges[1] + pieces_of * picked(from_right, from_right + REACH),
                ]
            )
            return list(select(held, edge_places, pieces_of, whole, after))
        if keep < held_frames:
            return [held[0][held[0].shape[0] - whole :], held[1][:whole]]
        return held

    def first_hop(own):
        assert hops[0] == (frames, False)
        return [[shifted(own, 1, 1), shifted(own, -1, 1)]]

    def selected(arrivals, after=()):
        for hop in range(1, len(hops)):
            to_send = forwarded(arrivals[-1], hops[hop - 1][0], *hops[hop], after if hop == len(hops) - 1 else ())
            if hop < len(hops) - 1:
                arrivals.append([shifted(to_send[0], 1, hop + 1), shifted(to_send[1], -1, hop + 1)])
        return to_send

    def last_hop(arrivals, to_send):
        arrivals.append([shifted(to_send[0], 1, len(hops)), shifted(to_send[1], -1, len(hops))])

    chunks = range(len(CHUNKS))
    near = (len(hops) - 1) * frames
    packed = [pack([k_proj, v_proj], [starts[c]], [widths[c]], team_size) for c in chunks]
    owned = [exchange(array) for array in packed]
    queries = exchange(pack([q_proj], starts, widths, team_size, after=packed[-1:]))
    arrivals, sent, tokens, outs = [], [], [], []
    partials = {}

    def attend_rest(c, after, cost):
        far = arrivals[c][-1]
        result, token = attend_far(codes, queries, far, partials[c], frames, near, lows[c], cost, after=after)
        tokens.append(token)
        if outs:
            result, outs[-1] = lax.optimization_barrier((result, outs[-1]))
        outs.append(exchange(result))

    for c in chunks:
        arrivals.append(first_hop(owned[c]))
        sent.append(selected(arrivals[c], after=partials[c - 1] if c > 0 else ()))
        order = [a[0] for a in arrivals[c][::-1]] + [owned[c]] + [a[1] for a in arrivals[c]]
        last_hop(arrivals[c], sent[c])
        if c > 0:
            attend_rest(c - 1, sent[c], None)
        after = sent[c] + tokens[-1:]
        cost = little if c == len(CHUNKS) - 1 else None
        partials[c] = list(attend_near(codes, queries, order, frames, near, lows[c], cost, after=after))
    attend_rest(chunks[-1], (), little)
    return unpack(outs, starts, model_width)


def solution(mesh):
    sizes = dict(mesh.shape)
    members = sizes["uly"] * sizes["rep"]
    heads = 40
    inner = max(
        i for i in range(1, sizes["ctx"] + 1) if sizes["ctx"] % i == 0 and heads % (i * members) == 0
    )
    outer = sizes["ctx"] // inner
    finer = Mesh(
        mesh.devices.reshape(sizes["groups"], outer, inner, sizes["uly"], sizes["rep"]),
        ("groups", "outer", "inner", "uly", "rep"),
    )
    split = P(("groups", "outer", "inner", "rep", "uly"), None)
    return jax.shard_map(
        functools.partial(on_device, outer, inner),
        mesh=finer,
        in_specs=(split, split, split, P("groups", None)),
        out_specs=split,
        check_vma=False,
    )
```

```python
import functools
import math

import jax
import jax.numpy as jnp
from jax import lax
from jax.experimental import pallas as pl
from jax.experimental.pallas import tpu as pltpu
from jax.sharding import Mesh, PartitionSpec as P

HD = 128
BLK = 128
BPF = 2
REACH = 7
CHUNKS = (2, 3)
PACK_VMEM = 60 * 1024 * 1024
NEAR_VMEM = 24 * 1024 * 1024
OTHER_VMEM = 14 * 1024 * 1024
little = dict(flops=1024, bytes_accessed=1024, transcendentals=0)
some = dict(flops=20_000_000_000, bytes_accessed=1024, transcendentals=0)
much = dict(flops=100_000_000_000, bytes_accessed=1024, transcendentals=0)

very_low = -1e30
to_log2 = math.log2(math.e) * HD ** -0.5


def staged_copies(steps, sems):
    count = len(steps)
    fetches = [pltpu.make_async_copy(s, stage, sems.at[i]) for i, (s, stage, t) in enumerate(steps)]
    puts = [pltpu.make_async_copy(stage, t, sems.at[count + i]) for i, (s, stage, t) in enumerate(steps)]
    for fetch in fetches:
        fetch.start()
    for fetch, put in zip(fetches, puts):
        fetch.wait()
        put.start()
    for put in puts:
        put.wait()


anywhere = pl.BlockSpec(memory_space=pl.ANY)
in_hbm = pl.BlockSpec(memory_space=pltpu.HBM)
in_vmem = pl.BlockSpec(memory_space=pltpu.VMEM)


def copy_call(plan, shapes, count, operands, scalars=(), after=(), cost=little):
    def body(*refs):
        first = len(scalars)
        last = first + len(operands)
        results = refs[last + len(after) :]
        n = len(shapes)
        staged_copies(plan(refs[:first], refs[first:last], results[:n], results[n : 2 * n]), results[2 * n])

    return pl.pallas_call(
        body,
        out_shape=shapes,
        in_specs=[pl.BlockSpec(memory_space=pltpu.SMEM)] * len(scalars) + [anywhere] * (len(operands) + len(after)),
        out_specs=[anywhere] * len(shapes),
        scratch_shapes=[pltpu.VMEM(s.shape, s.dtype) for s in shapes] + [pltpu.SemaphoreType.DMA((2 * count,))],
        compiler_params=pltpu.CompilerParams(vmem_limit_bytes=OTHER_VMEM),
        cost_estimate=pl.CostEstimate(**cost),
    )(*scalars, *operands, *after)


def pack(arrays, starts, widths, team_size, after=()):
    rows = arrays[0].shape[0]
    lows = [sum(widths[:i]) for i in range(len(widths))]
    count = len(arrays) * len(starts)

    def body(*refs):
        sources = refs[: len(arrays)]
        out, *stages, sems = refs[len(arrays) + len(after) :]
        fetches, puts = [], []
        for kind, source in enumerate(sources):
            for number, (start, width, low) in enumerate(zip(starts, widths, lows)):
                stage = stages[number].at[kind]
                place = len(fetches)
                columns = pl.ds(start, team_size * width)
                fetches.append(pltpu.make_async_copy(source.at[:, columns], stage, sems.at[place, team_size]))
                puts.append(
                    [
                        pltpu.make_async_copy(
                            stage.at[:, pl.ds(member * width, width)],
                            out.at[member, kind, :, pl.ds(low, width)],
                            sems.at[place, member],
                        )
                        for member in range(team_size)
                    ]
                )
        for fetch in fetches:
            fetch.start()
        for fetch, some_puts in zip(fetches, puts):
            fetch.wait()
            for put in some_puts:
                put.start()
        for some_puts in puts:
            for put in some_puts:
                put.wait()

    return pl.pallas_call(
        body,
        out_shape=jax.ShapeDtypeStruct((team_size, len(arrays), rows, sum(widths)), jnp.bfloat16),
        in_specs=[anywhere] * (len(arrays) + len(after)),
        out_specs=anywhere,
        scratch_shapes=[
            *[pltpu.VMEM((len(arrays), rows, team_size * width), jnp.bfloat16) for width in widths],
            pltpu.SemaphoreType.DMA((count, team_size + 1)),
        ],
        compiler_params=pltpu.CompilerParams(vmem_limit_bytes=PACK_VMEM),
        cost_estimate=pl.CostEstimate(**some),
    )(*arrays, *after)


def unpack(parts, starts, model_width):
    members, rows, _ = parts[0].shape
    count = members * len(parts)

    def body(*refs):
        *sources, out, sems = refs
        puts = []
        for start, source in zip(starts, sources):
            width = source.shape[2]
            for member in range(members):
                columns = pl.ds(start + member * width, width)
                puts.append(pltpu.make_async_copy(source.at[member], out.at[:, columns], sems.at[len(puts)]))
                puts[-1].start()
        for put in puts:
            put.wait()

    return pl.pallas_call(
        body,
        out_shape=jax.ShapeDtypeStruct((rows, model_width), jnp.bfloat16),
        in_specs=[pl.BlockSpec(memory_space=pltpu.VMEM)] * len(parts),
        out_specs=in_hbm,
        scratch_shapes=[pltpu.SemaphoreType.DMA((count,))],
        compiler_params=pltpu.CompilerParams(vmem_limit_bytes=8 * 1024 * 1024),
        cost_estimate=pl.CostEstimate(**little),
    )(*parts)


def select(held, places, count, whole, after=()):
    def plan(scalars, sources, outs, stages):
        (place_ref,) = scalars
        steps = []
        for side, (source, stage, out) in enumerate(zip(sources, stages, outs)):
            one = pl.ds(0 if side == 0 else whole, count)
            steps.append((source.at[pl.ds(place_ref[side], count)], stage.at[one], out.at[one]))
            for low in range(0, whole, count):
                rest = pl.ds(low + (count if side == 0 else 0), count)
                kept = pl.ds(low + (source.shape[0] - whole if side == 0 else 0), count)
                steps.append((source.at[kept], stage.at[rest], out.at[rest]))
        return steps

    shapes = [jax.ShapeDtypeStruct((count + whole,) + array.shape[1:], array.dtype) for array in held]
    return copy_call(plan, shapes, 2 * (1 + whole // count), held, scalars=[places], after=after, cost=much)


def columns_of(head):
    return pl.ds(pl.multiple_of(head * HD, HD), HD)


def flat(rows):
    return rows.reshape(rows.shape[0] * rows.shape[1], HD)


def masked_scores(queries, keys, masks):
    tiles = [[] for _ in range(BPF)]
    for first in range(0, len(keys), 2):
        some = jnp.concatenate(keys[first : first + 2], axis=0)
        scores = lax.dot_general(queries, some, (((1,), (1,)), ((), ())), preferred_element_type=jnp.float32)
        for side, mask in enumerate(masks[first : first + 2]):
            for b in range(BPF):
                tile = scores[b * BLK : (b + 1) * BLK, side * BLK : (side + 1) * BLK]
                tiles[b].append(tile if mask is None else tile + mask[b])
    return tiles


def largest(tiles):
    return jnp.max(functools.reduce(jnp.maximum, tiles), axis=1, keepdims=True)


def weighted(tiles, tops, values):
    weights = [
        jnp.concatenate([jnp.exp2((tile - tops[b]) * to_log2).astype(jnp.bfloat16) for tile in tiles[b]], axis=1)
        for b in range(BPF)
    ]
    values = jnp.concatenate(values, axis=0)
    values = jnp.concatenate([values, jnp.ones_like(values)], axis=1)
    product = jnp.dot(jnp.concatenate(weights, axis=0), values, preferred_element_type=jnp.float32)
    return product[:, :HD], product[:, HD:]


def mask_of(codes):
    return [jnp.where(code > 0, 0.0, very_low).astype(jnp.float32) for code in codes]


def each_head(heads, fetches, puts, work):
    for head in range(heads):
        for fetch in fetches(head):
            fetch.start()

    def one_head(head, carry):
        for fetch in fetches(head):
            fetch.wait()
        work(head)
        for put in puts(head):
            put.start()
        return carry

    lax.fori_loop(0, heads, one_head, 0)
    for head in range(heads):
        for put in puts(head):
            put.wait()


def near_kernel(frames, near, pieces_of, heads, first_head, code_ref, q_hbm, *refs):
    *piece_refs, acc_ref, top_ref, total_ref, q_ref, store, sems = refs
    per_frame = BPF * pieces_of
    width = frames + 2 * REACH

    def fetches(head):
        columns = columns_of(head)
        found = [(q_hbm.at[:, 0, :, columns_of(head + first_head)], q_ref.at[:, :, columns])]
        start = 0
        for piece in piece_refs:
            size = piece.shape[0]
            found.append((piece.at[:, :, :, columns], store.at[pl.ds(start, size), :, :, columns]))
            start += size
        return [pltpu.make_async_copy(a, b, sems.at[head, i]) for i, (a, b) in enumerate(found)]

    def item(frame, head):
        columns = columns_of(head)
        own = (frame + near) * BPF * pieces_of
        keys, values, masks = [], [], []
        for b in range(BPF):
            keys.append(flat(store[pl.ds(own + b * pieces_of, pieces_of), 0, :, columns]))
            values.append(flat(store[pl.ds(own + b * pieces_of, pieces_of), 1, :, columns]))
            masks.append(None)
        for other in range(frames + 2 * near - 1):
            relative = other - near
            relative = relative + jnp.where(relative >= frame, 1, 0)
            codes = [code_ref[(frame * BPF + b) * width + relative + REACH] for b in range(BPF)]
            pick = jnp.maximum(codes[0], codes[1]) // 2
            place = ((relative + near) * BPF + pick) * pieces_of
            keys.append(flat(store[pl.ds(place, pieces_of), 0, :, columns]))
            values.append(flat(store[pl.ds(place, pieces_of), 1, :, columns]))
            masks.append(mask_of(codes))
        queries = flat(q_ref[pl.ds(frame * per_frame, per_frame), :, columns])
        tiles = masked_scores(queries, keys, masks)
        tops = [largest(tiles[b]) for b in range(BPF)]
        mixed, totals = weighted(tiles, tops, values)
        acc_ref[head, frame] = mixed
        top_ref[head, frame] = jnp.broadcast_to(jnp.concatenate(tops, axis=0), mixed.shape)
        total_ref[head, frame] = totals

    together = math.gcd(frames, 4)

    def work(head):
        def step(index, carry):
            for offset in range(together):
                item(index * together + offset, head)
            return carry

        lax.fori_loop(0, frames // together, step, 0)

    each_head(heads, fetches, lambda head: [], work)


def far_kernel(frames, near, pieces_of, heads, first_head, code_ref, q_hbm, *refs):
    left_hbm, right_hbm, acc_ref, top_ref, total_ref, out_hbm, token, q_ref, left, right, out_ref, sems, put_sems = refs
    token[...] = jnp.zeros_like(token)
    per_frame = BPF * pieces_of
    width = frames + 2 * REACH

    def fetches(head):
        columns = columns_of(head)
        pairs = [
            (q_hbm.at[:, 0, :, columns_of(head + first_head)], q_ref.at[:, :, columns]),
            (left_hbm.at[:, :, :, columns], left.at[:, :, :, columns]),
            (right_hbm.at[:, :, :, columns], right.at[:, :, :, columns]),
        ]
        return [pltpu.make_async_copy(a, b, sems.at[head, i]) for i, (a, b) in enumerate(pairs)]

    def puts(head):
        columns = columns_of(head)
        return [pltpu.make_async_copy(out_ref.at[:, :, columns], out_hbm.at[:, :, columns], put_sems.at[head])]

    def item(frame, head):
        columns = columns_of(head)
        keys, values, masks = [], [], []
        for relative in [*range(-REACH, -near), *range(frames + near, frames + REACH)]:
            if abs(relative - frame) > REACH:
                continue
            codes = [code_ref[(frame * BPF + b) * width + relative + REACH] for b in range(BPF)]
            pick = jnp.maximum(codes[0], codes[1]) // 2
            if relative < 0:
                piece, place = left, (0 if relative == -REACH else (relative + REACH) * BPF - 1 + pick)
            else:
                first = (relative - frames - near) * BPF
                piece, place = right, (first if relative == frames + REACH - 1 else first + pick)
            keys.append(flat(piece[pl.ds(place * pieces_of, pieces_of), 0, :, columns]))
            values.append(flat(piece[pl.ds(place * pieces_of, pieces_of), 1, :, columns]))
            masks.append(mask_of(codes))
        queries = flat(q_ref[pl.ds(frame * per_frame, per_frame), :, columns])
        tiles = masked_scores(queries, keys, masks)
        near_top = top_ref[head, frame]
        tops = [jnp.maximum(largest(tiles[b]), near_top[b * BLK : (b + 1) * BLK]) for b in range(BPF)]
        mixed, totals = weighted(tiles, tops, values)
        shrink = jnp.exp2((near_top - jnp.concatenate(tops, axis=0)) * to_log2)
        result = (acc_ref[head, frame] * shrink + mixed) / (total_ref[head, frame] * shrink + totals)
        out_ref[pl.ds(frame * per_frame, per_frame), :, columns] = result.astype(jnp.bfloat16).reshape(
            per_frame, BLK // pieces_of, HD
        )

    def work(head):
        for frame in range(frames):
            item(frame, head)

    each_head(heads, fetches, puts, work)


def measured_cost(blocks):
    return dict(flops=6 * blocks * BPF * 4 * BLK * BLK * HD, bytes_accessed=1024, transcendentals=0)


def attend_near(codes, queries, pieces, frames, near, first_head, cost=None, after=()):
    members, _, rows, _ = queries.shape
    pieces_of = BLK // rows
    width = pieces[0].shape[3]
    heads = width // HD
    stored = sum(piece.shape[0] for piece in pieces)

    def body(code_ref, q_hbm, *refs):
        kept = refs[: len(pieces)] + refs[len(pieces) + len(after) :]
        near_kernel(frames, near, pieces_of, heads, first_head, code_ref, q_hbm, *kept)

    partial = jax.ShapeDtypeStruct((heads, frames, BPF * BLK, HD), jnp.float32)
    return pl.pallas_call(
        body,
        out_shape=[partial] * 3,
        in_specs=[pl.BlockSpec(memory_space=pltpu.SMEM)] + [anywhere] * (1 + len(pieces) + len(after)),
        out_specs=[in_vmem] * 3,
        scratch_shapes=[
            pltpu.VMEM((members, rows, width), jnp.bfloat16),
            pltpu.VMEM((stored, 2, rows, width), jnp.bfloat16),
            pltpu.SemaphoreType.DMA((heads, 1 + len(pieces))),
        ],
        compiler_params=pltpu.CompilerParams(vmem_limit_bytes=NEAR_VMEM),
        cost_estimate=pl.CostEstimate(**(cost or measured_cost(frames * heads * (frames + 2 * near + 1)))),
    )(codes, queries, *pieces, *after)


def attend_far(codes, queries, far, partials, frames, near, first_head, cost=None, after=()):
    members, _, rows, _ = queries.shape
    pieces_of = BLK // rows
    width = far[0].shape[3]
    heads = width // HD

    def body(code_ref, q_hbm, *refs):
        far_kernel(frames, near, pieces_of, heads, first_head, code_ref, q_hbm, *refs[:5], *refs[5 + len(after) :])

    result = jax.ShapeDtypeStruct((members, rows, width), jnp.bfloat16)
    return pl.pallas_call(
        body,
        out_shape=[result, jax.ShapeDtypeStruct((8, 128), jnp.float32)],
        in_specs=[pl.BlockSpec(memory_space=pltpu.SMEM)] + [anywhere] * 3 + [in_vmem] * 3 + [anywhere] * len(after),
        out_specs=[in_hbm, in_vmem],
        scratch_shapes=[
            pltpu.VMEM(result.shape, result.dtype),
            *[pltpu.VMEM(array.shape, array.dtype) for array in far],
            pltpu.VMEM(result.shape, result.dtype),
            pltpu.SemaphoreType.DMA((heads, 3)),
            pltpu.SemaphoreType.DMA((heads,)),
        ],
        compiler_params=pltpu.CompilerParams(vmem_limit_bytes=OTHER_VMEM),
        cost_estimate=pl.CostEstimate(**(cost or measured_cost(frames * heads * 4))),
    )(codes, queries, *far, *partials, *after)


def on_device(outer, inner, q_proj, k_proj, v_proj, kv_list):
    frames = inner
    rows, model_width = q_proj.shape
    team = ("inner", "rep", "uly")
    team_size = frames * BPF * BLK // rows
    heads_here = model_width // HD // team_size
    pieces_of = BLK // rows
    per_frame = BPF * pieces_of
    my_group = lax.axis_index("outer")

    def rows_of(reader_frame, count):
        start = jnp.clip(reader_frame * BPF, 0, kv_list.shape[0] - count * BPF)
        return lax.dynamic_slice_in_dim(kv_list, start, count * BPF, 0)

    lists = rows_of(my_group * frames, frames).reshape(frames * BPF, 1, -1)
    first_ids = BPF * (my_group * frames - REACH + lax.broadcasted_iota(jnp.int32, (1, frames + 2 * REACH, 1), 1))
    hits = jnp.where(lists == first_ids, 1, 0) + jnp.where(lists == first_ids + 1, 2, 0)
    codes = jnp.sum(jnp.where(lists >= 0, hits, 0), axis=-1).reshape(-1)

    def picked(reader_frame, holder_frame):
        return jnp.any(rows_of(reader_frame, 1) == holder_frame * BPF + 1).astype(jnp.int32)

    assert sum(CHUNKS) == heads_here
    widths = [heads * HD for heads in CHUNKS]
    lows = [sum(CHUNKS[:c]) for c in range(len(CHUNKS))]
    starts = [low * team_size * HD for low in lows]

    def exchange(array):
        return lax.all_to_all(array, team, split_axis=0, concat_axis=0, tiled=True)

    def shifted(array, heading, hop):
        places = range(outer)
        route = [(i, i + heading) for i in places if i + heading in places and i - (hop - 1) * heading in places]
        return lax.ppermute(array, "outer", route)

    hops = []
    for hop in range(1, -(-REACH // frames) + 1):
        spare = hop * frames - REACH
        hops.append((frames - max(0, spare), spare >= 0))

    def forwarded(held, held_frames, keep, single, after):
        whole = (keep - 1 if single else keep) * per_frame
        if single:
            from_left, from_right = (my_group + 1) * frames, my_group * frames - 1
            edges = held[0].shape[0] - whole - per_frame, whole
            edge_places = jnp.stack(
                [
                    edges[0] + pieces_of * picked(from_left, from_left - REACH),
                    edges[1] + pieces_of * picked(from_right, from_right + REACH),
                ]
            )
            return list(select(held, edge_places, pieces_of, whole, after))
        if keep < held_frames:
            return [held[0][held[0].shape[0] - whole :], held[1][:whole]]
        return held

    def first_hop(own):
        assert hops[0] == (frames, False)
        return [[shifted(own, 1, 1), shifted(own, -1, 1)]]

    def selected(arrivals, after=()):
        for hop in range(1, len(hops)):
            to_send = forwarded(arrivals[-1], hops[hop - 1][0], *hops[hop], after if hop == len(hops) - 1 else ())
            if hop < len(hops) - 1:
                arrivals.append([shifted(to_send[0], 1, hop + 1), shifted(to_send[1], -1, hop + 1)])
        return to_send

    def last_hop(arrivals, to_send):
        arrivals.append([shifted(to_send[0], 1, len(hops)), shifted(to_send[1], -1, len(hops))])

    chunks = range(len(CHUNKS))
    near = (len(hops) - 1) * frames
    packed = [pack([k_proj, v_proj], [starts[c]], [widths[c]], team_size) for c in chunks]
    owned = [exchange(array) for array in packed]
    queries = exchange(pack([q_proj], starts, widths, team_size, after=packed[-1:]))
    arrivals, sent, tokens, outs = [], [], [], []
    partials = {}

    def attend_rest(c, after, cost):
        far = arrivals[c][-1]
        result, token = attend_far(codes, queries, far, partials[c], frames, near, lows[c], cost, after=after)
        tokens.append(token)
        if outs:
            result, outs[-1] = lax.optimization_barrier((result, outs[-1]))
        outs.append(exchange(result))

    for c in chunks:
        arrivals.append(first_hop(owned[c]))
        sent.append(selected(arrivals[c], after=partials[c - 1] if c > 0 else ()))
        order = [a[0] for a in arrivals[c][::-1]] + [owned[c]] + [a[1] for a in arrivals[c]]
        last_hop(arrivals[c], sent[c])
        if c > 0:
            attend_rest(c - 1, sent[c], None)
        after = sent[c] + tokens[-1:]
        cost = little if c == len(CHUNKS) - 1 else None
        partials[c] = list(attend_near(codes, queries, order, frames, near, lows[c], cost, after=after))
    attend_rest(chunks[-1], (), little)
    return unpack(outs, starts, model_width)


def solution(mesh):
    sizes = dict(mesh.shape)
    members = sizes["uly"] * sizes["rep"]
    heads = 40
    inner = max(
        i for i in range(1, sizes["ctx"] + 1) if sizes["ctx"] % i == 0 and heads % (i * members) == 0
    )
    outer = sizes["ctx"] // inner
    finer = Mesh(
        mesh.devices.reshape(sizes["groups"], outer, inner, sizes["uly"], sizes["rep"]),
        ("groups", "outer", "inner", "uly", "rep"),
    )
    split = P(("groups", "outer", "inner", "rep", "uly"), None)
    return jax.shard_map(
        functools.partial(on_device, outer, inner),
        mesh=finer,
        in_specs=(split, split, split, P("groups", None)),
        out_specs=split,
        check_vma=False,
    )
```

```python
import functools
import math

import jax
import jax.numpy as jnp
from jax import lax
from jax.experimental import pallas as pl
from jax.experimental.pallas import tpu as pltpu
from jax.sharding import Mesh, PartitionSpec as P

HD = 128
BLK = 128
BPF = 2
REACH = 7
CHUNKS = (2, 3)
PACK_VMEM = 60 * 1024 * 1024
NEAR_VMEM = 24 * 1024 * 1024
OTHER_VMEM = 14 * 1024 * 1024
little = dict(flops=1024, bytes_accessed=1024, transcendentals=0)
some = dict(flops=20_000_000_000, bytes_accessed=1024, transcendentals=0)
much = dict(flops=100_000_000_000, bytes_accessed=1024, transcendentals=0)

very_low = -1e30
to_log2 = math.log2(math.e) * HD ** -0.5


def staged_copies(steps, sems):
    count = len(steps)
    fetches = [pltpu.make_async_copy(s, stage, sems.at[i]) for i, (s, stage, t) in enumerate(steps)]
    puts = [pltpu.make_async_copy(stage, t, sems.at[count + i]) for i, (s, stage, t) in enumerate(steps)]
    for fetch in fetches:
        fetch.start()
    for fetch, put in zip(fetches, puts):
        fetch.wait()
        put.start()
    for put in puts:
        put.wait()


anywhere = pl.BlockSpec(memory_space=pl.ANY)
in_hbm = pl.BlockSpec(memory_space=pltpu.HBM)
in_vmem = pl.BlockSpec(memory_space=pltpu.VMEM)


def copy_call(plan, shapes, count, operands, scalars=(), after=(), cost=little):
    def body(*refs):
        first = len(scalars)
        last = first + len(operands)
        results = refs[last + len(after) :]
        n = len(shapes)
        staged_copies(plan(refs[:first], refs[first:last], results[:n], results[n : 2 * n]), results[2 * n])

    return pl.pallas_call(
        body,
        out_shape=shapes,
        in_specs=[pl.BlockSpec(memory_space=pltpu.SMEM)] * len(scalars) + [anywhere] * (len(operands) + len(after)),
        out_specs=[anywhere] * len(shapes),
        scratch_shapes=[pltpu.VMEM(s.shape, s.dtype) for s in shapes] + [pltpu.SemaphoreType.DMA((2 * count,))],
        compiler_params=pltpu.CompilerParams(vmem_limit_bytes=OTHER_VMEM),
        cost_estimate=pl.CostEstimate(**cost),
    )(*scalars, *operands, *after)


def pack(arrays, starts, widths, team_size, after=()):
    rows = arrays[0].shape[0]
    lows = [sum(widths[:i]) for i in range(len(widths))]
    count = len(arrays) * len(starts)

    def body(*refs):
        sources = refs[: len(arrays)]
        out, *stages, sems = refs[len(arrays) + len(after) :]
        fetches, puts = [], []
        for kind, source in enumerate(sources):
            for number, (start, width, low) in enumerate(zip(starts, widths, lows)):
                stage = stages[number].at[kind]
                place = len(fetches)
                columns = pl.ds(start, team_size * width)
                fetches.append(pltpu.make_async_copy(source.at[:, columns], stage, sems.at[place, team_size]))
                puts.append(
                    [
                        pltpu.make_async_copy(
                            stage.at[:, pl.ds(member * width, width)],
                            out.at[member, kind, :, pl.ds(low, width)],
                            sems.at[place, member],
                        )
                        for member in range(team_size)
                    ]
                )
        for fetch in fetches:
            fetch.start()
        for fetch, some_puts in zip(fetches, puts):
            fetch.wait()
            for put in some_puts:
                put.start()
        for some_puts in puts:
            for put in some_puts:
                put.wait()

    return pl.pallas_call(
        body,
        out_shape=jax.ShapeDtypeStruct((team_size, len(arrays), rows, sum(widths)), jnp.bfloat16),
        in_specs=[anywhere] * (len(arrays) + len(after)),
        out_specs=anywhere,
        scratch_shapes=[
            *[pltpu.VMEM((len(arrays), rows, team_size * width), jnp.bfloat16) for width in widths],
            pltpu.SemaphoreType.DMA((count, team_size + 1)),
        ],
        compiler_params=pltpu.CompilerParams(vmem_limit_bytes=PACK_VMEM),
        cost_estimate=pl.CostEstimate(**some),
    )(*arrays, *after)


def unpack(parts, starts, model_width):
    members, rows, _ = parts[0].shape
    count = members * len(parts)

    def body(*refs):
        *sources, out, sems = refs
        puts = []
        for start, source in zip(starts, sources):
            width = source.shape[2]
            for member in range(members):
                columns = pl.ds(start + member * width, width)
                puts.append(pltpu.make_async_copy(source.at[member], out.at[:, columns], sems.at[len(puts)]))
                puts[-1].start()
        for put in puts:
            put.wait()

    return pl.pallas_call(
        body,
        out_shape=jax.ShapeDtypeStruct((rows, model_width), jnp.bfloat16),
        in_specs=[pl.BlockSpec(memory_space=pltpu.VMEM)] * len(parts),
        out_specs=in_hbm,
        scratch_shapes=[pltpu.SemaphoreType.DMA((count,))],
        compiler_params=pltpu.CompilerParams(vmem_limit_bytes=8 * 1024 * 1024),
        cost_estimate=pl.CostEstimate(**little),
    )(*parts)


def select(held, places, count, whole, after=()):
    def plan(scalars, sources, outs, stages):
        (place_ref,) = scalars
        steps = []
        for side, (source, stage, out) in enumerate(zip(sources, stages, outs)):
            one = pl.ds(0 if side == 0 else whole, count)
            steps.append((source.at[pl.ds(place_ref[side], count)], stage.at[one], out.at[one]))
            for low in range(0, whole, count):
                rest = pl.ds(low + (count if side == 0 else 0), count)
                kept = pl.ds(low + (source.shape[0] - whole if side == 0 else 0), count)
                steps.append((source.at[kept], stage.at[rest], out.at[rest]))
        return steps

    shapes = [jax.ShapeDtypeStruct((count + whole,) + array.shape[1:], array.dtype) for array in held]
    return copy_call(plan, shapes, 2 * (1 + whole // count), held, scalars=[places], after=after, cost=much)


def columns_of(head):
    return pl.ds(pl.multiple_of(head * HD, HD), HD)


def flat(rows):
    return rows.reshape(rows.shape[0] * rows.shape[1], HD)


def masked_scores(queries, keys, masks):
    tiles = [[] for _ in range(BPF)]
    for first in range(0, len(keys), 2):
        some = jnp.concatenate(keys[first : first + 2], axis=0)
        scores = lax.dot_general(queries, some, (((1,), (1,)), ((), ())), preferred_element_type=jnp.float32)
        for side, mask in enumerate(masks[first : first + 2]):
            for b in range(BPF):
                tile = scores[b * BLK : (b + 1) * BLK, side * BLK : (side + 1) * BLK]
                tiles[b].append(tile if mask is None else tile + mask[b])
    return tiles


def largest(tiles):
    return jnp.max(functools.reduce(jnp.maximum, tiles), axis=1, keepdims=True)


def weighted(tiles, tops, values):
    weights = [
        jnp.concatenate([jnp.exp2((tile - tops[b]) * to_log2).astype(jnp.bfloat16) for tile in tiles[b]], axis=1)
        for b in range(BPF)
    ]
    values = jnp.concatenate(values, axis=0)
    values = jnp.concatenate([values, jnp.ones_like(values)], axis=1)
    product = jnp.dot(jnp.concatenate(weights, axis=0), values, preferred_element_type=jnp.float32)
    return product[:, :HD], product[:, HD:]


def mask_of(codes):
    return [jnp.where(code > 0, 0.0, very_low).astype(jnp.float32) for code in codes]


def each_head(heads, fetches, puts, work, unrolled=False):
    for head in range(heads):
        for fetch in fetches(head):
            fetch.start()

    def one_head(head, carry):
        for fetch in fetches(head):
            fetch.wait()
        work(head)
        for put in puts(head):
            put.start()
        return carry

    if unrolled:
        for head in range(heads):
            one_head(jnp.int32(head), 0)
    else:
        lax.fori_loop(0, heads, one_head, 0)
    for head in range(heads):
        for put in puts(head):
            put.wait()


def near_kernel(frames, near, pieces_of, heads, first_head, code_ref, q_hbm, *refs):
    *piece_refs, acc_ref, top_ref, total_ref, q_ref, store, sems = refs
    per_frame = BPF * pieces_of
    width = frames + 2 * REACH

    def fetches(head):
        columns = columns_of(head)
        found = [(q_hbm.at[:, 0, :, columns_of(head + first_head)], q_ref.at[:, :, columns])]
        start = 0
        for piece in piece_refs:
            size = piece.shape[0]
            found.append((piece.at[:, :, :, columns], store.at[pl.ds(start, size), :, :, columns]))
            start += size
        return [pltpu.make_async_copy(a, b, sems.at[head, i]) for i, (a, b) in enumerate(found)]

    def item(frame, head):
        columns = columns_of(head)
        own = (frame + near) * BPF * pieces_of
        keys, values, masks = [], [], []
        for b in range(BPF):
            keys.append(flat(store[pl.ds(own + b * pieces_of, pieces_of), 0, :, columns]))
            values.append(flat(store[pl.ds(own + b * pieces_of, pieces_of), 1, :, columns]))
            masks.append(None)
        for other in range(frames + 2 * near - 1):
            relative = other - near
            relative = relative + jnp.where(relative >= frame, 1, 0)
            codes = [code_ref[(frame * BPF + b) * width + relative + REACH] for b in range(BPF)]
            pick = jnp.maximum(codes[0], codes[1]) // 2
            place = ((relative + near) * BPF + pick) * pieces_of
            keys.append(flat(store[pl.ds(place, pieces_of), 0, :, columns]))
            values.append(flat(store[pl.ds(place, pieces_of), 1, :, columns]))
            masks.append(mask_of(codes))
        queries = flat(q_ref[pl.ds(frame * per_frame, per_frame), :, columns])
        tiles = masked_scores(queries, keys, masks)
        tops = [largest(tiles[b]) for b in range(BPF)]
        mixed, totals = weighted(tiles, tops, values)
        acc_ref[head, frame] = mixed
        top_ref[head, frame] = jnp.broadcast_to(jnp.concatenate(tops, axis=0), mixed.shape)
        total_ref[head, frame] = totals

    together = math.gcd(frames, 4)

    def work(head):
        def step(index, carry):
            for offset in range(together):
                item(index * together + offset, head)
            return carry

        lax.fori_loop(0, frames // together, step, 0)

    each_head(heads, fetches, lambda head: [], work)


def far_kernel(frames, near, pieces_of, heads, first_head, code_ref, q_hbm, *refs):
    left_hbm, right_hbm, acc_ref, top_ref, total_ref, out_hbm, token, q_ref, left, right, out_ref, sems, put_sems = refs
    token[...] = jnp.zeros_like(token)
    per_frame = BPF * pieces_of
    width = frames + 2 * REACH

    def fetches(head):
        columns = columns_of(head)
        pairs = [
            (q_hbm.at[:, 0, :, columns_of(head + first_head)], q_ref.at[:, :, columns]),
            (left_hbm.at[:, :, :, columns], left.at[:, :, :, columns]),
            (right_hbm.at[:, :, :, columns], right.at[:, :, :, columns]),
        ]
        return [pltpu.make_async_copy(a, b, sems.at[head, i]) for i, (a, b) in enumerate(pairs)]

    def puts(head):
        columns = columns_of(head)
        return [pltpu.make_async_copy(out_ref.at[:, :, columns], out_hbm.at[:, :, columns], put_sems.at[head])]

    def item(frame, head):
        columns = columns_of(head)
        keys, values, masks = [], [], []
        for relative in [*range(-REACH, -near), *range(frames + near, frames + REACH)]:
            if abs(relative - frame) > REACH:
                continue
            codes = [code_ref[(frame * BPF + b) * width + relative + REACH] for b in range(BPF)]
            pick = jnp.maximum(codes[0], codes[1]) // 2
            if relative < 0:
                piece, place = left, (0 if relative == -REACH else (relative + REACH) * BPF - 1 + pick)
            else:
                first = (relative - frames - near) * BPF
                piece, place = right, (first if relative == frames + REACH - 1 else first + pick)
            keys.append(flat(piece[pl.ds(place * pieces_of, pieces_of), 0, :, columns]))
            values.append(flat(piece[pl.ds(place * pieces_of, pieces_of), 1, :, columns]))
            masks.append(mask_of(codes))
        queries = flat(q_ref[pl.ds(frame * per_frame, per_frame), :, columns])
        tiles = masked_scores(queries, keys, masks)
        near_top = top_ref[head, frame]
        tops = [jnp.maximum(largest(tiles[b]), near_top[b * BLK : (b + 1) * BLK]) for b in range(BPF)]
        mixed, totals = weighted(tiles, tops, values)
        shrink = jnp.exp2((near_top - jnp.concatenate(tops, axis=0)) * to_log2)
        result = (acc_ref[head, frame] * shrink + mixed) / (total_ref[head, frame] * shrink + totals)
        out_ref[pl.ds(frame * per_frame, per_frame), :, columns] = result.astype(jnp.bfloat16).reshape(
            per_frame, BLK // pieces_of, HD
        )

    def work(head):
        for frame in range(frames):
            item(frame, head)

    each_head(heads, fetches, puts, work, unrolled=True)


def measured_cost(blocks):
    return dict(flops=6 * blocks * BPF * 4 * BLK * BLK * HD, bytes_accessed=1024, transcendentals=0)


def attend_near(codes, queries, pieces, frames, near, first_head, cost=None, after=()):
    members, _, rows, _ = queries.shape
    pieces_of = BLK // rows
    width = pieces[0].shape[3]
    heads = width // HD
    stored = sum(piece.shape[0] for piece in pieces)

    def body(code_ref, q_hbm, *refs):
        kept = refs[: len(pieces)] + refs[len(pieces) + len(after) :]
        near_kernel(frames, near, pieces_of, heads, first_head, code_ref, q_hbm, *kept)

    partial = jax.ShapeDtypeStruct((heads, frames, BPF * BLK, HD), jnp.float32)
    return pl.pallas_call(
        body,
        out_shape=[partial] * 3,
        in_specs=[pl.BlockSpec(memory_space=pltpu.SMEM)] + [anywhere] * (1 + len(pieces) + len(after)),
        out_specs=[in_vmem] * 3,
        scratch_shapes=[
            pltpu.VMEM((members, rows, width), jnp.bfloat16),
            pltpu.VMEM((stored, 2, rows, width), jnp.bfloat16),
            pltpu.SemaphoreType.DMA((heads, 1 + len(pieces))),
        ],
        compiler_params=pltpu.CompilerParams(vmem_limit_bytes=NEAR_VMEM),
        cost_estimate=pl.CostEstimate(**(cost or measured_cost(frames * heads * (frames + 2 * near + 1)))),
    )(codes, queries, *pieces, *after)


def attend_far(codes, queries, far, partials, frames, near, first_head, cost=None, after=()):
    members, _, rows, _ = queries.shape
    pieces_of = BLK // rows
    width = far[0].shape[3]
    heads = width // HD

    def body(code_ref, q_hbm, *refs):
        far_kernel(frames, near, pieces_of, heads, first_head, code_ref, q_hbm, *refs[:5], *refs[5 + len(after) :])

    result = jax.ShapeDtypeStruct((members, rows, width), jnp.bfloat16)
    return pl.pallas_call(
        body,
        out_shape=[result, jax.ShapeDtypeStruct((8, 128), jnp.float32)],
        in_specs=[pl.BlockSpec(memory_space=pltpu.SMEM)] + [anywhere] * 3 + [in_vmem] * 3 + [anywhere] * len(after),
        out_specs=[in_hbm, in_vmem],
        scratch_shapes=[
            pltpu.VMEM(result.shape, result.dtype),
            *[pltpu.VMEM(array.shape, array.dtype) for array in far],
            pltpu.VMEM(result.shape, result.dtype),
            pltpu.SemaphoreType.DMA((heads, 3)),
            pltpu.SemaphoreType.DMA((heads,)),
        ],
        compiler_params=pltpu.CompilerParams(vmem_limit_bytes=OTHER_VMEM),
        cost_estimate=pl.CostEstimate(**(cost or measured_cost(frames * heads * 4))),
    )(codes, queries, *far, *partials, *after)


def on_device(outer, inner, q_proj, k_proj, v_proj, kv_list):
    frames = inner
    rows, model_width = q_proj.shape
    team = ("inner", "rep", "uly")
    team_size = frames * BPF * BLK // rows
    heads_here = model_width // HD // team_size
    pieces_of = BLK // rows
    per_frame = BPF * pieces_of
    my_group = lax.axis_index("outer")

    def rows_of(reader_frame, count):
        start = jnp.clip(reader_frame * BPF, 0, kv_list.shape[0] - count * BPF)
        return lax.dynamic_slice_in_dim(kv_list, start, count * BPF, 0)

    lists = rows_of(my_group * frames, frames).reshape(frames * BPF, 1, -1)
    first_ids = BPF * (my_group * frames - REACH + lax.broadcasted_iota(jnp.int32, (1, frames + 2 * REACH, 1), 1))
    hits = jnp.where(lists == first_ids, 1, 0) + jnp.where(lists == first_ids + 1, 2, 0)
    codes = jnp.sum(jnp.where(lists >= 0, hits, 0), axis=-1).reshape(-1)

    def picked(reader_frame, holder_frame):
        return jnp.any(rows_of(reader_frame, 1) == holder_frame * BPF + 1).astype(jnp.int32)

    assert sum(CHUNKS) == heads_here
    widths = [heads * HD for heads in CHUNKS]
    lows = [sum(CHUNKS[:c]) for c in range(len(CHUNKS))]
    starts = [low * team_size * HD for low in lows]

    def exchange(array):
        return lax.all_to_all(array, team, split_axis=0, concat_axis=0, tiled=True)

    def shifted(array, heading, hop):
        places = range(outer)
        route = [(i, i + heading) for i in places if i + heading in places and i - (hop - 1) * heading in places]
        return lax.ppermute(array, "outer", route)

    hops = []
    for hop in range(1, -(-REACH // frames) + 1):
        spare = hop * frames - REACH
        hops.append((frames - max(0, spare), spare >= 0))

    def forwarded(held, held_frames, keep, single, after):
        whole = (keep - 1 if single else keep) * per_frame
        if single:
            from_left, from_right = (my_group + 1) * frames, my_group * frames - 1
            edges = held[0].shape[0] - whole - per_frame, whole
            edge_places = jnp.stack(
                [
                    edges[0] + pieces_of * picked(from_left, from_left - REACH),
                    edges[1] + pieces_of * picked(from_right, from_right + REACH),
                ]
            )
            return list(select(held, edge_places, pieces_of, whole, after))
        if keep < held_frames:
            return [held[0][held[0].shape[0] - whole :], held[1][:whole]]
        return held

    def first_hop(own):
        assert hops[0] == (frames, False)
        return [[shifted(own, 1, 1), shifted(own, -1, 1)]]

    def selected(arrivals, after=()):
        for hop in range(1, len(hops)):
            to_send = forwarded(arrivals[-1], hops[hop - 1][0], *hops[hop], after if hop == len(hops) - 1 else ())
            if hop < len(hops) - 1:
                arrivals.append([shifted(to_send[0], 1, hop + 1), shifted(to_send[1], -1, hop + 1)])
        return to_send

    def last_hop(arrivals, to_send):
        arrivals.append([shifted(to_send[0], 1, len(hops)), shifted(to_send[1], -1, len(hops))])

    chunks = range(len(CHUNKS))
    near = (len(hops) - 1) * frames
    packed = [pack([k_proj, v_proj], [starts[c]], [widths[c]], team_size) for c in chunks]
    owned = [exchange(array) for array in packed]
    queries = exchange(pack([q_proj], starts, widths, team_size, after=packed[-1:]))
    arrivals, sent, tokens, outs = [], [], [], []
    partials = {}

    def attend_rest(c, after, cost):
        far = arrivals[c][-1]
        result, token = attend_far(codes, queries, far, partials[c], frames, near, lows[c], cost, after=after)
        tokens.append(token)
        if outs:
            result, outs[-1] = lax.optimization_barrier((result, outs[-1]))
        outs.append(exchange(result))

    for c in chunks:
        arrivals.append(first_hop(owned[c]))
        sent.append(selected(arrivals[c], after=partials[c - 1] if c > 0 else ()))
        order = [a[0] for a in arrivals[c][::-1]] + [owned[c]] + [a[1] for a in arrivals[c]]
        last_hop(arrivals[c], sent[c])
        if c > 0:
            attend_rest(c - 1, sent[c], None)
        after = sent[c] + tokens[-1:]
        cost = little if c == len(CHUNKS) - 1 else None
        partials[c] = list(attend_near(codes, queries, order, frames, near, lows[c], cost, after=after))
    attend_rest(chunks[-1], (), little)
    return unpack(outs, starts, model_width)


def solution(mesh):
    sizes = dict(mesh.shape)
    members = sizes["uly"] * sizes["rep"]
    heads = 40
    inner = max(
        i for i in range(1, sizes["ctx"] + 1) if sizes["ctx"] % i == 0 and heads % (i * members) == 0
    )
    outer = sizes["ctx"] // inner
    finer = Mesh(
        mesh.devices.reshape(sizes["groups"], outer, inner, sizes["uly"], sizes["rep"]),
        ("groups", "outer", "inner", "uly", "rep"),
    )
    split = P(("groups", "outer", "inner", "rep", "uly"), None)
    return jax.shard_map(
        functools.partial(on_device, outer, inner),
        mesh=finer,
        in_specs=(split, split, split, P("groups", None)),
        out_specs=split,
        check_vma=False,
    )
```
